32 devices in a mesh: dp: 2 (over core), wide: 8 (over z, y), narrow: 2 (over x).
Axes of the slice: x: 2, y: 2, z: 4, core: 2. Of those that a mesh axis runs over, the one named last changes fastest.
Arguments:
- enc_input: bfloat16 [16384, 768], P(('dp', 'wide', 'narrow')), may hold values from -6 to 6
- dec_input: bfloat16 [4096, 768], P(('dp', 'wide', 'narrow')), may hold values from -6 to 6
- enc_lengths: int32 [16, 4], P(('dp', 'wide')), may hold values from 1 to 512, 1024 in all within a row
- dec_lengths: int32 [16, 4], P(('dp', 'wide')), may hold values from 1 to 128, 256 in all within a row
- attn_query: bfloat16 [3, 768, 768], P(None, 'wide', 'narrow'), may hold values from -0.0546875 to 0.0546875
- attn_kv: bfloat16 [3, 2, 768, 768], P(None, None, 'wide', 'narrow'), may hold values from -0.21875 to 0.21875
- attn_out: bfloat16 [3, 768, 768], P(None, 'narrow', 'wide'), may hold values from -0.875 to 0.875
- ffn_up: bfloat16 [2, 768, 3072], P(None, 'wide', 'narrow'), may hold values from -0.21875 to 0.21875
- ffn_down: bfloat16 [2, 3072, 768], P(None, 'narrow', 'wide'), may hold values from -0.109375 to 0.109375
- gains: bfloat16 [6, 768], replicated, may hold values from 0.5 to 1.5
- rel_bias: bfloat16 [2, 32, 12], P(None, None, 'narrow'), may hold values from -4 to 4
- enc_cotangent: bfloat16 [16384, 768], P(('dp', 'wide', 'narrow')), may hold values from -6 to 6
- dec_cotangent: bfloat16 [4096, 768], P(('dp', 'wide', 'narrow')), may hold values from -6 to 6
Outputs:
- enc_output: bfloat16 [16384, 768], P(('dp', 'wide', 'narrow'))
- dec_output: bfloat16 [4096, 768], P(('dp', 'wide', 'narrow'))
- enc_grad: float32 [16384, 768], P(('dp', 'wide', 'narrow'))
- dec_grad: float32 [4096, 768], P(('dp', 'wide', 'narrow'))
- grad_query: float32 [3, 768, 768], P(None, 'wide', 'narrow')
- grad_kv: float32 [3, 2, 768, 768], P(None, None, 'wide', 'narrow')
- grad_out: float32 [3, 768, 768], P(None, 'narrow', 'wide')
- grad_up: float32 [2, 768, 3072], P(None, 'wide', 'narrow')
- grad_down: float32 [2, 3072, 768], P(None, 'narrow', 'wide')
- grad_gains: float32 [6, 768], replicated
- grad_bias: float32 [2, 32, 12], P(None, None, 'narrow')
The draws below stay inside these ranges and needn't reach their ends.
Inputs may be any that keep to these rules, and one draw needn't show every extreme that they name: `enc_lengths`: each row lists the lengths of 4 packed documents in order; they sum to 1024, and the longest is 512. `dec_lengths`: each row lists the decoder lengths of the same 4 documents in order; they sum to 256, and the longest is 128.
All inputs are finite; a program needn't handle non-finite values.
Results may differ from the reference program's by a relative error of at most 0.028.
Values may be sent and summed in bfloat16 or wider, within the bound.
A program may use at most 256 MiB of HBM per device.

```python
import math
import jax
import jax.numpy as jnp
import numpy as np
from jax import lax

D = 768
H = 12
DK = 64
FF = 3072
NB = 32
MAXD = 128
ENC = 1024
DEC = 256
DOCS = 4
NPACK = 16


def levels(key, extent, cuts, least, high):
    loudness, own = 1.0, jax.random.fold_in(key, 6)
    for axis_at, shards_of in cuts:
        heights = jnp.exp(jax.random.uniform(jax.random.fold_in(own, axis_at), (shards_of,), jnp.float32, least / len(cuts), high / len(cuts)))
        loudness = loudness * jnp.repeat(heights, extent[axis_at] // shards_of).reshape([-1 if axis == axis_at else 1 for axis in range(len(extent))])
    return loudness


def length_profile(number_of, total, bound, skew):
    loads = [(1 << 20) // math.isqrt(standing ** skew) + 1 for standing in range(2, number_of + 1)]
    surplus, given = total - bound - (number_of - 1), [1] * (number_of - 1)
    while surplus > 0:
        free = [i for i in range(number_of - 1) if given[i] < bound]
        mass, remaining = sum([loads[i] for i in free]), surplus
        for i in free:
            addition = min(bound - given[i], max(1, remaining * loads[i] // mass), surplus)
            given[i] = given[i] + addition
            surplus = surplus - addition
    return np.array([bound] + given)


def ragged_sizes(rng, amount, total, most, slope):
    if amount == 2:
        one = jax.random.randint(rng, (), max(1, total - most), min(most, total - 1) + 1)
        return jnp.stack([one, total - one])
    tallies = jnp.asarray(length_profile(amount, total, most, slope), jnp.int32)
    twos = (amount - 1) // 2
    source_of, sink = tallies[1:1 + 2 * twos:2], tallies[2:2 + 2 * twos:2]
    slack = jnp.minimum(source_of - 1, most - sink)
    shifted = jax.random.randint(jax.random.fold_in(rng, 1), (twos,), 0, 1 << 20) % (slack + 1)
    tallies = tallies.at[1:1 + 2 * twos:2].set(source_of - shifted).at[2:2 + 2 * twos:2].set(sink + shifted)
    return tallies[jax.random.permutation(jax.random.fold_in(rng, 2), amount)]


def gaussian(key, dims, deviation, most, cuts=(), kind=jnp.bfloat16):
    array = jax.random.normal(key, dims, jnp.float32) * deviation
    if len(cuts) > 0:
        array = levels(key, dims, cuts, -0.22, 0.18) * array
    return jnp.clip(array, min=-most, max=most).astype(kind)


def setup_inputs(seed: int = 0) -> dict:
    key_of = jax.random.split(jax.random.key(seed), 14)
    return {
        "enc_input": gaussian(key_of[0], (NPACK * ENC, D), 1.0, 6.0, ((0, 32),)),
        "dec_input": gaussian(key_of[1], (NPACK * DEC, D), 1.0, 6.0, ((0, 32),)),
        "enc_lengths": jax.vmap(lambda own: ragged_sizes(own, DOCS, ENC, ENC // 2, 0))(jax.random.split(key_of[2], NPACK)).reshape((NPACK, DOCS)).astype(jnp.int32),
        "dec_lengths": jax.vmap(lambda own: ragged_sizes(own, DOCS, DEC, DEC // 2, 0))(jax.random.split(key_of[3], NPACK)).reshape((NPACK, DOCS)).astype(jnp.int32),
        "attn_query": gaussian(key_of[4], (3, D, H * DK), (D * DK // 4) ** -0.5, 0.0546875, ((1, 8), (2, 2))),
        "attn_kv": gaussian(key_of[5], (3, 2, D, H * DK), D ** -0.5, 0.21875, ((2, 8), (3, 2))),
        "attn_out": gaussian(key_of[6], (3, H * DK, D), (H * DK // 16) ** -0.5, 0.875, ((1, 2), (2, 8))),
        "ffn_up": gaussian(key_of[7], (2, D, FF), D ** -0.5, 0.21875, ((1, 8), (2, 2))),
        "ffn_down": gaussian(key_of[8], (2, FF, D), FF ** -0.5, 0.109375, ((1, 2), (2, 8))),
        "gains": jnp.clip(1.0 + 0.1 * jax.random.normal(key_of[9], (6, D), jnp.float32), 0.5, 1.5).astype(jnp.bfloat16),
        "rel_bias": gaussian(key_of[10], (2, NB, H), 1.0, 4.0, ((2, 2),)),
        "enc_cotangent": gaussian(key_of[11], (NPACK * ENC, D), 1.0, 6.0, ((0, 32),)),
        "dec_cotangent": gaussian(key_of[12], (NPACK * DEC, D), 1.0, 6.0, ((0, 32),)),
    }


EPS = 1e-06
NEG = -1e+30
HIGH = lax.Precision.HIGHEST

@jax.custom_vjp
def low(v):
    return lax.optimization_barrier(v.astype(jnp.bfloat16)).astype(jnp.float32)

@jax.custom_vjp
def low_back(v):
    return v

def low_keep(v):
    return (low(v), None)

def low_pass(kept, grad):
    return (grad,)

def back_keep(v):
    return (v, None)

def back_low(kept, grad):
    return (low(grad),)
low.defvjp(low_keep, low_pass)
low_back.defvjp(back_keep, back_low)

def both_low(values):
    return low(low_back(values))

def cutoffs(exact, buckets):
    found = []
    reach = exact
    for target in range(exact + 1, buckets):
        while exact + math.floor(math.log(reach / exact) / math.log(MAXD / exact) * (buckets - exact)) < target:
            reach = reach + 1
        found.append(reach)
    return found

def bucket_index(relative, two_sided):
    if two_sided:
        width = NB // 2
        offset = jnp.where(relative > 0, width, 0)
        distance = jnp.abs(relative)
    else:
        width = NB
        offset = jnp.zeros_like(relative)
        distance = jnp.maximum(-relative, 0)
    exact = width // 2
    beyond = exact + sum(((distance >= limit).astype(jnp.int32) for limit in cutoffs(exact, width)))
    return offset + jnp.where(distance < exact, distance, beyond)

def segment_ids(lengths, count):
    bounds = jnp.cumsum(lengths).astype(jnp.int32)
    places = jnp.arange(count, dtype=jnp.int32)
    return lax.optimization_barrier(jnp.sum((places[:, None] >= bounds[None, :]).astype(jnp.int32), axis=1)).astype(jnp.int32)

def rms_norm(values, gain):
    return values * lax.rsqrt(lax.optimization_barrier(jnp.mean(values * values, axis=-1, keepdims=True)) + EPS) * gain

def attend(normed_query, normed_keys, weight_query, weight_key, weight_value, weight_out, table, two_sided, query_segments, key_segments, causal):
    count = normed_query.shape[0]
    cols = normed_keys.shape[0]
    query = both_low(jnp.dot(normed_query, weight_query, precision=HIGH)).reshape(count, H, DK)
    keys = both_low(jnp.dot(normed_keys, weight_key, precision=HIGH)).reshape(cols, H, DK)
    values = both_low(jnp.dot(normed_keys, weight_value, precision=HIGH)).reshape(cols, H, DK)
    block = min(512, count)
    key_places = jnp.arange(cols, dtype=jnp.int32)

    def one_block(index):
        first = (index * block).astype(jnp.int32)
        query_rows = lax.dynamic_slice_in_dim(query, first, block, 0)
        scores = jnp.einsum('qhd,khd->hqk', query_rows, keys, precision=HIGH)
        query_places = first + jnp.arange(block, dtype=jnp.int32)
        if table is not None:
            relative = key_places[None, :] - query_places[:, None]
            scores = scores + jnp.transpose(table[bucket_index(relative, two_sided)], (2, 0, 1))
        scores = low_back(scores)
        segs = lax.dynamic_slice_in_dim(query_segments, first, block, 0)
        allowed = segs[:, None] == key_segments[None, :]
        if causal:
            allowed = allowed & (key_places[None, :] <= query_places[:, None])
        scores = jnp.where(allowed[None], scores, NEG)
        probs = jnp.exp(scores - jax.nn.logsumexp(scores, axis=-1, keepdims=True))
        return jnp.einsum('hqk,khd->qhd', low(probs), values, precision=HIGH)
    context = lax.map(jax.checkpoint(one_block), jnp.arange(count // block, dtype=jnp.int32))
    context = both_low(context.reshape(count, H * DK))
    return low_back(jnp.dot(context, weight_out, precision=HIGH))

def feed_forward(normed, weight_up, weight_down):
    hidden = low_back(jnp.dot(normed, weight_up, precision=HIGH))
    active = low(jax.nn.gelu(hidden, approximate=True))
    return low_back(jnp.dot(active, weight_down, precision=HIGH))

def forward_pack(enc_state, dec_state, enc_len, dec_len, attn_query, attn_kv, attn_out, ffn_up, ffn_down, gains, rel_bias):
    enc_seg = segment_ids(enc_len, ENC)
    dec_seg = segment_ids(dec_len, DEC)
    normed = low(rms_norm(enc_state, gains[0]))
    enc_state = enc_state + attend(normed, normed, attn_query[0], attn_kv[0, 0], attn_kv[0, 1], attn_out[0], rel_bias[0], True, enc_seg, enc_seg, False)
    normed = low(rms_norm(enc_state, gains[1]))
    enc_state = enc_state + feed_forward(normed, ffn_up[0], ffn_down[0])
    memory = low(rms_norm(enc_state, gains[5]))
    normed = low(rms_norm(dec_state, gains[2]))
    dec_state = dec_state + attend(normed, normed, attn_query[1], attn_kv[1, 0], attn_kv[1, 1], attn_out[1], rel_bias[1], False, dec_seg, dec_seg, True)
    normed = low(rms_norm(dec_state, gains[3]))
    dec_state = dec_state + attend(normed, memory, attn_query[2], attn_kv[2, 0], attn_kv[2, 1], attn_out[2], None, False, dec_seg, enc_seg, False)
    normed = low(rms_norm(dec_state, gains[4]))
    dec_state = dec_state + feed_forward(normed, ffn_up[1], ffn_down[1])
    return (enc_state, dec_state)

def reference(enc_input, dec_input, enc_lengths, dec_lengths, attn_query, attn_kv, attn_out, ffn_up, ffn_down, gains, rel_bias, enc_cotangent, dec_cotangent):
    params = tuple((piece.astype(jnp.float32) for piece in (attn_query, attn_kv, attn_out, ffn_up, ffn_down, gains, rel_bias)))
    enc_rows = enc_input.astype(jnp.float32).reshape(NPACK, ENC, D)
    dec_rows = dec_input.astype(jnp.float32).reshape(NPACK, DEC, D)
    enc_cots = enc_cotangent.astype(jnp.float32).reshape(NPACK, ENC, D)
    dec_cots = dec_cotangent.astype(jnp.float32).reshape(NPACK, DEC, D)

    def one_pack(carry, inputs):
        enc_pack, dec_pack, enc_len, dec_len, enc_cot, dec_cot = inputs

        def forward(enc_state, dec_state, *weights):
            return forward_pack(enc_state, dec_state, enc_len, dec_len, *weights)
        outputs, pull = jax.vjp(forward, enc_pack, dec_pack, *params)
        grads = pull((enc_cot, dec_cot))
        carry = tuple((total + piece for total, piece in zip(carry, grads[2:])))
        return (carry, (outputs[0], outputs[1], grads[0], grads[1]))
    start = tuple((jnp.zeros_like(piece) for piece in params))
    totals, stacked = lax.scan(one_pack, start, (enc_rows, dec_rows, enc_lengths, dec_lengths, enc_cots, dec_cots))
    enc_output = stacked[0].reshape(NPACK * ENC, D).astype(jnp.bfloat16)
    dec_output = stacked[1].reshape(NPACK * DEC, D).astype(jnp.bfloat16)
    enc_grad = stacked[2].reshape(NPACK * ENC, D)
    dec_grad = stacked[3].reshape(NPACK * DEC, D)
    return (enc_output, dec_output, enc_grad, dec_grad, totals[0], totals[1], totals[2], totals[3], totals[4], totals[5], totals[6])
```

```python
import functools
import math

import jax
import jax.numpy as jnp
from jax import lax
from jax.sharding import PartitionSpec as P
import jax.experimental.pallas as pl
import jax.experimental.pallas.tpu as pltpu

H = 12
DK = 64
NB = 32
MAXD = 128
ENC = 1024
DEC = 256


EPS = 1e-06
NEG = -1e30
HIGH = lax.Precision.HIGHEST
VMEM_BYTES = 56 * 2**20


def cutoffs(exact, buckets):
    found = []
    reach = exact
    for target in range(exact + 1, buckets):
        while (
            exact + math.floor(math.log(reach / exact) / math.log(MAXD / exact) * (buckets - exact))
            < target
        ):
            reach = reach + 1
        found.append(reach)
    return found


def bucket_index(relative, two_sided):
    if two_sided:
        width = NB // 2
        offset = jnp.where(relative > 0, width, 0)
        distance = jnp.abs(relative)
    else:
        width = NB
        offset = jnp.zeros_like(relative)
        distance = jnp.maximum(-relative, 0)
    exact = width // 2
    beyond = exact + sum(((distance >= limit).astype(jnp.int32) for limit in cutoffs(exact, width)))
    return offset + jnp.where(distance < exact, distance, beyond)


def segment_ids(lengths, count):
    bounds = jnp.cumsum(lengths)
    places = jnp.arange(count, dtype=jnp.int32)
    return jnp.sum((places[:, None] >= bounds[None, :]).astype(jnp.int32), axis=1)


def rms_norm(values, gain):
    return values * lax.rsqrt(jnp.mean(values * values, axis=-1, keepdims=True) + EPS) * gain


def gelu_tanh(values):
    return jax.nn.gelu(values, approximate=True)


PAIR = 128


def offset_buckets(span, two_sided):
    places = jnp.arange(2 * span, dtype=jnp.int32)[None, :]
    relative = lax.rem(places - jnp.arange(8, dtype=jnp.int32)[:, None] + 2 * span, 2 * span) - span
    buckets = bucket_index(relative.reshape(-1), two_sided)
    return (buckets[None, :] == jnp.arange(NB, dtype=jnp.int32)[:, None]).astype(jnp.bfloat16)


def base_rows(table, span, two_sided):
    heads = table.shape[1]
    rows = lax.dot_general(
        table, offset_buckets(span, two_sided), (((0,), (0,)), ((), ())), preferred_element_type=jnp.float32
    )
    return rows.reshape(heads // 2, 2, 8, 2 * span)


def table_grad(offset_sums, span, two_sided):
    heads = 2 * offset_sums.shape[0]
    return lax.dot_general(
        offset_buckets(span, two_sided).astype(jnp.float32),
        offset_sums.reshape(heads, 16 * span),
        (((1,), (1,)), ((), ())),
        precision=HIGH,
        preferred_element_type=jnp.float32,
    )


def dot_nt(a, b):
    return lax.dot_general(a, b, (((1,), (1,)), ((), ())), preferred_element_type=jnp.float32)


def dot_tn(a, b):
    return lax.dot_general(a, b, (((0,), (0,)), ((), ())), preferred_element_type=jnp.float32)


def dot_nn(a, b):
    return lax.dot_general(a, b, (((1,), (0,)), ((), ())), preferred_element_type=jnp.float32)


def split_heads(block):
    lane = lax.broadcasted_iota(jnp.int32, block.shape, 1)
    zero = jnp.zeros_like(block)
    return jnp.where(lane < DK, block, zero), jnp.where(lane < DK, zero, block)


def attend_kernel(block, keys_count, causal, biased, *refs):
    if biased:
        qseg, kseg, base, q_ref, k_ref, v_ref, e_ref, c_ref, inv_ref, strip = refs
    else:
        qseg, kseg, q_ref, k_ref, v_ref, e_ref, c_ref, inv_ref = refs
    i = pl.program_id(1)
    if biased:
        wide = 2 * keys_count

        @pl.when(i == 0)
        def _():
            for head in range(2):
                rows = base[0, head]
                for a in range(block // 8):
                    strip[head, 8 * a : 8 * a + 8, :] = pltpu.roll(rows, (8 * a + wide - block) % wide, 1)

    allowed = qseg[...] == kseg[...]
    if causal:
        rows = lax.broadcasted_iota(jnp.int32, (block, keys_count), 0) + i * block
        allowed = allowed & (lax.broadcasted_iota(jnp.int32, (block, keys_count), 1) <= rows)
    q_heads = split_heads(q_ref[...])
    v_heads = split_heads(v_ref[...])
    inverses = []
    context = None
    for head in range(2):
        scores = dot_nt(q_heads[head], k_ref[...])
        if biased:
            start = pl.multiple_of((keys_count // block - 1 - i) * block, block)
            scores = scores + strip[head, :, pl.ds(start, keys_count)]
        scores = jnp.where(allowed, scores, NEG)
        highest = jnp.max(scores, axis=1, keepdims=True)
        weights = jnp.exp(scores - highest)
        inverses.append(1.0 / jnp.sum(weights, axis=1, keepdims=True))
        weights = weights.astype(jnp.bfloat16)
        e_ref[head] = weights
        part = dot_nn(weights, v_heads[head])
        context = part if context is None else context + part
    lane = lax.broadcasted_iota(jnp.int32, (block, PAIR), 1)
    inverse = jnp.where(lane < DK, inverses[0], inverses[1])
    inv_ref[...] = inverse
    c_ref[...] = (context * inverse).astype(jnp.bfloat16)


def attend_back_kernel(block, keys_count, steps, biased, *refs):
    if biased:
        q_ref, k_ref, v_ref, e_ref, c_ref, inv_ref, gc_ref, gq_ref, gk_ref, gv_ref, off_ref, gk_sum, gv_sum, strip = refs
    else:
        q_ref, k_ref, v_ref, e_ref, c_ref, inv_ref, gc_ref, gq_ref, gk_ref, gv_ref, gk_sum, gv_sum = refs
    i = pl.program_id(1)

    @pl.when(i == 0)
    def _():
        gk_sum[...] = jnp.zeros_like(gk_sum)
        gv_sum[...] = jnp.zeros_like(gv_sum)
        if biased:
            strip[...] = jnp.zeros_like(strip)

    scaled = (gc_ref[...].astype(jnp.float32) * inv_ref[...]).astype(jnp.bfloat16)
    product = scaled.astype(jnp.float32) * c_ref[...].astype(jnp.float32)
    lane = lax.broadcasted_iota(jnp.int32, (block, PAIR), 1)
    inner = (
        jnp.sum(jnp.where(lane < DK, product, 0.0), axis=1, keepdims=True),
        jnp.sum(jnp.where(lane < DK, 0.0, product), axis=1, keepdims=True),
    )
    g_heads = split_heads(scaled)
    q_heads = split_heads(q_ref[...])
    k_heads = split_heads(k_ref[...])
    gq = None
    for head in range(2):
        weights = e_ref[head]
        grad = dot_nt(g_heads[head], v_ref[...])
        grad = weights.astype(jnp.float32) * (grad - inner[head])
        if biased:
            start = pl.multiple_of((keys_count // block - 1 - i) * block, block)
            strip[head, :, pl.ds(start, keys_count)] += grad
        grad = grad.astype(jnp.bfloat16)
        part = dot_nn(grad, k_heads[head])
        gq = part if gq is None else gq + part
        gk_sum[...] += dot_tn(grad, q_heads[head])
        gv_sum[...] += dot_tn(weights, g_heads[head])
    gq_ref[...] = gq.astype(jnp.bfloat16)

    @pl.when(i == steps - 1)
    def _():
        gk_ref[...] = gk_sum[...].astype(jnp.bfloat16)
        gv_ref[...] = gv_sum[...].astype(jnp.bfloat16)
        if biased:
            wide = 2 * keys_count
            for head in range(2):
                total = jnp.zeros((8, wide), jnp.float32)
                for a in range(block // 8):
                    total = total + pltpu.roll(strip[head, 8 * a : 8 * a + 8, :], (block - 8 * a) % wide, 1)
                off_ref[0, head] = total


def attend_forward(query, keys, values, base, query_segments, key_segments, causal):
    count, cols = query.shape[0], keys.shape[0]
    pairs = query.shape[1] // PAIR
    block = min(256, count)
    steps = count // block
    row_spec = pl.BlockSpec((block, PAIR), lambda h, i: (i, h))
    key_spec = pl.BlockSpec((cols, PAIR), lambda h, i: (0, h))
    in_specs = [
        pl.BlockSpec((block, 1), lambda h, i: (i, 0)),
        pl.BlockSpec((1, cols), lambda h, i: (0, 0)),
    ]
    args = [query_segments[:, None], key_segments[None, :]]
    scratch = []
    if base is not None:
        in_specs.append(pl.BlockSpec((1, 2, 8, 2 * cols), lambda h, i: (h, 0, 0, 0)))
        args.append(base)
        scratch.append(pltpu.VMEM((2, block, 2 * cols), jnp.float32))
    return pl.pallas_call(
        functools.partial(attend_kernel, block, cols, causal, base is not None),
        grid=(pairs, steps),
        in_specs=in_specs + [row_spec, key_spec, key_spec],
        out_specs=[
            pl.BlockSpec((2, block, cols), lambda h, i: (h, i, 0)),
            row_spec,
            row_spec,
        ],
        out_shape=[
            jax.ShapeDtypeStruct((2 * pairs, count, cols), jnp.bfloat16),
            jax.ShapeDtypeStruct((count, pairs * PAIR), jnp.bfloat16),
            jax.ShapeDtypeStruct((count, pairs * PAIR), jnp.float32),
        ],
        scratch_shapes=scratch,
        compiler_params=pltpu.CompilerParams(vmem_limit_bytes=VMEM_BYTES),
        cost_estimate=pl.CostEstimate(
            flops=4 * count * cols * PAIR * 2 * pairs, bytes_accessed=2 * pairs * count * cols * 2, transcendentals=0
        ),
    )(*args, query, keys, values)


def attend_backward(query, keys, values, saved, grad_context, biased):
    weights, context, inverse = saved
    count, cols = query.shape[0], keys.shape[0]
    pairs = query.shape[1] // PAIR
    block = min(256, count)
    steps = count // block
    row_spec = pl.BlockSpec((block, PAIR), lambda h, i: (i, h))
    key_spec = pl.BlockSpec((cols, PAIR), lambda h, i: (0, h))
    out_specs = [row_spec, key_spec, key_spec]
    out_shape = [
        jax.ShapeDtypeStruct((count, pairs * PAIR), jnp.bfloat16),
        jax.ShapeDtypeStruct((cols, pairs * PAIR), jnp.bfloat16),
        jax.ShapeDtypeStruct((cols, pairs * PAIR), jnp.bfloat16),
    ]
    scratch = [pltpu.VMEM((cols, PAIR), jnp.float32), pltpu.VMEM((cols, PAIR), jnp.float32)]
    if biased:
        out_specs.append(pl.BlockSpec((1, 2, 8, 2 * cols), lambda h, i: (h, 0, 0, 0)))
        out_shape.append(jax.ShapeDtypeStruct((pairs, 2, 8, 2 * cols), jnp.float32))
        scratch.append(pltpu.VMEM((2, block, 2 * cols), jnp.float32))
    return pl.pallas_call(
        functools.partial(attend_back_kernel, block, cols, steps, biased),
        grid=(pairs, steps),
        in_specs=[
            row_spec,
            key_spec,
            key_spec,
            pl.BlockSpec((2, block, cols), lambda h, i: (h, i, 0)),
            row_spec,
            row_spec,
            row_spec,
        ],
        out_specs=out_specs,
        out_shape=out_shape,
        scratch_shapes=scratch,
        compiler_params=pltpu.CompilerParams(vmem_limit_bytes=VMEM_BYTES),
        cost_estimate=pl.CostEstimate(
            flops=8 * count * cols * PAIR * 2 * pairs, bytes_accessed=2 * pairs * count * cols * 2, transcendentals=0
        ),
    )(query, keys, values, weights, context, inverse, grad_context)


def ffn_backward(grad_rows, normed_rows, hidden, active, weight_up, weight_down):
    grad_active = jnp.einsum(
        "rd,fd->rf", grad_rows, weight_down, preferred_element_type=jnp.float32
    )
    grad_down = jnp.einsum("rf,rd->fd", active, grad_rows, preferred_element_type=jnp.float32)
    unused, pull = jax.vjp(gelu_tanh, hidden)
    grad_hidden = pull(grad_active)[0].astype(jnp.bfloat16)
    grad_up = jnp.einsum("rd,rf->df", normed_rows, grad_hidden, preferred_element_type=jnp.float32)
    grad_normed = jnp.einsum(
        "rf,df->rd", grad_hidden, weight_up, preferred_element_type=jnp.float32
    )
    return (grad_normed, grad_up, grad_down)


def norm_backward(values, gain, grad_normed):
    unused, pull = jax.vjp(rms_norm, values, gain)
    return pull(grad_normed)


def on_device(
    enc_input,
    dec_input,
    enc_lengths,
    dec_lengths,
    attn_query,
    attn_kv,
    attn_out,
    ffn_up,
    ffn_down,
    gains,
    rel_bias,
    enc_cotangent,
    dec_cotangent,
):
    weights = (
        lax.all_gather(attn_query, "wide", axis=1, tiled=True),
        lax.all_gather(attn_kv, "wide", axis=2, tiled=True),
        lax.all_gather(attn_out, "wide", axis=2, tiled=True),
        lax.all_gather(ffn_up, "wide", axis=1, tiled=True),
        lax.all_gather(ffn_down, "wide", axis=2, tiled=True),
    )
    gain_rows = gains.astype(jnp.float32)
    heads_local = rel_bias.shape[2]
    enc_segments = segment_ids(enc_lengths[0], ENC)
    dec_segments = segment_ids(dec_lengths[0], DEC)

    side = lax.axis_index("narrow")
    swap = [(0, 1), (1, 0)]

    def spread_rows(values):
        own = values.astype(jnp.bfloat16)
        other = lax.ppermute(own, "narrow", swap)
        return jnp.where(side == 0, jnp.concatenate([own, other]), jnp.concatenate([other, own]))

    def collect_rows(parts):
        half = parts.shape[0] // 2
        parts = parts.astype(jnp.bfloat16)
        other = lax.ppermute(lax.dynamic_slice_in_dim(parts, (1 - side) * half, half), "narrow", swap)
        own = lax.dynamic_slice_in_dim(parts, side * half, half)
        return own.astype(jnp.float32) + other.astype(jnp.float32)

    def attention_layer(normed_query, normed_keys, layer, base, query_segments, key_segments, causal):
        query = jnp.dot(normed_query, weights[0][layer], preferred_element_type=jnp.float32).astype(jnp.bfloat16)
        keys = jnp.dot(normed_keys, weights[1][layer, 0], preferred_element_type=jnp.float32).astype(jnp.bfloat16)
        values = jnp.dot(normed_keys, weights[1][layer, 1], preferred_element_type=jnp.float32).astype(jnp.bfloat16)
        saved = attend_forward(query, keys, values, base, query_segments, key_segments, causal)
        parts = jnp.dot(saved[1], weights[2][layer], preferred_element_type=jnp.float32)
        return ((query, keys, values, saved), collect_rows(parts))

    enc_start = enc_input.astype(jnp.float32)
    rows_a = spread_rows(rms_norm(enc_start, gain_rows[0]))
    kept_a, branch = attention_layer(
        rows_a, rows_a, 0, base_rows(rel_bias[0], ENC, True), enc_segments, enc_segments, False
    )
    enc_mid = enc_start + branch
    rows_b = spread_rows(rms_norm(enc_mid, gain_rows[1]))
    hidden_b = jnp.dot(rows_b, weights[3][0], preferred_element_type=jnp.float32)
    active_b = gelu_tanh(hidden_b).astype(jnp.bfloat16)
    enc_final = enc_mid + collect_rows(
        jnp.dot(active_b, weights[4][0], preferred_element_type=jnp.float32)
    )
    memory = spread_rows(rms_norm(enc_final, gain_rows[5]))
    dec_start = dec_input.astype(jnp.float32)
    rows_c = spread_rows(rms_norm(dec_start, gain_rows[2]))
    kept_c, branch = attention_layer(
        rows_c, rows_c, 1, base_rows(rel_bias[1], DEC, False), dec_segments, dec_segments, True
    )
    dec_one = dec_start + branch
    rows_d = spread_rows(rms_norm(dec_one, gain_rows[3]))
    kept_d, branch = attention_layer(
        rows_d, memory, 2, None, dec_segments, enc_segments, False
    )
    dec_two = dec_one + branch
    rows_e = spread_rows(rms_norm(dec_two, gain_rows[4]))
    hidden_e = jnp.dot(rows_e, weights[3][1], preferred_element_type=jnp.float32)
    active_e = gelu_tanh(hidden_e).astype(jnp.bfloat16)
    dec_final = dec_two + collect_rows(
        jnp.dot(active_e, weights[4][1], preferred_element_type=jnp.float32)
    )
    def attention_back(grad_state, kept, normed_query, normed_keys, layer, span, two_sided):
        grad_rows = spread_rows(grad_state)
        query, keys, values, saved = kept
        grad_context = dot_nt(grad_rows, weights[2][layer]).astype(jnp.bfloat16)
        grad_out = dot_tn(saved[1], grad_rows)
        result = attend_backward(query, keys, values, saved, grad_context, span > 0)
        grad_q, grad_k, grad_v = result[:3]
        sums = [
            dot_tn(normed_query, grad_q),
            dot_tn(normed_keys, grad_k),
            dot_tn(normed_keys, grad_v),
            grad_out,
            table_grad(result[3], span, two_sided) if span else None,
        ]
        query_part = dot_nt(grad_q, weights[0][layer])
        key_part = dot_nt(grad_k, weights[1][layer, 0]) + dot_nt(grad_v, weights[1][layer, 1])
        return (query_part, key_part, sums)

    grad_dec = dec_cotangent.astype(jnp.float32)
    grad_normed, up_e, down_e = ffn_backward(
        spread_rows(grad_dec), rows_e, hidden_e, active_e, weights[3][1], weights[4][1]
    )
    grad_back, gain_e = norm_backward(dec_two, gain_rows[4], collect_rows(grad_normed))
    grad_dec = grad_dec + grad_back
    query_part, memory_part, sums_d = attention_back(
        grad_dec, kept_d, rows_d, memory, 2, 0, False
    )
    grad_normed, grad_memory = collect_rows(query_part), collect_rows(memory_part)
    grad_back, gain_d = norm_backward(dec_one, gain_rows[3], grad_normed)
    grad_dec = grad_dec + grad_back
    query_part, key_part, sums_c = attention_back(
        grad_dec, kept_c, rows_c, rows_c, 1, DEC, False
    )
    grad_back, gain_c = norm_backward(dec_start, gain_rows[2], collect_rows(query_part + key_part))
    grad_dec = grad_dec + grad_back
    grad_enc = enc_cotangent.astype(jnp.float32)
    grad_back, gain_m = norm_backward(enc_final, gain_rows[5], grad_memory)
    grad_enc = grad_enc + grad_back
    grad_normed, up_b, down_b = ffn_backward(
        spread_rows(grad_enc), rows_b, hidden_b, active_b, weights[3][0], weights[4][0]
    )
    grad_back, gain_b = norm_backward(enc_mid, gain_rows[1], collect_rows(grad_normed))
    grad_enc = grad_enc + grad_back
    query_part, key_part, sums_a = attention_back(
        grad_enc, kept_a, rows_a, rows_a, 0, ENC, True
    )
    grad_back, gain_a = norm_backward(enc_start, gain_rows[0], collect_rows(query_part + key_part))
    grad_enc = grad_enc + grad_back
    grad_query = jnp.stack([sums_a[0], sums_c[0], sums_d[0]])
    grad_kv = jnp.stack(
        [
            jnp.stack([sums_a[1], sums_a[2]]),
            jnp.stack([sums_c[1], sums_c[2]]),
            jnp.stack([sums_d[1], sums_d[2]]),
        ]
    )
    grad_out = jnp.stack([sums_a[3], sums_c[3], sums_d[3]])
    grad_up = jnp.stack([up_b, up_e])
    grad_down = jnp.stack([down_b, down_e])
    tiles = (
        lax.psum_scatter(
            grad_query.astype(jnp.bfloat16), "wide", scatter_dimension=1, tiled=True
        ).astype(jnp.float32),
        lax.psum_scatter(
            grad_kv.astype(jnp.bfloat16), "wide", scatter_dimension=2, tiled=True
        ).astype(jnp.float32),
        lax.psum_scatter(
            grad_out.astype(jnp.bfloat16), "wide", scatter_dimension=2, tiled=True
        ).astype(jnp.float32),
        lax.psum_scatter(
            grad_up.astype(jnp.bfloat16), "wide", scatter_dimension=1, tiled=True
        ).astype(jnp.float32),
        lax.psum_scatter(
            grad_down.astype(jnp.bfloat16), "wide", scatter_dimension=2, tiled=True
        ).astype(jnp.float32),
    )
    tiles = (
        lax.psum(tiles[0].astype(jnp.bfloat16), "dp").astype(jnp.float32),
        lax.psum(tiles[1].astype(jnp.bfloat16), "dp").astype(jnp.float32),
        lax.psum(tiles[2].astype(jnp.bfloat16), "dp").astype(jnp.float32),
        lax.psum(tiles[3].astype(jnp.bfloat16), "dp").astype(jnp.float32),
        lax.psum(tiles[4].astype(jnp.bfloat16), "dp").astype(jnp.float32),
    )
    gain_grads = jnp.stack([gain_a, gain_b, gain_c, gain_d, gain_e, gain_m])
    column = lax.axis_index("narrow") * heads_local
    bias_local = jnp.stack([sums_a[4], sums_c[4]])
    bias_full = lax.dynamic_update_slice(
        jnp.zeros((2, NB, H), jnp.float32), bias_local, (0, 0, column)
    )
    gain_total, bias_total = lax.psum((gain_grads, bias_full), ("dp", "wide", "narrow"))
    bias_grad = lax.dynamic_slice(bias_total, (0, 0, column), (2, NB, heads_local))
    return (
        enc_final.astype(jnp.bfloat16),
        dec_final.astype(jnp.bfloat16),
        grad_enc,
        grad_dec,
        tiles[0],
        tiles[1],
        tiles[2],
        tiles[3],
        tiles[4],
        gain_total,
        bias_grad,
    )


def solution(mesh):
    return jax.shard_map(
        on_device,
        mesh=mesh,
        in_specs=(
            P(("dp", "wide", "narrow"), None),
            P(("dp", "wide", "narrow"), None),
            P(("dp", "wide"), None),
            P(("dp", "wide"), None),
            P(None, "wide", "narrow"),
            P(None, None, "wide", "narrow"),
            P(None, "narrow", "wide"),
            P(None, "wide", "narrow"),
            P(None, "narrow", "wide"),
            P(),
            P(None, None, "narrow"),
            P(("dp", "wide", "narrow"), None),
            P(("dp", "wide", "narrow"), None),
        ),
        out_specs=(
            P(("dp", "wide", "narrow"), None),
            P(("dp", "wide", "narrow"), None),
            P(("dp", "wide", "narrow"), None),
            P(("dp", "wide", "narrow"), None),
            P(None, "wide", "narrow"),
            P(None, None, "wide", "narrow"),
            P(None, "narrow", "wide"),
            P(None, "wide", "narrow"),
            P(None, "narrow", "wide"),
            P(),
            P(None, None, "narrow"),
        ),
        check_vma=False,
    )
```

```python
import functools
import math

import jax
import jax.numpy as jnp
from jax import lax
from jax.sharding import PartitionSpec as P
import jax.experimental.pallas as pl
import jax.experimental.pallas.tpu as pltpu

H = 12
DK = 64
NB = 32
MAXD = 128
ENC = 1024
DEC = 256


EPS = 1e-06
NEG = -1e30
HIGH = lax.Precision.HIGHEST
VMEM_BYTES = 60 * 2**20
GELU_A = math.sqrt(2.0 / math.pi)
GELU_B = 0.044715


def cutoffs(exact, buckets):
    found = []
    reach = exact
    for target in range(exact + 1, buckets):
        while (
            exact + math.floor(math.log(reach / exact) / math.log(MAXD / exact) * (buckets - exact))
            < target
        ):
            reach = reach + 1
        found.append(reach)
    return found


def bucket_index(relative, two_sided):
    if two_sided:
        width = NB // 2
        offset = jnp.where(relative > 0, width, 0)
        distance = jnp.abs(relative)
    else:
        width = NB
        offset = jnp.zeros_like(relative)
        distance = jnp.maximum(-relative, 0)
    exact = width // 2
    beyond = exact + sum(((distance >= limit).astype(jnp.int32) for limit in cutoffs(exact, width)))
    return offset + jnp.where(distance < exact, distance, beyond)


def segment_ids(lengths, count):
    bounds = jnp.cumsum(lengths)
    places = jnp.arange(count, dtype=jnp.int32)
    return jnp.sum((places[:, None] >= bounds[None, :]).astype(jnp.int32), axis=1)


def rms_norm(values, gain):
    return values * lax.rsqrt(jnp.mean(values * values, axis=-1, keepdims=True) + EPS) * gain


def gelu_tanh(values):
    return jax.nn.gelu(values, approximate=True)


PAIR = 128


def offset_buckets(span, two_sided):
    places = jnp.arange(2 * span, dtype=jnp.int32)[None, :]
    relative = lax.rem(places - jnp.arange(8, dtype=jnp.int32)[:, None] + 2 * span, 2 * span) - span
    buckets = bucket_index(relative.reshape(-1), two_sided)
    return (buckets[None, :] == jnp.arange(NB, dtype=jnp.int32)[:, None]).astype(jnp.bfloat16)


def base_rows(table, span, two_sided):
    heads = table.shape[1]
    rows = lax.dot_general(
        table, offset_buckets(span, two_sided), (((0,), (0,)), ((), ())), preferred_element_type=jnp.float32
    )
    return rows.reshape(heads // 2, 2, 8, 2 * span)


def table_grad(offset_sums, span, two_sided):
    heads = 2 * offset_sums.shape[0]
    return lax.dot_general(
        offset_buckets(span, two_sided).astype(jnp.float32),
        offset_sums.reshape(heads, 16 * span),
        (((1,), (1,)), ((), ())),
        precision=HIGH,
        preferred_element_type=jnp.float32,
    )


def dot_nt(a, b):
    return lax.dot_general(a, b, (((1,), (1,)), ((), ())), preferred_element_type=jnp.float32)


def dot_tn(a, b):
    return lax.dot_general(a, b, (((0,), (0,)), ((), ())), preferred_element_type=jnp.float32)


def dot_nn(a, b):
    return lax.dot_general(a, b, (((1,), (0,)), ((), ())), preferred_element_type=jnp.float32)


def split_heads(block):
    lane = lax.broadcasted_iota(jnp.int32, block.shape, 1)
    zero = jnp.zeros_like(block)
    return jnp.where(lane < DK, block, zero), jnp.where(lane < DK, zero, block)


def attend_kernel(block, keys_count, causal, biased, *refs):
    if biased:
        qseg, kseg, base, q_ref, k_ref, v_ref, e_ref, c_ref, inv_ref, strip = refs
    else:
        qseg, kseg, q_ref, k_ref, v_ref, e_ref, c_ref, inv_ref = refs
    i = pl.program_id(1)
    if biased:
        wide = 2 * keys_count

        @pl.when(i == 0)
        def _():
            for head in range(2):
                rows = base[0, head]
                for a in range(block // 8):
                    strip[head, 8 * a : 8 * a + 8, :] = pltpu.roll(rows, (8 * a + wide - block) % wide, 1)

    allowed = qseg[...] == kseg[...]
    if causal:
        rows = lax.broadcasted_iota(jnp.int32, (block, keys_count), 0) + i * block
        allowed = allowed & (lax.broadcasted_iota(jnp.int32, (block, keys_count), 1) <= rows)
    q_heads = split_heads(q_ref[...])
    v_heads = split_heads(v_ref[...])
    inverses = []
    context = None
    for head in range(2):
        scores = dot_nt(q_heads[head], k_ref[...])
        if biased:
            start = pl.multiple_of((keys_count // block - 1 - i) * block, block)
            scores = scores + strip[head, :, pl.ds(start, keys_count)]
        scores = jnp.where(allowed, scores, NEG)
        highest = jnp.max(scores, axis=1, keepdims=True)
        weights = jnp.exp(scores - highest)
        inverses.append(1.0 / jnp.sum(weights, axis=1, keepdims=True))
        weights = weights.astype(jnp.bfloat16)
        e_ref[head] = weights
        part = dot_nn(weights, v_heads[head])
        context = part if context is None else context + part
    lane = lax.broadcasted_iota(jnp.int32, (block, PAIR), 1)
    inverse = jnp.where(lane < DK, inverses[0], inverses[1])
    inv_ref[...] = inverse
    c_ref[...] = (context * inverse).astype(jnp.bfloat16)


def attend_back_kernel(block, keys_count, steps, biased, *refs):
    if biased:
        q_ref, k_ref, v_ref, e_ref, c_ref, inv_ref, gc_ref, gq_ref, gk_ref, gv_ref, off_ref, gk_sum, gv_sum, strip = refs
    else:
        q_ref, k_ref, v_ref, e_ref, c_ref, inv_ref, gc_ref, gq_ref, gk_ref, gv_ref, gk_sum, gv_sum = refs
    i = pl.program_id(1)

    @pl.when(i == 0)
    def _():
        gk_sum[...] = jnp.zeros_like(gk_sum)
        gv_sum[...] = jnp.zeros_like(gv_sum)
        if biased:
            strip[...] = jnp.zeros_like(strip)

    scaled = (gc_ref[...].astype(jnp.float32) * inv_ref[...]).astype(jnp.bfloat16)
    product = scaled.astype(jnp.float32) * c_ref[...].astype(jnp.float32)
    lane = lax.broadcasted_iota(jnp.int32, (block, PAIR), 1)
    inner = (
        jnp.sum(jnp.where(lane < DK, product, 0.0), axis=1, keepdims=True),
        jnp.sum(jnp.where(lane < DK, 0.0, product), axis=1, keepdims=True),
    )
    g_heads = split_heads(scaled)
    q_heads = split_heads(q_ref[...])
    k_heads = split_heads(k_ref[...])
    gq = None
    for head in range(2):
        weights = e_ref[head]
        grad = dot_nt(g_heads[head], v_ref[...])
        grad = weights.astype(jnp.float32) * (grad - inner[head])
        if biased:
            start = pl.multiple_of((keys_count // block - 1 - i) * block, block)
            strip[head, :, pl.ds(start, keys_count)] += grad
        grad = grad.astype(jnp.bfloat16)
        part = dot_nn(grad, k_heads[head])
        gq = part if gq is None else gq + part
        gk_sum[...] += dot_tn(grad, q_heads[head])
        gv_sum[...] += dot_tn(weights, g_heads[head])
    gq_ref[...] = gq.astype(jnp.bfloat16)

    @pl.when(i == steps - 1)
    def _():
        gk_ref[...] = gk_sum[...].astype(jnp.bfloat16)
        gv_ref[...] = gv_sum[...].astype(jnp.bfloat16)
        if biased:
            wide = 2 * keys_count
            for head in range(2):
                total = jnp.zeros((8, wide), jnp.float32)
                for a in range(block // 8):
                    total = total + pltpu.roll(strip[head, 8 * a : 8 * a + 8, :], (block - 8 * a) % wide, 1)
                off_ref[0, head] = total


def attend_forward(query, keys, values, base, query_segments, key_segments, causal):
    count, cols = query.shape[0], keys.shape[0]
    pairs = query.shape[1] // PAIR
    block = min(256, count)
    steps = count // block
    row_spec = pl.BlockSpec((block, PAIR), lambda h, i: (i, h))
    key_spec = pl.BlockSpec((cols, PAIR), lambda h, i: (0, h))
    in_specs = [
        pl.BlockSpec((block, 1), lambda h, i: (i, 0)),
        pl.BlockSpec((1, cols), lambda h, i: (0, 0)),
    ]
    args = [query_segments[:, None], key_segments[None, :]]
    scratch = []
    if base is not None:
        in_specs.append(pl.BlockSpec((1, 2, 8, 2 * cols), lambda h, i: (h, 0, 0, 0)))
        args.append(base)
        scratch.append(pltpu.VMEM((2, block, 2 * cols), jnp.float32))
    return pl.pallas_call(
        functools.partial(attend_kernel, block, cols, causal, base is not None),
        grid=(pairs, steps),
        in_specs=in_specs + [row_spec, key_spec, key_spec],
        out_specs=[
            pl.BlockSpec((2, block, cols), lambda h, i: (h, i, 0)),
            row_spec,
            row_spec,
        ],
        out_shape=[
            jax.ShapeDtypeStruct((2 * pairs, count, cols), jnp.bfloat16),
            jax.ShapeDtypeStruct((count, pairs * PAIR), jnp.bfloat16),
            jax.ShapeDtypeStruct((count, pairs * PAIR), jnp.float32),
        ],
        scratch_shapes=scratch,
        compiler_params=pltpu.CompilerParams(vmem_limit_bytes=VMEM_BYTES),
        cost_estimate=pl.CostEstimate(
            flops=4 * count * cols * PAIR * 2 * pairs, bytes_accessed=2 * pairs * count * cols * 2, transcendentals=0
        ),
    )(*args, query, keys, values)


def attend_backward(query, keys, values, saved, grad_context, biased):
    weights, context, inverse = saved
    count, cols = query.shape[0], keys.shape[0]
    pairs = query.shape[1] // PAIR
    block = min(256, count)
    steps = count // block
    row_spec = pl.BlockSpec((block, PAIR), lambda h, i: (i, h))
    key_spec = pl.BlockSpec((cols, PAIR), lambda h, i: (0, h))
    out_specs = [row_spec, key_spec, key_spec]
    out_shape = [
        jax.ShapeDtypeStruct((count, pairs * PAIR), jnp.bfloat16),
        jax.ShapeDtypeStruct((cols, pairs * PAIR), jnp.bfloat16),
        jax.ShapeDtypeStruct((cols, pairs * PAIR), jnp.bfloat16),
    ]
    scratch = [pltpu.VMEM((cols, PAIR), jnp.float32), pltpu.VMEM((cols, PAIR), jnp.float32)]
    if biased:
        out_specs.append(pl.BlockSpec((1, 2, 8, 2 * cols), lambda h, i: (h, 0, 0, 0)))
        out_shape.append(jax.ShapeDtypeStruct((pairs, 2, 8, 2 * cols), jnp.float32))
        scratch.append(pltpu.VMEM((2, block, 2 * cols), jnp.float32))
    return pl.pallas_call(
        functools.partial(attend_back_kernel, block, cols, steps, biased),
        grid=(pairs, steps),
        in_specs=[
            row_spec,
            key_spec,
            key_spec,
            pl.BlockSpec((2, block, cols), lambda h, i: (h, i, 0)),
            row_spec,
            row_spec,
            row_spec,
        ],
        out_specs=out_specs,
        out_shape=out_shape,
        scratch_shapes=scratch,
        compiler_params=pltpu.CompilerParams(vmem_limit_bytes=VMEM_BYTES),
        cost_estimate=pl.CostEstimate(
            flops=8 * count * cols * PAIR * 2 * pairs, bytes_accessed=2 * pairs * count * cols * 2, transcendentals=0
        ),
    )(query, keys, values, weights, context, inverse, grad_context)


MESH_IDS = pl.DeviceIdType.MESH
CHUNK = 256
ATT = 4 * 384


def any_spec():
    return pl.BlockSpec(memory_space=pl.ANY)


def vmem_spec():
    return pl.BlockSpec(memory_space=pltpu.VMEM)


def normed(values, gain):
    return values * lax.rsqrt(jnp.mean(values * values, axis=1, keepdims=True) + EPS) * gain


def gelu_pair(values):
    square = values * values
    inner = jnp.tanh(GELU_A * values * (1.0 + GELU_B * square))
    half = 0.5 * (1.0 + inner)
    slope = half + 0.5 * values * (1.0 - inner * inner) * (GELU_A * (1.0 + 3.0 * GELU_B * square))
    return values * half, slope


class Place:
    def __init__(self, wide):
        self.core = lax.axis_index("dp")
        self.wide = lax.axis_index("wide")
        self.side = lax.axis_index("narrow")
        self.count = wide
        self.fars = wide // 2
        self.far = self.wide // 2
        self.near = self.wide % 2

    def sibling(self):
        return (1 - self.core, self.wide, self.side)

    def across(self):
        return (self.core, self.wide, 1 - self.side)

    def beside(self):
        return (self.core, 2 * self.far + 1 - self.near, self.side)

    def along(self, step):
        return (self.core, 2 * lax.rem(self.far + step, self.fars) + self.near, self.side)

    def index_from(self, step):
        return 2 * lax.rem(self.far - step + self.fars, self.fars) + self.near

    def index_beside(self, step):
        return 2 * lax.rem(self.far - step + self.fars, self.fars) + 1 - self.near

    def greet(self):
        partners = [self.sibling(), self.across(), self.beside()]
        partners += [self.along(step) for step in range(1, self.fars)]
        barrier = pltpu.get_barrier_semaphore()
        for partner in partners:
            pl.semaphore_signal(barrier, inc=1, device_id=partner, device_id_type=MESH_IDS)
        pl.semaphore_wait(barrier, len(partners))


def remote(source, target, send, receive, partner):
    return pltpu.make_async_remote_copy(
        src_ref=source,
        dst_ref=target,
        send_sem=send,
        recv_sem=receive,
        device_id=partner,
        device_id_type=MESH_IDS,
    )


class Gather:
    def __init__(self, place, pack, groups, send, receive, local):
        self.place, self.pack, self.groups = place, pack, groups
        self.send, self.receive, self.local = send, receive, local
        self.rows = pack.shape[0]
        self.sent = []

    def at(self, group, index, core):
        first, width, target, offset = self.groups[group]
        half = width // 2
        start = pl.multiple_of(offset + core * half, 128)
        return target.at[pl.ds(pl.multiple_of(index * self.rows, 16), self.rows), pl.ds(start, half)]

    def own(self, group):
        first, width, target, offset = self.groups[group]
        half = width // 2
        return self.pack.at[:, pl.ds(pl.multiple_of(first + self.place.core * half, 128), half)]

    def local_copy(self, group):
        first, width, target, offset = self.groups[group]
        rows = pl.ds(pl.multiple_of(self.place.wide * self.rows, 16), self.rows)
        return pltpu.make_async_copy(
            self.pack.at[:, pl.ds(first, width)], target.at[rows, pl.ds(offset, width)], self.local.at[group]
        )

    def push(self, group, slot, source, index, partner):
        copy = remote(
            source,
            self.at(group, index, self.place.core),
            self.send.at[group, slot],
            self.receive.at[group, slot],
            partner,
        )
        copy.start()
        self.sent.append(copy)

    def await_slot(self, group, slot, index, core):
        block = self.at(group, index, core)
        remote(block, block, self.send.at[group, slot], self.receive.at[group, slot], self.place.sibling()).wait_recv()

    def start(self, group):
        place, fars = self.place, self.place.fars
        for step in range(1, fars):
            self.push(group, step - 1, self.own(group), place.wide, place.along(step))
        self.push(group, fars - 1, self.own(group), place.wide, place.beside())
        self.local_copy(group).start()

    def relay_along(self, group):
        place, fars = self.place, self.place.fars
        for step in range(1, fars):
            index = place.index_from(step)
            self.await_slot(group, step - 1, index, place.core)
            block = self.at(group, index, place.core)
            self.push(group, fars - 1 + step, block, index, place.beside())
            self.push(group, 2 * fars - 2 + step, block, index, place.sibling())

    def relay_beside(self, group):
        place, fars = self.place, self.place.fars
        for step in range(fars):
            index = place.index_beside(step)
            self.await_slot(group, fars - 1 + step, index, place.core)
            block = self.at(group, index, place.core)
            self.push(group, 3 * fars - 2 + step, block, index, place.sibling())

    def finish(self, group):
        place, fars = self.place, self.place.fars
        for step in range(1, fars):
            self.await_slot(group, 2 * fars - 2 + step, place.index_from(step), 1 - place.core)
        for step in range(fars):
            self.await_slot(group, 3 * fars - 2 + step, place.index_beside(step), 1 - place.core)
        self.local_copy(group).wait()

    def close(self):
        for copy in self.sent:
            copy.wait_send()


def gather_slots(wide):
    return 4 * (wide // 2) - 2


def softmax_pair(q_pair, k_pair, v_pair, allowed, biases, e_store):
    q_heads = split_heads(q_pair)
    v_heads = split_heads(v_pair)
    inverses = []
    context = None
    for head in range(2):
        scores = dot_nt(q_heads[head], k_pair)
        if biases is not None:
            scores = scores + biases(head)
        scores = jnp.where(allowed, scores, NEG)
        highest = jnp.max(scores, axis=1, keepdims=True)
        weights = jnp.exp(scores - highest)
        inverses.append(1.0 / jnp.sum(weights, axis=1, keepdims=True))
        weights = weights.astype(jnp.bfloat16)
        e_store(head, weights)
        part = dot_nn(weights, v_heads[head])
        context = part if context is None else context + part
    lane = lax.broadcasted_iota(jnp.int32, context.shape, 1)
    inverse = jnp.where(lane < DK, inverses[0], inverses[1])
    return inverse, (context * inverse).astype(jnp.bfloat16)


def build_strip(strip, base, pairs, block, span):
    def one(pair, carry):
        for head in range(2):
            rows = base[pair, head]
            for a in range(block // 8):
                strip[2 * pair + head, 8 * a : 8 * a + 8, :] = pltpu.roll(rows, (8 * a + 2 * span - block) % (2 * span), 1)
        return carry

    lax.fori_loop(0, pairs, one, 0)


def enc_forward_kernel(
    wide,
    x_own,
    pack,
    gains,
    base,
    qseg,
    kseg,
    w1,
    w2,
    n0,
    qkv,
    c,
    inv,
    e_all,
    e1,
    n1,
    slope_all,
    a_all,
    ef,
    mem,
    x_full,
    strip,
    e_buf,
    slope_buf,
    a_buf,
    y_send,
    y_recv,
    g_send,
    g_recv,
    g_local,
    x_sems,
    y_sems,
    z_sems,
    l_sems,
):
    place = Place(wide)
    side = place.side
    half = x_own.shape[0]
    rows = 2 * half
    steps = rows // CHUNK
    width = c.shape[1]
    ffn = a_all.shape[1]
    pairs = width // PAIR
    place.greet()
    gather = Gather(
        place,
        pack,
        [
            (0, 4 * width, w1, 0),
            (4 * width, 2 * ffn, w1, 4 * width),
            (4 * width + 2 * ffn, 8 * width, w2, 0),
            (12 * width + 2 * ffn, 2 * ffn, w2, 8 * width),
        ],
        g_send,
        g_recv,
        g_local,
    )
    mine = pl.ds(pl.multiple_of(side * half, 16), half)
    swap_x = remote(x_own, x_full.at[mine], x_sems.at[0], x_sems.at[1], place.across())
    gather.start(0)
    swap_x.start()
    keep_x = pltpu.make_async_copy(x_own, x_full.at[mine], l_sems.at[6])
    keep_x.start()
    build_strip(strip, base, pairs, CHUNK, rows)
    gather.relay_along(0)
    gather.start(1)
    keep_x.wait()
    gather.relay_beside(0)
    swap_x.wait()

    def norm_rows(i, carry):
        at = pl.ds(pl.multiple_of(i * CHUNK, CHUNK), CHUNK)
        n0[at, :] = normed(x_full[at, :].astype(jnp.float32), gains[0:1, :]).astype(jnp.bfloat16)
        return carry

    lax.fori_loop(0, steps, norm_rows, 0)
    gather.finish(0)

    def project(i, carry):
        at = pl.ds(pl.multiple_of(i * CHUNK, CHUNK), CHUNK)
        qkv[at, :] = dot_nn(n0[at, :], w1[:, : 3 * width]).astype(jnp.bfloat16)
        return carry

    lax.fori_loop(0, steps, project, 0)

    def lanes(base_lane, pair):
        return pl.ds(pl.multiple_of(base_lane + pair * PAIR, PAIR), PAIR)

    def save(i, kind):
        slot = i % 2
        at = pl.ds(i * CHUNK, CHUNK)
        if kind == 0:
            return pltpu.make_async_copy(e_buf.at[slot], e_all.at[:, at, :], l_sems.at[slot])
        if kind == 1:
            return pltpu.make_async_copy(slope_buf.at[slot], slope_all.at[at, :], l_sems.at[2 + slot])
        return pltpu.make_async_copy(a_buf.at[slot], a_all.at[at, :], l_sems.at[4 + slot])

    def swap_y(layer, i):
        at = pl.ds(i * CHUNK, CHUNK)
        sems = y_sems if layer == 0 else z_sems
        return remote(y_send.at[layer, at], y_recv.at[layer, at], sems.at[0, i], sems.at[1, i], place.across())

    def attend(i):
        at = slice(i * CHUNK, (i + 1) * CHUNK)
        slot = i % 2
        if i >= 2:
            save(i - 2, 0).wait()
        first = (steps - 1 - i) * CHUNK

        def one(pair, carry):
            allowed = qseg[at, :] == kseg[...]

            def bias(head):
                return strip[2 * pair + head, :, first : first + rows]

            def store(head, weights):
                e_buf[slot, 2 * pair + head] = weights

            inverse, context = softmax_pair(
                qkv[at, lanes(0, pair)],
                qkv[:, lanes(width, pair)],
                qkv[:, lanes(2 * width, pair)],
                allowed,
                bias,
                store,
            )
            inv[at, lanes(0, pair)] = inverse
            c[at, lanes(0, pair)] = context
            return carry

        lax.fori_loop(0, pairs, one, 0)
        save(i, 0).start()
        y_send[0, at, :] = dot_nt(c[at, :], w1[:, 3 * width : 4 * width]).astype(jnp.bfloat16)
        swap_y(0, i).start()

    def feed(i):
        at = slice(i * CHUNK, (i + 1) * CHUNK)
        slot = i % 2
        swap_y(0, i).wait_recv()
        both = y_send[0, at, :].astype(jnp.float32) + y_recv[0, at, :].astype(jnp.float32)
        middle = x_full[at, :].astype(jnp.float32) + both
        e1[at, :] = middle
        rounded = normed(middle, gains[1:2, :]).astype(jnp.bfloat16)
        n1[at, :] = rounded
        if i >= 2:
            save(i - 2, 1).wait()
            save(i - 2, 2).wait()

        def part(j, carry):
            cols = pl.ds(pl.multiple_of(4 * width + j * width, PAIR), width)
            here = pl.ds(pl.multiple_of(j * width, PAIR), width)
            active, slope = gelu_pair(dot_nn(n1[at, :], w1[:, cols]))
            a_buf[slot, :, here] = active.astype(jnp.bfloat16)
            slope_buf[slot, :, here] = slope.astype(jnp.bfloat16)
            return carry

        lax.fori_loop(0, ffn // width, part, 0)
        save(i, 1).start()
        save(i, 2).start()
        y_send[1, at, :] = dot_nt(a_buf[slot], w1[:, 4 * width + ffn :]).astype(jnp.bfloat16)
        swap_y(1, i).start()

    def last(i):
        at = slice(i * CHUNK, (i + 1) * CHUNK)
        swap_y(1, i).wait_recv()
        both = y_send[1, at, :].astype(jnp.float32) + y_recv[1, at, :].astype(jnp.float32)
        final = e1[at, :] + both
        ef[at, :] = final
        mem[at, :] = normed(final, gains[5:6, :]).astype(jnp.bfloat16)

    attend(0)
    gather.relay_along(1)
    gather.start(2)
    attend(1)
    gather.relay_beside(1)
    attend(2)
    gather.finish(1)
    feed(0)
    gather.relay_along(2)
    gather.start(3)
    attend(3)
    feed(1)
    gather.relay_beside(2)
    feed(2)
    gather.relay_along(3)
    feed(3)
    last(0)
    last(1)
    gather.relay_beside(3)
    last(2)
    last(3)
    gather.finish(2)
    gather.finish(3)
    gather.close()
    for i in range(steps):
        swap_y(0, i).wait_send()
        swap_y(1, i).wait_send()
    for i in range(steps - 2, steps):
        for kind in range(3):
            save(i, kind).wait()


def enc_forward(wide, x_own, pack, gains, base, segments):
    half, model = x_own.shape
    rows = 2 * half
    pairs = base.shape[0]
    width = pairs * PAIR
    ffn = (pack.shape[1] - 12 * width) // 4
    bf, f32 = jnp.bfloat16, jnp.float32
    shape = jax.ShapeDtypeStruct
    slots = gather_slots(wide)
    steps = rows // CHUNK
    return pl.pallas_call(
        functools.partial(enc_forward_kernel, wide),
        in_specs=[vmem_spec(), any_spec(), vmem_spec(), vmem_spec(), vmem_spec(), vmem_spec()],
        out_shape=[
            shape((model, 4 * width + 2 * ffn), bf),
            shape((model, 8 * width + 2 * ffn), bf),
            shape((rows, model), bf),
            shape((rows, 3 * width), bf),
            shape((rows, width), bf),
            shape((rows, width), f32),
            shape((2 * pairs, rows, rows), bf),
            shape((rows, model), f32),
            shape((rows, model), bf),
            shape((rows, ffn), bf),
            shape((rows, ffn), bf),
            shape((rows, model), f32),
            shape((rows, model), bf),
        ],
        out_specs=[
            vmem_spec(),
            any_spec(),
            vmem_spec(),
            vmem_spec(),
            vmem_spec(),
            vmem_spec(),
            any_spec(),
            vmem_spec(),
            vmem_spec(),
            any_spec(),
            any_spec(),
            vmem_spec(),
            vmem_spec(),
        ],
        scratch_shapes=[
            pltpu.VMEM((rows, model), bf),
            pltpu.VMEM((2 * pairs, CHUNK, 2 * rows), f32),
            pltpu.VMEM((2, 2 * pairs, CHUNK, rows), bf),
            pltpu.VMEM((2, CHUNK, ffn), bf),
            pltpu.VMEM((2, CHUNK, ffn), bf),
            pltpu.VMEM((2, rows, model), bf),
            pltpu.VMEM((2, rows, model), bf),
            pltpu.SemaphoreType.DMA((4, slots)),
            pltpu.SemaphoreType.DMA((4, slots)),
            pltpu.SemaphoreType.DMA((4,)),
            pltpu.SemaphoreType.DMA((2,)),
            pltpu.SemaphoreType.DMA((2, steps)),
            pltpu.SemaphoreType.DMA((2, steps)),
            pltpu.SemaphoreType.DMA((7,)),
        ],
        compiler_params=pltpu.CompilerParams(
            collective_id=0, has_side_effects=True, vmem_limit_bytes=VMEM_BYTES
        ),
        cost_estimate=pl.CostEstimate(flops=10**10, bytes_accessed=6 * 10**7, transcendentals=0),
    )(x_own, pack, gains, base, segments[:, None], segments[None, :])


def ffn_backward(grad_rows, normed_rows, hidden, active, weight_up, weight_down):
    grad_active = jnp.einsum(
        "rd,fd->rf", grad_rows, weight_down, preferred_element_type=jnp.float32
    )
    grad_down = jnp.einsum("rf,rd->fd", active, grad_rows, preferred_element_type=jnp.float32)
    unused, pull = jax.vjp(gelu_tanh, hidden)
    grad_hidden = pull(grad_active)[0].astype(jnp.bfloat16)
    grad_up = jnp.einsum("rd,rf->df", normed_rows, grad_hidden, preferred_element_type=jnp.float32)
    grad_normed = jnp.einsum(
        "rf,df->rd", grad_hidden, weight_up, preferred_element_type=jnp.float32
    )
    return (grad_normed, grad_up, grad_down)


def norm_backward(values, gain, grad_normed):
    unused, pull = jax.vjp(rms_norm, values, gain)
    return pull(grad_normed)


def pack_shards(attn_query, attn_kv, attn_out, ffn_up, ffn_down):
    def attention(layer):
        return [attn_query[layer], attn_kv[layer, 0], attn_kv[layer, 1], attn_out[layer].T]

    def feed(layer):
        return [ffn_up[layer], ffn_down[layer].T]

    return jnp.concatenate(attention(0) + feed(0) + attention(1) + attention(2) + feed(1), axis=1)


def ffn_back(grad_rows, normed_rows, slope, active, weight_up, weight_down):
    grad_active = dot_nn(grad_rows, weight_down)
    grad_down = dot_tn(active, grad_rows)
    grad_hidden = (slope.astype(jnp.float32) * grad_active).astype(jnp.bfloat16)
    return dot_nt(grad_hidden, weight_up), dot_tn(normed_rows, grad_hidden), grad_down


def on_device(
    wide,
    enc_input,
    dec_input,
    enc_lengths,
    dec_lengths,
    attn_query,
    attn_kv,
    attn_out,
    ffn_up,
    ffn_down,
    gains,
    rel_bias,
    enc_cotangent,
    dec_cotangent,
):
    gain_rows = gains.astype(jnp.float32)
    heads_local = rel_bias.shape[2]
    enc_segments = segment_ids(enc_lengths[0], ENC)
    dec_segments = segment_ids(dec_lengths[0], DEC)

    side = lax.axis_index("narrow")
    swap = [(0, 1), (1, 0)]

    def spread_rows(values):
        own = values.astype(jnp.bfloat16)
        other = lax.ppermute(own, "narrow", swap)
        return jnp.where(side == 0, jnp.concatenate([own, other]), jnp.concatenate([other, own]))

    def collect_rows(parts):
        half = parts.shape[0] // 2
        parts = parts.astype(jnp.bfloat16)
        other = lax.ppermute(lax.dynamic_slice_in_dim(parts, (1 - side) * half, half), "narrow", swap)
        own = lax.dynamic_slice_in_dim(parts, side * half, half)
        return own.astype(jnp.float32) + other.astype(jnp.float32)

    def attention_layer(normed_query, normed_keys, layer, base, query_segments, key_segments, causal):
        query = jnp.dot(normed_query, weights_q[layer], preferred_element_type=jnp.float32).astype(jnp.bfloat16)
        keys = jnp.dot(normed_keys, weights_k[layer], preferred_element_type=jnp.float32).astype(jnp.bfloat16)
        values = jnp.dot(normed_keys, weights_v[layer], preferred_element_type=jnp.float32).astype(jnp.bfloat16)
        saved = attend_forward(query, keys, values, base, query_segments, key_segments, causal)
        parts = dot_nt(saved[1], weights_o[layer])
        return ((query, keys, values, saved), collect_rows(parts))

    pack = pack_shards(attn_query, attn_kv, attn_out, ffn_up, ffn_down)
    w1, w2, rows_a, qkv_a, context_a, inverse_a, e_a, e1_full, rows_b, slope_b, active_b, ef_full, memory = enc_forward(
        wide, enc_input, pack, gain_rows, base_rows(rel_bias[0], ENC, True), enc_segments
    )
    width = DK * heads_local
    ffn = ffn_up.shape[2]
    layer_columns = [w1[:, : 4 * width], w2[:, : 4 * width], w2[:, 4 * width : 8 * width]]
    weights_q = [columns[:, :width] for columns in layer_columns]
    weights_k = [columns[:, width : 2 * width] for columns in layer_columns]
    weights_v = [columns[:, 2 * width : 3 * width] for columns in layer_columns]
    weights_o = [columns[:, 3 * width :] for columns in layer_columns]
    up = [w1[:, 4 * width : 4 * width + ffn], w2[:, 8 * width : 8 * width + ffn]]
    down = [w1[:, 4 * width + ffn :], w2[:, 8 * width + ffn :]]
    kept_a = (
        qkv_a[:, :width],
        qkv_a[:, width : 2 * width],
        qkv_a[:, 2 * width :],
        (e_a, context_a, inverse_a),
    )
    half = enc_input.shape[0]

    def own_rows(full):
        return lax.dynamic_slice_in_dim(full, side * half, half)

    enc_start = enc_input.astype(jnp.float32)
    enc_mid = own_rows(e1_full)
    enc_final = own_rows(ef_full)
    dec_start = dec_input.astype(jnp.float32)
    rows_c = spread_rows(rms_norm(dec_start, gain_rows[2]))
    kept_c, branch = attention_layer(
        rows_c, rows_c, 1, base_rows(rel_bias[1], DEC, False), dec_segments, dec_segments, True
    )
    dec_one = dec_start + branch
    rows_d = spread_rows(rms_norm(dec_one, gain_rows[3]))
    kept_d, branch = attention_layer(
        rows_d, memory, 2, None, dec_segments, enc_segments, False
    )
    dec_two = dec_one + branch
    rows_e = spread_rows(rms_norm(dec_two, gain_rows[4]))
    active_e, slope_e = gelu_pair(dot_nn(rows_e, up[1]))
    active_e = active_e.astype(jnp.bfloat16)
    dec_final = dec_two + collect_rows(
        dot_nt(active_e, down[1])
    )
    def attention_back(grad_state, kept, normed_query, normed_keys, layer, span, two_sided):
        grad_rows = spread_rows(grad_state)
        query, keys, values, saved = kept
        grad_context = dot_nn(grad_rows, weights_o[layer]).astype(jnp.bfloat16)
        grad_out = dot_tn(saved[1], grad_rows)
        result = attend_backward(query, keys, values, saved, grad_context, span > 0)
        grad_q, grad_k, grad_v = result[:3]
        sums = [
            dot_tn(normed_query, grad_q),
            dot_tn(normed_keys, grad_k),
            dot_tn(normed_keys, grad_v),
            grad_out,
            table_grad(result[3], span, two_sided) if span else None,
        ]
        query_part = dot_nt(grad_q, weights_q[layer])
        key_part = dot_nt(grad_k, weights_k[layer]) + dot_nt(grad_v, weights_v[layer])
        return (query_part, key_part, sums)

    grad_dec = dec_cotangent.astype(jnp.float32)
    grad_normed, up_e, down_e = ffn_back(
        spread_rows(grad_dec), rows_e, slope_e, active_e, up[1], down[1]
    )
    grad_back, gain_e = norm_backward(dec_two, gain_rows[4], collect_rows(grad_normed))
    grad_dec = grad_dec + grad_back
    query_part, memory_part, sums_d = attention_back(
        grad_dec, kept_d, rows_d, memory, 2, 0, False
    )
    grad_normed, grad_memory = collect_rows(query_part), collect_rows(memory_part)
    grad_back, gain_d = norm_backward(dec_one, gain_rows[3], grad_normed)
    grad_dec = grad_dec + grad_back
    query_part, key_part, sums_c = attention_back(
        grad_dec, kept_c, rows_c, rows_c, 1, DEC, False
    )
    grad_back, gain_c = norm_backward(dec_start, gain_rows[2], collect_rows(query_part + key_part))
    grad_dec = grad_dec + grad_back
    grad_enc = enc_cotangent.astype(jnp.float32)
    grad_back, gain_m = norm_backward(enc_final, gain_rows[5], grad_memory)
    grad_enc = grad_enc + grad_back
    grad_normed, up_b, down_b = ffn_back(
        spread_rows(grad_enc), rows_b, slope_b, active_b, up[0], down[0]
    )
    grad_back, gain_b = norm_backward(enc_mid, gain_rows[1], collect_rows(grad_normed))
    grad_enc = grad_enc + grad_back
    query_part, key_part, sums_a = attention_back(
        grad_enc, kept_a, rows_a, rows_a, 0, ENC, True
    )
    grad_back, gain_a = norm_backward(enc_start, gain_rows[0], collect_rows(query_part + key_part))
    grad_enc = grad_enc + grad_back
    grad_query = jnp.stack([sums_a[0], sums_c[0], sums_d[0]])
    grad_kv = jnp.stack(
        [
            jnp.stack([sums_a[1], sums_a[2]]),
            jnp.stack([sums_c[1], sums_c[2]]),
            jnp.stack([sums_d[1], sums_d[2]]),
        ]
    )
    grad_out = jnp.stack([sums_a[3], sums_c[3], sums_d[3]])
    grad_up = jnp.stack([up_b, up_e])
    grad_down = jnp.stack([down_b, down_e])
    tiles = (
        lax.psum_scatter(
            grad_query.astype(jnp.bfloat16), "wide", scatter_dimension=1, tiled=True
        ).astype(jnp.float32),
        lax.psum_scatter(
            grad_kv.astype(jnp.bfloat16), "wide", scatter_dimension=2, tiled=True
        ).astype(jnp.float32),
        lax.psum_scatter(
            grad_out.astype(jnp.bfloat16), "wide", scatter_dimension=2, tiled=True
        ).astype(jnp.float32),
        lax.psum_scatter(
            grad_up.astype(jnp.bfloat16), "wide", scatter_dimension=1, tiled=True
        ).astype(jnp.float32),
        lax.psum_scatter(
            grad_down.astype(jnp.bfloat16), "wide", scatter_dimension=2, tiled=True
        ).astype(jnp.float32),
    )
    tiles = (
        lax.psum(tiles[0].astype(jnp.bfloat16), "dp").astype(jnp.float32),
        lax.psum(tiles[1].astype(jnp.bfloat16), "dp").astype(jnp.float32),
        lax.psum(tiles[2].astype(jnp.bfloat16), "dp").astype(jnp.float32),
        lax.psum(tiles[3].astype(jnp.bfloat16), "dp").astype(jnp.float32),
        lax.psum(tiles[4].astype(jnp.bfloat16), "dp").astype(jnp.float32),
    )
    gain_grads = jnp.stack([gain_a, gain_b, gain_c, gain_d, gain_e, gain_m])
    column = lax.axis_index("narrow") * heads_local
    bias_local = jnp.stack([sums_a[4], sums_c[4]])
    bias_full = lax.dynamic_update_slice(
        jnp.zeros((2, NB, H), jnp.float32), bias_local, (0, 0, column)
    )
    gain_total, bias_total = lax.psum((gain_grads, bias_full), ("dp", "wide", "narrow"))
    bias_grad = lax.dynamic_slice(bias_total, (0, 0, column), (2, NB, heads_local))
    return (
        enc_final.astype(jnp.bfloat16),
        dec_final.astype(jnp.bfloat16),
        grad_enc,
        grad_dec,
        tiles[0],
        tiles[1],
        tiles[2],
        tiles[3],
        tiles[4],
        gain_total,
        bias_grad,
    )


def on_device_general(
    enc_input,
    dec_input,
    enc_lengths,
    dec_lengths,
    attn_query,
    attn_kv,
    attn_out,
    ffn_up,
    ffn_down,
    gains,
    rel_bias,
    enc_cotangent,
    dec_cotangent,
):
    weights = (
        lax.all_gather(attn_query, "wide", axis=1, tiled=True),
        lax.all_gather(attn_kv, "wide", axis=2, tiled=True),
        lax.all_gather(attn_out, "wide", axis=2, tiled=True),
        lax.all_gather(ffn_up, "wide", axis=1, tiled=True),
        lax.all_gather(ffn_down, "wide", axis=2, tiled=True),
    )
    gain_rows = gains.astype(jnp.float32)
    heads_local = rel_bias.shape[2]
    enc_segments = segment_ids(enc_lengths[0], ENC)
    dec_segments = segment_ids(dec_lengths[0], DEC)

    side = lax.axis_index("narrow")
    swap = [(0, 1), (1, 0)]

    def spread_rows(values):
        own = values.astype(jnp.bfloat16)
        other = lax.ppermute(own, "narrow", swap)
        return jnp.where(side == 0, jnp.concatenate([own, other]), jnp.concatenate([other, own]))

    def collect_rows(parts):
        half = parts.shape[0] // 2
        parts = parts.astype(jnp.bfloat16)
        other = lax.ppermute(lax.dynamic_slice_in_dim(parts, (1 - side) * half, half), "narrow", swap)
        own = lax.dynamic_slice_in_dim(parts, side * half, half)
        return own.astype(jnp.float32) + other.astype(jnp.float32)

    def attention_layer(normed_query, normed_keys, layer, base, query_segments, key_segments, causal):
        query = jnp.dot(normed_query, weights[0][layer], preferred_element_type=jnp.float32).astype(jnp.bfloat16)
        keys = jnp.dot(normed_keys, weights[1][layer, 0], preferred_element_type=jnp.float32).astype(jnp.bfloat16)
        values = jnp.dot(normed_keys, weights[1][layer, 1], preferred_element_type=jnp.float32).astype(jnp.bfloat16)
        saved = attend_forward(query, keys, values, base, query_segments, key_segments, causal)
        parts = jnp.dot(saved[1], weights[2][layer], preferred_element_type=jnp.float32)
        return ((query, keys, values, saved), collect_rows(parts))

    enc_start = enc_input.astype(jnp.float32)
    rows_a = spread_rows(rms_norm(enc_start, gain_rows[0]))
    kept_a, branch = attention_layer(
        rows_a, rows_a, 0, base_rows(rel_bias[0], ENC, True), enc_segments, enc_segments, False
    )
    enc_mid = enc_start + branch
    rows_b = spread_rows(rms_norm(enc_mid, gain_rows[1]))
    hidden_b = jnp.dot(rows_b, weights[3][0], preferred_element_type=jnp.float32)
    active_b = gelu_tanh(hidden_b).astype(jnp.bfloat16)
    enc_final = enc_mid + collect_rows(
        jnp.dot(active_b, weights[4][0], preferred_element_type=jnp.float32)
    )
    memory = spread_rows(rms_norm(enc_final, gain_rows[5]))
    dec_start = dec_input.astype(jnp.float32)
    rows_c = spread_rows(rms_norm(dec_start, gain_rows[2]))
    kept_c, branch = attention_layer(
        rows_c, rows_c, 1, base_rows(rel_bias[1], DEC, False), dec_segments, dec_segments, True
    )
    dec_one = dec_start + branch
    rows_d = spread_rows(rms_norm(dec_one, gain_rows[3]))
    kept_d, branch = attention_layer(
        rows_d, memory, 2, None, dec_segments, enc_segments, False
    )
    dec_two = dec_one + branch
    rows_e = spread_rows(rms_norm(dec_two, gain_rows[4]))
    hidden_e = jnp.dot(rows_e, weights[3][1], preferred_element_type=jnp.float32)
    active_e = gelu_tanh(hidden_e).astype(jnp.bfloat16)
    dec_final = dec_two + collect_rows(
        jnp.dot(active_e, weights[4][1], preferred_element_type=jnp.float32)
    )
    def attention_back(grad_state, kept, normed_query, normed_keys, layer, span, two_sided):
        grad_rows = spread_rows(grad_state)
        query, keys, values, saved = kept
        grad_context = dot_nt(grad_rows, weights[2][layer]).astype(jnp.bfloat16)
        grad_out = dot_tn(saved[1], grad_rows)
        result = attend_backward(query, keys, values, saved, grad_context, span > 0)
        grad_q, grad_k, grad_v = result[:3]
        sums = [
            dot_tn(normed_query, grad_q),
            dot_tn(normed_keys, grad_k),
            dot_tn(normed_keys, grad_v),
            grad_out,
            table_grad(result[3], span, two_sided) if span else None,
        ]
        query_part = dot_nt(grad_q, weights[0][layer])
        key_part = dot_nt(grad_k, weights[1][layer, 0]) + dot_nt(grad_v, weights[1][layer, 1])
        return (query_part, key_part, sums)

    grad_dec = dec_cotangent.astype(jnp.float32)
    grad_normed, up_e, down_e = ffn_backward(
        spread_rows(grad_dec), rows_e, hidden_e, active_e, weights[3][1], weights[4][1]
    )
    grad_back, gain_e = norm_backward(dec_two, gain_rows[4], collect_rows(grad_normed))
    grad_dec = grad_dec + grad_back
    query_part, memory_part, sums_d = attention_back(
        grad_dec, kept_d, rows_d, memory, 2, 0, False
    )
    grad_normed, grad_memory = collect_rows(query_part), collect_rows(memory_part)
    grad_back, gain_d = norm_backward(dec_one, gain_rows[3], grad_normed)
    grad_dec = grad_dec + grad_back
    query_part, key_part, sums_c = attention_back(
        grad_dec, kept_c, rows_c, rows_c, 1, DEC, False
    )
    grad_back, gain_c = norm_backward(dec_start, gain_rows[2], collect_rows(query_part + key_part))
    grad_dec = grad_dec + grad_back
    grad_enc = enc_cotangent.astype(jnp.float32)
    grad_back, gain_m = norm_backward(enc_final, gain_rows[5], grad_memory)
    grad_enc = grad_enc + grad_back
    grad_normed, up_b, down_b = ffn_backward(
        spread_rows(grad_enc), rows_b, hidden_b, active_b, weights[3][0], weights[4][0]
    )
    grad_back, gain_b = norm_backward(enc_mid, gain_rows[1], collect_rows(grad_normed))
    grad_enc = grad_enc + grad_back
    query_part, key_part, sums_a = attention_back(
        grad_enc, kept_a, rows_a, rows_a, 0, ENC, True
    )
    grad_back, gain_a = norm_backward(enc_start, gain_rows[0], collect_rows(query_part + key_part))
    grad_enc = grad_enc + grad_back
    grad_query = jnp.stack([sums_a[0], sums_c[0], sums_d[0]])
    grad_kv = jnp.stack(
        [
            jnp.stack([sums_a[1], sums_a[2]]),
            jnp.stack([sums_c[1], sums_c[2]]),
            jnp.stack([sums_d[1], sums_d[2]]),
        ]
    )
    grad_out = jnp.stack([sums_a[3], sums_c[3], sums_d[3]])
    grad_up = jnp.stack([up_b, up_e])
    grad_down = jnp.stack([down_b, down_e])
    tiles = (
        lax.psum_scatter(
            grad_query.astype(jnp.bfloat16), "wide", scatter_dimension=1, tiled=True
        ).astype(jnp.float32),
        lax.psum_scatter(
            grad_kv.astype(jnp.bfloat16), "wide", scatter_dimension=2, tiled=True
        ).astype(jnp.float32),
        lax.psum_scatter(
            grad_out.astype(jnp.bfloat16), "wide", scatter_dimension=2, tiled=True
        ).astype(jnp.float32),
        lax.psum_scatter(
            grad_up.astype(jnp.bfloat16), "wide", scatter_dimension=1, tiled=True
        ).astype(jnp.float32),
        lax.psum_scatter(
            grad_down.astype(jnp.bfloat16), "wide", scatter_dimension=2, tiled=True
        ).astype(jnp.float32),
    )
    tiles = (
        lax.psum(tiles[0].astype(jnp.bfloat16), "dp").astype(jnp.float32),
        lax.psum(tiles[1].astype(jnp.bfloat16), "dp").astype(jnp.float32),
        lax.psum(tiles[2].astype(jnp.bfloat16), "dp").astype(jnp.float32),
        lax.psum(tiles[3].astype(jnp.bfloat16), "dp").astype(jnp.float32),
        lax.psum(tiles[4].astype(jnp.bfloat16), "dp").astype(jnp.float32),
    )
    gain_grads = jnp.stack([gain_a, gain_b, gain_c, gain_d, gain_e, gain_m])
    column = lax.axis_index("narrow") * heads_local
    bias_local = jnp.stack([sums_a[4], sums_c[4]])
    bias_full = lax.dynamic_update_slice(
        jnp.zeros((2, NB, H), jnp.float32), bias_local, (0, 0, column)
    )
    gain_total, bias_total = lax.psum((gain_grads, bias_full), ("dp", "wide", "narrow"))
    bias_grad = lax.dynamic_slice(bias_total, (0, 0, column), (2, NB, heads_local))
    return (
        enc_final.astype(jnp.bfloat16),
        dec_final.astype(jnp.bfloat16),
        grad_enc,
        grad_dec,
        tiles[0],
        tiles[1],
        tiles[2],
        tiles[3],
        tiles[4],
        gain_total,
        bias_grad,
    )


def solution(mesh):
    wide = mesh.shape["wide"]

    def body(*args):
        if args[4].shape[1] % 16 or wide % 2:
            return on_device_general(*args)
        return on_device(wide, *args)

    return jax.shard_map(
        body,
        mesh=mesh,
        in_specs=(
            P(("dp", "wide", "narrow"), None),
            P(("dp", "wide", "narrow"), None),
            P(("dp", "wide"), None),
            P(("dp", "wide"), None),
            P(None, "wide", "narrow"),
            P(None, None, "wide", "narrow"),
            P(None, "narrow", "wide"),
            P(None, "wide", "narrow"),
            P(None, "narrow", "wide"),
            P(),
            P(None, None, "narrow"),
            P(("dp", "wide", "narrow"), None),
            P(("dp", "wide", "narrow"), None),
        ),
        out_specs=(
            P(("dp", "wide", "narrow"), None),
            P(("dp", "wide", "narrow"), None),
            P(("dp", "wide", "narrow"), None),
            P(("dp", "wide", "narrow"), None),
            P(None, "wide", "narrow"),
            P(None, None, "wide", "narrow"),
            P(None, "narrow", "wide"),
            P(None, "wide", "narrow"),
            P(None, "narrow", "wide"),
            P(),
            P(None, None, "narrow"),
        ),
        check_vma=False,
    )
```

```python
import functools
import math

import jax
import jax.numpy as jnp
from jax import lax
from jax.sharding import PartitionSpec as P
import jax.experimental.pallas as pl
import jax.experimental.pallas.tpu as pltpu

H = 12
DK = 64
NB = 32
MAXD = 128
ENC = 1024
DEC = 256


EPS = 1e-06
NEG = -1e30
HIGH = lax.Precision.HIGHEST
VMEM_BYTES = 60 * 2**20
GELU_A = math.sqrt(2.0 / math.pi)
GELU_B = 0.044715


def cutoffs(exact, buckets):
    found = []
    reach = exact
    for target in range(exact + 1, buckets):
        while (
            exact + math.floor(math.log(reach / exact) / math.log(MAXD / exact) * (buckets - exact))
            < target
        ):
            reach = reach + 1
        found.append(reach)
    return found


def bucket_index(relative, two_sided):
    if two_sided:
        width = NB // 2
        offset = jnp.where(relative > 0, width, 0)
        distance = jnp.abs(relative)
    else:
        width = NB
        offset = jnp.zeros_like(relative)
        distance = jnp.maximum(-relative, 0)
    exact = width // 2
    beyond = exact + sum(((distance >= limit).astype(jnp.int32) for limit in cutoffs(exact, width)))
    return offset + jnp.where(distance < exact, distance, beyond)


def segment_ids(lengths, count):
    bounds = jnp.cumsum(lengths)
    places = jnp.arange(count, dtype=jnp.int32)
    return jnp.sum((places[:, None] >= bounds[None, :]).astype(jnp.int32), axis=1)


def rms_norm(values, gain):
    return values * lax.rsqrt(jnp.mean(values * values, axis=-1, keepdims=True) + EPS) * gain


def gelu_tanh(values):
    return jax.nn.gelu(values, approximate=True)


PAIR = 128


def offset_buckets(span, two_sided):
    places = jnp.arange(2 * span, dtype=jnp.int32)[None, :]
    relative = lax.rem(places - jnp.arange(8, dtype=jnp.int32)[:, None] + 2 * span, 2 * span) - span
    buckets = bucket_index(relative.reshape(-1), two_sided)
    return (buckets[None, :] == jnp.arange(NB, dtype=jnp.int32)[:, None]).astype(jnp.bfloat16)


def base_rows(table, span, two_sided):
    heads = table.shape[1]
    rows = lax.dot_general(
        table, offset_buckets(span, two_sided), (((0,), (0,)), ((), ())), preferred_element_type=jnp.float32
    )
    return rows.reshape(heads // 2, 2, 8, 2 * span)


def table_grad(offset_sums, span, two_sided):
    heads = 2 * offset_sums.shape[0]
    return lax.dot_general(
        offset_buckets(span, two_sided).astype(jnp.float32),
        offset_sums.reshape(heads, 16 * span),
        (((1,), (1,)), ((), ())),
        precision=HIGH,
        preferred_element_type=jnp.float32,
    )


def dot_nt(a, b):
    return lax.dot_general(a, b, (((1,), (1,)), ((), ())), preferred_element_type=jnp.float32)


def dot_tn(a, b):
    return lax.dot_general(a, b, (((0,), (0,)), ((), ())), preferred_element_type=jnp.float32)


def dot_nn(a, b):
    return lax.dot_general(a, b, (((1,), (0,)), ((), ())), preferred_element_type=jnp.float32)


def split_heads(block):
    lane = lax.broadcasted_iota(jnp.int32, block.shape, 1)
    zero = jnp.zeros_like(block)
    return jnp.where(lane < DK, block, zero), jnp.where(lane < DK, zero, block)


def attend_kernel(block, keys_count, causal, biased, *refs):
    if biased:
        qseg, kseg, base, q_ref, k_ref, v_ref, e_ref, c_ref, inv_ref, strip = refs
    else:
        qseg, kseg, q_ref, k_ref, v_ref, e_ref, c_ref, inv_ref = refs
    i = pl.program_id(1)
    if biased:
        wide = 2 * keys_count

        @pl.when(i == 0)
        def _():
            for head in range(2):
                rows = base[0, head]
                for a in range(block // 8):
                    strip[head, 8 * a : 8 * a + 8, :] = pltpu.roll(rows, (8 * a + wide - block) % wide, 1)

    allowed = qseg[...] == kseg[...]
    if causal:
        rows = lax.broadcasted_iota(jnp.int32, (block, keys_count), 0) + i * block
        allowed = allowed & (lax.broadcasted_iota(jnp.int32, (block, keys_count), 1) <= rows)
    q_heads = split_heads(q_ref[...])
    v_heads = split_heads(v_ref[...])
    inverses = []
    context = None
    for head in range(2):
        scores = dot_nt(q_heads[head], k_ref[...])
        if biased:
            start = pl.multiple_of((keys_count // block - 1 - i) * block, block)
            scores = scores + strip[head, :, pl.ds(start, keys_count)]
        scores = jnp.where(allowed, scores, NEG)
        highest = jnp.max(scores, axis=1, keepdims=True)
        weights = jnp.exp(scores - highest)
        inverses.append(1.0 / jnp.sum(weights, axis=1, keepdims=True))
        weights = weights.astype(jnp.bfloat16)
        e_ref[head] = weights
        part = dot_nn(weights, v_heads[head])
        context = part if context is None else context + part
    lane = lax.broadcasted_iota(jnp.int32, (block, PAIR), 1)
    inverse = jnp.where(lane < DK, inverses[0], inverses[1])
    inv_ref[...] = inverse
    c_ref[...] = (context * inverse).astype(jnp.bfloat16)


def attend_back_kernel(block, keys_count, steps, biased, *refs):
    if biased:
        q_ref, k_ref, v_ref, e_ref, c_ref, inv_ref, gc_ref, gq_ref, gk_ref, gv_ref, off_ref, gk_sum, gv_sum, strip = refs
    else:
        q_ref, k_ref, v_ref, e_ref, c_ref, inv_ref, gc_ref, gq_ref, gk_ref, gv_ref, gk_sum, gv_sum = refs
    i = pl.program_id(1)

    @pl.when(i == 0)
    def _():
        gk_sum[...] = jnp.zeros_like(gk_sum)
        gv_sum[...] = jnp.zeros_like(gv_sum)
        if biased:
            strip[...] = jnp.zeros_like(strip)

    scaled = (gc_ref[...].astype(jnp.float32) * inv_ref[...]).astype(jnp.bfloat16)
    product = scaled.astype(jnp.float32) * c_ref[...].astype(jnp.float32)
    lane = lax.broadcasted_iota(jnp.int32, (block, PAIR), 1)
    inner = (
        jnp.sum(jnp.where(lane < DK, product, 0.0), axis=1, keepdims=True),
        jnp.sum(jnp.where(lane < DK, 0.0, product), axis=1, keepdims=True),
    )
    g_heads = split_heads(scaled)
    q_heads = split_heads(q_ref[...])
    k_heads = split_heads(k_ref[...])
    gq = None
    for head in range(2):
        weights = e_ref[head]
        grad = dot_nt(g_heads[head], v_ref[...])
        grad = weights.astype(jnp.float32) * (grad - inner[head])
        if biased:
            start = pl.multiple_of((keys_count // block - 1 - i) * block, block)
            strip[head, :, pl.ds(start, keys_count)] += grad
        grad = grad.astype(jnp.bfloat16)
        part = dot_nn(grad, k_heads[head])
        gq = part if gq is None else gq + part
        gk_sum[...] += dot_tn(grad, q_heads[head])
        gv_sum[...] += dot_tn(weights, g_heads[head])
    gq_ref[...] = gq.astype(jnp.bfloat16)

    @pl.when(i == steps - 1)
    def _():
        gk_ref[...] = gk_sum[...].astype(jnp.bfloat16)
        gv_ref[...] = gv_sum[...].astype(jnp.bfloat16)
        if biased:
            wide = 2 * keys_count
            for head in range(2):
                total = jnp.zeros((8, wide), jnp.float32)
                for a in range(block // 8):
                    total = total + pltpu.roll(strip[head, 8 * a : 8 * a + 8, :], (block - 8 * a) % wide, 1)
                off_ref[0, head] = total


def attend_forward(query, keys, values, base, query_segments, key_segments, causal):
    count, cols = query.shape[0], keys.shape[0]
    pairs = query.shape[1] // PAIR
    block = min(256, count)
    steps = count // block
    row_spec = pl.BlockSpec((block, PAIR), lambda h, i: (i, h))
    key_spec = pl.BlockSpec((cols, PAIR), lambda h, i: (0, h))
    in_specs = [
        pl.BlockSpec((block, 1), lambda h, i: (i, 0)),
        pl.BlockSpec((1, cols), lambda h, i: (0, 0)),
    ]
    args = [query_segments[:, None], key_segments[None, :]]
    scratch = []
    if base is not None:
        in_specs.append(pl.BlockSpec((1, 2, 8, 2 * cols), lambda h, i: (h, 0, 0, 0)))
        args.append(base)
        scratch.append(pltpu.VMEM((2, block, 2 * cols), jnp.float32))
    return pl.pallas_call(
        functools.partial(attend_kernel, block, cols, causal, base is not None),
        grid=(pairs, steps),
        in_specs=in_specs + [row_spec, key_spec, key_spec],
        out_specs=[
            pl.BlockSpec((2, block, cols), lambda h, i: (h, i, 0)),
            row_spec,
            row_spec,
        ],
        out_shape=[
            jax.ShapeDtypeStruct((2 * pairs, count, cols), jnp.bfloat16),
            jax.ShapeDtypeStruct((count, pairs * PAIR), jnp.bfloat16),
            jax.ShapeDtypeStruct((count, pairs * PAIR), jnp.float32),
        ],
        scratch_shapes=scratch,
        compiler_params=pltpu.CompilerParams(vmem_limit_bytes=VMEM_BYTES),
        cost_estimate=pl.CostEstimate(
            flops=4 * count * cols * PAIR * 2 * pairs, bytes_accessed=2 * pairs * count * cols * 2, transcendentals=0
        ),
    )(*args, query, keys, values)


def attend_backward(query, keys, values, saved, grad_context, biased):
    weights, context, inverse = saved
    count, cols = query.shape[0], keys.shape[0]
    pairs = query.shape[1] // PAIR
    block = min(256, count)
    steps = count // block
    row_spec = pl.BlockSpec((block, PAIR), lambda h, i: (i, h))
    key_spec = pl.BlockSpec((cols, PAIR), lambda h, i: (0, h))
    out_specs = [row_spec, key_spec, key_spec]
    out_shape = [
        jax.ShapeDtypeStruct((count, pairs * PAIR), jnp.bfloat16),
        jax.ShapeDtypeStruct((cols, pairs * PAIR), jnp.bfloat16),
        jax.ShapeDtypeStruct((cols, pairs * PAIR), jnp.bfloat16),
    ]
    scratch = [pltpu.VMEM((cols, PAIR), jnp.float32), pltpu.VMEM((cols, PAIR), jnp.float32)]
    if biased:
        out_specs.append(pl.BlockSpec((1, 2, 8, 2 * cols), lambda h, i: (h, 0, 0, 0)))
        out_shape.append(jax.ShapeDtypeStruct((pairs, 2, 8, 2 * cols), jnp.float32))
        scratch.append(pltpu.VMEM((2, block, 2 * cols), jnp.float32))
    return pl.pallas_call(
        functools.partial(attend_back_kernel, block, cols, steps, biased),
        grid=(pairs, steps),
        in_specs=[
            row_spec,
            key_spec,
            key_spec,
            pl.BlockSpec((2, block, cols), lambda h, i: (h, i, 0)),
            row_spec,
            row_spec,
            row_spec,
        ],
        out_specs=out_specs,
        out_shape=out_shape,
        scratch_shapes=scratch,
        compiler_params=pltpu.CompilerParams(vmem_limit_bytes=VMEM_BYTES),
        cost_estimate=pl.CostEstimate(
            flops=8 * count * cols * PAIR * 2 * pairs, bytes_accessed=2 * pairs * count * cols * 2, transcendentals=0
        ),
    )(query, keys, values, weights, context, inverse, grad_context)


MESH_IDS = pl.DeviceIdType.MESH
CHUNK = 256
ATT = 4 * 384


def any_spec():
    return pl.BlockSpec(memory_space=pl.ANY)


def vmem_spec():
    return pl.BlockSpec(memory_space=pltpu.VMEM)


def normed(values, gain):
    return values * lax.rsqrt(jnp.mean(values * values, axis=1, keepdims=True) + EPS) * gain


def gelu_pair(values):
    square = values * values
    inner = jnp.tanh(GELU_A * values * (1.0 + GELU_B * square))
    half = 0.5 * (1.0 + inner)
    slope = half + 0.5 * values * (1.0 - inner * inner) * (GELU_A * (1.0 + 3.0 * GELU_B * square))
    return values * half, slope


class Place:
    def __init__(self, wide):
        self.core = lax.axis_index("dp")
        self.wide = lax.axis_index("wide")
        self.side = lax.axis_index("narrow")
        self.count = wide
        self.fars = wide // 2
        self.far = self.wide // 2
        self.near = self.wide % 2

    def sibling(self):
        return (1 - self.core, self.wide, self.side)

    def across(self):
        return (self.core, self.wide, 1 - self.side)

    def beside(self):
        return (self.core, 2 * self.far + 1 - self.near, self.side)

    def along(self, step):
        return (self.core, 2 * lax.rem(self.far + step, self.fars) + self.near, self.side)

    def index_from(self, step):
        return 2 * lax.rem(self.far - step + self.fars, self.fars) + self.near

    def index_beside(self, step):
        return 2 * lax.rem(self.far - step + self.fars, self.fars) + 1 - self.near

    def greet(self):
        partners = [self.sibling(), self.across(), self.beside()]
        partners += [self.along(step) for step in range(1, self.fars)]
        barrier = pltpu.get_barrier_semaphore()
        for partner in partners:
            pl.semaphore_signal(barrier, inc=1, device_id=partner, device_id_type=MESH_IDS)
        pl.semaphore_wait(barrier, len(partners))


def remote(source, target, send, receive, partner):
    return pltpu.make_async_remote_copy(
        src_ref=source,
        dst_ref=target,
        send_sem=send,
        recv_sem=receive,
        device_id=partner,
        device_id_type=MESH_IDS,
    )


class Gather:
    def __init__(self, place, pack, groups, send, receive, local):
        self.place, self.pack, self.groups = place, pack, groups
        self.send, self.receive, self.local = send, receive, local
        self.rows = pack.shape[0]
        self.sent = []

    def at(self, group, index, core):
        first, width, target, offset = self.groups[group]
        half = width // 2
        start = pl.multiple_of(offset + core * half, 128)
        return target.at[pl.ds(pl.multiple_of(index * self.rows, 16), self.rows), pl.ds(start, half)]

    def own(self, group):
        first, width, target, offset = self.groups[group]
        half = width // 2
        return self.pack.at[:, pl.ds(pl.multiple_of(first + self.place.core * half, 128), half)]

    def local_copy(self, group):
        first, width, target, offset = self.groups[group]
        rows = pl.ds(pl.multiple_of(self.place.wide * self.rows, 16), self.rows)
        return pltpu.make_async_copy(
            self.pack.at[:, pl.ds(first, width)], target.at[rows, pl.ds(offset, width)], self.local.at[group]
        )

    def push(self, group, slot, source, index, partner):
        copy = remote(
            source,
            self.at(group, index, self.place.core),
            self.send.at[group, slot],
            self.receive.at[group, slot],
            partner,
        )
        copy.start()
        self.sent.append(copy)

    def await_slot(self, group, slot, index, core):
        block = self.at(group, index, core)
        remote(block, block, self.send.at[group, slot], self.receive.at[group, slot], self.place.sibling()).wait_recv()

    def start(self, group):
        place, fars = self.place, self.place.fars
        for step in range(1, fars):
            self.push(group, step - 1, self.own(group), place.wide, place.along(step))
        self.push(group, fars - 1, self.own(group), place.wide, place.beside())
        self.local_copy(group).start()

    def relay_along(self, group):
        place, fars = self.place, self.place.fars
        for step in range(1, fars):
            index = place.index_from(step)
            self.await_slot(group, step - 1, index, place.core)
            block = self.at(group, index, place.core)
            self.push(group, fars - 1 + step, block, index, place.beside())
            self.push(group, 2 * fars - 2 + step, block, index, place.sibling())

    def relay_beside(self, group):
        place, fars = self.place, self.place.fars
        for step in range(fars):
            index = place.index_beside(step)
            self.await_slot(group, fars - 1 + step, index, place.core)
            block = self.at(group, index, place.core)
            self.push(group, 3 * fars - 2 + step, block, index, place.sibling())

    def finish(self, group):
        place, fars = self.place, self.place.fars
        for step in range(1, fars):
            self.await_slot(group, 2 * fars - 2 + step, place.index_from(step), 1 - place.core)
        for step in range(fars):
            self.await_slot(group, 3 * fars - 2 + step, place.index_beside(step), 1 - place.core)
        self.local_copy(group).wait()

    def close(self):
        for copy in self.sent:
            copy.wait_send()


def gather_slots(wide):
    return 4 * (wide // 2) - 2


def softmax_pair(q_pair, k_pair, v_pair, allowed, biases, e_store):
    q_heads = split_heads(q_pair)
    v_heads = split_heads(v_pair)
    inverses = []
    context = None
    for head in range(2):
        scores = dot_nt(q_heads[head], k_pair)
        if biases is not None:
            scores = scores + biases(head)
        scores = jnp.where(allowed, scores, NEG)
        highest = jnp.max(scores, axis=1, keepdims=True)
        weights = jnp.exp(scores - highest)
        inverses.append(1.0 / jnp.sum(weights, axis=1, keepdims=True))
        weights = weights.astype(jnp.bfloat16)
        e_store(head, weights)
        part = dot_nn(weights, v_heads[head])
        context = part if context is None else context + part
    lane = lax.broadcasted_iota(jnp.int32, context.shape, 1)
    inverse = jnp.where(lane < DK, inverses[0], inverses[1])
    return inverse, (context * inverse).astype(jnp.bfloat16)


def build_strip(strip, base, pairs, block, span):
    def one(pair, carry):
        for head in range(2):
            rows = base[pair, head]
            for a in range(block // 8):
                strip[2 * pair + head, 8 * a : 8 * a + 8, :] = pltpu.roll(rows, (8 * a + 2 * span - block) % (2 * span), 1)
        return carry

    lax.fori_loop(0, pairs, one, 0)


def enc_forward_kernel(
    wide,
    x_own,
    pack,
    gains,
    base,
    qseg,
    kseg,
    w1,
    w2,
    n0,
    qkv,
    c,
    inv,
    e_all,
    e1,
    n1,
    slope_all,
    a_all,
    ef,
    mem,
    x_full,
    strip,
    e_buf,
    slope_buf,
    a_buf,
    y_send,
    y_recv,
    g_send,
    g_recv,
    g_local,
    x_sems,
    y_sems,
    z_sems,
    l_sems,
):
    place = Place(wide)
    side = place.side
    half = x_own.shape[0]
    rows = 2 * half
    steps = rows // CHUNK
    width = c.shape[1]
    ffn = a_all.shape[1]
    pairs = width // PAIR
    place.greet()
    gather = Gather(
        place,
        pack,
        [
            (0, 4 * width, w1, 0),
            (4 * width, 2 * ffn, w1, 4 * width),
            (4 * width + 2 * ffn, 8 * width, w2, 0),
            (12 * width + 2 * ffn, 2 * ffn, w2, 8 * width),
        ],
        g_send,
        g_recv,
        g_local,
    )
    mine = pl.ds(pl.multiple_of(side * half, 16), half)
    swap_x = remote(x_own, x_full.at[mine], x_sems.at[0], x_sems.at[1], place.across())
    gather.start(0)
    swap_x.start()
    keep_x = pltpu.make_async_copy(x_own, x_full.at[mine], l_sems.at[6])
    keep_x.start()
    build_strip(strip, base, pairs, CHUNK, rows)
    gather.relay_along(0)
    gather.start(1)
    keep_x.wait()
    gather.relay_beside(0)
    swap_x.wait()

    def norm_rows(i, carry):
        at = pl.ds(pl.multiple_of(i * CHUNK, CHUNK), CHUNK)
        n0[at, :] = normed(x_full[at, :].astype(jnp.float32), gains[0:1, :]).astype(jnp.bfloat16)
        return carry

    lax.fori_loop(0, steps, norm_rows, 0)
    gather.finish(0)

    def project(i, carry):
        at = pl.ds(pl.multiple_of(i * CHUNK, CHUNK), CHUNK)
        qkv[at, :] = dot_nn(n0[at, :], w1[:, : 3 * width]).astype(jnp.bfloat16)
        return carry

    lax.fori_loop(0, steps, project, 0)

    def lanes(base_lane, pair):
        return pl.ds(pl.multiple_of(base_lane + pair * PAIR, PAIR), PAIR)

    def save(i, kind):
        slot = i % 2
        at = pl.ds(i * CHUNK, CHUNK)
        if kind == 0:
            return pltpu.make_async_copy(e_buf.at[slot], e_all.at[:, at, :], l_sems.at[slot])
        if kind == 1:
            return pltpu.make_async_copy(slope_buf.at[slot], slope_all.at[at, :], l_sems.at[2 + slot])
        return pltpu.make_async_copy(a_buf.at[slot], a_all.at[at, :], l_sems.at[4 + slot])

    def swap_y(layer, i):
        at = pl.ds(i * CHUNK, CHUNK)
        sems = y_sems if layer == 0 else z_sems
        return remote(y_send.at[layer, at], y_recv.at[layer, at], sems.at[0, i], sems.at[1, i], place.across())

    def attend(i):
        at = slice(i * CHUNK, (i + 1) * CHUNK)
        slot = i % 2
        if i >= 2:
            save(i - 2, 0).wait()
        first = (steps - 1 - i) * CHUNK

        def one(pair, carry):
            allowed = qseg[at, :] == kseg[...]

            def bias(head):
                return strip[2 * pair + head, :, first : first + rows]

            def store(head, weights):
                e_buf[slot, 2 * pair + head] = weights

            inverse, context = softmax_pair(
                qkv[at, lanes(0, pair)],
                qkv[:, lanes(width, pair)],
                qkv[:, lanes(2 * width, pair)],
                allowed,
                bias,
                store,
            )
            inv[at, lanes(0, pair)] = inverse
            c[at, lanes(0, pair)] = context
            return carry

        lax.fori_loop(0, pairs, one, 0)
        save(i, 0).start()
        y_send[0, at, :] = dot_nt(c[at, :], w1[:, 3 * width : 4 * width]).astype(jnp.bfloat16)
        swap_y(0, i).start()

    def feed(i):
        at = slice(i * CHUNK, (i + 1) * CHUNK)
        slot = i % 2
        swap_y(0, i).wait_recv()
        both = y_send[0, at, :].astype(jnp.float32) + y_recv[0, at, :].astype(jnp.float32)
        middle = x_full[at, :].astype(jnp.float32) + both
        e1[at, :] = middle
        rounded = normed(middle, gains[1:2, :]).astype(jnp.bfloat16)
        n1[at, :] = rounded
        if i >= 2:
            save(i - 2, 1).wait()
            save(i - 2, 2).wait()

        def part(j, carry):
            cols = pl.ds(pl.multiple_of(4 * width + j * width, PAIR), width)
            here = pl.ds(pl.multiple_of(j * width, PAIR), width)
            active, slope = gelu_pair(dot_nn(n1[at, :], w1[:, cols]))
            a_buf[slot, :, here] = active.astype(jnp.bfloat16)
            slope_buf[slot, :, here] = slope.astype(jnp.bfloat16)
            return carry

        lax.fori_loop(0, ffn // width, part, 0)
        save(i, 1).start()
        save(i, 2).start()
        y_send[1, at, :] = dot_nt(a_buf[slot], w1[:, 4 * width + ffn :]).astype(jnp.bfloat16)
        swap_y(1, i).start()

    def last(i):
        at = slice(i * CHUNK, (i + 1) * CHUNK)
        swap_y(1, i).wait_recv()
        both = y_send[1, at, :].astype(jnp.float32) + y_recv[1, at, :].astype(jnp.float32)
        final = e1[at, :] + both
        ef[at, :] = final
        mem[at, :] = normed(final, gains[5:6, :]).astype(jnp.bfloat16)

    attend(0)
    gather.relay_along(1)
    gather.start(2)
    attend(1)
    gather.relay_beside(1)
    attend(2)
    gather.finish(1)
    feed(0)
    gather.relay_along(2)
    gather.start(3)
    attend(3)
    feed(1)
    gather.relay_beside(2)
    feed(2)
    gather.relay_along(3)
    feed(3)
    last(0)
    last(1)
    gather.relay_beside(3)
    last(2)
    last(3)
    gather.finish(2)
    gather.finish(3)
    gather.close()
    for i in range(steps):
        swap_y(0, i).wait_send()
        swap_y(1, i).wait_send()
    for i in range(steps - 2, steps):
        for kind in range(3):
            save(i, kind).wait()


def enc_forward(wide, x_own, pack, gains, base, segments):
    half, model = x_own.shape
    rows = 2 * half
    pairs = base.shape[0]
    width = pairs * PAIR
    ffn = (pack.shape[1] - 12 * width) // 4
    bf, f32 = jnp.bfloat16, jnp.float32
    shape = jax.ShapeDtypeStruct
    slots = gather_slots(wide)
    steps = rows // CHUNK
    return pl.pallas_call(
        functools.partial(enc_forward_kernel, wide),
        in_specs=[vmem_spec(), any_spec(), vmem_spec(), vmem_spec(), vmem_spec(), vmem_spec()],
        out_shape=[
            shape((model, 4 * width + 2 * ffn), bf),
            shape((model, 8 * width + 2 * ffn), bf),
            shape((rows, model), bf),
            shape((rows, 3 * width), bf),
            shape((rows, width), bf),
            shape((rows, width), f32),
            shape((2 * pairs, rows, rows), bf),
            shape((rows, model), f32),
            shape((rows, model), bf),
            shape((rows, ffn), bf),
            shape((rows, ffn), bf),
            shape((rows, model), f32),
            shape((rows, model), bf),
        ],
        out_specs=[
            vmem_spec(),
            any_spec(),
            vmem_spec(),
            vmem_spec(),
            vmem_spec(),
            vmem_spec(),
            any_spec(),
            vmem_spec(),
            vmem_spec(),
            any_spec(),
            any_spec(),
            vmem_spec(),
            vmem_spec(),
        ],
        scratch_shapes=[
            pltpu.VMEM((rows, model), bf),
            pltpu.VMEM((2 * pairs, CHUNK, 2 * rows), f32),
            pltpu.VMEM((2, 2 * pairs, CHUNK, rows), bf),
            pltpu.VMEM((2, CHUNK, ffn), bf),
            pltpu.VMEM((2, CHUNK, ffn), bf),
            pltpu.VMEM((2, rows, model), bf),
            pltpu.VMEM((2, rows, model), bf),
            pltpu.SemaphoreType.DMA((4, slots)),
            pltpu.SemaphoreType.DMA((4, slots)),
            pltpu.SemaphoreType.DMA((4,)),
            pltpu.SemaphoreType.DMA((2,)),
            pltpu.SemaphoreType.DMA((2, steps)),
            pltpu.SemaphoreType.DMA((2, steps)),
            pltpu.SemaphoreType.DMA((7,)),
        ],
        compiler_params=pltpu.CompilerParams(
            collective_id=0, has_side_effects=True, vmem_limit_bytes=VMEM_BYTES
        ),
        cost_estimate=pl.CostEstimate(flops=10**10, bytes_accessed=6 * 10**7, transcendentals=0),
    )(x_own, pack, gains, base, segments[:, None], segments[None, :])


def ffn_backward(grad_rows, normed_rows, hidden, active, weight_up, weight_down):
    grad_active = jnp.einsum(
        "rd,fd->rf", grad_rows, weight_down, preferred_element_type=jnp.float32
    )
    grad_down = jnp.einsum("rf,rd->fd", active, grad_rows, preferred_element_type=jnp.float32)
    unused, pull = jax.vjp(gelu_tanh, hidden)
    grad_hidden = pull(grad_active)[0].astype(jnp.bfloat16)
    grad_up = jnp.einsum("rd,rf->df", normed_rows, grad_hidden, preferred_element_type=jnp.float32)
    grad_normed = jnp.einsum(
        "rf,df->rd", grad_hidden, weight_up, preferred_element_type=jnp.float32
    )
    return (grad_normed, grad_up, grad_down)


def norm_backward(values, gain, grad_normed):
    unused, pull = jax.vjp(rms_norm, values, gain)
    return pull(grad_normed)


NEAR = 2 * CHUNK


def norm_back(values, gain, grad):
    scale = lax.rsqrt(jnp.mean(values * values, axis=1, keepdims=True) + EPS)
    scaled = grad * gain
    pulled = scale * (scaled - values * (scale * scale) * jnp.mean(scaled * values, axis=1, keepdims=True))
    return pulled, jnp.sum(grad * values * scale, axis=0, keepdims=True)


class Scatter:
    def __init__(self, place, rows, groups, tile, send, receive):
        self.place, self.rows, self.groups, self.tile = place, rows, groups, tile
        self.send, self.receive = send, receive
        self.sent = []

    def columns(self, group, core):
        first, width = self.groups[group]["first"], self.groups[group]["width"]
        return pl.ds(pl.multiple_of(first + core * (width // 2), 128), width // 2)

    def block(self, group, index):
        return self.groups[group]["grad"].at[
            pl.ds(pl.multiple_of(index * self.rows, 16), self.rows), self.columns(group, self.place.core)
        ]

    def push(self, group, slot, source, target, partner, arrival=None):
        arrival = slot if arrival is None else arrival
        copy = remote(source, target, self.send.at[group, slot], self.receive.at[group, arrival], partner)
        copy.start()
        self.sent.append(copy)

    def await_slot(self, group, slot, block):
        remote(block, block, self.send.at[group, 0], self.receive.at[group, slot], self.place.sibling()).wait_recv()

    def start(self, group):
        parts = self.groups[group]
        self.push(
            group, 0, parts["grad"].at[:, self.columns(group, 1 - self.place.core)], parts["core"], self.place.sibling()
        )

    def add_block(self, group, index, other):
        block = self.block(group, index)
        block[...] = (block[...].astype(jnp.float32) + other.astype(jnp.float32)).astype(jnp.bfloat16)
        return block

    def beside(self, group):
        parts, place = self.groups[group], self.place
        self.await_slot(group, 0, parts["core"])

        def received(index):
            return parts["core"][pl.ds(pl.multiple_of(index * self.rows, 16), self.rows), :]

        for step in range(place.fars):
            far = lax.rem(place.far + 1 + step, place.fars)
            index = 2 * far + 1 - place.near
            block = self.add_block(group, index, received(index))
            self.push(group, 1 + step, block, parts["beside"].at[step], place.beside())
        for step in range(place.fars):
            far = lax.rem(place.far + 1 + step, place.fars)
            index = 2 * far + place.near
            self.add_block(group, index, received(index))

    def along(self, group):
        parts, place = self.groups[group], self.place
        for step in range(1, place.fars):
            index = 2 * lax.rem(place.far + step, place.fars) + place.near
            self.await_slot(group, step, parts["beside"].at[step - 1])
            block = self.add_block(group, index, parts["beside"][step - 1])
            self.push(group, place.fars + step, block, parts["along"].at[step - 1], place.along(step))

    def total(self, group):
        parts, place = self.groups[group], self.place
        self.await_slot(group, place.fars, parts["beside"].at[place.fars - 1])
        value = self.block(group, place.wide)[...].astype(jnp.float32) + parts["beside"][place.fars - 1].astype(jnp.float32)
        for step in range(1, place.fars):
            self.await_slot(group, place.fars + step, parts["along"].at[step - 1])
            value = value + parts["along"][step - 1].astype(jnp.float32)
        half = parts["width"] // 2
        block = self.tile.at[:, pl.ds(pl.multiple_of(parts["out"] + place.core * half, 128), half)]
        block[...] = value.astype(jnp.bfloat16)
        self.push(group, 2 * place.fars, block, block, place.sibling())

    def finish(self, group):
        parts, place = self.groups[group], self.place
        half = parts["width"] // 2
        block = self.tile.at[:, pl.ds(pl.multiple_of(parts["out"] + (1 - place.core) * half, 128), half)]
        self.await_slot(group, 2 * place.fars, block)

    def close(self):
        for copy in self.sent:
            copy.wait_send()


def scatter_slots(wide):
    return 2 * (wide // 2) + 1


def scatter_buffers(wide, model, width):
    half, rows, fars = width // 2, model // wide, wide // 2
    return [
        pltpu.VMEM((model, half), jnp.bfloat16),
        pltpu.VMEM((fars, rows, half), jnp.bfloat16),
        pltpu.VMEM((fars - 1, rows, half), jnp.bfloat16),
    ]


def softmax_back_pair(q_pair, k_pair, v_pair, c_pair, inverse, gc_pair, weights, near):
    scaled = (gc_pair.astype(jnp.float32) * inverse).astype(jnp.bfloat16)
    product = scaled.astype(jnp.float32) * c_pair.astype(jnp.float32)
    lane = lax.broadcasted_iota(jnp.int32, product.shape, 1)
    inner = (
        jnp.sum(jnp.where(lane < DK, product, 0.0), axis=1, keepdims=True),
        jnp.sum(jnp.where(lane < DK, 0.0, product), axis=1, keepdims=True),
    )
    g_heads = split_heads(scaled)
    q_heads = split_heads(q_pair)
    k_heads = split_heads(k_pair)
    gq = None
    grads = []
    for head in range(2):
        grad = weights[head].astype(jnp.float32) * (dot_nt(g_heads[head], v_pair) - inner[head])
        if near is not None:
            near(head, grad)
        grad = grad.astype(jnp.bfloat16)
        grads.append(grad)
        part = dot_nn(grad, k_heads[head])
        gq = part if gq is None else gq + part
    gk = dot_tn(jnp.concatenate(grads, axis=0), jnp.concatenate(q_heads, axis=0))
    gv = dot_tn(jnp.concatenate([weights[0], weights[1]], axis=0), jnp.concatenate(g_heads, axis=0))
    return gq, gk, gv


def fold_near(rows):
    total = jnp.zeros((8, 2 * NEAR), jnp.float32)
    blank = jnp.zeros((8, NEAR), jnp.float32)
    for a in range(CHUNK // 8):
        wider = jnp.concatenate([rows[8 * a : 8 * a + 8, :], blank], axis=1)
        total = total + pltpu.roll(wider, (CHUNK - 8 * a) % (2 * NEAR), 1)
    return total


def near_table_grad(near_sums, far_sums):
    heads = near_sums.shape[0]
    places = jnp.arange(2 * NEAR, dtype=jnp.int32)[None, :]
    relative = places - jnp.arange(8, dtype=jnp.int32)[:, None] - CHUNK - NEAR // 4
    buckets = bucket_index(relative.reshape(-1), True)
    onehot = (buckets[None, :] == jnp.arange(NB, dtype=jnp.int32)[:, None]).astype(jnp.float32)
    near = lax.dot_general(
        onehot,
        near_sums.reshape(heads, 16 * NEAR),
        (((1,), (1,)), ((), ())),
        precision=HIGH,
        preferred_element_type=jnp.float32,
    )
    far = jnp.sum(far_sums, axis=(2, 3))
    ends = jnp.array([[NB // 2 - 1], [NB - 1]], jnp.int32)
    choose = (ends == jnp.arange(NB, dtype=jnp.int32)[None, :]).astype(jnp.float32)
    return near + lax.dot_general(choose, far, (((0,), (0,)), ((), ())), precision=HIGH, preferred_element_type=jnp.float32)


def enc_backward_kernel(
    wide,
    x_own,
    cot_own,
    cot_other,
    gains,
    memory_part,
    w1_in,
    n0_in,
    qkv_in,
    c_in,
    inv_in,
    e_all,
    e1_all,
    n1_in,
    slope_all,
    a_in,
    ef_all,
    grad_out,
    tile,
    gain_sums,
    near_sums,
    far_sums,
    w1,
    n0,
    qkv,
    c,
    inv,
    n1,
    active,
    cot,
    e_buf,
    state_buf,
    slope_buf,
    part_buf,
    m_recv,
    g_send,
    g_recv,
    state_grad,
    gy,
    gu,
    gqkv,
    gk_sum,
    gv_sum,
    strip,
    core_f,
    beside_f,
    along_f,
    beside_a,
    along_a,
    s_send,
    s_recv,
    m_sems,
    g_sems,
    l_sems,
    e_sems,
    t_sems,
    i_sems,
):
    place = Place(wide)
    side = place.side
    half = x_own.shape[0]
    rows = 2 * half
    steps = rows // CHUNK
    width = c.shape[1]
    ffn = active.shape[1]
    pairs = width // PAIR
    model = x_own.shape[1]
    bf, f32 = jnp.bfloat16, jnp.float32
    place.greet()

    def swap(kind, i):
        at = pl.ds(i * CHUNK, CHUNK)
        if kind == 0:
            return remote(memory_part.at[at], m_recv.at[at], m_sems.at[0, i], m_sems.at[1, i], place.across())
        return remote(g_send.at[at], g_recv.at[at], g_sems.at[0, i], g_sems.at[1, i], place.across())

    for i in range(steps):
        swap(0, i).start()

    def fetch(i):
        at = pl.ds(i * CHUNK, CHUNK)
        slot = i % 2
        return [
            pltpu.make_async_copy(ef_all.at[at], state_buf.at[slot], t_sems.at[0, slot]),
            pltpu.make_async_copy(slope_all.at[at], slope_buf.at[slot], t_sems.at[1, slot]),
            pltpu.make_async_copy(memory_part.at[at], part_buf.at[slot], t_sems.at[2, slot]),
        ]

    def fetch_state(i):
        at = pl.ds(i * CHUNK, CHUNK)
        return pltpu.make_async_copy(e1_all.at[at], state_buf.at[i % 2], t_sems.at[0, i % 2])

    def fetch_e(step):
        chunk, pair, slot = step // pairs, lax.rem(step, pairs), lax.rem(step, 2)
        at = pl.ds(pl.multiple_of(chunk * CHUNK, CHUNK), CHUNK)
        return pltpu.make_async_copy(e_all.at[pl.ds(2 * pair, 2), at, :], e_buf.at[slot], e_sems.at[slot])

    mine = pl.ds(pl.multiple_of(side * half, 16), half)
    theirs = pl.ds(pl.multiple_of((1 - side) * half, 16), half)
    loads = [
        pltpu.make_async_copy(cot_own, cot.at[mine], i_sems.at[0]),
        pltpu.make_async_copy(cot_other, cot.at[theirs], i_sems.at[1]),
        pltpu.make_async_copy(w1_in, w1, i_sems.at[2]),
        pltpu.make_async_copy(a_in, active, i_sems.at[3]),
        pltpu.make_async_copy(n1_in, n1, i_sems.at[4]),
        pltpu.make_async_copy(qkv_in, qkv, i_sems.at[5]),
        pltpu.make_async_copy(c_in, c, i_sems.at[6]),
        pltpu.make_async_copy(inv_in, inv, i_sems.at[7]),
        pltpu.make_async_copy(n0_in, n0, i_sems.at[8]),
    ]
    for load in loads[:2]:
        load.start()
    for load in fetch(0):
        load.start()
    for load in loads[2:]:
        load.start()
    gk_sum[...] = jnp.zeros_like(gk_sum)
    gv_sum[...] = jnp.zeros_like(gv_sum)
    strip[...] = jnp.zeros_like(strip)
    far_sums[...] = jnp.zeros_like(far_sums)
    gain_sums[...] = jnp.zeros_like(gain_sums)
    scatter = Scatter(
        place,
        model // wide,
        [
            dict(grad=w1, first=4 * width, width=2 * ffn, out=4 * width, core=core_f, beside=beside_f, along=along_f),
            dict(grad=gu.at[pl.ds(0, model)], first=0, width=4 * width, out=0, core=active.at[pl.ds(0, model), pl.ds(0, 2 * width)], beside=beside_a, along=along_a),
        ],
        tile,
        s_send,
        s_recv,
    )

    def own_weight(i):
        return jnp.where((i * CHUNK) // half == side, 1.0, 0.0).astype(f32)

    for load in loads[:3]:
        load.wait()

    for i in range(steps):
        at = slice(i * CHUNK, (i + 1) * CHUNK)
        slot = i % 2
        if i + 1 < steps:
            for load in fetch(i + 1):
                load.start()
        for load in fetch(i):
            load.wait()
        swap(0, i).wait_recv()
        grad = part_buf[slot].astype(f32) + m_recv[at, :].astype(f32)
        pulled, gain = norm_back(state_buf[slot], gains[5:6, :], grad)
        gain_sums[5:6, :] += gain * own_weight(i)
        total = cot[at, :].astype(f32) + pulled
        state_grad[at, :] = total
        gy[at, :] = total.astype(bf)

        def part(j, carry):
            cols = pl.ds(pl.multiple_of(4 * width + ffn + j * width, PAIR), width)
            here = pl.ds(pl.multiple_of(j * width, PAIR), width)
            grad_active = dot_nn(gy[at, :], w1[:, cols])
            gu[at, here] = (slope_buf[slot, :, here].astype(f32) * grad_active).astype(bf)
            return carry

        lax.fori_loop(0, ffn // width, part, 0)
        g_send[at, :] = dot_nt(gu[at, :], w1[:, 4 * width : 4 * width + ffn]).astype(bf)
        swap(1, i).start()
    for load in loads[3:]:
        load.wait()
    fetch_state(0).start()
    fetch_e(0).start()

    def weight_grads(t, carry):
        tile_rows = pl.ds(pl.multiple_of(t * CHUNK, CHUNK), CHUNK)
        w1[tile_rows, 4 * width : 4 * width + ffn] = dot_tn(n1[:, tile_rows], gu[...]).astype(bf)
        w1[tile_rows, 4 * width + ffn :] = dot_tn(gy[:, tile_rows], active[...]).astype(bf)
        return carry

    lax.fori_loop(0, model // CHUNK, weight_grads, 0)
    scatter.start(0)

    dw0 = gu
    l_send, l_recv = n1, m_recv

    def lanes(base_lane, pair):
        return pl.ds(pl.multiple_of(base_lane + pair * PAIR, PAIR), PAIR)

    def attend_back(i):
        at = slice(i * CHUNK, (i + 1) * CHUNK)
        slot = i % 2
        if i + 1 < steps:
            fetch_state(i + 1).start()
        fetch_state(i).wait()
        swap(1, i).wait_recv()
        grad = g_send[at, :].astype(f32) + g_recv[at, :].astype(f32)
        pulled, gain = norm_back(state_buf[slot], gains[1:2, :], grad)
        gain_sums[1:2, :] += gain * own_weight(i)
        total = state_grad[at, :] + pulled
        state_grad[at, :] = total
        gy[at, :] = total.astype(bf)
        g_send[at, :width] = dot_nn(gy[at, :], w1[:, 3 * width : 4 * width]).astype(bf)
        low, high = max(i * CHUNK - NEAR // 4, 0), min(i * CHUNK + CHUNK + NEAR // 4, rows)
        shift = low - (i * CHUNK - NEAR // 4)

        def one(pair, carry):
            step = i * pairs + pair

            @pl.when(step + 1 < steps * pairs)
            def _():
                fetch_e(step + 1).start()

            fetch_e(step).wait()
            e_slot = lax.rem(step, 2)

            def near(head, grad):
                strip[2 * pair + head, :, shift : shift + high - low] += grad[:, low:high]
                for edge, (start, end) in enumerate(((0, low), (high, rows))):
                    if end > start:
                        folded = jnp.sum(grad[:, start:end].reshape(CHUNK // 8, 8, end - start), axis=0)
                        wide_sum = folded[:, :128]
                        for lane in range(128, end - start, 128):
                            wide_sum = wide_sum + folded[:, lane : lane + 128]
                        far_sums[edge, 2 * pair + head] += wide_sum

            gq, gk, gv = softmax_back_pair(
                qkv[at, lanes(0, pair)],
                qkv[:, lanes(width, pair)],
                qkv[:, lanes(2 * width, pair)],
                c[at, lanes(0, pair)],
                inv[at, lanes(0, pair)],
                g_send[at, lanes(0, pair)],
                (e_buf[e_slot, 0], e_buf[e_slot, 1]),
                near,
            )
            gqkv[at, lanes(0, pair)] = gq.astype(bf)
            gk_sum[:, lanes(0, pair)] += gk
            gv_sum[:, lanes(0, pair)] += gv
            return carry

        lax.fori_loop(0, pairs, one, 0)

    for i in range(steps):
        swap(1, i).wait_send()
        attend_back(i)
        if i == 0:
            scatter.beside(0)
        if i == 2:
            scatter.along(0)
    gqkv[:, width : 2 * width] = gk_sum[...].astype(bf)
    gqkv[:, 2 * width :] = gv_sum[...].astype(bf)

    def weight_grads_a(t, carry):
        tile_rows = pl.ds(pl.multiple_of(t * CHUNK, CHUNK), CHUNK)
        dw0[tile_rows, : 3 * width] = dot_tn(n0[:, tile_rows], gqkv[...]).astype(bf)
        dw0[tile_rows, 3 * width :] = dot_tn(gy[:, tile_rows], c[...]).astype(bf)
        return carry

    lax.fori_loop(0, model // CHUNK, weight_grads_a, 0)
    scatter.start(1)
    last = []
    for part in range(half // CHUNK):
        there = pl.ds(pl.multiple_of((1 - side) * half + part * CHUNK, CHUNK), CHUNK)
        at = pl.ds(part * CHUNK, CHUNK)
        l_send[at, :] = dot_nt(gqkv[there, :], w1[:, : 3 * width]).astype(bf)
        last.append(remote(l_send.at[at], l_recv.at[at], l_sems.at[0, part], l_sems.at[1, part], place.across()))
        last[part].start()
        if part == 0:
            scatter.beside(1)
    scatter.total(0)

    def fold(head, carry):
        near_sums[head] = fold_near(strip[head])
        return carry

    lax.fori_loop(0, 2 * pairs, fold, 0)
    scatter.along(1)
    for part in range(half // CHUNK):
        here = pl.ds(pl.multiple_of(side * half + part * CHUNK, CHUNK), CHUNK)
        at = pl.ds(part * CHUNK, CHUNK)
        own = dot_nt(gqkv[here, :], w1[:, : 3 * width])
        last[part].wait_recv()
        grad = own + l_recv[at, :].astype(f32)
        pulled, gain = norm_back(x_own[at, :].astype(f32), gains[0:1, :], grad)
        gain_sums[0:1, :] += gain
        grad_out[at, :] = state_grad[here, :] + pulled
    scatter.total(1)
    scatter.finish(0)
    scatter.finish(1)
    scatter.close()
    for i in range(steps):
        swap(0, i).wait_send()
    for copy in last:
        copy.wait_send()


def enc_backward(wide, x_own, cot_own, cot_other, gains, memory_part, saved):
    half, model = x_own.shape
    rows = 2 * half
    w1, n0, qkv, c, inv, e_all, e1, n1, slope, active, ef = saved
    width, ffn = c.shape[1], active.shape[1]
    pairs = width // PAIR
    steps = rows // CHUNK
    bf, f32 = jnp.bfloat16, jnp.float32
    shape = jax.ShapeDtypeStruct
    dma = pltpu.SemaphoreType.DMA
    return pl.pallas_call(
        functools.partial(enc_backward_kernel, wide),
        in_specs=[vmem_spec(), any_spec(), any_spec(), vmem_spec()] + [any_spec()] * 12,
        out_shape=[
            shape((half, model), f32),
            shape((model // wide, 4 * width + 2 * ffn), bf),
            shape((8, model), f32),
            shape((2 * pairs, 8, 2 * NEAR), f32),
            shape((2, 2 * pairs, 8, 128), f32),
        ],
        out_specs=[vmem_spec()] * 5,
        scratch_shapes=[
            pltpu.VMEM(w1.shape, bf),
            pltpu.VMEM(n0.shape, bf),
            pltpu.VMEM(qkv.shape, bf),
            pltpu.VMEM(c.shape, bf),
            pltpu.VMEM(inv.shape, f32),
            pltpu.VMEM(n1.shape, bf),
            pltpu.VMEM(active.shape, bf),
            pltpu.VMEM((rows, model), bf),
            pltpu.VMEM((2, 2, CHUNK, rows), bf),
            pltpu.VMEM((2, CHUNK, model), f32),
            pltpu.VMEM((2, CHUNK, ffn), bf),
            pltpu.VMEM((2, CHUNK, model), bf),
            pltpu.VMEM((rows, model), bf),
            pltpu.VMEM((rows, model), bf),
            pltpu.VMEM((rows, model), bf),
            pltpu.VMEM((rows, model), f32),
            pltpu.VMEM((rows, model), bf),
            pltpu.VMEM((rows, ffn), bf),
            pltpu.VMEM((rows, 3 * width), bf),
            pltpu.VMEM((rows, width), f32),
            pltpu.VMEM((rows, width), f32),
            pltpu.VMEM((2 * pairs, CHUNK, NEAR), f32),
        ]
        + scatter_buffers(wide, model, 2 * ffn)
        + scatter_buffers(wide, model, 4 * width)[1:]
        + [
            dma((2, scatter_slots(wide))),
            dma((2, scatter_slots(wide))),
            dma((2, steps)),
            dma((2, steps)),
            dma((2, half // CHUNK)),
            dma((2,)),
            dma((3, 2)),
            dma((9,)),
        ],
        compiler_params=pltpu.CompilerParams(
            collective_id=1, has_side_effects=True, vmem_limit_bytes=VMEM_BYTES
        ),
        cost_estimate=pl.CostEstimate(flops=2 * 10**10, bytes_accessed=6 * 10**7, transcendentals=0),
    )(x_own, cot_own, cot_other, gains, memory_part, w1, n0, qkv, c, inv, e_all, e1, n1, slope, active, ef)


def scatter_kernel(wide, widths, grad_in, tile, grad, *refs):
    place = Place(wide)
    place.greet()
    load = pltpu.make_async_copy(grad_in, grad, refs[-1].at[0])
    load.start()
    groups = []
    first = 0
    for index, width in enumerate(widths):
        core, beside, along = refs[3 * index : 3 * index + 3]
        groups.append(dict(grad=grad, first=first, width=width, out=first, core=core, beside=beside, along=along))
        first += width
    scatter = Scatter(place, tile.shape[0], groups, tile, refs[-3], refs[-2])
    load.wait()
    count = len(widths)
    for group in range(count):
        scatter.start(group)
    for stage in (scatter.beside, scatter.along, scatter.total, scatter.finish):
        for group in range(count):
            stage(group)
    scatter.close()


def scatter_grads(wide, grad, widths):
    model, total = grad.shape
    buffers = []
    for width in widths:
        buffers += scatter_buffers(wide, model, width)
    dma = pltpu.SemaphoreType.DMA
    return pl.pallas_call(
        functools.partial(scatter_kernel, wide, widths),
        in_specs=[any_spec()],
        out_shape=jax.ShapeDtypeStruct((model // wide, total), jnp.bfloat16),
        out_specs=vmem_spec(),
        scratch_shapes=[pltpu.VMEM((model, total), jnp.bfloat16)]
        + buffers
        + [dma((len(widths), scatter_slots(wide))), dma((len(widths), scatter_slots(wide))), dma((1,))],
        compiler_params=pltpu.CompilerParams(
            collective_id=2, has_side_effects=True, vmem_limit_bytes=VMEM_BYTES
        ),
    )(grad)


def pack_shards(attn_query, attn_kv, attn_out, ffn_up, ffn_down):
    def attention(layer):
        return [attn_query[layer], attn_kv[layer, 0], attn_kv[layer, 1], attn_out[layer].T]

    def feed(layer):
        return [ffn_up[layer], ffn_down[layer].T]

    return jnp.concatenate(attention(0) + feed(0) + attention(1) + attention(2) + feed(1), axis=1)


def ffn_back(grad_rows, normed_rows, slope, active, weight_up, weight_down):
    grad_active = dot_nn(grad_rows, weight_down)
    grad_down = dot_tn(active, grad_rows)
    grad_hidden = (slope.astype(jnp.float32) * grad_active).astype(jnp.bfloat16)
    return dot_nt(grad_hidden, weight_up), dot_tn(normed_rows, grad_hidden), grad_down


def on_device(
    wide,
    enc_input,
    dec_input,
    enc_lengths,
    dec_lengths,
    attn_query,
    attn_kv,
    attn_out,
    ffn_up,
    ffn_down,
    gains,
    rel_bias,
    enc_cotangent,
    dec_cotangent,
):
    gain_rows = gains.astype(jnp.float32)
    heads_local = rel_bias.shape[2]
    enc_segments = segment_ids(enc_lengths[0], ENC)
    dec_segments = segment_ids(dec_lengths[0], DEC)

    side = lax.axis_index("narrow")
    swap = [(0, 1), (1, 0)]

    def spread_rows(values):
        own = values.astype(jnp.bfloat16)
        other = lax.ppermute(own, "narrow", swap)
        return jnp.where(side == 0, jnp.concatenate([own, other]), jnp.concatenate([other, own]))

    def collect_rows(parts):
        half = parts.shape[0] // 2
        parts = parts.astype(jnp.bfloat16)
        other = lax.ppermute(lax.dynamic_slice_in_dim(parts, (1 - side) * half, half), "narrow", swap)
        own = lax.dynamic_slice_in_dim(parts, side * half, half)
        return own.astype(jnp.float32) + other.astype(jnp.float32)

    def attention_layer(normed_query, normed_keys, layer, base, query_segments, key_segments, causal):
        query = jnp.dot(normed_query, weights_q[layer], preferred_element_type=jnp.float32).astype(jnp.bfloat16)
        keys = jnp.dot(normed_keys, weights_k[layer], preferred_element_type=jnp.float32).astype(jnp.bfloat16)
        values = jnp.dot(normed_keys, weights_v[layer], preferred_element_type=jnp.float32).astype(jnp.bfloat16)
        saved = attend_forward(query, keys, values, base, query_segments, key_segments, causal)
        parts = dot_nt(saved[1], weights_o[layer])
        return ((query, keys, values, saved), collect_rows(parts))

    cot_other = lax.ppermute(enc_cotangent, "narrow", swap)
    pack = pack_shards(attn_query, attn_kv, attn_out, ffn_up, ffn_down)
    w1, w2, rows_a, qkv_a, context_a, inverse_a, e_a, e1_full, rows_b, slope_b, active_b, ef_full, memory = enc_forward(
        wide, enc_input, pack, gain_rows, base_rows(rel_bias[0], ENC, True), enc_segments
    )
    width = DK * heads_local
    ffn = ffn_up.shape[2]
    layer_columns = [w1[:, : 4 * width], w2[:, : 4 * width], w2[:, 4 * width : 8 * width]]
    weights_q = [columns[:, :width] for columns in layer_columns]
    weights_k = [columns[:, width : 2 * width] for columns in layer_columns]
    weights_v = [columns[:, 2 * width : 3 * width] for columns in layer_columns]
    weights_o = [columns[:, 3 * width :] for columns in layer_columns]
    up = [w1[:, 4 * width : 4 * width + ffn], w2[:, 8 * width : 8 * width + ffn]]
    down = [w1[:, 4 * width + ffn :], w2[:, 8 * width + ffn :]]
    half = enc_input.shape[0]

    def own_rows(full):
        return lax.dynamic_slice_in_dim(full, side * half, half)

    enc_output = own_rows(ef_full).astype(jnp.bfloat16)
    dec_start = dec_input.astype(jnp.float32)
    rows_c = spread_rows(rms_norm(dec_start, gain_rows[2]))
    kept_c, branch = attention_layer(
        rows_c, rows_c, 1, base_rows(rel_bias[1], DEC, False), dec_segments, dec_segments, True
    )
    dec_one = dec_start + branch
    rows_d = spread_rows(rms_norm(dec_one, gain_rows[3]))
    kept_d, branch = attention_layer(
        rows_d, memory, 2, None, dec_segments, enc_segments, False
    )
    dec_two = dec_one + branch
    rows_e = spread_rows(rms_norm(dec_two, gain_rows[4]))
    active_e, slope_e = gelu_pair(dot_nn(rows_e, up[1]))
    active_e = active_e.astype(jnp.bfloat16)
    dec_final = dec_two + collect_rows(
        dot_nt(active_e, down[1])
    )
    def attention_back(grad_state, kept, normed_query, normed_keys, layer, span, two_sided):
        grad_rows = spread_rows(grad_state)
        query, keys, values, saved = kept
        grad_context = dot_nn(grad_rows, weights_o[layer]).astype(jnp.bfloat16)
        grad_out = dot_tn(saved[1], grad_rows)
        result = attend_backward(query, keys, values, saved, grad_context, span > 0)
        grad_q, grad_k, grad_v = result[:3]
        sums = [
            dot_tn(normed_query, grad_q),
            dot_tn(normed_keys, grad_k),
            dot_tn(normed_keys, grad_v),
            grad_out,
            table_grad(result[3], span, two_sided) if span else None,
        ]
        query_part = dot_nt(grad_q, weights_q[layer])
        key_part = dot_nt(grad_k, weights_k[layer]) + dot_nt(grad_v, weights_v[layer])
        return (query_part, key_part, sums)

    grad_dec = dec_cotangent.astype(jnp.float32)
    grad_normed, up_e, down_e = ffn_back(
        spread_rows(grad_dec), rows_e, slope_e, active_e, up[1], down[1]
    )
    grad_back, gain_e = norm_backward(dec_two, gain_rows[4], collect_rows(grad_normed))
    grad_dec = grad_dec + grad_back
    query_part, memory_part, sums_d = attention_back(
        grad_dec, kept_d, rows_d, memory, 2, 0, False
    )
    grad_normed = collect_rows(query_part)
    grad_back, gain_d = norm_backward(dec_one, gain_rows[3], grad_normed)
    grad_dec = grad_dec + grad_back
    query_part, key_part, sums_c = attention_back(
        grad_dec, kept_c, rows_c, rows_c, 1, DEC, False
    )
    grad_back, gain_c = norm_backward(dec_start, gain_rows[2], collect_rows(query_part + key_part))
    grad_dec = grad_dec + grad_back
    grad_dec_query = jnp.concatenate([sums_c[0], sums_c[1], sums_c[2], sums_c[3].T, sums_d[0], sums_d[1], sums_d[2], sums_d[3].T, up_e, down_e.T], axis=1)
    grad_enc, tile_one, gain_sums, near_sums, far_sums = enc_backward(
        wide,
        enc_input,
        enc_cotangent,
        cot_other,
        gain_rows,
        memory_part.astype(jnp.bfloat16),
        (w1, rows_a, qkv_a, context_a, inverse_a, e_a, e1_full, rows_b, slope_b, active_b, ef_full),
    )
    tile_two = scatter_grads(wide, grad_dec_query.astype(jnp.bfloat16), (2 * ffn, 4 * width, 4 * width))
    tile_one, tile_two = tile_one.astype(jnp.float32), tile_two.astype(jnp.float32)
    at_a, at_c, at_d = tile_one[:, : 4 * width], tile_two[:, : 4 * width], tile_two[:, 4 * width : 8 * width]
    layers = (at_a, at_c, at_d)
    feeds = (tile_one[:, 4 * width :], tile_two[:, 8 * width :])
    grad_query = jnp.stack([layer[:, :width] for layer in layers])
    grad_kv = jnp.stack(
        [jnp.stack([layer[:, width : 2 * width], layer[:, 2 * width : 3 * width]]) for layer in layers]
    )
    grad_out = jnp.stack([layer[:, 3 * width :].T for layer in layers])
    grad_up = jnp.stack([feed[:, :ffn] for feed in feeds])
    grad_down = jnp.stack([feed[:, ffn:].T for feed in feeds])
    gain_grads = gain_sums[:6] + jnp.stack(
        [jnp.zeros_like(gain_c), jnp.zeros_like(gain_c), gain_c, gain_d, gain_e, jnp.zeros_like(gain_c)]
    )
    column = side * heads_local
    bias_local = jnp.stack([near_table_grad(near_sums, far_sums), sums_c[4]])
    bias_full = lax.dynamic_update_slice(jnp.zeros((2, NB, H), jnp.float32), bias_local, (0, 0, column))
    gain_total, bias_total = lax.psum((gain_grads, bias_full), ("dp", "wide", "narrow"))
    bias_grad = lax.dynamic_slice(bias_total, (0, 0, column), (2, NB, heads_local))
    return (
        enc_output,
        dec_final.astype(jnp.bfloat16),
        grad_enc,
        grad_dec,
        grad_query,
        grad_kv,
        grad_out,
        grad_up,
        grad_down,
        gain_total,
        bias_grad,
    )


def on_device_general(
    enc_input,
    dec_input,
    enc_lengths,
    dec_lengths,
    attn_query,
    attn_kv,
    attn_out,
    ffn_up,
    ffn_down,
    gains,
    rel_bias,
    enc_cotangent,
    dec_cotangent,
):
    weights = (
        lax.all_gather(attn_query, "wide", axis=1, tiled=True),
        lax.all_gather(attn_kv, "wide", axis=2, tiled=True),
        lax.all_gather(attn_out, "wide", axis=2, tiled=True),
        lax.all_gather(ffn_up, "wide", axis=1, tiled=True),
        lax.all_gather(ffn_down, "wide", axis=2, tiled=True),
    )
    gain_rows = gains.astype(jnp.float32)
    heads_local = rel_bias.shape[2]
    enc_segments = segment_ids(enc_lengths[0], ENC)
    dec_segments = segment_ids(dec_lengths[0], DEC)

    side = lax.axis_index("narrow")
    swap = [(0, 1), (1, 0)]

    def spread_rows(values):
        own = values.astype(jnp.bfloat16)
        other = lax.ppermute(own, "narrow", swap)
        return jnp.where(side == 0, jnp.concatenate([own, other]), jnp.concatenate([other, own]))

    def collect_rows(parts):
        half = parts.shape[0] // 2
        parts = parts.astype(jnp.bfloat16)
        other = lax.ppermute(lax.dynamic_slice_in_dim(parts, (1 - side) * half, half), "narrow", swap)
        own = lax.dynamic_slice_in_dim(parts, side * half, half)
        return own.astype(jnp.float32) + other.astype(jnp.float32)

    def attention_layer(normed_query, normed_keys, layer, base, query_segments, key_segments, causal):
        query = jnp.dot(normed_query, weights[0][layer], preferred_element_type=jnp.float32).astype(jnp.bfloat16)
        keys = jnp.dot(normed_keys, weights[1][layer, 0], preferred_element_type=jnp.float32).astype(jnp.bfloat16)
        values = jnp.dot(normed_keys, weights[1][layer, 1], preferred_element_type=jnp.float32).astype(jnp.bfloat16)
        saved = attend_forward(query, keys, values, base, query_segments, key_segments, causal)
        parts = jnp.dot(saved[1], weights[2][layer], preferred_element_type=jnp.float32)
        return ((query, keys, values, saved), collect_rows(parts))

    enc_start = enc_input.astype(jnp.float32)
    rows_a = spread_rows(rms_norm(enc_start, gain_rows[0]))
    kept_a, branch = attention_layer(
        rows_a, rows_a, 0, base_rows(rel_bias[0], ENC, True), enc_segments, enc_segments, False
    )
    enc_mid = enc_start + branch
    rows_b = spread_rows(rms_norm(enc_mid, gain_rows[1]))
    hidden_b = jnp.dot(rows_b, weights[3][0], preferred_element_type=jnp.float32)
    active_b = gelu_tanh(hidden_b).astype(jnp.bfloat16)
    enc_final = enc_mid + collect_rows(
        jnp.dot(active_b, weights[4][0], preferred_element_type=jnp.float32)
    )
    memory = spread_rows(rms_norm(enc_final, gain_rows[5]))
    dec_start = dec_input.astype(jnp.float32)
    rows_c = spread_rows(rms_norm(dec_start, gain_rows[2]))
    kept_c, branch = attention_layer(
        rows_c, rows_c, 1, base_rows(rel_bias[1], DEC, False), dec_segments, dec_segments, True
    )
    dec_one = dec_start + branch
    rows_d = spread_rows(rms_norm(dec_one, gain_rows[3]))
    kept_d, branch = attention_layer(
        rows_d, memory, 2, None, dec_segments, enc_segments, False
    )
    dec_two = dec_one + branch
    rows_e = spread_rows(rms_norm(dec_two, gain_rows[4]))
    hidden_e = jnp.dot(rows_e, weights[3][1], preferred_element_type=jnp.float32)
    active_e = gelu_tanh(hidden_e).astype(jnp.bfloat16)
    dec_final = dec_two + collect_rows(
        jnp.dot(active_e, weights[4][1], preferred_element_type=jnp.float32)
    )
    def attention_back(grad_state, kept, normed_query, normed_keys, layer, span, two_sided):
        grad_rows = spread_rows(grad_state)
        query, keys, values, saved = kept
        grad_context = dot_nt(grad_rows, weights[2][layer]).astype(jnp.bfloat16)
        grad_out = dot_tn(saved[1], grad_rows)
        result = attend_backward(query, keys, values, saved, grad_context, span > 0)
        grad_q, grad_k, grad_v = result[:3]
        sums = [
            dot_tn(normed_query, grad_q),
            dot_tn(normed_keys, grad_k),
            dot_tn(normed_keys, grad_v),
            grad_out,
            table_grad(result[3], span, two_sided) if span else None,
        ]
        query_part = dot_nt(grad_q, weights[0][layer])
        key_part = dot_nt(grad_k, weights[1][layer, 0]) + dot_nt(grad_v, weights[1][layer, 1])
        return (query_part, key_part, sums)

    grad_dec = dec_cotangent.astype(jnp.float32)
    grad_normed, up_e, down_e = ffn_backward(
        spread_rows(grad_dec), rows_e, hidden_e, active_e, weights[3][1], weights[4][1]
    )
    grad_back, gain_e = norm_backward(dec_two, gain_rows[4], collect_rows(grad_normed))
    grad_dec = grad_dec + grad_back
    query_part, memory_part, sums_d = attention_back(
        grad_dec, kept_d, rows_d, memory, 2, 0, False
    )
    grad_normed, grad_memory = collect_rows(query_part), collect_rows(memory_part)
    grad_back, gain_d = norm_backward(dec_one, gain_rows[3], grad_normed)
    grad_dec = grad_dec + grad_back
    query_part, key_part, sums_c = attention_back(
        grad_dec, kept_c, rows_c, rows_c, 1, DEC, False
    )
    grad_back, gain_c = norm_backward(dec_start, gain_rows[2], collect_rows(query_part + key_part))
    grad_dec = grad_dec + grad_back
    grad_enc = enc_cotangent.astype(jnp.float32)
    grad_back, gain_m = norm_backward(enc_final, gain_rows[5], grad_memory)
    grad_enc = grad_enc + grad_back
    grad_normed, up_b, down_b = ffn_backward(
        spread_rows(grad_enc), rows_b, hidden_b, active_b, weights[3][0], weights[4][0]
    )
    grad_back, gain_b = norm_backward(enc_mid, gain_rows[1], collect_rows(grad_normed))
    grad_enc = grad_enc + grad_back
    query_part, key_part, sums_a = attention_back(
        grad_enc, kept_a, rows_a, rows_a, 0, ENC, True
    )
    grad_back, gain_a = norm_backward(enc_start, gain_rows[0], collect_rows(query_part + key_part))
    grad_enc = grad_enc + grad_back
    grad_query = jnp.stack([sums_a[0], sums_c[0], sums_d[0]])
    grad_kv = jnp.stack(
        [
            jnp.stack([sums_a[1], sums_a[2]]),
            jnp.stack([sums_c[1], sums_c[2]]),
            jnp.stack([sums_d[1], sums_d[2]]),
        ]
    )
    grad_out = jnp.stack([sums_a[3], sums_c[3], sums_d[3]])
    grad_up = jnp.stack([up_b, up_e])
    grad_down = jnp.stack([down_b, down_e])
    tiles = (
        lax.psum_scatter(
            grad_query.astype(jnp.bfloat16), "wide", scatter_dimension=1, tiled=True
        ).astype(jnp.float32),
        lax.psum_scatter(
            grad_kv.astype(jnp.bfloat16), "wide", scatter_dimension=2, tiled=True
        ).astype(jnp.float32),
        lax.psum_scatter(
            grad_out.astype(jnp.bfloat16), "wide", scatter_dimension=2, tiled=True
        ).astype(jnp.float32),
        lax.psum_scatter(
            grad_up.astype(jnp.bfloat16), "wide", scatter_dimension=1, tiled=True
        ).astype(jnp.float32),
        lax.psum_scatter(
            grad_down.astype(jnp.bfloat16), "wide", scatter_dimension=2, tiled=True
        ).astype(jnp.float32),
    )
    tiles = (
        lax.psum(tiles[0].astype(jnp.bfloat16), "dp").astype(jnp.float32),
        lax.psum(tiles[1].astype(jnp.bfloat16), "dp").astype(jnp.float32),
        lax.psum(tiles[2].astype(jnp.bfloat16), "dp").astype(jnp.float32),
        lax.psum(tiles[3].astype(jnp.bfloat16), "dp").astype(jnp.float32),
        lax.psum(tiles[4].astype(jnp.bfloat16), "dp").astype(jnp.float32),
    )
    gain_grads = jnp.stack([gain_a, gain_b, gain_c, gain_d, gain_e, gain_m])
    column = lax.axis_index("narrow") * heads_local
    bias_local = jnp.stack([sums_a[4], sums_c[4]])
    bias_full = lax.dynamic_update_slice(
        jnp.zeros((2, NB, H), jnp.float32), bias_local, (0, 0, column)
    )
    gain_total, bias_total = lax.psum((gain_grads, bias_full), ("dp", "wide", "narrow"))
    bias_grad = lax.dynamic_slice(bias_total, (0, 0, column), (2, NB, heads_local))
    return (
        enc_final.astype(jnp.bfloat16),
        dec_final.astype(jnp.bfloat16),
        grad_enc,
        grad_dec,
        tiles[0],
        tiles[1],
        tiles[2],
        tiles[3],
        tiles[4],
        gain_total,
        bias_grad,
    )


def solution(mesh):
    wide = mesh.shape["wide"]

    def body(*args):
        if args[4].shape[1] % 16 or wide % 2:
            return on_device_general(*args)
        return on_device(wide, *args)

    return jax.shard_map(
        body,
        mesh=mesh,
        in_specs=(
            P(("dp", "wide", "narrow"), None),
            P(("dp", "wide", "narrow"), None),
            P(("dp", "wide"), None),
            P(("dp", "wide"), None),
            P(None, "wide", "narrow"),
            P(None, None, "wide", "narrow"),
            P(None, "narrow", "wide"),
            P(None, "wide", "narrow"),
            P(None, "narrow", "wide"),
            P(),
            P(None, None, "narrow"),
            P(("dp", "wide", "narrow"), None),
            P(("dp", "wide", "narrow"), None),
        ),
        out_specs=(
            P(("dp", "wide", "narrow"), None),
            P(("dp", "wide", "narrow"), None),
            P(("dp", "wide", "narrow"), None),
            P(("dp", "wide", "narrow"), None),
            P(None, "wide", "narrow"),
            P(None, None, "wide", "narrow"),
            P(None, "narrow", "wide"),
            P(None, "wide", "narrow"),
            P(None, "narrow", "wide"),
            P(),
            P(None, None, "narrow"),
        ),
        check_vma=False,
    )
```

```python
import functools
import math

import jax
import jax.numpy as jnp
from jax import lax
from jax.sharding import PartitionSpec as P
import jax.experimental.pallas as pl
import jax.experimental.pallas.tpu as pltpu

H = 12
DK = 64
NB = 32
MAXD = 128
ENC = 1024
DEC = 256


EPS = 1e-06
NEG = -1e30
HIGH = lax.Precision.HIGHEST
VMEM_BYTES = 60 * 2**20
GELU_A = math.sqrt(2.0 / math.pi)
GELU_B = 0.044715


def cutoffs(exact, buckets):
    found = []
    reach = exact
    for target in range(exact + 1, buckets):
        while (
            exact + math.floor(math.log(reach / exact) / math.log(MAXD / exact) * (buckets - exact))
            < target
        ):
            reach = reach + 1
        found.append(reach)
    return found


def bucket_index(relative, two_sided):
    if two_sided:
        width = NB // 2
        offset = jnp.where(relative > 0, width, 0)
        distance = jnp.abs(relative)
    else:
        width = NB
        offset = jnp.zeros_like(relative)
        distance = jnp.maximum(-relative, 0)
    exact = width // 2
    beyond = exact + sum(((distance >= limit).astype(jnp.int32) for limit in cutoffs(exact, width)))
    return offset + jnp.where(distance < exact, distance, beyond)


def segment_ids(lengths, count):
    bounds = jnp.cumsum(lengths)
    places = jnp.arange(count, dtype=jnp.int32)
    return jnp.sum((places[:, None] >= bounds[None, :]).astype(jnp.int32), axis=1)


def rms_norm(values, gain):
    return values * lax.rsqrt(jnp.mean(values * values, axis=-1, keepdims=True) + EPS) * gain


def gelu_tanh(values):
    return jax.nn.gelu(values, approximate=True)


PAIR = 128


def offset_buckets(span, two_sided):
    places = jnp.arange(2 * span, dtype=jnp.int32)[None, :]
    relative = lax.rem(places - jnp.arange(8, dtype=jnp.int32)[:, None] + 2 * span, 2 * span) - span
    buckets = bucket_index(relative.reshape(-1), two_sided)
    return (buckets[None, :] == jnp.arange(NB, dtype=jnp.int32)[:, None]).astype(jnp.bfloat16)


def base_rows(table, span, two_sided):
    heads = table.shape[1]
    rows = lax.dot_general(
        table, offset_buckets(span, two_sided), (((0,), (0,)), ((), ())), preferred_element_type=jnp.float32
    )
    return rows.reshape(heads // 2, 2, 8, 2 * span)


def table_grad(offset_sums, span, two_sided):
    heads = 2 * offset_sums.shape[0]
    return lax.dot_general(
        offset_buckets(span, two_sided).astype(jnp.float32),
        offset_sums.reshape(heads, 16 * span),
        (((1,), (1,)), ((), ())),
        precision=HIGH,
        preferred_element_type=jnp.float32,
    )


def dot_nt(a, b):
    return lax.dot_general(a, b, (((1,), (1,)), ((), ())), preferred_element_type=jnp.float32)


def dot_tn(a, b):
    return lax.dot_general(a, b, (((0,), (0,)), ((), ())), preferred_element_type=jnp.float32)


def dot_nn(a, b):
    return lax.dot_general(a, b, (((1,), (0,)), ((), ())), preferred_element_type=jnp.float32)


def split_heads(block):
    lane = lax.broadcasted_iota(jnp.int32, block.shape, 1)
    zero = jnp.zeros_like(block)
    return jnp.where(lane < DK, block, zero), jnp.where(lane < DK, zero, block)


def attend_kernel(block, keys_count, causal, biased, *refs):
    if biased:
        qseg, kseg, base, q_ref, k_ref, v_ref, e_ref, c_ref, inv_ref, strip = refs
    else:
        qseg, kseg, q_ref, k_ref, v_ref, e_ref, c_ref, inv_ref = refs
    i = pl.program_id(1)
    if biased:
        wide = 2 * keys_count

        @pl.when(i == 0)
        def _():
            for head in range(2):
                rows = base[0, head]
                for a in range(block // 8):
                    strip[head, 8 * a : 8 * a + 8, :] = pltpu.roll(rows, (8 * a + wide - block) % wide, 1)

    allowed = qseg[...] == kseg[...]
    if causal:
        rows = lax.broadcasted_iota(jnp.int32, (block, keys_count), 0) + i * block
        allowed = allowed & (lax.broadcasted_iota(jnp.int32, (block, keys_count), 1) <= rows)
    q_heads = split_heads(q_ref[...])
    v_heads = split_heads(v_ref[...])
    inverses = []
    context = None
    for head in range(2):
        scores = dot_nt(q_heads[head], k_ref[...])
        if biased:
            start = pl.multiple_of((keys_count // block - 1 - i) * block, block)
            scores = scores + strip[head, :, pl.ds(start, keys_count)]
        scores = jnp.where(allowed, scores, NEG)
        highest = jnp.max(scores, axis=1, keepdims=True)
        weights = jnp.exp(scores - highest)
        inverses.append(1.0 / jnp.sum(weights, axis=1, keepdims=True))
        weights = weights.astype(jnp.bfloat16)
        e_ref[head] = weights
        part = dot_nn(weights, v_heads[head])
        context = part if context is None else context + part
    lane = lax.broadcasted_iota(jnp.int32, (block, PAIR), 1)
    inverse = jnp.where(lane < DK, inverses[0], inverses[1])
    inv_ref[...] = inverse
    c_ref[...] = (context * inverse).astype(jnp.bfloat16)


def attend_back_kernel(block, keys_count, steps, biased, *refs):
    if biased:
        q_ref, k_ref, v_ref, e_ref, c_ref, inv_ref, gc_ref, gq_ref, gk_ref, gv_ref, off_ref, gk_sum, gv_sum, strip = refs
    else:
        q_ref, k_ref, v_ref, e_ref, c_ref, inv_ref, gc_ref, gq_ref, gk_ref, gv_ref, gk_sum, gv_sum = refs
    i = pl.program_id(1)

    @pl.when(i == 0)
    def _():
        gk_sum[...] = jnp.zeros_like(gk_sum)
        gv_sum[...] = jnp.zeros_like(gv_sum)
        if biased:
            strip[...] = jnp.zeros_like(strip)

    scaled = (gc_ref[...].astype(jnp.float32) * inv_ref[...]).astype(jnp.bfloat16)
    product = scaled.astype(jnp.float32) * c_ref[...].astype(jnp.float32)
    lane = lax.broadcasted_iota(jnp.int32, (block, PAIR), 1)
    inner = (
        jnp.sum(jnp.where(lane < DK, product, 0.0), axis=1, keepdims=True),
        jnp.sum(jnp.where(lane < DK, 0.0, product), axis=1, keepdims=True),
    )
    g_heads = split_heads(scaled)
    q_heads = split_heads(q_ref[...])
    k_heads = split_heads(k_ref[...])
    gq = None
    for head in range(2):
        weights = e_ref[head]
        grad = dot_nt(g_heads[head], v_ref[...])
        grad = weights.astype(jnp.float32) * (grad - inner[head])
        if biased:
            start = pl.multiple_of((keys_count // block - 1 - i) * block, block)
            strip[head, :, pl.ds(start, keys_count)] += grad
        grad = grad.astype(jnp.bfloat16)
        part = dot_nn(grad, k_heads[head])
        gq = part if gq is None else gq + part
        gk_sum[...] += dot_tn(grad, q_heads[head])
        gv_sum[...] += dot_tn(weights, g_heads[head])
    gq_ref[...] = gq.astype(jnp.bfloat16)

    @pl.when(i == steps - 1)
    def _():
        gk_ref[...] = gk_sum[...].astype(jnp.bfloat16)
        gv_ref[...] = gv_sum[...].astype(jnp.bfloat16)
        if biased:
            wide = 2 * keys_count
            for head in range(2):
                total = jnp.zeros((8, wide), jnp.float32)
                for a in range(block // 8):
                    total = total + pltpu.roll(strip[head, 8 * a : 8 * a + 8, :], (block - 8 * a) % wide, 1)
                off_ref[0, head] = total


def attend_forward(query, keys, values, base, query_segments, key_segments, causal):
    count, cols = query.shape[0], keys.shape[0]
    pairs = query.shape[1] // PAIR
    block = min(256, count)
    steps = count // block
    row_spec = pl.BlockSpec((block, PAIR), lambda h, i: (i, h))
    key_spec = pl.BlockSpec((cols, PAIR), lambda h, i: (0, h))
    in_specs = [
        pl.BlockSpec((block, 1), lambda h, i: (i, 0)),
        pl.BlockSpec((1, cols), lambda h, i: (0, 0)),
    ]
    args = [query_segments[:, None], key_segments[None, :]]
    scratch = []
    if base is not None:
        in_specs.append(pl.BlockSpec((1, 2, 8, 2 * cols), lambda h, i: (h, 0, 0, 0)))
        args.append(base)
        scratch.append(pltpu.VMEM((2, block, 2 * cols), jnp.float32))
    return pl.pallas_call(
        functools.partial(attend_kernel, block, cols, causal, base is not None),
        grid=(pairs, steps),
        in_specs=in_specs + [row_spec, key_spec, key_spec],
        out_specs=[
            pl.BlockSpec((2, block, cols), lambda h, i: (h, i, 0)),
            row_spec,
            row_spec,
        ],
        out_shape=[
            jax.ShapeDtypeStruct((2 * pairs, count, cols), jnp.bfloat16),
            jax.ShapeDtypeStruct((count, pairs * PAIR), jnp.bfloat16),
            jax.ShapeDtypeStruct((count, pairs * PAIR), jnp.float32),
        ],
        scratch_shapes=scratch,
        compiler_params=pltpu.CompilerParams(vmem_limit_bytes=VMEM_BYTES),
        cost_estimate=pl.CostEstimate(
            flops=4 * count * cols * PAIR * 2 * pairs, bytes_accessed=2 * pairs * count * cols * 2, transcendentals=0
        ),
    )(*args, query, keys, values)


def attend_backward(query, keys, values, saved, grad_context, biased):
    weights, context, inverse = saved
    count, cols = query.shape[0], keys.shape[0]
    pairs = query.shape[1] // PAIR
    block = min(256, count)
    steps = count // block
    row_spec = pl.BlockSpec((block, PAIR), lambda h, i: (i, h))
    key_spec = pl.BlockSpec((cols, PAIR), lambda h, i: (0, h))
    out_specs = [row_spec, key_spec, key_spec]
    out_shape = [
        jax.ShapeDtypeStruct((count, pairs * PAIR), jnp.bfloat16),
        jax.ShapeDtypeStruct((cols, pairs * PAIR), jnp.bfloat16),
        jax.ShapeDtypeStruct((cols, pairs * PAIR), jnp.bfloat16),
    ]
    scratch = [pltpu.VMEM((cols, PAIR), jnp.float32), pltpu.VMEM((cols, PAIR), jnp.float32)]
    if biased:
        out_specs.append(pl.BlockSpec((1, 2, 8, 2 * cols), lambda h, i: (h, 0, 0, 0)))
        out_shape.append(jax.ShapeDtypeStruct((pairs, 2, 8, 2 * cols), jnp.float32))
        scratch.append(pltpu.VMEM((2, block, 2 * cols), jnp.float32))
    return pl.pallas_call(
        functools.partial(attend_back_kernel, block, cols, steps, biased),
        grid=(pairs, steps),
        in_specs=[
            row_spec,
            key_spec,
            key_spec,
            pl.BlockSpec((2, block, cols), lambda h, i: (h, i, 0)),
            row_spec,
            row_spec,
            row_spec,
        ],
        out_specs=out_specs,
        out_shape=out_shape,
        scratch_shapes=scratch,
        compiler_params=pltpu.CompilerParams(vmem_limit_bytes=VMEM_BYTES),
        cost_estimate=pl.CostEstimate(
            flops=8 * count * cols * PAIR * 2 * pairs, bytes_accessed=2 * pairs * count * cols * 2, transcendentals=0
        ),
    )(query, keys, values, weights, context, inverse, grad_context)


MESH_IDS = pl.DeviceIdType.MESH
CHUNK = 256
ATT = 4 * 384


def any_spec():
    return pl.BlockSpec(memory_space=pl.ANY)


def vmem_spec():
    return pl.BlockSpec(memory_space=pltpu.VMEM)


def normed(values, gain):
    return values * lax.rsqrt(jnp.mean(values * values, axis=1, keepdims=True) + EPS) * gain


def gelu_pair(values):
    square = values * values
    inner = jnp.tanh(GELU_A * values * (1.0 + GELU_B * square))
    half = 0.5 * (1.0 + inner)
    slope = half + 0.5 * values * (1.0 - inner * inner) * (GELU_A * (1.0 + 3.0 * GELU_B * square))
    return values * half, slope


class Place:
    def __init__(self, wide):
        self.core = lax.axis_index("dp")
        self.wide = lax.axis_index("wide")
        self.side = lax.axis_index("narrow")
        self.count = wide
        self.fars = wide // 2
        self.far = self.wide // 2
        self.near = self.wide % 2

    def sibling(self):
        return (1 - self.core, self.wide, self.side)

    def across(self):
        return (self.core, self.wide, 1 - self.side)

    def beside(self):
        return (self.core, 2 * self.far + 1 - self.near, self.side)

    def along(self, step):
        return (self.core, 2 * lax.rem(self.far + step, self.fars) + self.near, self.side)

    def index_from(self, step):
        return 2 * lax.rem(self.far - step + self.fars, self.fars) + self.near

    def index_beside(self, step):
        return 2 * lax.rem(self.far - step + self.fars, self.fars) + 1 - self.near

    def greet(self):
        partners = [self.sibling(), self.across(), self.beside()]
        partners += [self.along(step) for step in range(1, self.fars)]
        barrier = pltpu.get_barrier_semaphore()
        for partner in partners:
            pl.semaphore_signal(barrier, inc=1, device_id=partner, device_id_type=MESH_IDS)
        pl.semaphore_wait(barrier, len(partners))


def remote(source, target, send, receive, partner):
    return pltpu.make_async_remote_copy(
        src_ref=source,
        dst_ref=target,
        send_sem=send,
        recv_sem=receive,
        device_id=partner,
        device_id_type=MESH_IDS,
    )


class Gather:
    def __init__(self, place, pack, groups, send, receive, local):
        self.place, self.pack, self.groups = place, pack, groups
        self.send, self.receive, self.local = send, receive, local
        self.rows = pack.shape[0]
        self.sent = []

    def at(self, group, index, core):
        first, width, target, offset = self.groups[group]
        half = width // 2
        start = pl.multiple_of(offset + core * half, 128)
        return target.at[pl.ds(pl.multiple_of(index * self.rows, 16), self.rows), pl.ds(start, half)]

    def own(self, group):
        first, width, target, offset = self.groups[group]
        half = width // 2
        return self.pack.at[:, pl.ds(pl.multiple_of(first + self.place.core * half, 128), half)]

    def local_copy(self, group):
        first, width, target, offset = self.groups[group]
        rows = pl.ds(pl.multiple_of(self.place.wide * self.rows, 16), self.rows)
        return pltpu.make_async_copy(
            self.pack.at[:, pl.ds(first, width)], target.at[rows, pl.ds(offset, width)], self.local.at[group]
        )

    def push(self, group, slot, source, index, partner):
        copy = remote(
            source,
            self.at(group, index, self.place.core),
            self.send.at[group, slot],
            self.receive.at[group, slot],
            partner,
        )
        copy.start()
        self.sent.append(copy)

    def await_slot(self, group, slot, index, core):
        block = self.at(group, index, core)
        remote(block, block, self.send.at[group, slot], self.receive.at[group, slot], self.place.sibling()).wait_recv()

    def start(self, group):
        place, fars = self.place, self.place.fars
        for step in range(1, fars):
            self.push(group, step - 1, self.own(group), place.wide, place.along(step))
        self.push(group, fars - 1, self.own(group), place.wide, place.beside())
        self.local_copy(group).start()

    def relay_along(self, group):
        place, fars = self.place, self.place.fars
        for step in range(1, fars):
            index = place.index_from(step)
            self.await_slot(group, step - 1, index, place.core)
            block = self.at(group, index, place.core)
            self.push(group, fars - 1 + step, block, index, place.beside())
            self.push(group, 2 * fars - 2 + step, block, index, place.sibling())

    def relay_beside(self, group):
        place, fars = self.place, self.place.fars
        for step in range(fars):
            index = place.index_beside(step)
            self.await_slot(group, fars - 1 + step, index, place.core)
            block = self.at(group, index, place.core)
            self.push(group, 3 * fars - 2 + step, block, index, place.sibling())

    def finish(self, group):
        place, fars = self.place, self.place.fars
        for step in range(1, fars):
            self.await_slot(group, 2 * fars - 2 + step, place.index_from(step), 1 - place.core)
        for step in range(fars):
            self.await_slot(group, 3 * fars - 2 + step, place.index_beside(step), 1 - place.core)
        self.local_copy(group).wait()

    def close(self):
        for copy in self.sent:
            copy.wait_send()


def gather_slots(wide):
    return 4 * (wide // 2) - 2


def softmax_pair(q_pair, k_pair, v_pair, allowed, biases, e_store):
    q_heads = split_heads(q_pair)
    v_heads = split_heads(v_pair)
    inverses = []
    context = None
    for head in range(2):
        scores = dot_nt(q_heads[head], k_pair)
        if biases is not None:
            scores = scores + biases(head)
        scores = jnp.where(allowed, scores, NEG)
        highest = jnp.max(scores, axis=1, keepdims=True)
        weights = jnp.exp(scores - highest)
        inverses.append(1.0 / jnp.sum(weights, axis=1, keepdims=True))
        weights = weights.astype(jnp.bfloat16)
        e_store(head, weights)
        part = dot_nn(weights, v_heads[head])
        context = part if context is None else context + part
    lane = lax.broadcasted_iota(jnp.int32, context.shape, 1)
    inverse = jnp.where(lane < DK, inverses[0], inverses[1])
    return inverse, (context * inverse).astype(jnp.bfloat16)


def build_strip(strip, base, pairs, block, span):
    def one(pair, carry):
        for head in range(2):
            rows = base[pair, head]
            for a in range(block // 8):
                strip[2 * pair + head, 8 * a : 8 * a + 8, :] = pltpu.roll(rows, (8 * a + 2 * span - block) % (2 * span), 1)
        return carry

    lax.fori_loop(0, pairs, one, 0)


def enc_forward_kernel(
    wide,
    x_own,
    pack,
    gains,
    base,
    qseg,
    kseg,
    w1,
    w2,
    n0,
    qkv,
    c,
    inv,
    e_all,
    e1,
    n1,
    slope_all,
    a_all,
    ef,
    mem,
    x_full,
    strip,
    e_buf,
    slope_buf,
    a_buf,
    y_send,
    y_recv,
    g_send,
    g_recv,
    g_local,
    x_sems,
    y_sems,
    z_sems,
    l_sems,
):
    place = Place(wide)
    side = place.side
    half = x_own.shape[0]
    rows = 2 * half
    steps = rows // CHUNK
    width = c.shape[1]
    ffn = a_all.shape[1]
    pairs = width // PAIR
    place.greet()
    gather = Gather(
        place,
        pack,
        [
            (0, 4 * width, w1, 0),
            (4 * width, 2 * ffn, w1, 4 * width),
            (4 * width + 2 * ffn, 8 * width, w2, 0),
            (12 * width + 2 * ffn, 2 * ffn, w2, 8 * width),
        ],
        g_send,
        g_recv,
        g_local,
    )
    mine = pl.ds(pl.multiple_of(side * half, 16), half)
    swap_x = remote(x_own, x_full.at[mine], x_sems.at[0], x_sems.at[1], place.across())
    gather.start(0)
    swap_x.start()
    keep_x = pltpu.make_async_copy(x_own, x_full.at[mine], l_sems.at[6])
    keep_x.start()
    build_strip(strip, base, pairs, CHUNK, rows)
    gather.relay_along(0)
    gather.start(1)
    keep_x.wait()
    gather.relay_beside(0)
    swap_x.wait()

    def norm_rows(i, carry):
        at = pl.ds(pl.multiple_of(i * CHUNK, CHUNK), CHUNK)
        n0[at, :] = normed(x_full[at, :].astype(jnp.float32), gains[0:1, :]).astype(jnp.bfloat16)
        return carry

    lax.fori_loop(0, steps, norm_rows, 0)
    gather.finish(0)

    def project(i, carry):
        at = pl.ds(pl.multiple_of(i * CHUNK, CHUNK), CHUNK)
        qkv[at, :] = dot_nn(n0[at, :], w1[:, : 3 * width]).astype(jnp.bfloat16)
        return carry

    lax.fori_loop(0, steps, project, 0)

    def lanes(base_lane, pair):
        return pl.ds(pl.multiple_of(base_lane + pair * PAIR, PAIR), PAIR)

    def save(i, kind):
        slot = i % 2
        at = pl.ds(i * CHUNK, CHUNK)
        if kind == 0:
            return pltpu.make_async_copy(e_buf.at[slot], e_all.at[:, at, :], l_sems.at[slot])
        if kind == 1:
            return pltpu.make_async_copy(slope_buf.at[slot], slope_all.at[at, :], l_sems.at[2 + slot])
        return pltpu.make_async_copy(a_buf.at[slot], a_all.at[at, :], l_sems.at[4 + slot])

    def swap_y(layer, i):
        at = pl.ds(i * CHUNK, CHUNK)
        sems = y_sems if layer == 0 else z_sems
        return remote(y_send.at[layer, at], y_recv.at[layer, at], sems.at[0, i], sems.at[1, i], place.across())

    def attend(i):
        at = slice(i * CHUNK, (i + 1) * CHUNK)
        slot = i % 2
        if i >= 2:
            save(i - 2, 0).wait()
        first = (steps - 1 - i) * CHUNK

        def one(pair, carry):
            allowed = qseg[at, :] == kseg[...]

            def bias(head):
                return strip[2 * pair + head, :, first : first + rows]

            def store(head, weights):
                e_buf[slot, 2 * pair + head] = weights

            inverse, context = softmax_pair(
                qkv[at, lanes(0, pair)],
                qkv[:, lanes(width, pair)],
                qkv[:, lanes(2 * width, pair)],
                allowed,
                bias,
                store,
            )
            inv[at, lanes(0, pair)] = inverse
            c[at, lanes(0, pair)] = context
            return carry

        lax.fori_loop(0, pairs, one, 0)
        save(i, 0).start()
        y_send[0, at, :] = dot_nt(c[at, :], w1[:, 3 * width : 4 * width]).astype(jnp.bfloat16)
        swap_y(0, i).start()

    def feed(i):
        at = slice(i * CHUNK, (i + 1) * CHUNK)
        slot = i % 2
        swap_y(0, i).wait_recv()
        both = y_send[0, at, :].astype(jnp.float32) + y_recv[0, at, :].astype(jnp.float32)
        middle = x_full[at, :].astype(jnp.float32) + both
        e1[at, :] = middle
        rounded = normed(middle, gains[1:2, :]).astype(jnp.bfloat16)
        n1[at, :] = rounded
        if i >= 2:
            save(i - 2, 1).wait()
            save(i - 2, 2).wait()

        def part(j, carry):
            cols = pl.ds(pl.multiple_of(4 * width + j * width, PAIR), width)
            here = pl.ds(pl.multiple_of(j * width, PAIR), width)
            active, slope = gelu_pair(dot_nn(n1[at, :], w1[:, cols]))
            a_buf[slot, :, here] = active.astype(jnp.bfloat16)
            slope_buf[slot, :, here] = slope.astype(jnp.bfloat16)
            return carry

        lax.fori_loop(0, ffn // width, part, 0)
        save(i, 1).start()
        save(i, 2).start()
        y_send[1, at, :] = dot_nt(a_buf[slot], w1[:, 4 * width + ffn :]).astype(jnp.bfloat16)
        swap_y(1, i).start()

    def last(i):
        at = slice(i * CHUNK, (i + 1) * CHUNK)
        swap_y(1, i).wait_recv()
        both = y_send[1, at, :].astype(jnp.float32) + y_recv[1, at, :].astype(jnp.float32)
        final = e1[at, :] + both
        ef[at, :] = final
        mem[at, :] = normed(final, gains[5:6, :]).astype(jnp.bfloat16)

    attend(0)
    gather.relay_along(1)
    gather.start(2)
    attend(1)
    gather.relay_beside(1)
    attend(2)
    gather.finish(1)
    feed(0)
    gather.relay_along(2)
    gather.start(3)
    attend(3)
    feed(1)
    gather.relay_beside(2)
    feed(2)
    gather.relay_along(3)
    feed(3)
    last(0)
    last(1)
    gather.relay_beside(3)
    last(2)
    last(3)
    gather.finish(2)
    gather.finish(3)
    gather.close()
    for i in range(steps):
        swap_y(0, i).wait_send()
        swap_y(1, i).wait_send()
    for i in range(steps - 2, steps):
        for kind in range(3):
            save(i, kind).wait()


def enc_forward(wide, x_own, pack, gains, base, segments):
    half, model = x_own.shape
    rows = 2 * half
    pairs = base.shape[0]
    width = pairs * PAIR
    ffn = (pack.shape[1] - 12 * width) // 4
    bf, f32 = jnp.bfloat16, jnp.float32
    shape = jax.ShapeDtypeStruct
    slots = gather_slots(wide)
    steps = rows // CHUNK
    return pl.pallas_call(
        functools.partial(enc_forward_kernel, wide),
        in_specs=[vmem_spec(), any_spec(), vmem_spec(), vmem_spec(), vmem_spec(), vmem_spec()],
        out_shape=[
            shape((model, 4 * width + 2 * ffn), bf),
            shape((model, 8 * width + 2 * ffn), bf),
            shape((rows, model), bf),
            shape((rows, 3 * width), bf),
            shape((rows, width), bf),
            shape((rows, width), f32),
            shape((2 * pairs, rows, rows), bf),
            shape((rows, model), f32),
            shape((rows, model), bf),
            shape((rows, ffn), bf),
            shape((rows, ffn), bf),
            shape((rows, model), f32),
            shape((rows, model), bf),
        ],
        out_specs=[
            vmem_spec(),
            any_spec(),
            vmem_spec(),
            vmem_spec(),
            vmem_spec(),
            vmem_spec(),
            any_spec(),
            vmem_spec(),
            vmem_spec(),
            any_spec(),
            any_spec(),
            vmem_spec(),
            vmem_spec(),
        ],
        scratch_shapes=[
            pltpu.VMEM((rows, model), bf),
            pltpu.VMEM((2 * pairs, CHUNK, 2 * rows), f32),
            pltpu.VMEM((2, 2 * pairs, CHUNK, rows), bf),
            pltpu.VMEM((2, CHUNK, ffn), bf),
            pltpu.VMEM((2, CHUNK, ffn), bf),
            pltpu.VMEM((2, rows, model), bf),
            pltpu.VMEM((2, rows, model), bf),
            pltpu.SemaphoreType.DMA((4, slots)),
            pltpu.SemaphoreType.DMA((4, slots)),
            pltpu.SemaphoreType.DMA((4,)),
            pltpu.SemaphoreType.DMA((2,)),
            pltpu.SemaphoreType.DMA((2, steps)),
            pltpu.SemaphoreType.DMA((2, steps)),
            pltpu.SemaphoreType.DMA((7,)),
        ],
        compiler_params=pltpu.CompilerParams(
            collective_id=0, has_side_effects=True, vmem_limit_bytes=VMEM_BYTES
        ),
        cost_estimate=pl.CostEstimate(flops=10**10, bytes_accessed=6 * 10**7, transcendentals=0),
    )(x_own, pack, gains, base, segments[:, None], segments[None, :])


NEAR = 2 * CHUNK


def norm_back(values, gain, grad):
    scale = lax.rsqrt(jnp.mean(values * values, axis=1, keepdims=True) + EPS)
    scaled = grad * gain
    pulled = scale * (scaled - values * (scale * scale) * jnp.mean(scaled * values, axis=1, keepdims=True))
    return pulled, jnp.sum(grad * values * scale, axis=0, keepdims=True)


class Scatter:
    def __init__(self, place, rows, groups, tile, send, receive):
        self.place, self.rows, self.groups, self.tile = place, rows, groups, tile
        self.send, self.receive = send, receive
        self.sent = []

    def columns(self, group, core):
        first, width = self.groups[group]["first"], self.groups[group]["width"]
        return pl.ds(pl.multiple_of(first + core * (width // 2), 128), width // 2)

    def block(self, group, index):
        return self.groups[group]["grad"].at[
            pl.ds(pl.multiple_of(index * self.rows, 16), self.rows), self.columns(group, self.place.core)
        ]

    def push(self, group, slot, source, target, partner, arrival=None):
        arrival = slot if arrival is None else arrival
        copy = remote(source, target, self.send.at[group, slot], self.receive.at[group, arrival], partner)
        copy.start()
        self.sent.append(copy)

    def await_slot(self, group, slot, block):
        remote(block, block, self.send.at[group, 0], self.receive.at[group, slot], self.place.sibling()).wait_recv()

    def start(self, group):
        parts = self.groups[group]
        self.push(
            group, 0, parts["grad"].at[:, self.columns(group, 1 - self.place.core)], parts["core"], self.place.sibling()
        )

    def add_block(self, group, index, other):
        block = self.block(group, index)
        block[...] = (block[...].astype(jnp.float32) + other.astype(jnp.float32)).astype(jnp.bfloat16)
        return block

    def beside(self, group):
        parts, place = self.groups[group], self.place
        self.await_slot(group, 0, parts["core"])

        def received(index):
            return parts["core"][pl.ds(pl.multiple_of(index * self.rows, 16), self.rows), :]

        for step in range(place.fars):
            far = lax.rem(place.far + 1 + step, place.fars)
            index = 2 * far + 1 - place.near
            block = self.add_block(group, index, received(index))
            self.push(group, 1 + step, block, parts["beside"].at[step], place.beside())
        for step in range(place.fars):
            far = lax.rem(place.far + 1 + step, place.fars)
            index = 2 * far + place.near
            self.add_block(group, index, received(index))

    def along(self, group):
        parts, place = self.groups[group], self.place
        for step in range(1, place.fars):
            index = 2 * lax.rem(place.far + step, place.fars) + place.near
            self.await_slot(group, step, parts["beside"].at[step - 1])
            block = self.add_block(group, index, parts["beside"][step - 1])
            self.push(group, place.fars + step, block, parts["along"].at[step - 1], place.along(step))

    def total(self, group):
        parts, place = self.groups[group], self.place
        self.await_slot(group, place.fars, parts["beside"].at[place.fars - 1])
        value = self.block(group, place.wide)[...].astype(jnp.float32) + parts["beside"][place.fars - 1].astype(jnp.float32)
        for step in range(1, place.fars):
            self.await_slot(group, place.fars + step, parts["along"].at[step - 1])
            value = value + parts["along"][step - 1].astype(jnp.float32)
        half = parts["width"] // 2
        block = self.tile.at[:, pl.ds(pl.multiple_of(parts["out"] + place.core * half, 128), half)]
        block[...] = value.astype(jnp.bfloat16)
        self.push(group, 2 * place.fars, block, block, place.sibling())

    def finish(self, group):
        parts, place = self.groups[group], self.place
        half = parts["width"] // 2
        block = self.tile.at[:, pl.ds(pl.multiple_of(parts["out"] + (1 - place.core) * half, 128), half)]
        self.await_slot(group, 2 * place.fars, block)

    def close(self):
        for copy in self.sent:
            copy.wait_send()


def scatter_slots(wide):
    return 2 * (wide // 2) + 1


def scatter_buffers(wide, model, width):
    half, rows, fars = width // 2, model // wide, wide // 2
    return [
        pltpu.VMEM((model, half), jnp.bfloat16),
        pltpu.VMEM((fars, rows, half), jnp.bfloat16),
        pltpu.VMEM((fars - 1, rows, half), jnp.bfloat16),
    ]


def softmax_back_pair(q_pair, k_pair, v_pair, c_pair, inverse, gc_pair, weights, near):
    scaled = (gc_pair.astype(jnp.float32) * inverse).astype(jnp.bfloat16)
    product = scaled.astype(jnp.float32) * c_pair.astype(jnp.float32)
    lane = lax.broadcasted_iota(jnp.int32, product.shape, 1)
    inner = (
        jnp.sum(jnp.where(lane < DK, product, 0.0), axis=1, keepdims=True),
        jnp.sum(jnp.where(lane < DK, 0.0, product), axis=1, keepdims=True),
    )
    g_heads = split_heads(scaled)
    q_heads = split_heads(q_pair)
    k_heads = split_heads(k_pair)
    gq = None
    grads = []
    for head in range(2):
        grad = weights[head].astype(jnp.float32) * (dot_nt(g_heads[head], v_pair) - inner[head])
        if near is not None:
            near(head, grad)
        grad = grad.astype(jnp.bfloat16)
        grads.append(grad)
        part = dot_nn(grad, k_heads[head])
        gq = part if gq is None else gq + part
    gk = dot_tn(jnp.concatenate(grads, axis=0), jnp.concatenate(q_heads, axis=0))
    gv = dot_tn(jnp.concatenate([weights[0], weights[1]], axis=0), jnp.concatenate(g_heads, axis=0))
    return gq, gk, gv


def fold_near(rows):
    total = jnp.zeros((8, 2 * NEAR), jnp.float32)
    blank = jnp.zeros((8, NEAR), jnp.float32)
    for a in range(CHUNK // 8):
        wider = jnp.concatenate([rows[8 * a : 8 * a + 8, :], blank], axis=1)
        total = total + pltpu.roll(wider, (CHUNK - 8 * a) % (2 * NEAR), 1)
    return total


def near_table_grad(near_sums, far_sums):
    heads = near_sums.shape[0]
    places = jnp.arange(2 * NEAR, dtype=jnp.int32)[None, :]
    relative = places - jnp.arange(8, dtype=jnp.int32)[:, None] - CHUNK - NEAR // 4
    buckets = bucket_index(relative.reshape(-1), True)
    onehot = (buckets[None, :] == jnp.arange(NB, dtype=jnp.int32)[:, None]).astype(jnp.float32)
    near = lax.dot_general(
        onehot,
        near_sums.reshape(heads, 16 * NEAR),
        (((1,), (1,)), ((), ())),
        precision=HIGH,
        preferred_element_type=jnp.float32,
    )
    far = jnp.sum(far_sums, axis=(2, 3))
    ends = jnp.array([[NB // 2 - 1], [NB - 1]], jnp.int32)
    choose = (ends == jnp.arange(NB, dtype=jnp.int32)[None, :]).astype(jnp.float32)
    return near + lax.dot_general(choose, far, (((0,), (0,)), ((), ())), precision=HIGH, preferred_element_type=jnp.float32)


def enc_backward_kernel(
    wide,
    x_own,
    cot_own,
    cot_other,
    gains,
    part_own,
    part_other,
    w1_in,
    n0_in,
    qkv_in,
    c_in,
    inv_in,
    e_all,
    e1_all,
    n1_in,
    slope_all,
    a_in,
    ef_all,
    grad_out,
    tile,
    gain_sums,
    near_sums,
    far_sums,
    w1,
    n0,
    qkv,
    c,
    inv,
    n1,
    active,
    cot,
    e_buf,
    state_buf,
    slope_buf,
    part_buf,
    other_buf,
    g_send,
    g_recv,
    l_recv,
    state_grad,
    gy,
    gu,
    gqkv,
    gk_sum,
    gv_sum,
    strip,
    core_f,
    beside_f,
    along_f,
    beside_a,
    along_a,
    s_send,
    s_recv,
    g_sems,
    l_sems,
    e_sems,
    t_sems,
    i_sems,
):
    place = Place(wide)
    side = place.side
    half = x_own.shape[0]
    rows = 2 * half
    steps = rows // CHUNK
    width = c.shape[1]
    ffn = active.shape[1]
    pairs = width // PAIR
    model = x_own.shape[1]
    bf, f32 = jnp.bfloat16, jnp.float32
    place.greet()

    def swap(i):
        at = pl.ds(i * CHUNK, CHUNK)
        return remote(g_send.at[at], g_recv.at[at], g_sems.at[0, i], g_sems.at[1, i], place.across())

    def fetch(i):
        at = pl.ds(i * CHUNK, CHUNK)
        slot = i % 2
        return [
            pltpu.make_async_copy(ef_all.at[at], state_buf.at[slot], t_sems.at[0, slot]),
            pltpu.make_async_copy(slope_all.at[at], slope_buf.at[slot], t_sems.at[1, slot]),
            pltpu.make_async_copy(part_own.at[at], part_buf.at[slot], t_sems.at[2, slot]),
            pltpu.make_async_copy(part_other.at[at], other_buf.at[slot], t_sems.at[3, slot]),
        ]

    def fetch_state(i):
        at = pl.ds(i * CHUNK, CHUNK)
        return pltpu.make_async_copy(e1_all.at[at], state_buf.at[i % 2], t_sems.at[0, i % 2])

    def fetch_e(step):
        chunk, pair, slot = step // pairs, lax.rem(step, pairs), lax.rem(step, 2)
        at = pl.ds(pl.multiple_of(chunk * CHUNK, CHUNK), CHUNK)
        return pltpu.make_async_copy(e_all.at[pl.ds(2 * pair, 2), at, :], e_buf.at[slot], e_sems.at[slot])

    mine = pl.ds(pl.multiple_of(side * half, 16), half)
    theirs = pl.ds(pl.multiple_of((1 - side) * half, 16), half)
    loads = [
        pltpu.make_async_copy(cot_own, cot.at[mine], i_sems.at[0]),
        pltpu.make_async_copy(cot_other, cot.at[theirs], i_sems.at[1]),
        pltpu.make_async_copy(w1_in, w1, i_sems.at[2]),
        pltpu.make_async_copy(a_in, active, i_sems.at[3]),
        pltpu.make_async_copy(n1_in, n1, i_sems.at[4]),
        pltpu.make_async_copy(qkv_in, qkv, i_sems.at[5]),
        pltpu.make_async_copy(c_in, c, i_sems.at[6]),
        pltpu.make_async_copy(inv_in, inv, i_sems.at[7]),
        pltpu.make_async_copy(n0_in, n0, i_sems.at[8]),
    ]
    for load in loads[:2]:
        load.start()
    for load in fetch(0):
        load.start()
    for load in loads[2:]:
        load.start()
    gk_sum[...] = jnp.zeros_like(gk_sum)
    gv_sum[...] = jnp.zeros_like(gv_sum)
    strip[...] = jnp.zeros_like(strip)
    far_sums[...] = jnp.zeros_like(far_sums)
    gain_sums[...] = jnp.zeros_like(gain_sums)
    scatter = Scatter(
        place,
        model // wide,
        [
            dict(grad=w1, first=4 * width, width=2 * ffn, out=4 * width, core=core_f, beside=beside_f, along=along_f),
            dict(grad=gu.at[pl.ds(0, model)], first=0, width=4 * width, out=0, core=active.at[pl.ds(0, model), pl.ds(0, 2 * width)], beside=beside_a, along=along_a),
        ],
        tile,
        s_send,
        s_recv,
    )

    def own_weight(i):
        return jnp.where((i * CHUNK) // half == side, 1.0, 0.0).astype(f32)

    for load in loads[:3]:
        load.wait()

    for i in range(steps):
        at = slice(i * CHUNK, (i + 1) * CHUNK)
        slot = i % 2
        if i + 1 < steps:
            for load in fetch(i + 1):
                load.start()
        for load in fetch(i):
            load.wait()
        grad = part_buf[slot].astype(f32) + other_buf[slot].astype(f32)
        pulled, gain = norm_back(state_buf[slot], gains[5:6, :], grad)
        gain_sums[5:6, :] += gain * own_weight(i)
        total = cot[at, :].astype(f32) + pulled
        state_grad[at, :] = total
        gy[at, :] = total.astype(bf)

        def part(j, carry):
            cols = pl.ds(pl.multiple_of(4 * width + ffn + j * width, PAIR), width)
            here = pl.ds(pl.multiple_of(j * width, PAIR), width)
            grad_active = dot_nn(gy[at, :], w1[:, cols])
            gu[at, here] = (slope_buf[slot, :, here].astype(f32) * grad_active).astype(bf)
            return carry

        lax.fori_loop(0, ffn // width, part, 0)
        g_send[at, :] = dot_nt(gu[at, :], w1[:, 4 * width : 4 * width + ffn]).astype(bf)
        swap(i).start()
    for load in loads[3:]:
        load.wait()
    fetch_state(0).start()
    fetch_e(0).start()

    def weight_grads(t, carry):
        tile_rows = pl.ds(pl.multiple_of(t * CHUNK, CHUNK), CHUNK)
        w1[tile_rows, 4 * width : 4 * width + ffn] = dot_tn(n1[:, tile_rows], gu[...]).astype(bf)
        w1[tile_rows, 4 * width + ffn :] = dot_tn(gy[:, tile_rows], active[...]).astype(bf)
        return carry

    lax.fori_loop(0, model // CHUNK, weight_grads, 0)
    scatter.start(0)

    dw0 = gu
    l_send = n1

    def lanes(base_lane, pair):
        return pl.ds(pl.multiple_of(base_lane + pair * PAIR, PAIR), PAIR)

    def attend_back(i):
        at = slice(i * CHUNK, (i + 1) * CHUNK)
        slot = i % 2
        if i + 1 < steps:
            fetch_state(i + 1).start()
        fetch_state(i).wait()
        swap(i).wait_recv()
        grad = g_send[at, :].astype(f32) + g_recv[at, :].astype(f32)
        pulled, gain = norm_back(state_buf[slot], gains[1:2, :], grad)
        gain_sums[1:2, :] += gain * own_weight(i)
        total = state_grad[at, :] + pulled
        state_grad[at, :] = total
        gy[at, :] = total.astype(bf)
        g_send[at, :width] = dot_nn(gy[at, :], w1[:, 3 * width : 4 * width]).astype(bf)
        low, high = max(i * CHUNK - NEAR // 4, 0), min(i * CHUNK + CHUNK + NEAR // 4, rows)
        shift = low - (i * CHUNK - NEAR // 4)

        def one(pair, carry):
            step = i * pairs + pair

            @pl.when(step + 1 < steps * pairs)
            def _():
                fetch_e(step + 1).start()

            fetch_e(step).wait()
            e_slot = lax.rem(step, 2)

            def near(head, grad):
                strip[2 * pair + head, :, shift : shift + high - low] += grad[:, low:high]
                for edge, (start, end) in enumerate(((0, low), (high, rows))):
                    if end > start:
                        folded = jnp.sum(grad[:, start:end].reshape(CHUNK // 8, 8, end - start), axis=0)
                        wide_sum = folded[:, :128]
                        for lane in range(128, end - start, 128):
                            wide_sum = wide_sum + folded[:, lane : lane + 128]
                        far_sums[edge, 2 * pair + head] += wide_sum

            gq, gk, gv = softmax_back_pair(
                qkv[at, lanes(0, pair)],
                qkv[:, lanes(width, pair)],
                qkv[:, lanes(2 * width, pair)],
                c[at, lanes(0, pair)],
                inv[at, lanes(0, pair)],
                g_send[at, lanes(0, pair)],
                (e_buf[e_slot, 0], e_buf[e_slot, 1]),
                near,
            )
            gqkv[at, lanes(0, pair)] = gq.astype(bf)
            gk_sum[:, lanes(0, pair)] += gk
            gv_sum[:, lanes(0, pair)] += gv
            return carry

        lax.fori_loop(0, pairs, one, 0)

    for i in range(steps):
        swap(i).wait_send()
        attend_back(i)
        if i == 0:
            scatter.beside(0)
        if i == 2:
            scatter.along(0)
    gqkv[:, width : 2 * width] = gk_sum[...].astype(bf)
    gqkv[:, 2 * width :] = gv_sum[...].astype(bf)

    def weight_grads_a(t, carry):
        tile_rows = pl.ds(pl.multiple_of(t * CHUNK, CHUNK), CHUNK)
        dw0[tile_rows, : 3 * width] = dot_tn(n0[:, tile_rows], gqkv[...]).astype(bf)
        dw0[tile_rows, 3 * width :] = dot_tn(gy[:, tile_rows], c[...]).astype(bf)
        return carry

    lax.fori_loop(0, model // CHUNK, weight_grads_a, 0)
    scatter.start(1)
    last = []
    for part in range(half // CHUNK):
        there = pl.ds(pl.multiple_of((1 - side) * half + part * CHUNK, CHUNK), CHUNK)
        at = pl.ds(part * CHUNK, CHUNK)
        l_send[at, :] = dot_nt(gqkv[there, :], w1[:, : 3 * width]).astype(bf)
        last.append(remote(l_send.at[at], l_recv.at[at], l_sems.at[0, part], l_sems.at[1, part], place.across()))
        last[part].start()
        if part == 0:
            scatter.beside(1)
    scatter.total(0)

    def fold(head, carry):
        near_sums[head] = fold_near(strip[head])
        return carry

    lax.fori_loop(0, 2 * pairs, fold, 0)
    scatter.along(1)
    for part in range(half // CHUNK):
        here = pl.ds(pl.multiple_of(side * half + part * CHUNK, CHUNK), CHUNK)
        at = pl.ds(part * CHUNK, CHUNK)
        own = dot_nt(gqkv[here, :], w1[:, : 3 * width])
        last[part].wait_recv()
        grad = own + l_recv[at, :].astype(f32)
        pulled, gain = norm_back(x_own[at, :].astype(f32), gains[0:1, :], grad)
        gain_sums[0:1, :] += gain
        grad_out[at, :] = state_grad[here, :] + pulled
    scatter.total(1)
    scatter.finish(0)
    scatter.finish(1)
    scatter.close()
    for copy in last:
        copy.wait_send()


def enc_backward(wide, x_own, cot_own, cot_other, gains, part_own, part_other, saved):
    half, model = x_own.shape
    rows = 2 * half
    w1, n0, qkv, c, inv, e_all, e1, n1, slope, active, ef = saved
    width, ffn = c.shape[1], active.shape[1]
    pairs = width // PAIR
    steps = rows // CHUNK
    bf, f32 = jnp.bfloat16, jnp.float32
    shape = jax.ShapeDtypeStruct
    dma = pltpu.SemaphoreType.DMA
    return pl.pallas_call(
        functools.partial(enc_backward_kernel, wide),
        in_specs=[vmem_spec(), any_spec(), any_spec(), vmem_spec()] + [any_spec()] * 13,
        out_shape=[
            shape((half, model), f32),
            shape((model // wide, 4 * width + 2 * ffn), bf),
            shape((8, model), f32),
            shape((2 * pairs, 8, 2 * NEAR), f32),
            shape((2, 2 * pairs, 8, 128), f32),
        ],
        out_specs=[vmem_spec()] * 5,
        scratch_shapes=[
            pltpu.VMEM(w1.shape, bf),
            pltpu.VMEM(n0.shape, bf),
            pltpu.VMEM(qkv.shape, bf),
            pltpu.VMEM(c.shape, bf),
            pltpu.VMEM(inv.shape, f32),
            pltpu.VMEM(n1.shape, bf),
            pltpu.VMEM(active.shape, bf),
            pltpu.VMEM((rows, model), bf),
            pltpu.VMEM((2, 2, CHUNK, rows), bf),
            pltpu.VMEM((2, CHUNK, model), f32),
            pltpu.VMEM((2, CHUNK, ffn), bf),
            pltpu.VMEM((2, CHUNK, model), bf),
            pltpu.VMEM((2, CHUNK, model), bf),
            pltpu.VMEM((rows, model), bf),
            pltpu.VMEM((rows, model), bf),
            pltpu.VMEM((half, model), bf),
            pltpu.VMEM((rows, model), f32),
            pltpu.VMEM((rows, model), bf),
            pltpu.VMEM((rows, ffn), bf),
            pltpu.VMEM((rows, 3 * width), bf),
            pltpu.VMEM((rows, width), f32),
            pltpu.VMEM((rows, width), f32),
            pltpu.VMEM((2 * pairs, CHUNK, NEAR), f32),
        ]
        + scatter_buffers(wide, model, 2 * ffn)
        + scatter_buffers(wide, model, 4 * width)[1:]
        + [
            dma((2, scatter_slots(wide))),
            dma((2, scatter_slots(wide))),
            dma((2, steps)),
            dma((2, half // CHUNK)),
            dma((2,)),
            dma((4, 2)),
            dma((9,)),
        ],
        compiler_params=pltpu.CompilerParams(
            collective_id=1, has_side_effects=True, vmem_limit_bytes=VMEM_BYTES
        ),
        cost_estimate=pl.CostEstimate(flops=2 * 10**10, bytes_accessed=6 * 10**7, transcendentals=0),
    )(x_own, cot_own, cot_other, gains, part_own, part_other, w1, n0, qkv, c, inv, e_all, e1, n1, slope, active, ef)


def fold_offsets(grad):
    rows = grad.shape[0]
    total = jnp.zeros((8, 2 * rows), jnp.float32)
    blank = jnp.zeros((8, rows), jnp.float32)
    for a in range(rows // 8):
        wider = jnp.concatenate([grad[8 * a : 8 * a + 8, :], blank], axis=1)
        total = total + pltpu.roll(wider, (rows - 8 * a) % (2 * rows), 1)
    return total


def decoder_kernel(
    wide,
    dec_own,
    dcot_own,
    cot_own,
    gains,
    base,
    qseg,
    kseg,
    mseg,
    mem_in,
    w_in,
    dec_out,
    dec_grad,
    tile,
    gain_sums,
    off_sums,
    part_own,
    part_other,
    cot_other,
    w,
    mem,
    dec,
    dcot,
    state,
    normals,
    qkv,
    c,
    inv,
    e_self,
    e_cross,
    strip,
    kv,
    active,
    ga,
    gu,
    grad_state,
    gy,
    gqkv,
    gkv,
    y_send,
    y_recv,
    dw,
    core_f,
    beside_f,
    along_f,
    core_d,
    beside_d,
    along_d,
    core_c,
    beside_c,
    along_c,
    s_send,
    s_recv,
    y_sems,
    x_sems,
    p_sems,
    o_sems,
    i_sems,
):
    place = Place(wide)
    side = place.side
    half = dec_own.shape[0]
    rows = 2 * half
    model = dec_own.shape[1]
    width = c.shape[2]
    ffn = active.shape[1]
    pairs = width // PAIR
    span = mem.shape[0]
    bf, f32 = jnp.bfloat16, jnp.float32
    place.greet()
    mine = pl.ds(pl.multiple_of(side * half, 16), half)
    theirs = pl.ds(pl.multiple_of((1 - side) * half, 16), half)
    at_d, at_f = 4 * width, 8 * width

    inputs = [
        remote(dec_own, dec.at[mine], x_sems.at[0, 0], x_sems.at[1, 0], place.across()),
        remote(dcot_own, dcot.at[mine], x_sems.at[0, 1], x_sems.at[1, 1], place.across()),
    ]
    inputs[0].start()
    inputs[1].start()
    cot_part = cot_own.shape[0] // 4

    def swap_cot(i):
        at = pl.ds(i * cot_part, cot_part)
        return remote(cot_own.at[at], cot_other.at[at], x_sems.at[0, 2 + i], x_sems.at[1, 2 + i], place.across())

    def load_w(first, count, sem):
        cols = pl.ds(first, count)
        return pltpu.make_async_copy(w_in.at[:, cols], w.at[:, cols], i_sems.at[sem])

    loads = [
        load_w(0, 4 * width, 0),
        load_w(at_d, 4 * width, 1),
        pltpu.make_async_copy(mem_in, mem, i_sems.at[2]),
        load_w(at_f, 2 * ffn, 3),
        pltpu.make_async_copy(dec_own, dec.at[mine], i_sems.at[4]),
        pltpu.make_async_copy(dcot_own, dcot.at[mine], i_sems.at[5]),
    ]
    for load in (loads[4], loads[5], loads[0], loads[2], loads[1], loads[3]):
        load.start()
    build_strip(strip, base, pairs, rows, rows)
    gain_sums[...] = jnp.zeros_like(gain_sums)
    scatter = Scatter(
        place,
        model // wide,
        [
            dict(grad=w, first=at_f, width=2 * ffn, out=at_f, core=core_f, beside=beside_f, along=along_f),
            dict(grad=dw, first=at_d, width=4 * width, out=at_d, core=core_d, beside=beside_d, along=along_d),
            dict(grad=dw, first=0, width=4 * width, out=0, core=core_c, beside=beside_c, along=along_c),
        ],
        tile,
        s_send,
        s_recv,
    )

    def swap(kind):
        return remote(y_send.at[kind], y_recv.at[kind], y_sems.at[0, kind], y_sems.at[1, kind], place.across())

    def send_branch(kind, value):
        y_send[kind] = value.astype(bf)
        swap(kind).start()

    def branch(kind):
        swap(kind).wait_recv()
        return y_send[kind].astype(f32) + y_recv[kind].astype(f32)

    def lanes(base_lane, pair):
        return pl.ds(pl.multiple_of(base_lane + pair * PAIR, PAIR), PAIR)

    def norm_to(index, gain, value):
        state[index] = value
        normals[index] = normed(value, gains[gain : gain + 1, :]).astype(bf)

    loads[4].wait()
    inputs[0].wait_recv()
    norm_to(0, 2, dec[...].astype(f32))
    loads[0].wait()
    qkv[:, : 3 * width] = dot_nn(normals[0], w[:, : 3 * width]).astype(bf)

    def self_pair(pair, carry):
        allowed = qseg[...] == kseg[...]
        allowed = allowed & (
            lax.broadcasted_iota(jnp.int32, (rows, rows), 1) <= lax.broadcasted_iota(jnp.int32, (rows, rows), 0)
        )

        def bias(head):
            return strip[2 * pair + head, :, :rows]

        def store(head, weights):
            e_self[2 * pair + head] = weights

        inverse, context = softmax_pair(
            qkv[:, lanes(0, pair)], qkv[:, lanes(width, pair)], qkv[:, lanes(2 * width, pair)], allowed, bias, store
        )
        inv[0, :, lanes(0, pair)] = inverse
        c[0, :, lanes(0, pair)] = context
        return carry

    lax.fori_loop(0, pairs, self_pair, 0)
    send_branch(0, dot_nt(c[0], w[:, 3 * width : 4 * width]))
    swap_cot(0).start()

    loads[2].wait()
    loads[1].wait()

    def cross_keys(i, carry):
        at = pl.ds(pl.multiple_of(i * CHUNK, CHUNK), CHUNK)
        kv[at, :] = dot_nn(mem[at, :], w[:, at_d + width : at_d + 3 * width]).astype(bf)
        return carry

    lax.fori_loop(0, span // CHUNK, cross_keys, 0)
    norm_to(1, 3, state[0] + branch(0))
    qkv[:, 3 * width :] = dot_nn(normals[1], w[:, at_d : at_d + width]).astype(bf)

    def cross_pair(pair, carry):
        allowed = qseg[...] == mseg[...]

        def store(head, weights):
            e_cross[2 * pair + head] = weights

        inverse, context = softmax_pair(
            qkv[:, lanes(3 * width, pair)], kv[:, lanes(0, pair)], kv[:, lanes(width, pair)], allowed, None, store
        )
        inv[1, :, lanes(0, pair)] = inverse
        c[1, :, lanes(0, pair)] = context
        return carry

    lax.fori_loop(0, pairs, cross_pair, 0)
    send_branch(1, dot_nt(c[1], w[:, at_d + 3 * width : at_d + 4 * width]))
    swap_cot(1).start()

    loads[5].wait()
    inputs[1].wait_recv()
    loads[3].wait()
    ga[...] = dot_nn(dcot[...], w[:, at_f + ffn :]).astype(f32)
    norm_to(2, 4, state[1] + branch(1))

    def hidden(j, carry):
        here = pl.ds(pl.multiple_of(j * width, PAIR), width)
        cols = pl.ds(pl.multiple_of(at_f + j * width, PAIR), width)
        value, turn = gelu_pair(dot_nn(normals[2], w[:, cols]))
        active[:, here] = value.astype(bf)
        gu[:, here] = (turn * ga[:, here]).astype(bf)
        return carry

    lax.fori_loop(0, ffn // width, hidden, 0)
    send_branch(3, dot_nt(gu[...], w[:, at_f : at_f + ffn]))
    send_branch(2, dot_nt(active[...], w[:, at_f + ffn :]))
    swap_cot(2).start()

    def feed_grads(t, carry):
        tile_rows = pl.ds(pl.multiple_of(t * CHUNK, CHUNK), CHUNK)
        w[tile_rows, at_f : at_f + ffn] = dot_tn(normals[2, :, tile_rows], gu[...]).astype(bf)
        w[tile_rows, at_f + ffn :] = dot_tn(dcot[:, tile_rows], active[...]).astype(bf)
        return carry

    lax.fori_loop(0, model // CHUNK, feed_grads, 0)
    scatter.start(0)

    row = lax.broadcasted_iota(jnp.int32, (rows, 1), 0)
    counted = jnp.where(row // half == side, 1.0, 0.0).astype(f32)

    def pull(index, gain, grad):
        values = state[index]
        pulled, unused = norm_back(values, gains[gain : gain + 1, :], grad)
        scale = lax.rsqrt(jnp.mean(values * values, axis=1, keepdims=True) + EPS) * counted
        gain_sums[gain : gain + 1, :] += jnp.sum(grad * values * scale, axis=0, keepdims=True)
        return pulled

    grad_state[...] = dcot[...].astype(f32) + pull(2, 4, branch(3))
    gy[1] = grad_state[...].astype(bf)
    gc = dot_nn(gy[1], w[:, at_d + 3 * width : at_d + 4 * width]).astype(bf)
    y_send[5, :, :width] = gc

    def cross_back(pair, carry):
        gq, gk, gv = softmax_back_pair(
            qkv[:, lanes(3 * width, pair)],
            kv[:, lanes(0, pair)],
            kv[:, lanes(width, pair)],
            c[1, :, lanes(0, pair)],
            inv[1, :, lanes(0, pair)],
            y_send[5, :, lanes(0, pair)],
            (e_cross[2 * pair], e_cross[2 * pair + 1]),
            None,
        )
        gqkv[:, lanes(3 * width, pair)] = gq.astype(bf)
        gkv[:, lanes(0, pair)] = gk.astype(bf)
        gkv[:, lanes(width, pair)] = gv.astype(bf)
        return carry

    lax.fori_loop(0, pairs, cross_back, 0)
    send_branch(4, dot_nt(gqkv[:, 3 * width :], w[:, at_d : at_d + width]))

    part = kv

    def swap_part(i):
        at = pl.ds(pl.multiple_of(i * CHUNK, CHUNK), CHUNK)
        return remote(part.at[at], part_other.at[at], p_sems.at[0, i], p_sems.at[1, i], place.across())

    def keep_part(i):
        at = pl.ds(pl.multiple_of(i * CHUNK, CHUNK), CHUNK)
        return pltpu.make_async_copy(part.at[at], part_own.at[at], o_sems.at[i])

    for i in range(span // CHUNK):
        at = pl.ds(i * CHUNK, CHUNK)
        part[at, :] = dot_nt(gkv[at, :], w[:, at_d + width : at_d + 3 * width]).astype(bf)
        swap_part(i).start()
        keep_part(i).start()
        if i == 0:
            scatter.beside(0)
    swap_cot(3).start()

    def cross_grads(t, carry):
        tile_rows = pl.ds(pl.multiple_of(t * CHUNK, CHUNK), CHUNK)
        dw[tile_rows, at_d : at_d + width] = dot_tn(normals[1, :, tile_rows], gqkv[:, 3 * width :]).astype(bf)
        dw[tile_rows, at_d + width : at_d + 3 * width] = dot_tn(mem[:, tile_rows], gkv[...]).astype(bf)
        dw[tile_rows, at_d + 3 * width : at_f] = dot_tn(gy[1, :, tile_rows], c[1]).astype(bf)
        return carry

    lax.fori_loop(0, model // CHUNK, cross_grads, 0)
    scatter.start(1)

    grad_state[...] = grad_state[...] + pull(1, 3, branch(4))
    gy[0] = grad_state[...].astype(bf)
    y_send[5, :, :width] = dot_nn(gy[0], w[:, 3 * width : 4 * width]).astype(bf)

    def self_back(pair, carry):
        def near(head, grad):
            off_sums[pair, head] = fold_offsets(grad)

        gq, gk, gv = softmax_back_pair(
            qkv[:, lanes(0, pair)],
            qkv[:, lanes(width, pair)],
            qkv[:, lanes(2 * width, pair)],
            c[0, :, lanes(0, pair)],
            inv[0, :, lanes(0, pair)],
            y_send[5, :, lanes(0, pair)],
            (e_self[2 * pair], e_self[2 * pair + 1]),
            near,
        )
        gqkv[:, lanes(0, pair)] = gq.astype(bf)
        gqkv[:, lanes(width, pair)] = gk.astype(bf)
        gqkv[:, lanes(2 * width, pair)] = gv.astype(bf)
        return carry

    lax.fori_loop(0, pairs, self_back, 0)

    def self_grads(t, carry):
        tile_rows = pl.ds(pl.multiple_of(t * CHUNK, CHUNK), CHUNK)
        dw[tile_rows, : 3 * width] = dot_tn(normals[0, :, tile_rows], gqkv[:, : 3 * width]).astype(bf)
        dw[tile_rows, 3 * width : at_d] = dot_tn(gy[0, :, tile_rows], c[0]).astype(bf)
        return carry

    lax.fori_loop(0, model // CHUNK, self_grads, 0)
    scatter.start(2)
    scatter.beside(1)
    scatter.along(0)
    y_send[5] = dot_nt(gqkv[:, : 3 * width], w[:, : 3 * width]).astype(bf)
    back = remote(y_send.at[5, theirs], y_recv.at[5, theirs], y_sems.at[0, 5], y_sems.at[1, 5], place.across())
    back.start()
    scatter.beside(2)
    scatter.total(0)
    scatter.along(1)
    back.wait_recv()
    grad = y_send[5, mine, :].astype(f32) + y_recv[5, mine, :].astype(f32)
    pulled, gain = norm_back(state[0, mine, :], gains[2:3, :], grad)
    gain_sums[2:3, :] += gain
    dec_grad[...] = grad_state[mine, :] + pulled
    swap(2).wait_recv()
    dec_out[...] = (state[2, mine, :] + y_send[2, mine, :].astype(f32) + y_recv[2, mine, :].astype(f32)).astype(bf)
    scatter.along(2)
    scatter.total(1)
    scatter.total(2)
    for i in range(span // CHUNK):
        swap_part(i).wait()
        keep_part(i).wait()
    for i in range(4):
        swap_cot(i).wait()
    for group in range(3):
        scatter.finish(group)
    scatter.close()
    for copy in inputs:
        copy.wait_send()
    for kind in range(5):
        swap(kind).wait_send()
    back.wait_send()


def decoder(wide, dec_own, dcot_own, cot_own, gains, base, dec_segments, enc_segments, mem, w2):
    half, model = dec_own.shape
    rows = 2 * half
    span = mem.shape[0]
    pairs = base.shape[0]
    width = pairs * PAIR
    ffn = (w2.shape[1] - 8 * width) // 2
    bf, f32 = jnp.bfloat16, jnp.float32
    shape = jax.ShapeDtypeStruct
    dma = pltpu.SemaphoreType.DMA
    return pl.pallas_call(
        functools.partial(decoder_kernel, wide),
        in_specs=[any_spec()] * 3 + [vmem_spec()] * 5 + [any_spec()] * 2,
        out_shape=[
            shape((half, model), bf),
            shape((half, model), f32),
            shape((model // wide, w2.shape[1]), bf),
            shape((8, model), f32),
            shape((pairs, 2, 8, 2 * rows), f32),
            shape((span, model), bf),
            shape((span, model), bf),
            shape(cot_own.shape, bf),
        ],
        out_specs=[vmem_spec()] * 5 + [any_spec()] * 3,
        scratch_shapes=[
            pltpu.VMEM(w2.shape, bf),
            pltpu.VMEM((span, model), bf),
            pltpu.VMEM((rows, model), bf),
            pltpu.VMEM((rows, model), bf),
            pltpu.VMEM((3, rows, model), f32),
            pltpu.VMEM((3, rows, model), bf),
            pltpu.VMEM((rows, 4 * width), bf),
            pltpu.VMEM((2, rows, width), bf),
            pltpu.VMEM((2, rows, width), f32),
            pltpu.VMEM((2 * pairs, rows, rows), bf),
            pltpu.VMEM((2 * pairs, rows, span), bf),
            pltpu.VMEM((2 * pairs, rows, 2 * rows), f32),
            pltpu.VMEM((span, 2 * width), bf),
            pltpu.VMEM((rows, ffn), bf),
            pltpu.VMEM((rows, ffn), f32),
            pltpu.VMEM((rows, ffn), bf),
            pltpu.VMEM((rows, model), f32),
            pltpu.VMEM((2, rows, model), bf),
            pltpu.VMEM((rows, 4 * width), bf),
            pltpu.VMEM((span, 2 * width), bf),
            pltpu.VMEM((6, rows, model), bf),
            pltpu.VMEM((6, rows, model), bf),
            pltpu.VMEM((model, 8 * width), bf),
        ]
        + scatter_buffers(wide, model, 2 * ffn)
        + scatter_buffers(wide, model, 4 * width)
        + scatter_buffers(wide, model, 4 * width)
        + [
            dma((3, scatter_slots(wide))),
            dma((3, scatter_slots(wide))),
            dma((2, 6)),
            dma((2, 6)),
            dma((2, span // CHUNK)),
            dma((span // CHUNK,)),
            dma((6,)),
        ],
        compiler_params=pltpu.CompilerParams(
            collective_id=2, has_side_effects=True, vmem_limit_bytes=VMEM_BYTES
        ),
        cost_estimate=pl.CostEstimate(flops=10**10, bytes_accessed=6 * 10**7, transcendentals=0),
    )(
        dec_own,
        dcot_own,
        cot_own,
        gains,
        base,
        dec_segments[:, None],
        dec_segments[None, :],
        enc_segments[None, :],
        mem,
        w2,
    )


def sum_kernel(wide, value, total, held, send, receive):
    place = Place(wide)
    place.greet()
    held[0] = value[...]
    for stage, partner in enumerate((place.sibling(), place.across(), place.beside())):
        copy = remote(held.at[stage], held.at[4 + stage], send.at[stage], receive.at[stage], partner)
        copy.start()
        copy.wait()
        held[stage + 1] = held[stage] + held[4 + stage]
    copies = []
    for step in range(1, place.fars):
        copies.append(
            remote(held.at[3], held.at[7 + place.far], send.at[2 + step], receive.at[2 + step], place.along(step))
        )
        copies[-1].start()
    for copy in copies:
        copy.wait()
    result = None
    for far in range(place.fars):
        part = jnp.where(place.far == far, held[3], held[7 + far])
        result = part if result is None else result + part
    total[...] = result


def sum_all(wide, value):
    fars = wide // 2
    dma = pltpu.SemaphoreType.DMA
    return pl.pallas_call(
        functools.partial(sum_kernel, wide),
        in_specs=[vmem_spec()],
        out_shape=jax.ShapeDtypeStruct(value.shape, value.dtype),
        out_specs=vmem_spec(),
        scratch_shapes=[pltpu.VMEM((7 + fars,) + value.shape, value.dtype), dma((2 + fars,)), dma((2 + fars,))],
        compiler_params=pltpu.CompilerParams(collective_id=3, has_side_effects=True),
    )(value)


def pack_shards(attn_query, attn_kv, attn_out, ffn_up, ffn_down):
    def attention(layer):
        return [attn_query[layer], attn_kv[layer, 0], attn_kv[layer, 1], attn_out[layer].T]

    def feed(layer):
        return [ffn_up[layer], ffn_down[layer].T]

    return jnp.concatenate(attention(0) + feed(0) + attention(1) + attention(2) + feed(1), axis=1)


def on_device(
    wide,
    enc_input,
    dec_input,
    enc_lengths,
    dec_lengths,
    attn_query,
    attn_kv,
    attn_out,
    ffn_up,
    ffn_down,
    gains,
    rel_bias,
    enc_cotangent,
    dec_cotangent,
):
    gain_rows = gains.astype(jnp.float32)
    heads_local = rel_bias.shape[2]
    enc_segments = segment_ids(enc_lengths[0], ENC)
    dec_segments = segment_ids(dec_lengths[0], DEC)
    side = lax.axis_index("narrow")
    width, ffn = DK * heads_local, ffn_up.shape[2]
    half = enc_input.shape[0]
    pack = pack_shards(attn_query, attn_kv, attn_out, ffn_up, ffn_down)
    w1, w2, n0, qkv, context, inverse, weights, e1, n1, slope, active, ef, memory = enc_forward(
        wide, enc_input, pack, gain_rows, base_rows(rel_bias[0], ENC, True), enc_segments
    )
    dec_output, grad_dec, tile_two, dec_gains, off_sums, part_own, part_other, cot_other = decoder(
        wide,
        dec_input,
        dec_cotangent,
        enc_cotangent,
        gain_rows,
        base_rows(rel_bias[1], DEC, False),
        dec_segments,
        enc_segments,
        memory,
        w2,
    )
    grad_enc, tile_one, enc_gains, near_sums, far_sums = enc_backward(
        wide,
        enc_input,
        enc_cotangent,
        cot_other,
        gain_rows,
        part_own,
        part_other,
        (w1, n0, qkv, context, inverse, weights, e1, n1, slope, active, ef),
    )
    column = side * heads_local
    bias_local = jnp.stack([near_table_grad(near_sums, far_sums), table_grad(off_sums, DEC, False)])
    bias_full = lax.dynamic_update_slice(jnp.zeros((2, NB, H), jnp.float32), bias_local, (0, 0, column))
    gain_local = enc_gains + dec_gains
    model = gain_local.shape[1]
    sums = sum_all(wide, jnp.concatenate([gain_local[:6], bias_full.reshape(-1, model), gain_local[6:7]]))
    bias_grad = lax.dynamic_slice(sums[6:7].reshape(2, NB, H), (0, 0, column), (2, NB, heads_local))
    tile_one, tile_two = tile_one.astype(jnp.float32), tile_two.astype(jnp.float32)
    layers = (tile_one[:, : 4 * width], tile_two[:, : 4 * width], tile_two[:, 4 * width : 8 * width])
    feeds = (tile_one[:, 4 * width :], tile_two[:, 8 * width :])
    return (
        lax.dynamic_slice_in_dim(ef, side * half, half).astype(jnp.bfloat16),
        dec_output,
        grad_enc,
        grad_dec,
        jnp.stack([layer[:, :width] for layer in layers]),
        jnp.stack([jnp.stack([layer[:, width : 2 * width], layer[:, 2 * width : 3 * width]]) for layer in layers]),
        jnp.stack([layer[:, 3 * width :].T for layer in layers]),
        jnp.stack([feed[:, :ffn] for feed in feeds]),
        jnp.stack([feed[:, ffn:].T for feed in feeds]),
        sums[:6],
        bias_grad,
    )


def ffn_backward(grad_rows, normed_rows, hidden, active, weight_up, weight_down):
    grad_active = jnp.einsum(
        "rd,fd->rf", grad_rows, weight_down, preferred_element_type=jnp.float32
    )
    grad_down = jnp.einsum("rf,rd->fd", active, grad_rows, preferred_element_type=jnp.float32)
    unused, pull = jax.vjp(gelu_tanh, hidden)
    grad_hidden = pull(grad_active)[0].astype(jnp.bfloat16)
    grad_up = jnp.einsum("rd,rf->df", normed_rows, grad_hidden, preferred_element_type=jnp.float32)
    grad_normed = jnp.einsum(
        "rf,df->rd", grad_hidden, weight_up, preferred_element_type=jnp.float32
    )
    return (grad_normed, grad_up, grad_down)


def norm_backward(values, gain, grad_normed):
    unused, pull = jax.vjp(rms_norm, values, gain)
    return pull(grad_normed)


def on_device_general(
    enc_input,
    dec_input,
    enc_lengths,
    dec_lengths,
    attn_query,
    attn_kv,
    attn_out,
    ffn_up,
    ffn_down,
    gains,
    rel_bias,
    enc_cotangent,
    dec_cotangent,
):
    weights = (
        lax.all_gather(attn_query, "wide", axis=1, tiled=True),
        lax.all_gather(attn_kv, "wide", axis=2, tiled=True),
        lax.all_gather(attn_out, "wide", axis=2, tiled=True),
        lax.all_gather(ffn_up, "wide", axis=1, tiled=True),
        lax.all_gather(ffn_down, "wide", axis=2, tiled=True),
    )
    gain_rows = gains.astype(jnp.float32)
    heads_local = rel_bias.shape[2]
    enc_segments = segment_ids(enc_lengths[0], ENC)
    dec_segments = segment_ids(dec_lengths[0], DEC)

    side = lax.axis_index("narrow")
    swap = [(0, 1), (1, 0)]

    def spread_rows(values):
        own = values.astype(jnp.bfloat16)
        other = lax.ppermute(own, "narrow", swap)
        return jnp.where(side == 0, jnp.concatenate([own, other]), jnp.concatenate([other, own]))

    def collect_rows(parts):
        half = parts.shape[0] // 2
        parts = parts.astype(jnp.bfloat16)
        other = lax.ppermute(lax.dynamic_slice_in_dim(parts, (1 - side) * half, half), "narrow", swap)
        own = lax.dynamic_slice_in_dim(parts, side * half, half)
        return own.astype(jnp.float32) + other.astype(jnp.float32)

    def attention_layer(normed_query, normed_keys, layer, base, query_segments, key_segments, causal):
        query = jnp.dot(normed_query, weights[0][layer], preferred_element_type=jnp.float32).astype(jnp.bfloat16)
        keys = jnp.dot(normed_keys, weights[1][layer, 0], preferred_element_type=jnp.float32).astype(jnp.bfloat16)
        values = jnp.dot(normed_keys, weights[1][layer, 1], preferred_element_type=jnp.float32).astype(jnp.bfloat16)
        saved = attend_forward(query, keys, values, base, query_segments, key_segments, causal)
        parts = jnp.dot(saved[1], weights[2][layer], preferred_element_type=jnp.float32)
        return ((query, keys, values, saved), collect_rows(parts))

    enc_start = enc_input.astype(jnp.float32)
    rows_a = spread_rows(rms_norm(enc_start, gain_rows[0]))
    kept_a, branch = attention_layer(
        rows_a, rows_a, 0, base_rows(rel_bias[0], ENC, True), enc_segments, enc_segments, False
    )
    enc_mid = enc_start + branch
    rows_b = spread_rows(rms_norm(enc_mid, gain_rows[1]))
    hidden_b = jnp.dot(rows_b, weights[3][0], preferred_element_type=jnp.float32)
    active_b = gelu_tanh(hidden_b).astype(jnp.bfloat16)
    enc_final = enc_mid + collect_rows(
        jnp.dot(active_b, weights[4][0], preferred_element_type=jnp.float32)
    )
    memory = spread_rows(rms_norm(enc_final, gain_rows[5]))
    dec_start = dec_input.astype(jnp.float32)
    rows_c = spread_rows(rms_norm(dec_start, gain_rows[2]))
    kept_c, branch = attention_layer(
        rows_c, rows_c, 1, base_rows(rel_bias[1], DEC, False), dec_segments, dec_segments, True
    )
    dec_one = dec_start + branch
    rows_d = spread_rows(rms_norm(dec_one, gain_rows[3]))
    kept_d, branch = attention_layer(
        rows_d, memory, 2, None, dec_segments, enc_segments, False
    )
    dec_two = dec_one + branch
    rows_e = spread_rows(rms_norm(dec_two, gain_rows[4]))
    hidden_e = jnp.dot(rows_e, weights[3][1], preferred_element_type=jnp.float32)
    active_e = gelu_tanh(hidden_e).astype(jnp.bfloat16)
    dec_final = dec_two + collect_rows(
        jnp.dot(active_e, weights[4][1], preferred_element_type=jnp.float32)
    )
    def attention_back(grad_state, kept, normed_query, normed_keys, layer, span, two_sided):
        grad_rows = spread_rows(grad_state)
        query, keys, values, saved = kept
        grad_context = dot_nt(grad_rows, weights[2][layer]).astype(jnp.bfloat16)
        grad_out = dot_tn(saved[1], grad_rows)
        result = attend_backward(query, keys, values, saved, grad_context, span > 0)
        grad_q, grad_k, grad_v = result[:3]
        sums = [
            dot_tn(normed_query, grad_q),
            dot_tn(normed_keys, grad_k),
            dot_tn(normed_keys, grad_v),
            grad_out,
            table_grad(result[3], span, two_sided) if span else None,
        ]
        query_part = dot_nt(grad_q, weights[0][layer])
        key_part = dot_nt(grad_k, weights[1][layer, 0]) + dot_nt(grad_v, weights[1][layer, 1])
        return (query_part, key_part, sums)

    grad_dec = dec_cotangent.astype(jnp.float32)
    grad_normed, up_e, down_e = ffn_backward(
        spread_rows(grad_dec), rows_e, hidden_e, active_e, weights[3][1], weights[4][1]
    )
    grad_back, gain_e = norm_backward(dec_two, gain_rows[4], collect_rows(grad_normed))
    grad_dec = grad_dec + grad_back
    query_part, memory_part, sums_d = attention_back(
        grad_dec, kept_d, rows_d, memory, 2, 0, False
    )
    grad_normed, grad_memory = collect_rows(query_part), collect_rows(memory_part)
    grad_back, gain_d = norm_backward(dec_one, gain_rows[3], grad_normed)
    grad_dec = grad_dec + grad_back
    query_part, key_part, sums_c = attention_back(
        grad_dec, kept_c, rows_c, rows_c, 1, DEC, False
    )
    grad_back, gain_c = norm_backward(dec_start, gain_rows[2], collect_rows(query_part + key_part))
    grad_dec = grad_dec + grad_back
    grad_enc = enc_cotangent.astype(jnp.float32)
    grad_back, gain_m = norm_backward(enc_final, gain_rows[5], grad_memory)
    grad_enc = grad_enc + grad_back
    grad_normed, up_b, down_b = ffn_backward(
        spread_rows(grad_enc), rows_b, hidden_b, active_b, weights[3][0], weights[4][0]
    )
    grad_back, gain_b = norm_backward(enc_mid, gain_rows[1], collect_rows(grad_normed))
    grad_enc = grad_enc + grad_back
    query_part, key_part, sums_a = attention_back(
        grad_enc, kept_a, rows_a, rows_a, 0, ENC, True
    )
    grad_back, gain_a = norm_backward(enc_start, gain_rows[0], collect_rows(query_part + key_part))
    grad_enc = grad_enc + grad_back
    grad_query = jnp.stack([sums_a[0], sums_c[0], sums_d[0]])
    grad_kv = jnp.stack(
        [
            jnp.stack([sums_a[1], sums_a[2]]),
            jnp.stack([sums_c[1], sums_c[2]]),
            jnp.stack([sums_d[1], sums_d[2]]),
        ]
    )
    grad_out = jnp.stack([sums_a[3], sums_c[3], sums_d[3]])
    grad_up = jnp.stack([up_b, up_e])
    grad_down = jnp.stack([down_b, down_e])
    tiles = (
        lax.psum_scatter(
            grad_query.astype(jnp.bfloat16), "wide", scatter_dimension=1, tiled=True
        ).astype(jnp.float32),
        lax.psum_scatter(
            grad_kv.astype(jnp.bfloat16), "wide", scatter_dimension=2, tiled=True
        ).astype(jnp.float32),
        lax.psum_scatter(
            grad_out.astype(jnp.bfloat16), "wide", scatter_dimension=2, tiled=True
        ).astype(jnp.float32),
        lax.psum_scatter(
            grad_up.astype(jnp.bfloat16), "wide", scatter_dimension=1, tiled=True
        ).astype(jnp.float32),
        lax.psum_scatter(
            grad_down.astype(jnp.bfloat16), "wide", scatter_dimension=2, tiled=True
        ).astype(jnp.float32),
    )
    tiles = (
        lax.psum(tiles[0].astype(jnp.bfloat16), "dp").astype(jnp.float32),
        lax.psum(tiles[1].astype(jnp.bfloat16), "dp").astype(jnp.float32),
        lax.psum(tiles[2].astype(jnp.bfloat16), "dp").astype(jnp.float32),
        lax.psum(tiles[3].astype(jnp.bfloat16), "dp").astype(jnp.float32),
        lax.psum(tiles[4].astype(jnp.bfloat16), "dp").astype(jnp.float32),
    )
    gain_grads = jnp.stack([gain_a, gain_b, gain_c, gain_d, gain_e, gain_m])
    column = lax.axis_index("narrow") * heads_local
    bias_local = jnp.stack([sums_a[4], sums_c[4]])
    bias_full = lax.dynamic_update_slice(
        jnp.zeros((2, NB, H), jnp.float32), bias_local, (0, 0, column)
    )
    gain_total, bias_total = lax.psum((gain_grads, bias_full), ("dp", "wide", "narrow"))
    bias_grad = lax.dynamic_slice(bias_total, (0, 0, column), (2, NB, heads_local))
    return (
        enc_final.astype(jnp.bfloat16),
        dec_final.astype(jnp.bfloat16),
        grad_enc,
        grad_dec,
        tiles[0],
        tiles[1],
        tiles[2],
        tiles[3],
        tiles[4],
        gain_total,
        bias_grad,
    )


def solution(mesh):
    wide = mesh.shape["wide"]

    def body(*args):
        if args[4].shape[1] % 16 or wide % 2:
            return on_device_general(*args)
        return on_device(wide, *args)

    return jax.shard_map(
        body,
        mesh=mesh,
        in_specs=(
            P(("dp", "wide", "narrow"), None),
            P(("dp", "wide", "narrow"), None),
            P(("dp", "wide"), None),
            P(("dp", "wide"), None),
            P(None, "wide", "narrow"),
            P(None, None, "wide", "narrow"),
            P(None, "narrow", "wide"),
            P(None, "wide", "narrow"),
            P(None, "narrow", "wide"),
            P(),
            P(None, None, "narrow"),
            P(("dp", "wide", "narrow"), None),
            P(("dp", "wide", "narrow"), None),
        ),
        out_specs=(
            P(("dp", "wide", "narrow"), None),
            P(("dp", "wide", "narrow"), None),
            P(("dp", "wide", "narrow"), None),
            P(("dp", "wide", "narrow"), None),
            P(None, "wide", "narrow"),
            P(None, None, "wide", "narrow"),
            P(None, "narrow", "wide"),
            P(None, "wide", "narrow"),
            P(None, "narrow", "wide"),
            P(),
            P(None, None, "narrow"),
        ),
        check_vma=False,
    )
```

```python
import functools
import math

import jax
import jax.numpy as jnp
from jax import lax
from jax.sharding import PartitionSpec as P
import jax.experimental.pallas as pl
import jax.experimental.pallas.tpu as pltpu

H = 12
DK = 64
NB = 32
MAXD = 128
ENC = 1024
DEC = 256


EPS = 1e-06
NEG = -1e30
HIGH = lax.Precision.HIGHEST
VMEM_BYTES = 62 * 2**20
GELU_A = math.sqrt(2.0 / math.pi)
GELU_B = 0.044715


def cutoffs(exact, buckets):
    found = []
    reach = exact
    for target in range(exact + 1, buckets):
        while (
            exact + math.floor(math.log(reach / exact) / math.log(MAXD / exact) * (buckets - exact))
            < target
        ):
            reach = reach + 1
        found.append(reach)
    return found


def bucket_index(relative, two_sided):
    if two_sided:
        width = NB // 2
        offset = jnp.where(relative > 0, width, 0)
        distance = jnp.abs(relative)
    else:
        width = NB
        offset = jnp.zeros_like(relative)
        distance = jnp.maximum(-relative, 0)
    exact = width // 2
    beyond = exact + sum(((distance >= limit).astype(jnp.int32) for limit in cutoffs(exact, width)))
    return offset + jnp.where(distance < exact, distance, beyond)


def segment_ids(lengths, count):
    bounds = jnp.cumsum(lengths)
    places = jnp.arange(count, dtype=jnp.int32)
    return jnp.sum((places[:, None] >= bounds[None, :]).astype(jnp.int32), axis=1)


def rms_norm(values, gain):
    return values * lax.rsqrt(jnp.mean(values * values, axis=-1, keepdims=True) + EPS) * gain


def gelu_tanh(values):
    return jax.nn.gelu(values, approximate=True)


PAIR = 128


def offset_buckets(span, two_sided):
    places = jnp.arange(2 * span, dtype=jnp.int32)[None, :]
    relative = lax.rem(places - jnp.arange(8, dtype=jnp.int32)[:, None] + 2 * span, 2 * span) - span
    buckets = bucket_index(relative.reshape(-1), two_sided)
    return (buckets[None, :] == jnp.arange(NB, dtype=jnp.int32)[:, None]).astype(jnp.bfloat16)


def base_rows(table, span, two_sided):
    heads = table.shape[1]
    rows = lax.dot_general(
        table, offset_buckets(span, two_sided), (((0,), (0,)), ((), ())), preferred_element_type=jnp.float32
    )
    return rows.reshape(heads // 2, 2, 8, 2 * span)


def table_grad(offset_sums, span, two_sided):
    heads = 2 * offset_sums.shape[0]
    return lax.dot_general(
        offset_buckets(span, two_sided).astype(jnp.float32),
        offset_sums.reshape(heads, 16 * span),
        (((1,), (1,)), ((), ())),
        precision=HIGH,
        preferred_element_type=jnp.float32,
    )


def dot_nt(a, b):
    return lax.dot_general(a, b, (((1,), (1,)), ((), ())), preferred_element_type=jnp.float32)


def dot_tn(a, b):
    return lax.dot_general(a, b, (((0,), (0,)), ((), ())), preferred_element_type=jnp.float32)


def dot_nn(a, b):
    return lax.dot_general(a, b, (((1,), (0,)), ((), ())), preferred_element_type=jnp.float32)


def split_heads(block):
    lane = lax.broadcasted_iota(jnp.int32, block.shape, 1)
    zero = jnp.zeros_like(block)
    return jnp.where(lane < DK, block, zero), jnp.where(lane < DK, zero, block)


def attend_kernel(block, keys_count, causal, biased, *refs):
    if biased:
        qseg, kseg, base, q_ref, k_ref, v_ref, e_ref, c_ref, inv_ref, strip = refs
    else:
        qseg, kseg, q_ref, k_ref, v_ref, e_ref, c_ref, inv_ref = refs
    i = pl.program_id(1)
    if biased:
        wide = 2 * keys_count

        @pl.when(i == 0)
        def _():
            for head in range(2):
                rows = base[0, head]
                for a in range(block // 8):
                    strip[head, 8 * a : 8 * a + 8, :] = pltpu.roll(rows, (8 * a + wide - block) % wide, 1)

    allowed = qseg[...] == kseg[...]
    if causal:
        rows = lax.broadcasted_iota(jnp.int32, (block, keys_count), 0) + i * block
        allowed = allowed & (lax.broadcasted_iota(jnp.int32, (block, keys_count), 1) <= rows)
    q_heads = split_heads(q_ref[...])
    v_heads = split_heads(v_ref[...])
    inverses = []
    context = None
    for head in range(2):
        scores = dot_nt(q_heads[head], k_ref[...])
        if biased:
            start = pl.multiple_of((keys_count // block - 1 - i) * block, block)
            scores = scores + strip[head, :, pl.ds(start, keys_count)]
        scores = jnp.where(allowed, scores, NEG)
        highest = jnp.max(scores, axis=1, keepdims=True)
        weights = jnp.exp(scores - highest)
        inverses.append(1.0 / jnp.sum(weights, axis=1, keepdims=True))
        weights = weights.astype(jnp.bfloat16)
        e_ref[head] = weights
        part = dot_nn(weights, v_heads[head])
        context = part if context is None else context + part
    lane = lax.broadcasted_iota(jnp.int32, (block, PAIR), 1)
    inverse = jnp.where(lane < DK, inverses[0], inverses[1])
    inv_ref[...] = inverse
    c_ref[...] = (context * inverse).astype(jnp.bfloat16)


def attend_back_kernel(block, keys_count, steps, biased, *refs):
    if biased:
        q_ref, k_ref, v_ref, e_ref, c_ref, inv_ref, gc_ref, gq_ref, gk_ref, gv_ref, off_ref, gk_sum, gv_sum, strip = refs
    else:
        q_ref, k_ref, v_ref, e_ref, c_ref, inv_ref, gc_ref, gq_ref, gk_ref, gv_ref, gk_sum, gv_sum = refs
    i = pl.program_id(1)

    @pl.when(i == 0)
    def _():
        gk_sum[...] = jnp.zeros_like(gk_sum)
        gv_sum[...] = jnp.zeros_like(gv_sum)
        if biased:
            strip[...] = jnp.zeros_like(strip)

    scaled = (gc_ref[...].astype(jnp.float32) * inv_ref[...]).astype(jnp.bfloat16)
    product = scaled.astype(jnp.float32) * c_ref[...].astype(jnp.float32)
    lane = lax.broadcasted_iota(jnp.int32, (block, PAIR), 1)
    inner = (
        jnp.sum(jnp.where(lane < DK, product, 0.0), axis=1, keepdims=True),
        jnp.sum(jnp.where(lane < DK, 0.0, product), axis=1, keepdims=True),
    )
    g_heads = split_heads(scaled)
    q_heads = split_heads(q_ref[...])
    k_heads = split_heads(k_ref[...])
    gq = None
    for head in range(2):
        weights = e_ref[head]
        grad = dot_nt(g_heads[head], v_ref[...])
        grad = weights.astype(jnp.float32) * (grad - inner[head])
        if biased:
            start = pl.multiple_of((keys_count // block - 1 - i) * block, block)
            strip[head, :, pl.ds(start, keys_count)] += grad
        grad = grad.astype(jnp.bfloat16)
        part = dot_nn(grad, k_heads[head])
        gq = part if gq is None else gq + part
        gk_sum[...] += dot_tn(grad, q_heads[head])
        gv_sum[...] += dot_tn(weights, g_heads[head])
    gq_ref[...] = gq.astype(jnp.bfloat16)

    @pl.when(i == steps - 1)
    def _():
        gk_ref[...] = gk_sum[...].astype(jnp.bfloat16)
        gv_ref[...] = gv_sum[...].astype(jnp.bfloat16)
        if biased:
            wide = 2 * keys_count
            for head in range(2):
                total = jnp.zeros((8, wide), jnp.float32)
                for a in range(block // 8):
                    total = total + pltpu.roll(strip[head, 8 * a : 8 * a + 8, :], (block - 8 * a) % wide, 1)
                off_ref[0, head] = total


def attend_forward(query, keys, values, base, query_segments, key_segments, causal):
    count, cols = query.shape[0], keys.shape[0]
    pairs = query.shape[1] // PAIR
    block = min(256, count)
    steps = count // block
    row_spec = pl.BlockSpec((block, PAIR), lambda h, i: (i, h))
    key_spec = pl.BlockSpec((cols, PAIR), lambda h, i: (0, h))
    in_specs = [
        pl.BlockSpec((block, 1), lambda h, i: (i, 0)),
        pl.BlockSpec((1, cols), lambda h, i: (0, 0)),
    ]
    args = [query_segments[:, None], key_segments[None, :]]
    scratch = []
    if base is not None:
        in_specs.append(pl.BlockSpec((1, 2, 8, 2 * cols), lambda h, i: (h, 0, 0, 0)))
        args.append(base)
        scratch.append(pltpu.VMEM((2, block, 2 * cols), jnp.float32))
    return pl.pallas_call(
        functools.partial(attend_kernel, block, cols, causal, base is not None),
        grid=(pairs, steps),
        in_specs=in_specs + [row_spec, key_spec, key_spec],
        out_specs=[
            pl.BlockSpec((2, block, cols), lambda h, i: (h, i, 0)),
            row_spec,
            row_spec,
        ],
        out_shape=[
            jax.ShapeDtypeStruct((2 * pairs, count, cols), jnp.bfloat16),
            jax.ShapeDtypeStruct((count, pairs * PAIR), jnp.bfloat16),
            jax.ShapeDtypeStruct((count, pairs * PAIR), jnp.float32),
        ],
        scratch_shapes=scratch,
        compiler_params=pltpu.CompilerParams(vmem_limit_bytes=VMEM_BYTES),
        cost_estimate=pl.CostEstimate(
            flops=4 * count * cols * PAIR * 2 * pairs, bytes_accessed=2 * pairs * count * cols * 2, transcendentals=0
        ),
    )(*args, query, keys, values)


def attend_backward(query, keys, values, saved, grad_context, biased):
    weights, context, inverse = saved
    count, cols = query.shape[0], keys.shape[0]
    pairs = query.shape[1] // PAIR
    block = min(256, count)
    steps = count // block
    row_spec = pl.BlockSpec((block, PAIR), lambda h, i: (i, h))
    key_spec = pl.BlockSpec((cols, PAIR), lambda h, i: (0, h))
    out_specs = [row_spec, key_spec, key_spec]
    out_shape = [
        jax.ShapeDtypeStruct((count, pairs * PAIR), jnp.bfloat16),
        jax.ShapeDtypeStruct((cols, pairs * PAIR), jnp.bfloat16),
        jax.ShapeDtypeStruct((cols, pairs * PAIR), jnp.bfloat16),
    ]
    scratch = [pltpu.VMEM((cols, PAIR), jnp.float32), pltpu.VMEM((cols, PAIR), jnp.float32)]
    if biased:
        out_specs.append(pl.BlockSpec((1, 2, 8, 2 * cols), lambda h, i: (h, 0, 0, 0)))
        out_shape.append(jax.ShapeDtypeStruct((pairs, 2, 8, 2 * cols), jnp.float32))
        scratch.append(pltpu.VMEM((2, block, 2 * cols), jnp.float32))
    return pl.pallas_call(
        functools.partial(attend_back_kernel, block, cols, steps, biased),
        grid=(pairs, steps),
        in_specs=[
            row_spec,
            key_spec,
            key_spec,
            pl.BlockSpec((2, block, cols), lambda h, i: (h, i, 0)),
            row_spec,
            row_spec,
            row_spec,
        ],
        out_specs=out_specs,
        out_shape=out_shape,
        scratch_shapes=scratch,
        compiler_params=pltpu.CompilerParams(vmem_limit_bytes=VMEM_BYTES),
        cost_estimate=pl.CostEstimate(
            flops=8 * count * cols * PAIR * 2 * pairs, bytes_accessed=2 * pairs * count * cols * 2, transcendentals=0
        ),
    )(query, keys, values, weights, context, inverse, grad_context)


MESH_IDS = pl.DeviceIdType.MESH
CHUNK = 256
ATT = 4 * 384


def any_spec():
    return pl.BlockSpec(memory_space=pl.ANY)


def vmem_spec():
    return pl.BlockSpec(memory_space=pltpu.VMEM)


def normed(values, gain):
    return values * lax.rsqrt(jnp.mean(values * values, axis=1, keepdims=True) + EPS) * gain


def gelu_pair(values):
    square = values * values
    inner = jnp.tanh(GELU_A * values * (1.0 + GELU_B * square))
    half = 0.5 * (1.0 + inner)
    slope = half + 0.5 * values * (1.0 - inner * inner) * (GELU_A * (1.0 + 3.0 * GELU_B * square))
    return values * half, slope


class Place:
    def __init__(self, wide):
        self.core = lax.axis_index("dp")
        self.wide = lax.axis_index("wide")
        self.side = lax.axis_index("narrow")
        self.count = wide
        self.fars = wide // 2
        self.far = self.wide // 2
        self.near = self.wide % 2

    def sibling(self):
        return (1 - self.core, self.wide, self.side)

    def across(self):
        return (self.core, self.wide, 1 - self.side)

    def beside(self):
        return (self.core, 2 * self.far + 1 - self.near, self.side)

    def along(self, step):
        return (self.core, 2 * lax.rem(self.far + step, self.fars) + self.near, self.side)

    def index_from(self, step):
        return 2 * lax.rem(self.far - step + self.fars, self.fars) + self.near

    def index_beside(self, step):
        return 2 * lax.rem(self.far - step + self.fars, self.fars) + 1 - self.near

    def greet(self):
        partners = [self.sibling(), self.across(), self.beside()]
        partners += [self.along(step) for step in range(1, self.fars)]
        barrier = pltpu.get_barrier_semaphore()
        for partner in partners:
            pl.semaphore_signal(barrier, inc=1, device_id=partner, device_id_type=MESH_IDS)
        pl.semaphore_wait(barrier, len(partners))


def remote(source, target, send, receive, partner):
    return pltpu.make_async_remote_copy(
        src_ref=source,
        dst_ref=target,
        send_sem=send,
        recv_sem=receive,
        device_id=partner,
        device_id_type=MESH_IDS,
    )


class Gather:
    def __init__(self, place, pack, groups, send, receive, local):
        self.place, self.pack, self.groups = place, pack, groups
        self.send, self.receive, self.local = send, receive, local
        self.rows = pack.shape[0]
        self.sent = []

    def at(self, group, index, core):
        first, width, target, offset = self.groups[group]
        half = width // 2
        start = pl.multiple_of(offset + core * half, 128)
        return target.at[pl.ds(pl.multiple_of(index * self.rows, 16), self.rows), pl.ds(start, half)]

    def own(self, group):
        first, width, target, offset = self.groups[group]
        half = width // 2
        return self.pack.at[:, pl.ds(pl.multiple_of(first + self.place.core * half, 128), half)]

    def local_copy(self, group):
        first, width, target, offset = self.groups[group]
        rows = pl.ds(pl.multiple_of(self.place.wide * self.rows, 16), self.rows)
        return pltpu.make_async_copy(
            self.pack.at[:, pl.ds(first, width)], target.at[rows, pl.ds(offset, width)], self.local.at[group]
        )

    def push(self, group, slot, source, index, partner):
        copy = remote(
            source,
            self.at(group, index, self.place.core),
            self.send.at[group, slot],
            self.receive.at[group, slot],
            partner,
        )
        copy.start()
        self.sent.append(copy)

    def await_slot(self, group, slot, index, core):
        block = self.at(group, index, core)
        remote(block, block, self.send.at[group, slot], self.receive.at[group, slot], self.place.sibling()).wait_recv()

    def start(self, group):
        place, fars = self.place, self.place.fars
        for step in range(1, fars):
            self.push(group, step - 1, self.own(group), place.wide, place.along(step))
        self.push(group, fars - 1, self.own(group), place.wide, place.beside())
        self.local_copy(group).start()

    def relay_along(self, group):
        place, fars = self.place, self.place.fars
        for step in range(1, fars):
            index = place.index_from(step)
            self.await_slot(group, step - 1, index, place.core)
            block = self.at(group, index, place.core)
            self.push(group, fars - 1 + step, block, index, place.beside())
            self.push(group, 2 * fars - 2 + step, block, index, place.sibling())

    def relay_beside(self, group):
        place, fars = self.place, self.place.fars
        for step in range(fars):
            index = place.index_beside(step)
            self.await_slot(group, fars - 1 + step, index, place.core)
            block = self.at(group, index, place.core)
            self.push(group, 3 * fars - 2 + step, block, index, place.sibling())

    def finish(self, group):
        place, fars = self.place, self.place.fars
        for step in range(1, fars):
            self.await_slot(group, 2 * fars - 2 + step, place.index_from(step), 1 - place.core)
        for step in range(fars):
            self.await_slot(group, 3 * fars - 2 + step, place.index_beside(step), 1 - place.core)
        self.local_copy(group).wait()

    def close(self):
        for copy in self.sent:
            copy.wait_send()


def gather_slots(wide):
    return 4 * (wide // 2) - 2


def softmax_pair(q_pair, k_pair, v_pair, allowed, biases, e_store):
    q_heads = split_heads(q_pair)
    v_heads = split_heads(v_pair)
    inverses = []
    context = None
    for head in range(2):
        scores = dot_nt(q_heads[head], k_pair)
        if biases is not None:
            scores = scores + biases(head)
        scores = jnp.where(allowed, scores, NEG)
        highest = jnp.max(scores, axis=1, keepdims=True)
        weights = jnp.exp(scores - highest)
        inverses.append(1.0 / jnp.sum(weights, axis=1, keepdims=True))
        weights = weights.astype(jnp.bfloat16)
        e_store(head, weights)
        part = dot_nn(weights, v_heads[head])
        context = part if context is None else context + part
    lane = lax.broadcasted_iota(jnp.int32, context.shape, 1)
    inverse = jnp.where(lane < DK, inverses[0], inverses[1])
    return inverse, (context * inverse).astype(jnp.bfloat16)


def build_strip(strip, base, pairs, block, span):
    def one(pair, carry):
        for head in range(2):
            rows = base[pair, head]
            for a in range(block // 8):
                strip[2 * pair + head, 8 * a : 8 * a + 8, :] = pltpu.roll(rows, (8 * a + 2 * span - block) % (2 * span), 1)
        return carry

    lax.fori_loop(0, pairs, one, 0)


NEAR = 2 * CHUNK
EDGE = NEAR // 4


def near_buckets():
    places = jnp.arange(2 * NEAR, dtype=jnp.int32)[None, :]
    relative = places - jnp.arange(8, dtype=jnp.int32)[:, None] - CHUNK - EDGE
    buckets = bucket_index(relative.reshape(-1), True)
    return (buckets[None, :] == jnp.arange(NB, dtype=jnp.int32)[:, None]).astype(jnp.bfloat16)


def near_rows(table):
    rows = lax.dot_general(
        table, near_buckets(), (((0,), (0,)), ((), ())), preferred_element_type=jnp.float32
    )
    return rows.reshape(table.shape[1] // 2, 2, 8, 2 * NEAR)


def build_near(strip, base, pairs):
    def one(pair, carry):
        for head in range(2):
            rows = base[pair, head]
            for a in range(CHUNK // 8):
                turned = pltpu.roll(rows, (2 * NEAR - CHUNK + 8 * a) % (2 * NEAR), 1)
                strip[2 * pair + head, 8 * a : 8 * a + 8, :] = turned[:, :NEAR]
        return carry

    lax.fori_loop(0, pairs, one, 0)


def near_window(i, rows):
    low, high = max(i * CHUNK - EDGE, 0), min(i * CHUNK + CHUNK + EDGE, rows)
    return low, high, low - (i * CHUNK - EDGE)


def near_bias(strip, base, pair, head, i, rows):
    low, high, shift = near_window(i, rows)
    parts = [strip[2 * pair + head, :, shift : shift + high - low]]
    if low > 0:
        parts.insert(0, jnp.broadcast_to(base[pair, head, 0:1, 0:1], (CHUNK, low)))
    if high < rows:
        parts.append(jnp.broadcast_to(base[pair, head, 0:1, 2 * NEAR - 1 : 2 * NEAR], (CHUNK, rows - high)))
    return jnp.concatenate(parts, axis=1)


def enc_forward_kernel(
    wide,
    x_own,
    dec_own,
    dcot_own,
    query_in,
    kv_in,
    out_in,
    up_in,
    down_in,
    gains,
    base,
    qseg,
    kseg,
    w1_all,
    w2,
    n0_all,
    qkv_all,
    c_all,
    inv_all,
    e_all,
    e1_all,
    n1_all,
    slope_all,
    a_all,
    ef_all,
    mem_all,
    dec_other,
    dcot_other,
    pack,
    w1,
    n0,
    qkv,
    c,
    inv,
    e1,
    n1,
    ef,
    mem,
    x_full,
    strip,
    e_buf,
    slope_buf,
    a_buf,
    y_send,
    y_recv,
    g_send,
    g_recv,
    g_local,
    x_sems,
    y_sems,
    z_sems,
    l_sems,
    p_sems,
    o_sems,
):
    place = Place(wide)
    side = place.side
    half = x_own.shape[0]
    rows = 2 * half
    steps = rows // CHUNK
    width = c.shape[1]
    ffn = up_in.shape[2]
    pairs = width // PAIR
    pieces = []
    for layer in range(3):
        first = (0, 4 * width + 2 * ffn, 8 * width + 2 * ffn)[layer]
        pieces += [(query_in.at[layer], first), (kv_in.at[layer, 0], first + width)]
        pieces += [(kv_in.at[layer, 1], first + 2 * width), (out_in.at[layer], first + 3 * width)]
    pieces += [(up_in.at[0], 4 * width), (down_in.at[0], 4 * width + ffn), (up_in.at[1], 12 * width + 2 * ffn)]
    packs = [
        pltpu.make_async_copy(piece, pack.at[:, pl.ds(first, piece.shape[1])], p_sems.at[index])
        for index, (piece, first) in enumerate(pieces)
    ]
    for copy in packs:
        copy.start()
    place.greet()
    gather = Gather(
        place,
        pack,
        [
            (0, 4 * width, w1, 0),
            (4 * width, 2 * ffn, w1, 4 * width),
            (4 * width + 2 * ffn, 8 * width, w2, 0),
            (12 * width + 2 * ffn, ffn, w2, 8 * width),
        ],
        g_send,
        g_recv,
        g_local,
    )
    mine = pl.ds(pl.multiple_of(side * half, 16), half)
    swap_x = remote(x_own, x_full.at[mine], x_sems.at[0], x_sems.at[1], place.across())
    swap_x.start()
    for copy in packs:
        copy.wait()
    gather.start(0)
    keep_x = pltpu.make_async_copy(x_own, x_full.at[mine], l_sems.at[6])
    keep_x.start()
    build_near(strip, base, pairs)
    gather.relay_along(0)
    gather.start(1)
    keep_x.wait()
    gather.relay_beside(0)
    swap_x.wait()
    later = [
        remote(dec_own, dec_other, x_sems.at[2], x_sems.at[3], place.across()),
        remote(dcot_own, dcot_other, x_sems.at[4], x_sems.at[5], place.across()),
    ]
    for copy in later:
        copy.start()
    stores = []

    def store_out(source, target):
        stores.append(pltpu.make_async_copy(source, target, o_sems.at[len(stores)]))
        stores[-1].start()


    def norm_rows(i, carry):
        at = pl.ds(pl.multiple_of(i * CHUNK, CHUNK), CHUNK)
        n0[at, :] = normed(x_full[at, :].astype(jnp.float32), gains[0:1, :]).astype(jnp.bfloat16)
        return carry

    lax.fori_loop(0, steps, norm_rows, 0)
    gather.finish(0)

    def project(i, carry):
        at = pl.ds(pl.multiple_of(i * CHUNK, CHUNK), CHUNK)
        qkv[at, :] = dot_nn(n0[at, :], w1[:, : 3 * width]).astype(jnp.bfloat16)
        return carry

    lax.fori_loop(0, steps, project, 0)
    store_out(n0, n0_all)
    store_out(qkv, qkv_all)

    def lanes(base_lane, pair):
        return pl.ds(pl.multiple_of(base_lane + pair * PAIR, PAIR), PAIR)

    def save(i, kind):
        slot = i % 2
        at = pl.ds(i * CHUNK, CHUNK)
        if kind == 0:
            return pltpu.make_async_copy(e_buf.at[slot], e_all.at[:, at, :], l_sems.at[slot])
        if kind == 1:
            return pltpu.make_async_copy(slope_buf.at[slot], slope_all.at[at, :], l_sems.at[2 + slot])
        return pltpu.make_async_copy(a_buf.at[slot], a_all.at[at, :], l_sems.at[4 + slot])

    def swap_y(layer, i):
        at = pl.ds(i * CHUNK, CHUNK)
        sems = y_sems if layer == 0 else z_sems
        return remote(y_send.at[layer, at], y_recv.at[layer, at], sems.at[0, i], sems.at[1, i], place.across())

    def attend(i):
        at = pl.ds(i * CHUNK, CHUNK)
        slot = i % 2
        if i >= 2:
            save(i - 2, 0).wait()

        def one(pair, carry):
            allowed = qseg[at, :] == kseg[...]

            def bias(head):
                return near_bias(strip, base, pair, head, i, rows)

            def store(head, weights):
                e_buf[slot, 2 * pair + head] = weights

            inverse, context = softmax_pair(
                qkv[at, lanes(0, pair)],
                qkv[:, lanes(width, pair)],
                qkv[:, lanes(2 * width, pair)],
                allowed,
                bias,
                store,
            )
            inv[at, lanes(0, pair)] = inverse
            c[at, lanes(0, pair)] = context
            return carry

        lax.fori_loop(0, pairs, one, 0)
        save(i, 0).start()
        store_out(c.at[at], c_all.at[at])
        store_out(inv.at[at], inv_all.at[at])
        y_send[0, at, :] = dot_nt(c[at, :], w1[:, 3 * width : 4 * width]).astype(jnp.bfloat16)
        swap_y(0, i).start()

    def feed(i):
        at = pl.ds(i * CHUNK, CHUNK)
        slot = i % 2
        swap_y(0, i).wait_recv()
        both = y_send[0, at, :].astype(jnp.float32) + y_recv[0, at, :].astype(jnp.float32)
        middle = x_full[at, :].astype(jnp.float32) + both
        e1[at, :] = middle
        rounded = normed(middle, gains[1:2, :]).astype(jnp.bfloat16)
        n1[at, :] = rounded
        store_out(e1.at[at], e1_all.at[at])
        store_out(n1.at[at], n1_all.at[at])
        if i >= 2:
            save(i - 2, 1).wait()
            save(i - 2, 2).wait()

        def part(j, carry):
            cols = pl.ds(pl.multiple_of(4 * width + j * width, PAIR), width)
            here = pl.ds(pl.multiple_of(j * width, PAIR), width)
            active, slope = gelu_pair(dot_nn(n1[at, :], w1[:, cols]))
            a_buf[slot, :, here] = active.astype(jnp.bfloat16)
            slope_buf[slot, :, here] = slope.astype(jnp.bfloat16)
            return carry

        lax.fori_loop(0, ffn // width, part, 0)
        save(i, 1).start()
        save(i, 2).start()
        y_send[1, at, :] = dot_nt(a_buf[slot], w1[:, 4 * width + ffn :]).astype(jnp.bfloat16)
        swap_y(1, i).start()

    def last(i):
        at = pl.ds(i * CHUNK, CHUNK)
        swap_y(1, i).wait_recv()
        both = y_send[1, at, :].astype(jnp.float32) + y_recv[1, at, :].astype(jnp.float32)
        final = e1[at, :] + both
        ef[at, :] = final
        mem[at, :] = normed(final, gains[5:6, :]).astype(jnp.bfloat16)
        store_out(ef.at[at], ef_all.at[at])
        store_out(mem.at[at], mem_all.at[at])

    attend(0)
    gather.relay_along(1)
    gather.start(2)
    attend(1)
    gather.relay_beside(1)
    attend(2)
    gather.finish(1)
    store_out(w1, w1_all)
    feed(0)
    gather.relay_along(2)
    gather.start(3)
    attend(3)
    feed(1)
    gather.relay_beside(2)
    feed(2)
    gather.relay_along(3)
    feed(3)
    last(0)
    last(1)
    gather.relay_beside(3)
    last(2)
    last(3)
    gather.finish(2)
    gather.finish(3)
    gather.close()
    for copy in later:
        copy.wait()
    for copy in stores:
        copy.wait()
    for i in range(steps):
        swap_y(0, i).wait_send()
        swap_y(1, i).wait_send()
    for i in range(steps - 2, steps):
        for kind in range(3):
            save(i, kind).wait()


def enc_forward(wide, x_own, dec_own, dcot_own, weights, gains, base, segments):
    half, model = x_own.shape
    rows = 2 * half
    pairs = base.shape[0]
    width = pairs * PAIR
    ffn = weights[3].shape[2]
    bf, f32 = jnp.bfloat16, jnp.float32
    shape = jax.ShapeDtypeStruct
    dma = pltpu.SemaphoreType.DMA
    slots = gather_slots(wide)
    steps = rows // CHUNK
    saved = [
        ((model, 4 * width + 2 * ffn), bf),
        ((rows, model), bf),
        ((rows, 3 * width), bf),
        ((rows, width), bf),
        ((rows, width), f32),
        ((rows, model), f32),
        ((rows, model), bf),
        ((rows, model), f32),
        ((rows, model), bf),
    ]
    kept = [shape(*pair) for pair in saved]
    out_shape = (
        [kept[0], shape((model, 8 * width + ffn), bf)]
        + kept[1:5]
        + [shape((2 * pairs, rows, rows), bf)]
        + kept[5:7]
        + [shape((rows, ffn), bf), shape((rows, ffn), bf)]
        + kept[7:]
        + [shape(dec_own.shape, bf), shape(dcot_own.shape, bf)]
    )
    return pl.pallas_call(
        functools.partial(enc_forward_kernel, wide),
        in_specs=[vmem_spec()] + [any_spec()] * 7 + [vmem_spec()] * 4,
        out_shape=out_shape,
        out_specs=[any_spec()] * len(out_shape),
        scratch_shapes=[pltpu.VMEM((x_own.shape[1] // wide, 12 * width + 3 * ffn), bf)]
        + [pltpu.VMEM(*pair) for pair in saved]
        + [
            pltpu.VMEM((rows, model), bf),
            pltpu.VMEM((2 * pairs, CHUNK, NEAR), f32),
            pltpu.VMEM((2, 2 * pairs, CHUNK, rows), bf),
            pltpu.VMEM((2, CHUNK, ffn), bf),
            pltpu.VMEM((2, CHUNK, ffn), bf),
            pltpu.VMEM((2, rows, model), bf),
            pltpu.VMEM((2, rows, model), bf),
            dma((4, slots)),
            dma((4, slots)),
            dma((4,)),
            dma((6,)),
            dma((2, steps)),
            dma((2, steps)),
            dma((7,)),
            dma((15,)),
            dma((3 + 6 * steps,)),
        ],
        compiler_params=pltpu.CompilerParams(
            collective_id=0, has_side_effects=True, vmem_limit_bytes=VMEM_BYTES
        ),
        cost_estimate=pl.CostEstimate(flops=10**10, bytes_accessed=6 * 10**7, transcendentals=0),
    )(x_own, dec_own, dcot_own, *weights, gains, base, segments[:, None], segments[None, :])


def norm_back(values, gain, grad):
    scale = lax.rsqrt(jnp.mean(values * values, axis=1, keepdims=True) + EPS)
    scaled = grad * gain
    pulled = scale * (scaled - values * (scale * scale) * jnp.mean(scaled * values, axis=1, keepdims=True))
    return pulled, jnp.sum(grad * values * scale, axis=0, keepdims=True)


class Scatter:
    def __init__(self, place, rows, groups, tile, send, receive):
        self.place, self.rows, self.groups, self.tile = place, rows, groups, tile
        self.send, self.receive = send, receive
        self.sent = []

    def columns(self, group, core):
        first, width = self.groups[group]["first"], self.groups[group]["width"]
        return pl.ds(pl.multiple_of(first + core * (width // 2), 128), width // 2)

    def block(self, group, index):
        return self.groups[group]["grad"].at[
            pl.ds(pl.multiple_of(index * self.rows, 16), self.rows), self.columns(group, self.place.core)
        ]

    def push(self, group, slot, source, target, partner, arrival=None):
        arrival = slot if arrival is None else arrival
        copy = remote(source, target, self.send.at[group, slot], self.receive.at[group, arrival], partner)
        copy.start()
        self.sent.append(copy)

    def await_slot(self, group, slot, block):
        remote(block, block, self.send.at[group, 0], self.receive.at[group, slot], self.place.sibling()).wait_recv()

    def start(self, group):
        parts = self.groups[group]
        self.push(
            group, 0, parts["grad"].at[:, self.columns(group, 1 - self.place.core)], parts["core"], self.place.sibling()
        )

    def add_block(self, group, index, other):
        block = self.block(group, index)
        block[...] = (block[...].astype(jnp.float32) + other.astype(jnp.float32)).astype(jnp.bfloat16)
        return block

    def beside(self, group):
        parts, place = self.groups[group], self.place
        self.await_slot(group, 0, parts["core"])

        def received(index):
            return parts["core"][pl.ds(pl.multiple_of(index * self.rows, 16), self.rows), :]

        for step in range(place.fars):
            far = lax.rem(place.far + 1 + step, place.fars)
            index = 2 * far + 1 - place.near
            block = self.add_block(group, index, received(index))
            self.push(group, 1 + step, block, parts["beside"].at[step], place.beside())
        for step in range(place.fars):
            far = lax.rem(place.far + 1 + step, place.fars)
            index = 2 * far + place.near
            self.add_block(group, index, received(index))

    def along(self, group):
        parts, place = self.groups[group], self.place
        for step in range(1, place.fars):
            index = 2 * lax.rem(place.far + step, place.fars) + place.near
            self.await_slot(group, step, parts["beside"].at[step - 1])
            block = self.add_block(group, index, parts["beside"][step - 1])
            self.push(group, place.fars + step, block, parts["along"].at[step - 1], place.along(step))

    def total(self, group):
        parts, place = self.groups[group], self.place
        self.await_slot(group, place.fars, parts["beside"].at[place.fars - 1])
        value = self.block(group, place.wide)[...].astype(jnp.float32) + parts["beside"][place.fars - 1].astype(jnp.float32)
        for step in range(1, place.fars):
            self.await_slot(group, place.fars + step, parts["along"].at[step - 1])
            value = value + parts["along"][step - 1].astype(jnp.float32)
        half = parts["width"] // 2
        block = self.tile.at[:, pl.ds(pl.multiple_of(parts["out"] + place.core * half, 128), half)]
        block[...] = value.astype(jnp.bfloat16)
        self.push(group, 2 * place.fars, block, block, place.sibling())

    def finish(self, group):
        parts, place = self.groups[group], self.place
        half = parts["width"] // 2
        block = self.tile.at[:, pl.ds(pl.multiple_of(parts["out"] + (1 - place.core) * half, 128), half)]
        self.await_slot(group, 2 * place.fars, block)

    def close(self):
        for copy in self.sent:
            copy.wait_send()


def scatter_slots(wide):
    return 2 * (wide // 2) + 1


def scatter_buffers(wide, model, width):
    half, rows, fars = width // 2, model // wide, wide // 2
    return [
        pltpu.VMEM((model, half), jnp.bfloat16),
        pltpu.VMEM((fars, rows, half), jnp.bfloat16),
        pltpu.VMEM((fars - 1, rows, half), jnp.bfloat16),
    ]


def softmax_back_pair(q_pair, k_pair, v_pair, c_pair, inverse, gc_pair, weights, near):
    scaled = (gc_pair.astype(jnp.float32) * inverse).astype(jnp.bfloat16)
    product = scaled.astype(jnp.float32) * c_pair.astype(jnp.float32)
    lane = lax.broadcasted_iota(jnp.int32, product.shape, 1)
    inner = (
        jnp.sum(jnp.where(lane < DK, product, 0.0), axis=1, keepdims=True),
        jnp.sum(jnp.where(lane < DK, 0.0, product), axis=1, keepdims=True),
    )
    g_heads = split_heads(scaled)
    q_heads = split_heads(q_pair)
    k_heads = split_heads(k_pair)
    gq = None
    grads = []
    for head in range(2):
        grad = weights[head].astype(jnp.float32) * (dot_nt(g_heads[head], v_pair) - inner[head])
        if near is not None:
            near(head, grad)
        grad = grad.astype(jnp.bfloat16)
        grads.append(grad)
        part = dot_nn(grad, k_heads[head])
        gq = part if gq is None else gq + part
    gk = dot_tn(jnp.concatenate(grads, axis=0), jnp.concatenate(q_heads, axis=0))
    gv = dot_tn(jnp.concatenate([weights[0], weights[1]], axis=0), jnp.concatenate(g_heads, axis=0))
    return gq, gk, gv


def fold_near(rows):
    total = jnp.zeros((8, 2 * NEAR), jnp.float32)
    blank = jnp.zeros((8, NEAR), jnp.float32)
    for a in range(CHUNK // 8):
        wider = jnp.concatenate([rows[8 * a : 8 * a + 8, :], blank], axis=1)
        total = total + pltpu.roll(wider, (CHUNK - 8 * a) % (2 * NEAR), 1)
    return total


def bucket_sums(rows, offset, two_sided):
    span = rows.shape[1]
    relative = lax.broadcasted_iota(jnp.int32, (span, 128), 0) - offset
    onehot = bucket_index(relative, two_sided) == lax.broadcasted_iota(jnp.int32, (span, 128), 1)
    return lax.dot_general(
        rows,
        onehot.astype(jnp.float32),
        (((1,), (0,)), ((), ())),
        precision=HIGH,
        preferred_element_type=jnp.float32,
    )


def fold_rows(rows):
    span = rows.shape[1]
    total = rows[0:1, :]
    for b in range(1, 8):
        total = total + pltpu.roll(rows, span - b, 1)[b : b + 1, :]
    return total


class Total:
    def __init__(self, place, held, send, receive):
        self.place, self.held, self.send, self.receive = place, held, send, receive
        partners = (place.sibling(), place.across(), place.beside())
        self.copies = [
            remote(held.at[stage], held.at[4 + stage], send.at[stage], receive.at[stage], partner)
            for stage, partner in enumerate(partners)
        ]
        self.last = [
            remote(held.at[3], held.at[7 + place.far], send.at[2 + step], receive.at[2 + step], place.along(step))
            for step in range(1, place.fars)
        ]

    def start(self):
        self.copies[0].start()

    def step(self, stage):
        held = self.held
        self.copies[stage].wait()
        held[stage + 1] = held[stage] + held[4 + stage]
        for copy in [self.copies[stage + 1]] if stage < 2 else self.last:
            copy.start()

    def finish(self):
        for copy in self.last:
            copy.wait()
        result = None
        for far in range(self.place.fars):
            part = jnp.where(self.place.far == far, self.held[3], self.held[7 + far])
            result = part if result is None else result + part
        return result


def enc_backward_kernel(
    wide,
    x_own,
    cot_own,
    cot_other,
    gains,
    dec_gains,
    dec_table,
    part_own,
    part_other,
    dw1_in,
    w1_in,
    n0_in,
    qkv_in,
    c_in,
    inv_in,
    e_all,
    e1_all,
    n1_in,
    slope_all,
    a_in,
    ef_all,
    grad_out,
    tile,
    total_sums,
    part_late,
    gain_sums,
    far_sums,
    folded,
    held,
    w1,
    dw1,
    qkv,
    c,
    inv,
    n1,
    active,
    cot,
    e_buf,
    state_buf,
    slope_buf,
    part_buf,
    other_buf,
    g_send,
    g_recv,
    l_recv,
    state_grad,
    gy,
    gu,
    gqkv,
    gk_sum,
    gv_sum,
    strip,
    core_f,
    beside_f,
    along_f,
    beside_a,
    along_a,
    s_send,
    s_recv,
    t_send,
    t_recv,
    m_sems,
    g_sems,
    l_sems,
    e_sems,
    t_sems,
    i_sems,
):
    place = Place(wide)
    side = place.side
    half = x_own.shape[0]
    rows = 2 * half
    steps = rows // CHUNK
    width = c.shape[1]
    ffn = active.shape[1]
    pairs = width // PAIR
    model = x_own.shape[1]
    bf, f32 = jnp.bfloat16, jnp.float32
    place.greet()

    def swap(i):
        at = pl.ds(i * CHUNK, CHUNK)
        return remote(g_send.at[at], g_recv.at[at], g_sems.at[0, i], g_sems.at[1, i], place.across())

    late = part_late.shape[0] // CHUNK

    def swap_late(i):
        return remote(
            part_own.at[pl.ds((steps - late + i) * CHUNK, CHUNK)],
            part_late.at[pl.ds(i * CHUNK, CHUNK)],
            m_sems.at[0, i],
            m_sems.at[1, i],
            place.across(),
        )

    for i in range(late):
        swap_late(i).start()

    def other_part(i):
        if i < steps - late:
            return part_other.at[pl.ds(i * CHUNK, CHUNK)]
        return part_late.at[pl.ds((i - steps + late) * CHUNK, CHUNK)]

    def fetch(i):
        at = pl.ds(i * CHUNK, CHUNK)
        slot = i % 2
        return [
            pltpu.make_async_copy(ef_all.at[at], state_buf.at[slot], t_sems.at[0, slot]),
            pltpu.make_async_copy(slope_all.at[at], slope_buf.at[slot], t_sems.at[1, slot]),
            pltpu.make_async_copy(part_own.at[at], part_buf.at[slot], t_sems.at[2, slot]),
            pltpu.make_async_copy(other_part(i), other_buf.at[slot], t_sems.at[3, slot]),
        ]

    def fetch_state(i):
        at = pl.ds(i * CHUNK, CHUNK)
        return pltpu.make_async_copy(e1_all.at[at], state_buf.at[i % 2], t_sems.at[0, i % 2])

    def fetch_e(step):
        chunk, pair, slot = step // pairs, lax.rem(step, pairs), lax.rem(step, 2)
        at = pl.ds(pl.multiple_of(chunk * CHUNK, CHUNK), CHUNK)
        return pltpu.make_async_copy(e_all.at[pl.ds(2 * pair, 2), at, :], e_buf.at[slot], e_sems.at[slot])

    mine = pl.ds(pl.multiple_of(side * half, 16), half)
    theirs = pl.ds(pl.multiple_of((1 - side) * half, 16), half)
    loads = [
        pltpu.make_async_copy(cot_own, cot.at[mine], i_sems.at[0]),
        pltpu.make_async_copy(cot_other, cot.at[theirs], i_sems.at[1]),
        pltpu.make_async_copy(w1_in, w1, i_sems.at[2]),
        pltpu.make_async_copy(a_in, active, i_sems.at[3]),
        pltpu.make_async_copy(n1_in, n1, i_sems.at[4]),
        pltpu.make_async_copy(qkv_in, qkv, i_sems.at[5]),
        pltpu.make_async_copy(c_in, c, i_sems.at[6]),
        pltpu.make_async_copy(inv_in, inv, i_sems.at[7]),
        pltpu.make_async_copy(dw1_in, dw1, i_sems.at[8]),
    ]
    loads[8].start()
    for load in loads[:2]:
        load.start()
    for load in fetch(0):
        load.start()
    for load in loads[2:8]:
        load.start()
    gk_sum[...] = jnp.zeros_like(gk_sum)
    gv_sum[...] = jnp.zeros_like(gv_sum)
    strip[...] = jnp.zeros_like(strip)
    far_sums[...] = jnp.zeros_like(far_sums)
    gain_sums[...] = jnp.zeros_like(gain_sums)
    scatter = Scatter(
        place,
        model // wide,
        [
            dict(
                grad=dw1,
                first=0,
                width=4 * width,
                out=4 * width + 2 * ffn,
                core=gqkv.at[pl.ds(0, model), pl.ds(0, 2 * width)],
                beside=beside_a,
                along=along_a,
            ),
            dict(grad=w1, first=4 * width, width=2 * ffn, out=4 * width, core=core_f, beside=beside_f, along=along_f),
            dict(grad=gu.at[pl.ds(0, model)], first=0, width=4 * width, out=0, core=active.at[pl.ds(0, model), pl.ds(0, 2 * width)], beside=beside_a, along=along_a),
        ],
        tile,
        s_send,
        s_recv,
    )

    def own_weight(i):
        return jnp.where((i * CHUNK) // half == side, 1.0, 0.0).astype(f32)

    loads[8].wait()
    scatter.start(0)
    for load in loads[:3]:
        load.wait()

    for i in range(steps):
        at = slice(i * CHUNK, (i + 1) * CHUNK)
        slot = i % 2
        if i + 1 < steps:
            if i + 1 >= steps - late:
                swap_late(i + 1 - steps + late).wait_recv()
            for load in fetch(i + 1):
                load.start()
        for load in fetch(i):
            load.wait()
        grad = part_buf[slot].astype(f32) + other_buf[slot].astype(f32)
        pulled, gain = norm_back(state_buf[slot], gains[5:6, :], grad)
        gain_sums[5:6, :] += gain * own_weight(i)
        total = cot[at, :].astype(f32) + pulled
        state_grad[at, :] = total
        gy[at, :] = total.astype(bf)

        def part(j, carry):
            cols = pl.ds(pl.multiple_of(4 * width + ffn + j * width, PAIR), width)
            here = pl.ds(pl.multiple_of(j * width, PAIR), width)
            grad_active = dot_nn(gy[at, :], w1[:, cols])
            gu[at, here] = (slope_buf[slot, :, here].astype(f32) * grad_active).astype(bf)
            return carry

        lax.fori_loop(0, ffn // width, part, 0)
        g_send[at, :] = dot_nt(gu[at, :], w1[:, 4 * width : 4 * width + ffn]).astype(bf)
        swap(i).start()
        if i == 0:
            scatter.beside(0)
        if i == 2:
            scatter.along(0)
    for load in loads[3:8]:
        load.wait()
    fetch_state(0).start()
    fetch_e(0).start()

    def weight_grads(t, carry):
        tile_rows = pl.ds(pl.multiple_of(t * CHUNK, CHUNK), CHUNK)
        w1[tile_rows, 4 * width : 4 * width + ffn] = dot_tn(n1[:, tile_rows], gu[...]).astype(bf)
        w1[tile_rows, 4 * width + ffn :] = dot_tn(gy[:, tile_rows], active[...]).astype(bf)
        return carry

    lax.fori_loop(0, model // CHUNK, weight_grads, 0)
    scatter.total(0)
    scatter.start(1)
    n0 = cot
    late_loads = [
        pltpu.make_async_copy(n0_in, n0, i_sems.at[0]),
        pltpu.make_async_copy(x_own, n1.at[pl.ds(half, half)], i_sems.at[1]),
    ]
    for load in late_loads:
        load.start()

    dw0 = gu
    l_send = n1

    def lanes(base_lane, pair):
        return pl.ds(pl.multiple_of(base_lane + pair * PAIR, PAIR), PAIR)

    def attend_back(i):
        at = slice(i * CHUNK, (i + 1) * CHUNK)
        slot = i % 2
        if i + 1 < steps:
            fetch_state(i + 1).start()
        fetch_state(i).wait()
        swap(i).wait_recv()
        grad = g_send[at, :].astype(f32) + g_recv[at, :].astype(f32)
        pulled, gain = norm_back(state_buf[slot], gains[1:2, :], grad)
        gain_sums[1:2, :] += gain * own_weight(i)
        total = state_grad[at, :] + pulled
        state_grad[at, :] = total
        gy[at, :] = total.astype(bf)
        g_send[at, :width] = dot_nn(gy[at, :], w1[:, 3 * width : 4 * width]).astype(bf)
        low, high, shift = near_window(i, rows)

        def one(pair, carry):
            step = i * pairs + pair

            @pl.when(step + 1 < steps * pairs)
            def _():
                fetch_e(step + 1).start()

            fetch_e(step).wait()
            e_slot = lax.rem(step, 2)

            def near(head, grad):
                strip[2 * pair + head, :, shift : shift + high - low] += grad[:, low:high]
                for edge, (start, end) in enumerate(((0, low), (high, rows))):
                    if end > start:
                        folded = jnp.sum(grad[:, start:end].reshape(CHUNK // 8, 8, end - start), axis=0)
                        wide_sum = folded[:, :128]
                        for lane in range(128, end - start, 128):
                            wide_sum = wide_sum + folded[:, lane : lane + 128]
                        far_sums[edge, 2 * pair + head] += wide_sum

            gq, gk, gv = softmax_back_pair(
                qkv[at, lanes(0, pair)],
                qkv[:, lanes(width, pair)],
                qkv[:, lanes(2 * width, pair)],
                c[at, lanes(0, pair)],
                inv[at, lanes(0, pair)],
                g_send[at, lanes(0, pair)],
                (e_buf[e_slot, 0], e_buf[e_slot, 1]),
                near,
            )
            gqkv[at, lanes(0, pair)] = gq.astype(bf)
            gk_sum[:, lanes(0, pair)] += gk
            gv_sum[:, lanes(0, pair)] += gv
            return carry

        lax.fori_loop(0, pairs, one, 0)

    for i in range(steps):
        swap(i).wait_send()
        attend_back(i)
        if i == 0:
            scatter.beside(1)
        if i == 2:
            scatter.along(1)
    for load in late_loads:
        load.wait()
    gqkv[:, width : 2 * width] = gk_sum[...].astype(bf)
    gqkv[:, 2 * width :] = gv_sum[...].astype(bf)

    def weight_grads_a(t, carry):
        tile_rows = pl.ds(pl.multiple_of(t * CHUNK, CHUNK), CHUNK)
        dw0[tile_rows, : 3 * width] = dot_tn(n0[:, tile_rows], gqkv[...]).astype(bf)
        dw0[tile_rows, 3 * width :] = dot_tn(gy[:, tile_rows], c[...]).astype(bf)
        return carry

    lax.fori_loop(0, model // CHUNK, weight_grads_a, 0)
    scatter.start(2)
    last = []
    for part in range(half // CHUNK):
        there = pl.ds(pl.multiple_of((1 - side) * half + part * CHUNK, CHUNK), CHUNK)
        at = pl.ds(part * CHUNK, CHUNK)
        l_send[at, :] = dot_nt(gqkv[there, :], w1[:, : 3 * width]).astype(bf)
        last.append(remote(l_send.at[at], l_recv.at[at], l_sems.at[0, part], l_sems.at[1, part], place.across()))
        last[part].start()
        if part == 0:
            scatter.beside(2)
    scatter.total(1)
    summed = Total(place, held, t_send, t_recv)
    folded[...] = jnp.zeros_like(folded)

    def fold(head, carry):
        folded[pl.ds(head, 1), :] = fold_rows(fold_near(strip[head]))
        return carry

    lax.fori_loop(0, 2 * pairs, fold, 0)
    table = bucket_sums(folded[...], CHUNK + EDGE, True)
    bucket = lax.broadcasted_iota(jnp.int32, (1, 128), 1)
    for head in range(2 * pairs):
        far = [jnp.sum(far_sums[edge, head]) for edge in range(2)]
        folded[head : head + 1, :128] = jnp.where(
            bucket == NB // 2 - 1, far[0], jnp.where(bucket == NB - 1, far[1], 0.0)
        )
    table = table + folded[:, :128]
    scatter.along(2)
    for part in range(half // CHUNK):
        here = pl.ds(pl.multiple_of(side * half + part * CHUNK, CHUNK), CHUNK)
        at = pl.ds(part * CHUNK, CHUNK)
        own = dot_nt(gqkv[here, :], w1[:, : 3 * width])
        last[part].wait_recv()
        grad = own + l_recv[at, :].astype(f32)
        pulled, gain = norm_back(n1[pl.ds(half + part * CHUNK, CHUNK), :].astype(f32), gains[0:1, :], grad)
        gain_sums[0:1, :] += gain
        grad_out[at, :] = state_grad[here, :] + pulled
    held[0] = jnp.zeros_like(held[0])
    held[0, :8, :] = gain_sums[...] + dec_gains[...]
    held[0, 8:, pl.ds(pl.multiple_of(side * 256, 128), 128)] = table
    held[0, 8:, pl.ds(pl.multiple_of(side * 256 + 128, 128), 128)] = dec_table[...]
    summed.start()
    scatter.total(2)
    scatter.finish(0)
    scatter.finish(1)
    summed.step(0)
    summed.step(1)
    summed.step(2)
    scatter.finish(2)
    scatter.close()
    total_sums[...] = summed.finish()
    for i in range(late):
        swap_late(i).wait_send()
    for copy in last:
        copy.wait_send()


def enc_backward(wide, x_own, cot_own, cot_other, gains, dec_gains, dec_table, part_own, part_other, dw1, saved):
    half, model = x_own.shape
    rows = 2 * half
    w1, n0, qkv, c, inv, e_all, e1, n1, slope, active, ef = saved
    width, ffn = c.shape[1], active.shape[1]
    pairs = width // PAIR
    steps = rows // CHUNK
    bf, f32 = jnp.bfloat16, jnp.float32
    shape = jax.ShapeDtypeStruct
    dma = pltpu.SemaphoreType.DMA
    return pl.pallas_call(
        functools.partial(enc_backward_kernel, wide),
        in_specs=[any_spec()] * 3 + [vmem_spec()] * 3 + [any_spec()] * 14,
        out_shape=[
            shape((half, model), f32),
            shape((model // wide, 8 * width + 2 * ffn), bf),
            shape((16, model), f32),
            shape((rows - part_other.shape[0], model), bf),
        ],
        out_specs=[vmem_spec()] * 3 + [any_spec()],
        scratch_shapes=[
            pltpu.VMEM((8, model), f32),
            pltpu.VMEM((2, 2 * pairs, 8, 128), f32),
            pltpu.VMEM((8, 2 * NEAR), f32),
            pltpu.VMEM((7 + wide // 2, 16, model), f32),
            pltpu.VMEM(w1.shape, bf),
            pltpu.VMEM(dw1.shape, bf),
            pltpu.VMEM(qkv.shape, bf),
            pltpu.VMEM(c.shape, bf),
            pltpu.VMEM(inv.shape, f32),
            pltpu.VMEM(n1.shape, bf),
            pltpu.VMEM(active.shape, bf),
            pltpu.VMEM((rows, model), bf),
            pltpu.VMEM((2, 2, CHUNK, rows), bf),
            pltpu.VMEM((2, CHUNK, model), f32),
            pltpu.VMEM((2, CHUNK, ffn), bf),
            pltpu.VMEM((2, CHUNK, model), bf),
            pltpu.VMEM((2, CHUNK, model), bf),
            pltpu.VMEM((rows, model), bf),
            pltpu.VMEM((rows, model), bf),
            pltpu.VMEM((half, model), bf),
            pltpu.VMEM((rows, model), f32),
            pltpu.VMEM((rows, model), bf),
            pltpu.VMEM((rows, ffn), bf),
            pltpu.VMEM((rows, 3 * width), bf),
            pltpu.VMEM((rows, width), f32),
            pltpu.VMEM((rows, width), f32),
            pltpu.VMEM((2 * pairs, CHUNK, NEAR), f32),
        ]
        + scatter_buffers(wide, model, 2 * ffn)
        + scatter_buffers(wide, model, 4 * width)[1:]
        + [
            dma((3, scatter_slots(wide))),
            dma((3, scatter_slots(wide))),
            dma((2 + wide // 2,)),
            dma((2 + wide // 2,)),
            dma((2, steps)),
            dma((2, steps)),
            dma((2, half // CHUNK)),
            dma((2,)),
            dma((4, 2)),
            dma((9,)),
        ],
        compiler_params=pltpu.CompilerParams(
            collective_id=1, has_side_effects=True, vmem_limit_bytes=VMEM_BYTES
        ),
        cost_estimate=pl.CostEstimate(flops=2 * 10**10, bytes_accessed=6 * 10**7, transcendentals=0),
    )(x_own, cot_own, cot_other, gains, dec_gains, dec_table, part_own, part_other, dw1, w1, n0, qkv, c, inv, e_all, e1, n1, slope, active, ef)


def fold_offsets(grad):
    rows = grad.shape[0]
    total = jnp.zeros((8, 2 * rows), jnp.float32)
    blank = jnp.zeros((8, rows), jnp.float32)
    for a in range(rows // 8):
        wider = jnp.concatenate([grad[8 * a : 8 * a + 8, :], blank], axis=1)
        total = total + pltpu.roll(wider, (rows - 8 * a) % (2 * rows), 1)
    return total


def decoder_kernel(
    wide,
    dec_own,
    dec_other,
    dcot_own,
    dcot_other,
    cot_own,
    down_in,
    gains,
    base,
    qseg,
    kseg,
    mseg,
    mem_in,
    w_in,
    dec_out,
    dec_grad,
    tile,
    gain_sums,
    table,
    part_own,
    part_other,
    cot_other,
    dw1_all,
    pack,
    folded,
    w,
    mem,
    dec,
    dcot,
    state,
    normals,
    qkv,
    c,
    inv,
    e_self,
    e_cross,
    strip,
    kv,
    active,
    ga,
    gu,
    grad_state,
    gy,
    gqkv,
    gkv,
    y_send,
    y_recv,
    dw,
    core_f,
    beside_f,
    along_f,
    core_d,
    beside_d,
    along_d,
    s_send,
    s_recv,
    g_send,
    g_recv,
    g_local,
    y_sems,
    x_sems,
    p_sems,
    o_sems,
    i_sems,
):
    place = Place(wide)
    side = place.side
    half = dec_own.shape[0]
    rows = 2 * half
    model = dec_own.shape[1]
    width = c.shape[2]
    ffn = active.shape[1]
    pairs = width // PAIR
    span = mem.shape[0]
    bf, f32 = jnp.bfloat16, jnp.float32
    place.greet()
    mine = pl.ds(pl.multiple_of(side * half, 16), half)
    theirs = pl.ds(pl.multiple_of((1 - side) * half, 16), half)
    at_d, at_f = 4 * width, 8 * width

    gather = Gather(place, pack, [(0, ffn, w, at_f + ffn)], g_send, g_recv, g_local)
    cot_part = cot_own.shape[0] // 4

    def swap_cot(i):
        at = pl.ds(i * cot_part, cot_part)
        return remote(cot_own.at[at], cot_other.at[at], x_sems.at[0, i], x_sems.at[1, i], place.across())

    def load_w(first, count, sem):
        cols = pl.ds(first, count)
        return pltpu.make_async_copy(w_in.at[:, cols], w.at[:, cols], i_sems.at[sem])

    loads = [
        load_w(0, 4 * width, 0),
        load_w(at_d, 4 * width, 1),
        pltpu.make_async_copy(mem_in, mem, i_sems.at[2]),
        load_w(at_f, ffn, 3),
        pltpu.make_async_copy(dec_own, dec.at[mine], i_sems.at[4]),
        pltpu.make_async_copy(dcot_own, dcot.at[mine], i_sems.at[5]),
        pltpu.make_async_copy(dec_other, dec.at[theirs], i_sems.at[6]),
        pltpu.make_async_copy(dcot_other, dcot.at[theirs], i_sems.at[7]),
        pltpu.make_async_copy(down_in, pack, i_sems.at[8]),
    ]
    for index in (8, 4, 6, 0, 5, 7, 2, 1, 3):
        loads[index].start()
    swap_cot(0).start()
    swap_cot(1).start()
    loads[8].wait()
    gather.start(0)
    build_strip(strip, base, pairs, rows, rows)
    gain_sums[...] = jnp.zeros_like(gain_sums)
    folded[...] = jnp.zeros_like(folded)
    scatter = Scatter(
        place,
        model // wide,
        [
            dict(grad=w, first=at_f, width=2 * ffn, out=4 * width, core=core_f, beside=beside_f, along=along_f),
            dict(grad=dw, first=at_d, width=4 * width, out=0, core=core_d, beside=beside_d, along=along_d),
        ],
        tile,
        s_send,
        s_recv,
    )

    def swap(kind):
        return remote(y_send.at[kind], y_recv.at[kind], y_sems.at[0, kind], y_sems.at[1, kind], place.across())

    def send_branch(kind, value):
        y_send[kind] = value.astype(bf)
        swap(kind).start()

    def branch(kind):
        swap(kind).wait_recv()
        return y_send[kind].astype(f32) + y_recv[kind].astype(f32)

    def lanes(base_lane, pair):
        return pl.ds(pl.multiple_of(base_lane + pair * PAIR, PAIR), PAIR)

    def norm_to(index, gain, value):
        state[index] = value
        normals[index] = normed(value, gains[gain : gain + 1, :]).astype(bf)

    loads[4].wait()
    loads[6].wait()
    norm_to(0, 2, dec[...].astype(f32))
    loads[0].wait()
    qkv[:, : 3 * width] = dot_nn(normals[0], w[:, : 3 * width]).astype(bf)

    def self_pair(pair, carry):
        allowed = qseg[...] == kseg[...]
        allowed = allowed & (
            lax.broadcasted_iota(jnp.int32, (rows, rows), 1) <= lax.broadcasted_iota(jnp.int32, (rows, rows), 0)
        )

        def bias(head):
            return strip[2 * pair + head, :, :rows]

        def store(head, weights):
            e_self[2 * pair + head] = weights

        inverse, context = softmax_pair(
            qkv[:, lanes(0, pair)], qkv[:, lanes(width, pair)], qkv[:, lanes(2 * width, pair)], allowed, bias, store
        )
        inv[0, :, lanes(0, pair)] = inverse
        c[0, :, lanes(0, pair)] = context
        return carry

    lax.fori_loop(0, pairs, self_pair, 0)
    send_branch(0, dot_nt(c[0], w[:, 3 * width : 4 * width]))

    loads[2].wait()
    loads[1].wait()

    def cross_keys(i, carry):
        at = pl.ds(pl.multiple_of(i * CHUNK, CHUNK), CHUNK)
        kv[at, :] = dot_nn(mem[at, :], w[:, at_d + width : at_d + 3 * width]).astype(bf)
        return carry

    lax.fori_loop(0, span // CHUNK, cross_keys, 0)
    gather.relay_along(0)
    norm_to(1, 3, state[0] + branch(0))
    swap_cot(2).start()
    qkv[:, 3 * width :] = dot_nn(normals[1], w[:, at_d : at_d + width]).astype(bf)

    def cross_pair(pair, carry):
        allowed = qseg[...] == mseg[...]

        def store(head, weights):
            e_cross[2 * pair + head] = weights

        inverse, context = softmax_pair(
            qkv[:, lanes(3 * width, pair)], kv[:, lanes(0, pair)], kv[:, lanes(width, pair)], allowed, None, store
        )
        inv[1, :, lanes(0, pair)] = inverse
        c[1, :, lanes(0, pair)] = context
        return carry

    lax.fori_loop(0, pairs, cross_pair, 0)
    send_branch(1, dot_nt(c[1], w[:, at_d + 3 * width : at_d + 4 * width]))
    gather.relay_beside(0)

    for index in (5, 7, 3):
        loads[index].wait()
    gather.finish(0)
    ga[...] = dot_nn(dcot[...], w[:, at_f + ffn :]).astype(f32)
    norm_to(2, 4, state[1] + branch(1))
    swap_cot(3).start()

    def hidden(j, carry):
        here = pl.ds(pl.multiple_of(j * width, PAIR), width)
        cols = pl.ds(pl.multiple_of(at_f + j * width, PAIR), width)
        value, turn = gelu_pair(dot_nn(normals[2], w[:, cols]))
        active[:, here] = value.astype(bf)
        gu[:, here] = (turn * ga[:, here]).astype(bf)
        return carry

    lax.fori_loop(0, ffn // width, hidden, 0)
    send_branch(3, dot_nt(gu[...], w[:, at_f : at_f + ffn]))
    y_send[2] = dot_nt(active[...], w[:, at_f + ffn :]).astype(bf)

    def feed_grads(t, carry):
        tile_rows = pl.ds(pl.multiple_of(t * CHUNK, CHUNK), CHUNK)
        w[tile_rows, at_f : at_f + ffn] = dot_tn(normals[2, :, tile_rows], gu[...]).astype(bf)
        w[tile_rows, at_f + ffn :] = dot_tn(dcot[:, tile_rows], active[...]).astype(bf)
        return carry

    gather.close()
    lax.fori_loop(0, model // CHUNK, feed_grads, 0)
    scatter.start(0)
    scatter.beside(0)

    row = lax.broadcasted_iota(jnp.int32, (rows, 1), 0)
    counted = jnp.where(row // half == side, 1.0, 0.0).astype(f32)

    def pull(index, gain, grad):
        values = state[index]
        pulled, unused = norm_back(values, gains[gain : gain + 1, :], grad)
        scale = lax.rsqrt(jnp.mean(values * values, axis=1, keepdims=True) + EPS) * counted
        gain_sums[gain : gain + 1, :] += jnp.sum(grad * values * scale, axis=0, keepdims=True)
        return pulled

    grad_state[...] = dcot[...].astype(f32) + pull(2, 4, branch(3))
    swap(2).start()
    gy[1] = grad_state[...].astype(bf)
    gc = dot_nn(gy[1], w[:, at_d + 3 * width : at_d + 4 * width]).astype(bf)
    y_send[5, :, :width] = gc

    def cross_back(pair, carry):
        gq, gk, gv = softmax_back_pair(
            qkv[:, lanes(3 * width, pair)],
            kv[:, lanes(0, pair)],
            kv[:, lanes(width, pair)],
            c[1, :, lanes(0, pair)],
            inv[1, :, lanes(0, pair)],
            y_send[5, :, lanes(0, pair)],
            (e_cross[2 * pair], e_cross[2 * pair + 1]),
            None,
        )
        gqkv[:, lanes(3 * width, pair)] = gq.astype(bf)
        gkv[:, lanes(0, pair)] = gk.astype(bf)
        gkv[:, lanes(width, pair)] = gv.astype(bf)
        return carry

    lax.fori_loop(0, pairs, cross_back, 0)
    send_branch(4, dot_nt(gqkv[:, 3 * width :], w[:, at_d : at_d + width]))

    part = kv

    def swap_part(i):
        at = pl.ds(pl.multiple_of(i * CHUNK, CHUNK), CHUNK)
        return remote(part.at[at], part_other.at[at], p_sems.at[0, i], p_sems.at[1, i], place.across())

    def keep_part(i):
        at = pl.ds(pl.multiple_of(i * CHUNK, CHUNK), CHUNK)
        return pltpu.make_async_copy(part.at[at], part_own.at[at], o_sems.at[i])

    for i in range(span // CHUNK):
        at = pl.ds(i * CHUNK, CHUNK)
        part[at, :] = dot_nt(gkv[at, :], w[:, at_d + width : at_d + 3 * width]).astype(bf)
        keep_part(i).start()

    def cross_grads(t, carry):
        tile_rows = pl.ds(pl.multiple_of(t * CHUNK, CHUNK), CHUNK)
        dw[tile_rows, at_d : at_d + width] = dot_tn(normals[1, :, tile_rows], gqkv[:, 3 * width :]).astype(bf)
        dw[tile_rows, at_d + width : at_d + 3 * width] = dot_tn(mem[:, tile_rows], gkv[...]).astype(bf)
        dw[tile_rows, at_d + 3 * width : at_f] = dot_tn(gy[1, :, tile_rows], c[1]).astype(bf)
        return carry

    lax.fori_loop(0, model // CHUNK, cross_grads, 0)
    scatter.start(1)
    scatter.along(0)

    grad_state[...] = grad_state[...] + pull(1, 3, branch(4))
    early = part_other.shape[0] // CHUNK
    swap_part(0).start()
    gy[0] = grad_state[...].astype(bf)
    y_send[5, :, :width] = dot_nn(gy[0], w[:, 3 * width : 4 * width]).astype(bf)

    def self_back(pair, carry):
        def near(head, grad):
            folded[pl.ds(2 * pair + head, 1), :] = fold_rows(fold_offsets(grad))

        gq, gk, gv = softmax_back_pair(
            qkv[:, lanes(0, pair)],
            qkv[:, lanes(width, pair)],
            qkv[:, lanes(2 * width, pair)],
            c[0, :, lanes(0, pair)],
            inv[0, :, lanes(0, pair)],
            y_send[5, :, lanes(0, pair)],
            (e_self[2 * pair], e_self[2 * pair + 1]),
            near,
        )
        gqkv[:, lanes(0, pair)] = gq.astype(bf)
        gqkv[:, lanes(width, pair)] = gk.astype(bf)
        gqkv[:, lanes(2 * width, pair)] = gv.astype(bf)
        return carry

    lax.fori_loop(0, pairs, self_back, 0)

    y_send[5] = dot_nt(gqkv[:, : 3 * width], w[:, : 3 * width]).astype(bf)
    back = remote(y_send.at[5, theirs], y_recv.at[5, theirs], y_sems.at[0, 5], y_sems.at[1, 5], place.across())
    back.start()
    for i in range(1, early):
        swap_part(i).start()
    scatter.beside(1)

    def self_grads(t, carry):
        tile_rows = pl.ds(pl.multiple_of(t * CHUNK, CHUNK), CHUNK)
        dw[tile_rows, : 3 * width] = dot_tn(normals[0, :, tile_rows], gqkv[:, : 3 * width]).astype(bf)
        dw[tile_rows, 3 * width : at_d] = dot_tn(gy[0, :, tile_rows], c[0]).astype(bf)
        return carry

    lax.fori_loop(0, model // CHUNK, self_grads, 0)
    keep_dw = pltpu.make_async_copy(dw.at[:, pl.ds(0, at_d)], dw1_all, i_sems.at[0])
    keep_dw.start()
    table[...] = bucket_sums(folded[...], rows, False)
    scatter.total(0)
    scatter.along(1)
    back.wait_recv()
    grad = y_send[5, mine, :].astype(f32) + y_recv[5, mine, :].astype(f32)
    pulled, gain = norm_back(state[0, mine, :], gains[2:3, :], grad)
    gain_sums[2:3, :] += gain
    dec_grad[...] = grad_state[mine, :] + pulled
    swap(2).wait_recv()
    dec_out[...] = (state[2, mine, :] + y_send[2, mine, :].astype(f32) + y_recv[2, mine, :].astype(f32)).astype(bf)
    scatter.total(1)
    for i in range(early):
        swap_part(i).wait()
    for i in range(span // CHUNK):
        keep_part(i).wait()
    keep_dw.wait()
    for i in range(4):
        swap_cot(i).wait()
    for group in range(2):
        scatter.finish(group)
    scatter.close()
    for kind in range(5):
        swap(kind).wait_send()
    back.wait_send()


def decoder(wide, dec_rows, dcot_rows, cot_own, down, gains, base, dec_segments, enc_segments, mem, w2):
    half, model = dec_rows[0].shape
    rows = 2 * half
    span = mem.shape[0]
    pairs = base.shape[0]
    width = pairs * PAIR
    ffn = down.shape[1]
    late = span // CHUNK // 2 * CHUNK
    bf, f32 = jnp.bfloat16, jnp.float32
    shape = jax.ShapeDtypeStruct
    dma = pltpu.SemaphoreType.DMA
    return pl.pallas_call(
        functools.partial(decoder_kernel, wide),
        in_specs=[any_spec()] * 6 + [vmem_spec()] * 5 + [any_spec()] * 2,
        out_shape=[
            shape((half, model), bf),
            shape((half, model), f32),
            shape((model // wide, 4 * width + 2 * ffn), bf),
            shape((8, model), f32),
            shape((8, 128), f32),
            shape((span, model), bf),
            shape((late, model), bf),
            shape(cot_own.shape, bf),
            shape((model, 4 * width), bf),
        ],
        out_specs=[vmem_spec()] * 5 + [any_spec()] * 4,
        scratch_shapes=[
            pltpu.VMEM(down.shape, bf),
            pltpu.VMEM((8, 2 * rows), f32),
            pltpu.VMEM((model, 8 * width + 2 * ffn), bf),
            pltpu.VMEM((span, model), bf),
            pltpu.VMEM((rows, model), bf),
            pltpu.VMEM((rows, model), bf),
            pltpu.VMEM((3, rows, model), f32),
            pltpu.VMEM((3, rows, model), bf),
            pltpu.VMEM((rows, 4 * width), bf),
            pltpu.VMEM((2, rows, width), bf),
            pltpu.VMEM((2, rows, width), f32),
            pltpu.VMEM((2 * pairs, rows, rows), bf),
            pltpu.VMEM((2 * pairs, rows, span), bf),
            pltpu.VMEM((2 * pairs, rows, 2 * rows), f32),
            pltpu.VMEM((span, 2 * width), bf),
            pltpu.VMEM((rows, ffn), bf),
            pltpu.VMEM((rows, ffn), f32),
            pltpu.VMEM((rows, ffn), bf),
            pltpu.VMEM((rows, model), f32),
            pltpu.VMEM((2, rows, model), bf),
            pltpu.VMEM((rows, 4 * width), bf),
            pltpu.VMEM((span, 2 * width), bf),
            pltpu.VMEM((6, rows, model), bf),
            pltpu.VMEM((6, rows, model), bf),
            pltpu.VMEM((model, 8 * width), bf),
        ]
        + scatter_buffers(wide, model, 2 * ffn)
        + scatter_buffers(wide, model, 4 * width)
        + [
            dma((2, scatter_slots(wide))),
            dma((2, scatter_slots(wide))),
            dma((1, gather_slots(wide))),
            dma((1, gather_slots(wide))),
            dma((1,)),
            dma((2, 6)),
            dma((2, 4)),
            dma((2, span // CHUNK)),
            dma((span // CHUNK,)),
            dma((9,)),
        ],
        compiler_params=pltpu.CompilerParams(
            collective_id=2, has_side_effects=True, vmem_limit_bytes=VMEM_BYTES
        ),
        cost_estimate=pl.CostEstimate(flops=10**10, bytes_accessed=6 * 10**7, transcendentals=0),
    )(
        *dec_rows,
        *dcot_rows,
        cot_own,
        down,
        gains,
        base,
        dec_segments[:, None],
        dec_segments[None, :],
        enc_segments[None, :],
        mem,
        w2,
    )


def on_device(
    wide,
    enc_input,
    dec_input,
    enc_lengths,
    dec_lengths,
    attn_query,
    attn_kv,
    attn_out,
    ffn_up,
    ffn_down,
    gains,
    rel_bias,
    enc_cotangent,
    dec_cotangent,
):
    gain_rows = gains.astype(jnp.float32)
    heads_local = rel_bias.shape[2]
    enc_segments = segment_ids(enc_lengths[0], ENC)
    dec_segments = segment_ids(dec_lengths[0], DEC)
    side = lax.axis_index("narrow")
    width, ffn = DK * heads_local, ffn_up.shape[2]
    half = enc_input.shape[0]
    down = ffn_down.transpose(0, 2, 1)
    weights = (attn_query, attn_kv, attn_out.transpose(0, 2, 1), ffn_up, down)
    w1, w2, n0, qkv, context, inverse, exps, e1, n1, slope, active, ef, memory, dec_other, dcot_other = enc_forward(
        wide, enc_input, dec_input, dec_cotangent, weights, gain_rows, near_rows(rel_bias[0]), enc_segments
    )
    dec_output, grad_dec, tile_two, dec_gains, dec_table, part_own, part_other, cot_other, dw1 = decoder(
        wide,
        (dec_input, dec_other),
        (dec_cotangent, dcot_other),
        enc_cotangent,
        down[1],
        gain_rows,
        base_rows(rel_bias[1], DEC, False),
        dec_segments,
        enc_segments,
        memory,
        w2,
    )
    grad_enc, tile_one, sums, unused = enc_backward(
        wide,
        enc_input,
        enc_cotangent,
        cot_other,
        gain_rows,
        dec_gains,
        dec_table,
        part_own,
        part_other,
        dw1,
        (w1, n0, qkv, context, inverse, exps, e1, n1, slope, active, ef),
    )
    tables = lax.dynamic_slice_in_dim(sums[8 : 8 + heads_local], side * 256, 256, 1)
    bias_grad = jnp.stack([tables[:, :NB].T, tables[:, 128 : 128 + NB].T])
    tile_one, tile_two = tile_one.astype(jnp.float32), tile_two.astype(jnp.float32)
    layers = (tile_one[:, : 4 * width], tile_one[:, 4 * width + 2 * ffn :], tile_two[:, : 4 * width])
    feeds = (tile_one[:, 4 * width : 4 * width + 2 * ffn], tile_two[:, 4 * width :])
    return (
        lax.dynamic_slice_in_dim(ef, side * half, half).astype(jnp.bfloat16),
        dec_output,
        grad_enc,
        grad_dec,
        jnp.stack([layer[:, :width] for layer in layers]),
        jnp.stack([jnp.stack([layer[:, width : 2 * width], layer[:, 2 * width : 3 * width]]) for layer in layers]),
        jnp.stack([layer[:, 3 * width :].T for layer in layers]),
        jnp.stack([feed[:, :ffn] for feed in feeds]),
        jnp.stack([feed[:, ffn:].T for feed in feeds]),
        sums[:6],
        bias_grad,
    )


def ffn_backward(grad_rows, normed_rows, hidden, active, weight_up, weight_down):
    grad_active = jnp.einsum(
        "rd,fd->rf", grad_rows, weight_down, preferred_element_type=jnp.float32
    )
    grad_down = jnp.einsum("rf,rd->fd", active, grad_rows, preferred_element_type=jnp.float32)
    unused, pull = jax.vjp(gelu_tanh, hidden)
    grad_hidden = pull(grad_active)[0].astype(jnp.bfloat16)
    grad_up = jnp.einsum("rd,rf->df", normed_rows, grad_hidden, preferred_element_type=jnp.float32)
    grad_normed = jnp.einsum(
        "rf,df->rd", grad_hidden, weight_up, preferred_element_type=jnp.float32
    )
    return (grad_normed, grad_up, grad_down)


def norm_backward(values, gain, grad_normed):
    unused, pull = jax.vjp(rms_norm, values, gain)
    return pull(grad_normed)


def on_device_general(
    enc_input,
    dec_input,
    enc_lengths,
    dec_lengths,
    attn_query,
    attn_kv,
    attn_out,
    ffn_up,
    ffn_down,
    gains,
    rel_bias,
    enc_cotangent,
    dec_cotangent,
):
    weights = (
        lax.all_gather(attn_query, "wide", axis=1, tiled=True),
        lax.all_gather(attn_kv, "wide", axis=2, tiled=True),
        lax.all_gather(attn_out, "wide", axis=2, tiled=True),
        lax.all_gather(ffn_up, "wide", axis=1, tiled=True),
        lax.all_gather(ffn_down, "wide", axis=2, tiled=True),
    )
    gain_rows = gains.astype(jnp.float32)
    heads_local = rel_bias.shape[2]
    enc_segments = segment_ids(enc_lengths[0], ENC)
    dec_segments = segment_ids(dec_lengths[0], DEC)

    side = lax.axis_index("narrow")
    swap = [(0, 1), (1, 0)]

    def spread_rows(values):
        own = values.astype(jnp.bfloat16)
        other = lax.ppermute(own, "narrow", swap)
        return jnp.where(side == 0, jnp.concatenate([own, other]), jnp.concatenate([other, own]))

    def collect_rows(parts):
        half = parts.shape[0] // 2
        parts = parts.astype(jnp.bfloat16)
        other = lax.ppermute(lax.dynamic_slice_in_dim(parts, (1 - side) * half, half), "narrow", swap)
        own = lax.dynamic_slice_in_dim(parts, side * half, half)
        return own.astype(jnp.float32) + other.astype(jnp.float32)

    def attention_layer(normed_query, normed_keys, layer, base, query_segments, key_segments, causal):
        query = jnp.dot(normed_query, weights[0][layer], preferred_element_type=jnp.float32).astype(jnp.bfloat16)
        keys = jnp.dot(normed_keys, weights[1][layer, 0], preferred_element_type=jnp.float32).astype(jnp.bfloat16)
        values = jnp.dot(normed_keys, weights[1][layer, 1], preferred_element_type=jnp.float32).astype(jnp.bfloat16)
        saved = attend_forward(query, keys, values, base, query_segments, key_segments, causal)
        parts = jnp.dot(saved[1], weights[2][layer], preferred_element_type=jnp.float32)
        return ((query, keys, values, saved), collect_rows(parts))

    enc_start = enc_input.astype(jnp.float32)
    rows_a = spread_rows(rms_norm(enc_start, gain_rows[0]))
    kept_a, branch = attention_layer(
        rows_a, rows_a, 0, base_rows(rel_bias[0], ENC, True), enc_segments, enc_segments, False
    )
    enc_mid = enc_start + branch
    rows_b = spread_rows(rms_norm(enc_mid, gain_rows[1]))
    hidden_b = jnp.dot(rows_b, weights[3][0], preferred_element_type=jnp.float32)
    active_b = gelu_tanh(hidden_b).astype(jnp.bfloat16)
    enc_final = enc_mid + collect_rows(
        jnp.dot(active_b, weights[4][0], preferred_element_type=jnp.float32)
    )
    memory = spread_rows(rms_norm(enc_final, gain_rows[5]))
    dec_start = dec_input.astype(jnp.float32)
    rows_c = spread_rows(rms_norm(dec_start, gain_rows[2]))
    kept_c, branch = attention_layer(
        rows_c, rows_c, 1, base_rows(rel_bias[1], DEC, False), dec_segments, dec_segments, True
    )
    dec_one = dec_start + branch
    rows_d = spread_rows(rms_norm(dec_one, gain_rows[3]))
    kept_d, branch = attention_layer(
        rows_d, memory, 2, None, dec_segments, enc_segments, False
    )
    dec_two = dec_one + branch
    rows_e = spread_rows(rms_norm(dec_two, gain_rows[4]))
    hidden_e = jnp.dot(rows_e, weights[3][1], preferred_element_type=jnp.float32)
    active_e = gelu_tanh(hidden_e).astype(jnp.bfloat16)
    dec_final = dec_two + collect_rows(
        jnp.dot(active_e, weights[4][1], preferred_element_type=jnp.float32)
    )
    def attention_back(grad_state, kept, normed_query, normed_keys, layer, span, two_sided):
        grad_rows = spread_rows(grad_state)
        query, keys, values, saved = kept
        grad_context = dot_nt(grad_rows, weights[2][layer]).astype(jnp.bfloat16)
        grad_out = dot_tn(saved[1], grad_rows)
        result = attend_backward(query, keys, values, saved, grad_context, span > 0)
        grad_q, grad_k, grad_v = result[:3]
        sums = [
            dot_tn(normed_query, grad_q),
            dot_tn(normed_keys, grad_k),
            dot_tn(normed_keys, grad_v),
            grad_out,
            table_grad(result[3], span, two_sided) if span else None,
        ]
        query_part = dot_nt(grad_q, weights[0][layer])
        key_part = dot_nt(grad_k, weights[1][layer, 0]) + dot_nt(grad_v, weights[1][layer, 1])
        return (query_part, key_part, sums)

    grad_dec = dec_cotangent.astype(jnp.float32)
    grad_normed, up_e, down_e = ffn_backward(
        spread_rows(grad_dec), rows_e, hidden_e, active_e, weights[3][1], weights[4][1]
    )
    grad_back, gain_e = norm_backward(dec_two, gain_rows[4], collect_rows(grad_normed))
    grad_dec = grad_dec + grad_back
    query_part, memory_part, sums_d = attention_back(
        grad_dec, kept_d, rows_d, memory, 2, 0, False
    )
    grad_normed, grad_memory = collect_rows(query_part), collect_rows(memory_part)
    grad_back, gain_d = norm_backward(dec_one, gain_rows[3], grad_normed)
    grad_dec = grad_dec + grad_back
    query_part, key_part, sums_c = attention_back(
        grad_dec, kept_c, rows_c, rows_c, 1, DEC, False
    )
    grad_back, gain_c = norm_backward(dec_start, gain_rows[2], collect_rows(query_part + key_part))
    grad_dec = grad_dec + grad_back
    grad_enc = enc_cotangent.astype(jnp.float32)
    grad_back, gain_m = norm_backward(enc_final, gain_rows[5], grad_memory)
    grad_enc = grad_enc + grad_back
    grad_normed, up_b, down_b = ffn_backward(
        spread_rows(grad_enc), rows_b, hidden_b, active_b, weights[3][0], weights[4][0]
    )
    grad_back, gain_b = norm_backward(enc_mid, gain_rows[1], collect_rows(grad_normed))
    grad_enc = grad_enc + grad_back
    query_part, key_part, sums_a = attention_back(
        grad_enc, kept_a, rows_a, rows_a, 0, ENC, True
    )
    grad_back, gain_a = norm_backward(enc_start, gain_rows[0], collect_rows(query_part + key_part))
    grad_enc = grad_enc + grad_back
    grad_query = jnp.stack([sums_a[0], sums_c[0], sums_d[0]])
    grad_kv = jnp.stack(
        [
            jnp.stack([sums_a[1], sums_a[2]]),
            jnp.stack([sums_c[1], sums_c[2]]),
            jnp.stack([sums_d[1], sums_d[2]]),
        ]
    )
    grad_out = jnp.stack([sums_a[3], sums_c[3], sums_d[3]])
    grad_up = jnp.stack([up_b, up_e])
    grad_down = jnp.stack([down_b, down_e])
    tiles = (
        lax.psum_scatter(
            grad_query.astype(jnp.bfloat16), "wide", scatter_dimension=1, tiled=True
        ).astype(jnp.float32),
        lax.psum_scatter(
            grad_kv.astype(jnp.bfloat16), "wide", scatter_dimension=2, tiled=True
        ).astype(jnp.float32),
        lax.psum_scatter(
            grad_out.astype(jnp.bfloat16), "wide", scatter_dimension=2, tiled=True
        ).astype(jnp.float32),
        lax.psum_scatter(
            grad_up.astype(jnp.bfloat16), "wide", scatter_dimension=1, tiled=True
        ).astype(jnp.float32),
        lax.psum_scatter(
            grad_down.astype(jnp.bfloat16), "wide", scatter_dimension=2, tiled=True
        ).astype(jnp.float32),
    )
    tiles = (
        lax.psum(tiles[0].astype(jnp.bfloat16), "dp").astype(jnp.float32),
        lax.psum(tiles[1].astype(jnp.bfloat16), "dp").astype(jnp.float32),
        lax.psum(tiles[2].astype(jnp.bfloat16), "dp").astype(jnp.float32),
        lax.psum(tiles[3].astype(jnp.bfloat16), "dp").astype(jnp.float32),
        lax.psum(tiles[4].astype(jnp.bfloat16), "dp").astype(jnp.float32),
    )
    gain_grads = jnp.stack([gain_a, gain_b, gain_c, gain_d, gain_e, gain_m])
    column = lax.axis_index("narrow") * heads_local
    bias_local = jnp.stack([sums_a[4], sums_c[4]])
    bias_full = lax.dynamic_update_slice(
        jnp.zeros((2, NB, H), jnp.float32), bias_local, (0, 0, column)
    )
    gain_total, bias_total = lax.psum((gain_grads, bias_full), ("dp", "wide", "narrow"))
    bias_grad = lax.dynamic_slice(bias_total, (0, 0, column), (2, NB, heads_local))
    return (
        enc_final.astype(jnp.bfloat16),
        dec_final.astype(jnp.bfloat16),
        grad_enc,
        grad_dec,
        tiles[0],
        tiles[1],
        tiles[2],
        tiles[3],
        tiles[4],
        gain_total,
        bias_grad,
    )


def solution(mesh):
    wide = mesh.shape["wide"]

    def body(*args):
        if args[4].shape[1] % 16 or wide % 2:
            return on_device_general(*args)
        return on_device(wide, *args)

    return jax.shard_map(
        body,
        mesh=mesh,
        in_specs=(
            P(("dp", "wide", "narrow"), None),
            P(("dp", "wide", "narrow"), None),
            P(("dp", "wide"), None),
            P(("dp", "wide"), None),
            P(None, "wide", "narrow"),
            P(None, None, "wide", "narrow"),
            P(None, "narrow", "wide"),
            P(None, "wide", "narrow"),
            P(None, "narrow", "wide"),
            P(),
            P(None, None, "narrow"),
            P(("dp", "wide", "narrow"), None),
            P(("dp", "wide", "narrow"), None),
        ),
        out_specs=(
            P(("dp", "wide", "narrow"), None),
            P(("dp", "wide", "narrow"), None),
            P(("dp", "wide", "narrow"), None),
            P(("dp", "wide", "narrow"), None),
            P(None, "wide", "narrow"),
            P(None, None, "wide", "narrow"),
            P(None, "narrow", "wide"),
            P(None, "wide", "narrow"),
            P(None, "narrow", "wide"),
            P(),
            P(None, None, "narrow"),
        ),
        check_vma=False,
    )
```

```python
import functools
import math

import jax
import jax.numpy as jnp
from jax import lax
from jax.sharding import PartitionSpec as P
import jax.experimental.pallas as pl
import jax.experimental.pallas.tpu as pltpu

H = 12
DK = 64
NB = 32
MAXD = 128
ENC = 1024
DEC = 256


EPS = 1e-06
NEG = -1e30
HIGH = lax.Precision.HIGHEST
VMEM_BYTES = 62 * 2**20
GELU_A = math.sqrt(2.0 / math.pi)
GELU_B = 0.044715


def cutoffs(exact, buckets):
    found = []
    reach = exact
    for target in range(exact + 1, buckets):
        while (
            exact + math.floor(math.log(reach / exact) / math.log(MAXD / exact) * (buckets - exact))
            < target
        ):
            reach = reach + 1
        found.append(reach)
    return found


def bucket_index(relative, two_sided):
    if two_sided:
        width = NB // 2
        offset = jnp.where(relative > 0, width, 0)
        distance = jnp.abs(relative)
    else:
        width = NB
        offset = jnp.zeros_like(relative)
        distance = jnp.maximum(-relative, 0)
    exact = width // 2
    beyond = exact + sum(((distance >= limit).astype(jnp.int32) for limit in cutoffs(exact, width)))
    return offset + jnp.where(distance < exact, distance, beyond)


def segment_ids(lengths, count):
    bounds = jnp.cumsum(lengths)
    places = jnp.arange(count, dtype=jnp.int32)
    return jnp.sum((places[:, None] >= bounds[None, :]).astype(jnp.int32), axis=1)


def rms_norm(values, gain):
    return values * lax.rsqrt(jnp.mean(values * values, axis=-1, keepdims=True) + EPS) * gain


def gelu_tanh(values):
    return jax.nn.gelu(values, approximate=True)


PAIR = 128


def offset_buckets(span, two_sided):
    places = jnp.arange(2 * span, dtype=jnp.int32)[None, :]
    relative = lax.rem(places - jnp.arange(8, dtype=jnp.int32)[:, None] + 2 * span, 2 * span) - span
    buckets = bucket_index(relative.reshape(-1), two_sided)
    return (buckets[None, :] == jnp.arange(NB, dtype=jnp.int32)[:, None]).astype(jnp.bfloat16)


def base_rows(table, span, two_sided):
    heads = table.shape[1]
    rows = lax.dot_general(
        table, offset_buckets(span, two_sided), (((0,), (0,)), ((), ())), preferred_element_type=jnp.float32
    )
    return rows.reshape(heads // 2, 2, 8, 2 * span)


def table_grad(offset_sums, span, two_sided):
    heads = 2 * offset_sums.shape[0]
    return lax.dot_general(
        offset_buckets(span, two_sided).astype(jnp.float32),
        offset_sums.reshape(heads, 16 * span),
        (((1,), (1,)), ((), ())),
        precision=HIGH,
        preferred_element_type=jnp.float32,
    )


def dot_nt(a, b):
    return lax.dot_general(a, b, (((1,), (1,)), ((), ())), preferred_element_type=jnp.float32)


def dot_tn(a, b):
    return lax.dot_general(a, b, (((0,), (0,)), ((), ())), preferred_element_type=jnp.float32)


def dot_nn(a, b):
    return lax.dot_general(a, b, (((1,), (0,)), ((), ())), preferred_element_type=jnp.float32)


def split_heads(block):
    lane = lax.broadcasted_iota(jnp.int32, block.shape, 1)
    zero = jnp.zeros_like(block)
    return jnp.where(lane < DK, block, zero), jnp.where(lane < DK, zero, block)


def attend_kernel(block, keys_count, causal, biased, *refs):
    if biased:
        qseg, kseg, base, q_ref, k_ref, v_ref, e_ref, c_ref, inv_ref, strip = refs
    else:
        qseg, kseg, q_ref, k_ref, v_ref, e_ref, c_ref, inv_ref = refs
    i = pl.program_id(1)
    if biased:
        wide = 2 * keys_count

        @pl.when(i == 0)
        def _():
            for head in range(2):
                rows = base[0, head]
                for a in range(block // 8):
                    strip[head, 8 * a : 8 * a + 8, :] = pltpu.roll(rows, (8 * a + wide - block) % wide, 1)

    allowed = qseg[...] == kseg[...]
    if causal:
        rows = lax.broadcasted_iota(jnp.int32, (block, keys_count), 0) + i * block
        allowed = allowed & (lax.broadcasted_iota(jnp.int32, (block, keys_count), 1) <= rows)
    q_heads = split_heads(q_ref[...])
    v_heads = split_heads(v_ref[...])
    inverses = []
    context = None
    for head in range(2):
        scores = dot_nt(q_heads[head], k_ref[...])
        if biased:
            start = pl.multiple_of((keys_count // block - 1 - i) * block, block)
            scores = scores + strip[head, :, pl.ds(start, keys_count)]
        scores = jnp.where(allowed, scores, NEG)
        highest = jnp.max(scores, axis=1, keepdims=True)
        weights = jnp.exp(scores - highest)
        inverses.append(1.0 / jnp.sum(weights, axis=1, keepdims=True))
        weights = weights.astype(jnp.bfloat16)
        e_ref[head] = weights
        part = dot_nn(weights, v_heads[head])
        context = part if context is None else context + part
    lane = lax.broadcasted_iota(jnp.int32, (block, PAIR), 1)
    inverse = jnp.where(lane < DK, inverses[0], inverses[1])
    inv_ref[...] = inverse
    c_ref[...] = (context * inverse).astype(jnp.bfloat16)


def attend_back_kernel(block, keys_count, steps, biased, *refs):
    if biased:
        q_ref, k_ref, v_ref, e_ref, c_ref, inv_ref, gc_ref, gq_ref, gk_ref, gv_ref, off_ref, gk_sum, gv_sum, strip = refs
    else:
        q_ref, k_ref, v_ref, e_ref, c_ref, inv_ref, gc_ref, gq_ref, gk_ref, gv_ref, gk_sum, gv_sum = refs
    i = pl.program_id(1)

    @pl.when(i == 0)
    def _():
        gk_sum[...] = jnp.zeros_like(gk_sum)
        gv_sum[...] = jnp.zeros_like(gv_sum)
        if biased:
            strip[...] = jnp.zeros_like(strip)

    scaled = (gc_ref[...].astype(jnp.float32) * inv_ref[...]).astype(jnp.bfloat16)
    product = scaled.astype(jnp.float32) * c_ref[...].astype(jnp.float32)
    lane = lax.broadcasted_iota(jnp.int32, (block, PAIR), 1)
    inner = (
        jnp.sum(jnp.where(lane < DK, product, 0.0), axis=1, keepdims=True),
        jnp.sum(jnp.where(lane < DK, 0.0, product), axis=1, keepdims=True),
    )
    g_heads = split_heads(scaled)
    q_heads = split_heads(q_ref[...])
    k_heads = split_heads(k_ref[...])
    gq = None
    for head in range(2):
        weights = e_ref[head]
        grad = dot_nt(g_heads[head], v_ref[...])
        grad = weights.astype(jnp.float32) * (grad - inner[head])
        if biased:
            start = pl.multiple_of((keys_count // block - 1 - i) * block, block)
            strip[head, :, pl.ds(start, keys_count)] += grad
        grad = grad.astype(jnp.bfloat16)
        part = dot_nn(grad, k_heads[head])
        gq = part if gq is None else gq + part
        gk_sum[...] += dot_tn(grad, q_heads[head])
        gv_sum[...] += dot_tn(weights, g_heads[head])
    gq_ref[...] = gq.astype(jnp.bfloat16)

    @pl.when(i == steps - 1)
    def _():
        gk_ref[...] = gk_sum[...].astype(jnp.bfloat16)
        gv_ref[...] = gv_sum[...].astype(jnp.bfloat16)
        if biased:
            wide = 2 * keys_count
            for head in range(2):
                total = jnp.zeros((8, wide), jnp.float32)
                for a in range(block // 8):
                    total = total + pltpu.roll(strip[head, 8 * a : 8 * a + 8, :], (block - 8 * a) % wide, 1)
                off_ref[0, head] = total


def attend_forward(query, keys, values, base, query_segments, key_segments, causal):
    count, cols = query.shape[0], keys.shape[0]
    pairs = query.shape[1] // PAIR
    block = min(256, count)
    steps = count // block
    row_spec = pl.BlockSpec((block, PAIR), lambda h, i: (i, h))
    key_spec = pl.BlockSpec((cols, PAIR), lambda h, i: (0, h))
    in_specs = [
        pl.BlockSpec((block, 1), lambda h, i: (i, 0)),
        pl.BlockSpec((1, cols), lambda h, i: (0, 0)),
    ]
    args = [query_segments[:, None], key_segments[None, :]]
    scratch = []
    if base is not None:
        in_specs.append(pl.BlockSpec((1, 2, 8, 2 * cols), lambda h, i: (h, 0, 0, 0)))
        args.append(base)
        scratch.append(pltpu.VMEM((2, block, 2 * cols), jnp.float32))
    return pl.pallas_call(
        functools.partial(attend_kernel, block, cols, causal, base is not None),
        grid=(pairs, steps),
        in_specs=in_specs + [row_spec, key_spec, key_spec],
        out_specs=[
            pl.BlockSpec((2, block, cols), lambda h, i: (h, i, 0)),
            row_spec,
            row_spec,
        ],
        out_shape=[
            jax.ShapeDtypeStruct((2 * pairs, count, cols), jnp.bfloat16),
            jax.ShapeDtypeStruct((count, pairs * PAIR), jnp.bfloat16),
            jax.ShapeDtypeStruct((count, pairs * PAIR), jnp.float32),
        ],
        scratch_shapes=scratch,
        compiler_params=pltpu.CompilerParams(vmem_limit_bytes=VMEM_BYTES),
        cost_estimate=pl.CostEstimate(
            flops=4 * count * cols * PAIR * 2 * pairs, bytes_accessed=2 * pairs * count * cols * 2, transcendentals=0
        ),
    )(*args, query, keys, values)


def attend_backward(query, keys, values, saved, grad_context, biased):
    weights, context, inverse = saved
    count, cols = query.shape[0], keys.shape[0]
    pairs = query.shape[1] // PAIR
    block = min(256, count)
    steps = count // block
    row_spec = pl.BlockSpec((block, PAIR), lambda h, i: (i, h))
    key_spec = pl.BlockSpec((cols, PAIR), lambda h, i: (0, h))
    out_specs = [row_spec, key_spec, key_spec]
    out_shape = [
        jax.ShapeDtypeStruct((count, pairs * PAIR), jnp.bfloat16),
        jax.ShapeDtypeStruct((cols, pairs * PAIR), jnp.bfloat16),
        jax.ShapeDtypeStruct((cols, pairs * PAIR), jnp.bfloat16),
    ]
    scratch = [pltpu.VMEM((cols, PAIR), jnp.float32), pltpu.VMEM((cols, PAIR), jnp.float32)]
    if biased:
        out_specs.append(pl.BlockSpec((1, 2, 8, 2 * cols), lambda h, i: (h, 0, 0, 0)))
        out_shape.append(jax.ShapeDtypeStruct((pairs, 2, 8, 2 * cols), jnp.float32))
        scratch.append(pltpu.VMEM((2, block, 2 * cols), jnp.float32))
    return pl.pallas_call(
        functools.partial(attend_back_kernel, block, cols, steps, biased),
        grid=(pairs, steps),
        in_specs=[
            row_spec,
            key_spec,
            key_spec,
            pl.BlockSpec((2, block, cols), lambda h, i: (h, i, 0)),
            row_spec,
            row_spec,
            row_spec,
        ],
        out_specs=out_specs,
        out_shape=out_shape,
        scratch_shapes=scratch,
        compiler_params=pltpu.CompilerParams(vmem_limit_bytes=VMEM_BYTES),
        cost_estimate=pl.CostEstimate(
            flops=8 * count * cols * PAIR * 2 * pairs, bytes_accessed=2 * pairs * count * cols * 2, transcendentals=0
        ),
    )(query, keys, values, weights, context, inverse, grad_context)


MESH_IDS = pl.DeviceIdType.MESH
CHUNK = 256
ATT = 4 * 384


def any_spec():
    return pl.BlockSpec(memory_space=pl.ANY)


def vmem_spec():
    return pl.BlockSpec(memory_space=pltpu.VMEM)


def normed(values, gain):
    return values * lax.rsqrt(jnp.mean(values * values, axis=1, keepdims=True) + EPS) * gain


def gelu_pair(values):
    square = values * values
    inner = jnp.tanh(GELU_A * values * (1.0 + GELU_B * square))
    half = 0.5 * (1.0 + inner)
    slope = half + 0.5 * values * (1.0 - inner * inner) * (GELU_A * (1.0 + 3.0 * GELU_B * square))
    return values * half, slope


class Place:
    def __init__(self, wide):
        self.core = lax.axis_index("dp")
        self.wide = lax.axis_index("wide")
        self.side = lax.axis_index("narrow")
        self.count = wide
        self.fars = wide // 2
        self.far = self.wide // 2
        self.near = self.wide % 2

    def sibling(self):
        return (1 - self.core, self.wide, self.side)

    def across(self):
        return (self.core, self.wide, 1 - self.side)

    def beside(self):
        return (self.core, 2 * self.far + 1 - self.near, self.side)

    def along(self, step):
        return (self.core, 2 * lax.rem(self.far + step, self.fars) + self.near, self.side)

    def index_from(self, step):
        return 2 * lax.rem(self.far - step + self.fars, self.fars) + self.near

    def index_beside(self, step):
        return 2 * lax.rem(self.far - step + self.fars, self.fars) + 1 - self.near

    def greet(self):
        partners = [self.sibling(), self.across(), self.beside()]
        partners += [self.along(step) for step in range(1, self.fars)]
        barrier = pltpu.get_barrier_semaphore()
        for partner in partners:
            pl.semaphore_signal(barrier, inc=1, device_id=partner, device_id_type=MESH_IDS)
        pl.semaphore_wait(barrier, len(partners))


def remote(source, target, send, receive, partner):
    return pltpu.make_async_remote_copy(
        src_ref=source,
        dst_ref=target,
        send_sem=send,
        recv_sem=receive,
        device_id=partner,
        device_id_type=MESH_IDS,
    )


class Gather:
    def __init__(self, place, pack, groups, send, receive, local):
        self.place, self.pack, self.groups = place, pack, groups
        self.send, self.receive, self.local = send, receive, local
        self.rows = pack.shape[0]
        self.sent = []

    def at(self, group, index, core):
        first, width, target, offset = self.groups[group]
        half = width // 2
        start = pl.multiple_of(offset + core * half, 128)
        return target.at[pl.ds(pl.multiple_of(index * self.rows, 16), self.rows), pl.ds(start, half)]

    def own(self, group):
        first, width, target, offset = self.groups[group]
        half = width // 2
        return self.pack.at[:, pl.ds(pl.multiple_of(first + self.place.core * half, 128), half)]

    def local_copy(self, group):
        first, width, target, offset = self.groups[group]
        rows = pl.ds(pl.multiple_of(self.place.wide * self.rows, 16), self.rows)
        return pltpu.make_async_copy(
            self.pack.at[:, pl.ds(first, width)], target.at[rows, pl.ds(offset, width)], self.local.at[group]
        )

    def push(self, group, slot, source, index, partner):
        copy = remote(
            source,
            self.at(group, index, self.place.core),
            self.send.at[group, slot],
            self.receive.at[group, slot],
            partner,
        )
        copy.start()
        self.sent.append(copy)

    def await_slot(self, group, slot, index, core):
        block = self.at(group, index, core)
        remote(block, block, self.send.at[group, slot], self.receive.at[group, slot], self.place.sibling()).wait_recv()

    def start(self, group):
        place, fars = self.place, self.place.fars
        for step in range(1, fars):
            self.push(group, step - 1, self.own(group), place.wide, place.along(step))
        self.push(group, fars - 1, self.own(group), place.wide, place.beside())
        self.local_copy(group).start()

    def relay_along(self, group):
        place, fars = self.place, self.place.fars
        for step in range(1, fars):
            index = place.index_from(step)
            self.await_slot(group, step - 1, index, place.core)
            block = self.at(group, index, place.core)
            self.push(group, fars - 1 + step, block, index, place.beside())
            self.push(group, 2 * fars - 2 + step, block, index, place.sibling())

    def relay_beside(self, group):
        place, fars = self.place, self.place.fars
        for step in range(fars):
            index = place.index_beside(step)
            self.await_slot(group, fars - 1 + step, index, place.core)
            block = self.at(group, index, place.core)
            self.push(group, 3 * fars - 2 + step, block, index, place.sibling())

    def finish(self, group):
        place, fars = self.place, self.place.fars
        for step in range(1, fars):
            self.await_slot(group, 2 * fars - 2 + step, place.index_from(step), 1 - place.core)
        for step in range(fars):
            self.await_slot(group, 3 * fars - 2 + step, place.index_beside(step), 1 - place.core)
        self.local_copy(group).wait()

    def close(self):
        for copy in self.sent:
            copy.wait_send()


def gather_slots(wide):
    return 4 * (wide // 2) - 2


def softmax_pair(q_pair, k_pair, v_pair, allowed, biases, e_store):
    q_heads = split_heads(q_pair)
    v_heads = split_heads(v_pair)
    inverses = []
    context = None
    for head in range(2):
        scores = dot_nt(q_heads[head], k_pair)
        if biases is not None:
            scores = scores + biases(head)
        scores = jnp.where(allowed, scores, NEG)
        highest = jnp.max(scores, axis=1, keepdims=True)
        weights = jnp.exp(scores - highest)
        inverses.append(1.0 / jnp.sum(weights, axis=1, keepdims=True))
        weights = weights.astype(jnp.bfloat16)
        e_store(head, weights)
        part = dot_nn(weights, v_heads[head])
        context = part if context is None else context + part
    lane = lax.broadcasted_iota(jnp.int32, context.shape, 1)
    inverse = jnp.where(lane < DK, inverses[0], inverses[1])
    return inverse, (context * inverse).astype(jnp.bfloat16)


def build_strip(strip, base, pairs, block, span):
    def one(pair, carry):
        for head in range(2):
            rows = base[pair, head]
            for a in range(block // 8):
                strip[2 * pair + head, 8 * a : 8 * a + 8, :] = pltpu.roll(rows, (8 * a + 2 * span - block) % (2 * span), 1)
        return carry

    lax.fori_loop(0, pairs, one, 0)


NEAR = 2 * CHUNK
EDGE = NEAR // 4


def near_buckets():
    places = jnp.arange(2 * NEAR, dtype=jnp.int32)[None, :]
    relative = places - jnp.arange(8, dtype=jnp.int32)[:, None] - CHUNK - EDGE
    buckets = bucket_index(relative.reshape(-1), True)
    return (buckets[None, :] == jnp.arange(NB, dtype=jnp.int32)[:, None]).astype(jnp.bfloat16)


def near_rows(table):
    rows = lax.dot_general(
        table, near_buckets(), (((0,), (0,)), ((), ())), preferred_element_type=jnp.float32
    )
    return rows.reshape(table.shape[1] // 2, 2, 8, 2 * NEAR)


def build_near(strip, base, pairs):
    def one(pair, carry):
        for head in range(2):
            rows = base[pair, head]
            for a in range(CHUNK // 8):
                turned = pltpu.roll(rows, (2 * NEAR - CHUNK + 8 * a) % (2 * NEAR), 1)
                strip[2 * pair + head, 8 * a : 8 * a + 8, :] = turned[:, :NEAR]
        return carry

    lax.fori_loop(0, pairs, one, 0)


def near_window(i, rows):
    low, high = max(i * CHUNK - EDGE, 0), min(i * CHUNK + CHUNK + EDGE, rows)
    return low, high, low - (i * CHUNK - EDGE)


def near_bias(strip, base, pair, head, i, rows):
    low, high, shift = near_window(i, rows)
    parts = [strip[2 * pair + head, :, shift : shift + high - low]]
    if low > 0:
        parts.insert(0, jnp.broadcast_to(base[pair, head, 0:1, 0:1], (CHUNK, low)))
    if high < rows:
        parts.append(jnp.broadcast_to(base[pair, head, 0:1, 2 * NEAR - 1 : 2 * NEAR], (CHUNK, rows - high)))
    return jnp.concatenate(parts, axis=1)


def enc_forward_kernel(
    wide,
    x_own,
    dec_own,
    dcot_own,
    cot_own,
    query_in,
    kv_in,
    out_in,
    up_in,
    down_in,
    gains,
    base,
    qseg,
    kseg,
    w1_all,
    w2,
    n0_all,
    qkv_all,
    c_all,
    inv_all,
    e_all,
    e1_all,
    n1_all,
    slope_all,
    a_all,
    ef_all,
    mem_all,
    dec_other,
    dcot_other,
    cot_other,
    pack,
    w1,
    n0,
    qkv,
    c,
    inv,
    e1,
    n1,
    ef,
    mem,
    x_full,
    strip,
    e_buf,
    slope_buf,
    a_buf,
    y_send,
    y_recv,
    g_send,
    g_recv,
    g_local,
    x_sems,
    y_sems,
    z_sems,
    l_sems,
    p_sems,
    o_sems,
):
    place = Place(wide)
    side = place.side
    half = x_own.shape[0]
    rows = 2 * half
    steps = rows // CHUNK
    width = c.shape[1]
    ffn = up_in.shape[2]
    pairs = width // PAIR
    pieces = []
    for layer in range(3):
        first = (0, 4 * width + 2 * ffn, 8 * width + 2 * ffn)[layer]
        pieces += [(query_in.at[layer], first), (kv_in.at[layer, 0], first + width)]
        pieces += [(kv_in.at[layer, 1], first + 2 * width), (out_in.at[layer], first + 3 * width)]
    pieces += [(up_in.at[0], 4 * width), (down_in.at[0], 4 * width + ffn), (up_in.at[1], 12 * width + 2 * ffn)]
    packs = [
        pltpu.make_async_copy(piece, pack.at[:, pl.ds(first, piece.shape[1])], p_sems.at[index])
        for index, (piece, first) in enumerate(pieces)
    ]
    for copy in packs:
        copy.start()
    place.greet()
    gather = Gather(
        place,
        pack,
        [
            (0, 2 * width, w1, 0),
            (2 * width, 2 * width, w1, 2 * width),
            (4 * width, ffn, w1, 4 * width),
            (4 * width + ffn, ffn, w1, 4 * width + ffn),
            (4 * width + 2 * ffn, 4 * width, w2, 0),
            (8 * width + 2 * ffn, 4 * width, w2, 4 * width),
            (12 * width + 2 * ffn, ffn, w2, 8 * width),
        ],
        g_send,
        g_recv,
        g_local,
    )
    mine = pl.ds(pl.multiple_of(side * half, 16), half)
    swap_x = remote(x_own, x_full.at[mine], x_sems.at[0], x_sems.at[1], place.across())
    swap_x.start()
    for copy in packs[:4]:
        copy.wait()
    gather.start(0)
    gather.start(1)
    for copy in packs[4:]:
        copy.wait()
    keep_x = pltpu.make_async_copy(x_own, x_full.at[mine], l_sems.at[6])
    keep_x.start()
    build_near(strip, base, pairs)
    gather.relay_along(0)
    gather.relay_along(1)
    gather.start(2)
    keep_x.wait()
    gather.relay_beside(0)
    gather.relay_beside(1)
    swap_x.wait()
    later = [
        remote(dec_own, dec_other, x_sems.at[2], x_sems.at[3], place.across()),
        remote(dcot_own, dcot_other, x_sems.at[4], x_sems.at[5], place.across()),
        remote(cot_own.at[pl.ds(0, half // 2)], cot_other, x_sems.at[6], x_sems.at[7], place.across()),
    ]
    for copy in later:
        copy.start()
    stores = []

    def store_out(source, target):
        stores.append(pltpu.make_async_copy(source, target, o_sems.at[len(stores)]))
        stores[-1].start()


    def norm_rows(i, carry):
        at = pl.ds(pl.multiple_of(i * CHUNK, CHUNK), CHUNK)
        n0[at, :] = normed(x_full[at, :].astype(jnp.float32), gains[0:1, :]).astype(jnp.bfloat16)
        return carry

    lax.fori_loop(0, steps, norm_rows, 0)
    gather.finish(0)
    gather.finish(1)

    def project(i, carry):
        at = pl.ds(pl.multiple_of(i * CHUNK, CHUNK), CHUNK)
        qkv[at, :] = dot_nn(n0[at, :], w1[:, : 3 * width]).astype(jnp.bfloat16)
        return carry

    lax.fori_loop(0, steps, project, 0)
    store_out(n0, n0_all)
    store_out(qkv, qkv_all)

    def lanes(base_lane, pair):
        return pl.ds(pl.multiple_of(base_lane + pair * PAIR, PAIR), PAIR)

    def save(i, kind):
        slot = i % 2
        at = pl.ds(i * CHUNK, CHUNK)
        if kind == 0:
            return pltpu.make_async_copy(e_buf.at[slot], e_all.at[:, at, :], l_sems.at[slot])
        if kind == 1:
            return pltpu.make_async_copy(slope_buf.at[slot], slope_all.at[at, :], l_sems.at[2 + slot])
        return pltpu.make_async_copy(a_buf.at[slot], a_all.at[at, :], l_sems.at[4 + slot])

    def swap_y(layer, i):
        at = pl.ds(i * CHUNK, CHUNK)
        sems = y_sems if layer == 0 else z_sems
        return remote(y_send.at[layer, at], y_recv.at[layer, at], sems.at[0, i], sems.at[1, i], place.across())

    def attend(i):
        at = pl.ds(i * CHUNK, CHUNK)
        slot = i % 2
        if i >= 2:
            save(i - 2, 0).wait()

        def one(pair, carry):
            allowed = qseg[at, :] == kseg[...]

            def bias(head):
                return near_bias(strip, base, pair, head, i, rows)

            def store(head, weights):
                e_buf[slot, 2 * pair + head] = weights

            inverse, context = softmax_pair(
                qkv[at, lanes(0, pair)],
                qkv[:, lanes(width, pair)],
                qkv[:, lanes(2 * width, pair)],
                allowed,
                bias,
                store,
            )
            inv[at, lanes(0, pair)] = inverse
            c[at, lanes(0, pair)] = context
            return carry

        lax.fori_loop(0, pairs, one, 0)
        save(i, 0).start()
        store_out(c.at[at], c_all.at[at])
        store_out(inv.at[at], inv_all.at[at])
        y_send[0, at, :] = dot_nt(c[at, :], w1[:, 3 * width : 4 * width]).astype(jnp.bfloat16)
        swap_y(0, i).start()

    def feed(i):
        at = pl.ds(i * CHUNK, CHUNK)
        slot = i % 2
        swap_y(0, i).wait_recv()
        both = y_send[0, at, :].astype(jnp.float32) + y_recv[0, at, :].astype(jnp.float32)
        middle = x_full[at, :].astype(jnp.float32) + both
        e1[at, :] = middle
        rounded = normed(middle, gains[1:2, :]).astype(jnp.bfloat16)
        n1[at, :] = rounded
        store_out(e1.at[at], e1_all.at[at])
        store_out(n1.at[at], n1_all.at[at])
        if i >= 2:
            save(i - 2, 1).wait()
            save(i - 2, 2).wait()

        def part(j, carry):
            cols = pl.ds(pl.multiple_of(4 * width + j * width, PAIR), width)
            here = pl.ds(pl.multiple_of(j * width, PAIR), width)
            active, slope = gelu_pair(dot_nn(n1[at, :], w1[:, cols]))
            a_buf[slot, :, here] = active.astype(jnp.bfloat16)
            slope_buf[slot, :, here] = slope.astype(jnp.bfloat16)
            return carry

        lax.fori_loop(0, ffn // width, part, 0)
        save(i, 1).start()
        save(i, 2).start()
        y_send[1, at, :] = dot_nt(a_buf[slot], w1[:, 4 * width + ffn :]).astype(jnp.bfloat16)
        swap_y(1, i).start()

    def last(i):
        at = pl.ds(i * CHUNK, CHUNK)
        swap_y(1, i).wait_recv()
        both = y_send[1, at, :].astype(jnp.float32) + y_recv[1, at, :].astype(jnp.float32)
        final = e1[at, :] + both
        ef[at, :] = final
        mem[at, :] = normed(final, gains[5:6, :]).astype(jnp.bfloat16)
        store_out(ef.at[at], ef_all.at[at])
        store_out(mem.at[at], mem_all.at[at])

    gather.start(3)
    gather.relay_along(2)
    attend(0)
    gather.start(4)
    gather.relay_along(3)
    gather.relay_beside(2)
    attend(1)
    gather.start(5)
    gather.relay_along(4)
    gather.relay_beside(3)
    gather.finish(2)
    attend(2)
    gather.finish(3)
    store_out(w1, w1_all)
    feed(0)
    gather.start(6)
    gather.relay_along(5)
    gather.relay_beside(4)
    attend(3)
    feed(1)
    gather.relay_beside(5)
    gather.relay_along(6)
    feed(2)
    feed(3)
    last(0)
    gather.relay_beside(6)
    last(1)
    last(2)
    last(3)
    for group in range(4, 7):
        gather.finish(group)
    gather.close()
    for copy in later:
        copy.wait()
    for copy in stores:
        copy.wait()
    for i in range(steps):
        swap_y(0, i).wait_send()
        swap_y(1, i).wait_send()
    for i in range(steps - 2, steps):
        for kind in range(3):
            save(i, kind).wait()


def enc_forward(wide, x_own, dec_own, dcot_own, cot_own, weights, gains, base, segments):
    half, model = x_own.shape
    rows = 2 * half
    pairs = base.shape[0]
    width = pairs * PAIR
    ffn = weights[3].shape[2]
    bf, f32 = jnp.bfloat16, jnp.float32
    shape = jax.ShapeDtypeStruct
    dma = pltpu.SemaphoreType.DMA
    slots = gather_slots(wide)
    steps = rows // CHUNK
    saved = [
        ((model, 4 * width + 2 * ffn), bf),
        ((rows, model), bf),
        ((rows, 3 * width), bf),
        ((rows, width), bf),
        ((rows, width), f32),
        ((rows, model), f32),
        ((rows, model), bf),
        ((rows, model), f32),
        ((rows, model), bf),
    ]
    kept = [shape(*pair) for pair in saved]
    out_shape = (
        [kept[0], shape((model, 8 * width + ffn), bf)]
        + kept[1:5]
        + [shape((2 * pairs, rows, rows), bf)]
        + kept[5:7]
        + [shape((rows, ffn), bf), shape((rows, ffn), bf)]
        + kept[7:]
        + [shape(dec_own.shape, bf), shape(dcot_own.shape, bf), shape((half // 2, model), bf)]
    )
    return pl.pallas_call(
        functools.partial(enc_forward_kernel, wide),
        in_specs=[vmem_spec()] + [any_spec()] * 8 + [vmem_spec()] * 4,
        out_shape=out_shape,
        out_specs=[any_spec()] * len(out_shape),
        scratch_shapes=[pltpu.VMEM((x_own.shape[1] // wide, 12 * width + 3 * ffn), bf)]
        + [pltpu.VMEM(*pair) for pair in saved]
        + [
            pltpu.VMEM((rows, model), bf),
            pltpu.VMEM((2 * pairs, CHUNK, NEAR), f32),
            pltpu.VMEM((2, 2 * pairs, CHUNK, rows), bf),
            pltpu.VMEM((2, CHUNK, ffn), bf),
            pltpu.VMEM((2, CHUNK, ffn), bf),
            pltpu.VMEM((2, rows, model), bf),
            pltpu.VMEM((2, rows, model), bf),
            dma((7, slots)),
            dma((7, slots)),
            dma((7,)),
            dma((8,)),
            dma((2, steps)),
            dma((2, steps)),
            dma((7,)),
            dma((15,)),
            dma((3 + 6 * steps,)),
        ],
        compiler_params=pltpu.CompilerParams(
            collective_id=0, has_side_effects=True, vmem_limit_bytes=VMEM_BYTES
        ),
        cost_estimate=pl.CostEstimate(flops=10**10, bytes_accessed=6 * 10**7, transcendentals=0),
    )(x_own, dec_own, dcot_own, cot_own, *weights, gains, base, segments[:, None], segments[None, :])


def norm_back(values, gain, grad):
    scale = lax.rsqrt(jnp.mean(values * values, axis=1, keepdims=True) + EPS)
    scaled = grad * gain
    pulled = scale * (scaled - values * (scale * scale) * jnp.mean(scaled * values, axis=1, keepdims=True))
    return pulled, jnp.sum(grad * values * scale, axis=0, keepdims=True)


class Scatter:
    def __init__(self, place, rows, groups, tile, send, receive):
        self.place, self.rows, self.groups, self.tile = place, rows, groups, tile
        self.send, self.receive = send, receive
        self.sent = []

    def columns(self, group, core):
        first, width = self.groups[group]["first"], self.groups[group]["width"]
        if self.groups[group]["core"] is None:
            return pl.ds(first, width // 2)
        return pl.ds(pl.multiple_of(first + core * (width // 2), 128), width // 2)

    def block(self, group, index):
        return self.groups[group]["grad"].at[
            pl.ds(pl.multiple_of(index * self.rows, 16), self.rows), self.columns(group, self.place.core)
        ]

    def push(self, group, slot, source, target, partner, arrival=None):
        arrival = slot if arrival is None else arrival
        copy = remote(source, target, self.send.at[group, slot], self.receive.at[group, arrival], partner)
        copy.start()
        self.sent.append(copy)

    def await_slot(self, group, slot, block):
        remote(block, block, self.send.at[group, 0], self.receive.at[group, slot], self.place.sibling()).wait_recv()

    def start(self, group):
        parts = self.groups[group]
        self.push(
            group, 0, parts["grad"].at[:, self.columns(group, 1 - self.place.core)], parts["core"], self.place.sibling()
        )

    def add_block(self, group, index, other):
        block = self.block(group, index)
        block[...] = (block[...].astype(jnp.float32) + other.astype(jnp.float32)).astype(jnp.bfloat16)
        return block

    def merge(self, group):
        parts = self.groups[group]
        self.await_slot(group, 0, parts["core"])
        for index in range(self.place.count):
            self.add_block(group, index, parts["core"][index * self.rows : (index + 1) * self.rows, :])

    def beside(self, group):
        parts, place = self.groups[group], self.place
        if parts["core"] is None:
            for step in range(place.fars):
                index = 2 * lax.rem(place.far + 1 + step, place.fars) + 1 - place.near
                self.push(group, 1 + step, self.block(group, index), parts["beside"].at[step], place.beside())
            return
        self.await_slot(group, 0, parts["core"])

        def received(index):
            return parts["core"][pl.ds(pl.multiple_of(index * self.rows, 16), self.rows), :]

        for step in range(place.fars):
            far = lax.rem(place.far + 1 + step, place.fars)
            index = 2 * far + 1 - place.near
            block = self.add_block(group, index, received(index))
            self.push(group, 1 + step, block, parts["beside"].at[step], place.beside())
        for step in range(place.fars):
            far = lax.rem(place.far + 1 + step, place.fars)
            index = 2 * far + place.near
            self.add_block(group, index, received(index))

    def along(self, group):
        parts, place = self.groups[group], self.place
        for step in range(1, place.fars):
            index = 2 * lax.rem(place.far + step, place.fars) + place.near
            self.await_slot(group, step, parts["beside"].at[step - 1])
            block = self.add_block(group, index, parts["beside"][step - 1])
            self.push(group, place.fars + step, block, parts["along"].at[step - 1], place.along(step))

    def total(self, group):
        parts, place = self.groups[group], self.place
        self.await_slot(group, place.fars, parts["beside"].at[place.fars - 1])
        value = self.block(group, place.wide)[...].astype(jnp.float32) + parts["beside"][place.fars - 1].astype(jnp.float32)
        for step in range(1, place.fars):
            self.await_slot(group, place.fars + step, parts["along"].at[step - 1])
            value = value + parts["along"][step - 1].astype(jnp.float32)
        half = parts["width"] // 2
        block = self.tile.at[:, pl.ds(pl.multiple_of(parts["out"] + place.core * half, 128), half)]
        block[...] = value.astype(jnp.bfloat16)
        self.push(group, 2 * place.fars, block, block, place.sibling())

    def finish(self, group):
        parts, place = self.groups[group], self.place
        half = parts["width"] // 2
        block = self.tile.at[:, pl.ds(pl.multiple_of(parts["out"] + (1 - place.core) * half, 128), half)]
        self.await_slot(group, 2 * place.fars, block)

    def close(self):
        for copy in self.sent:
            copy.wait_send()


def half_group(grad, first, width, out, part, core, beside, along):
    at = pl.ds(part * (width // 2), width // 2)
    return dict(
        grad=grad,
        first=first,
        width=width,
        out=out,
        core=core.at[:, at],
        beside=beside.at[:, :, at],
        along=along.at[:, :, at],
    )


def scatter_slots(wide):
    return 2 * (wide // 2) + 1


def scatter_buffers(wide, model, width):
    half, rows, fars = width // 2, model // wide, wide // 2
    return [
        pltpu.VMEM((model, half), jnp.bfloat16),
        pltpu.VMEM((fars, rows, half), jnp.bfloat16),
        pltpu.VMEM((fars - 1, rows, half), jnp.bfloat16),
    ]


def softmax_back_pair(q_pair, k_pair, v_pair, c_pair, inverse, gc_pair, weights, near):
    scaled = (gc_pair.astype(jnp.float32) * inverse).astype(jnp.bfloat16)
    product = scaled.astype(jnp.float32) * c_pair.astype(jnp.float32)
    lane = lax.broadcasted_iota(jnp.int32, product.shape, 1)
    inner = (
        jnp.sum(jnp.where(lane < DK, product, 0.0), axis=1, keepdims=True),
        jnp.sum(jnp.where(lane < DK, 0.0, product), axis=1, keepdims=True),
    )
    g_heads = split_heads(scaled)
    q_heads = split_heads(q_pair)
    k_heads = split_heads(k_pair)
    gq = None
    grads = []
    for head in range(2):
        grad = weights[head].astype(jnp.float32) * (dot_nt(g_heads[head], v_pair) - inner[head])
        if near is not None:
            near(head, grad)
        grad = grad.astype(jnp.bfloat16)
        grads.append(grad)
        part = dot_nn(grad, k_heads[head])
        gq = part if gq is None else gq + part
    gk = dot_tn(jnp.concatenate(grads, axis=0), jnp.concatenate(q_heads, axis=0))
    gv = dot_tn(jnp.concatenate([weights[0], weights[1]], axis=0), jnp.concatenate(g_heads, axis=0))
    return gq, gk, gv


def fold_near(rows):
    total = jnp.zeros((8, 2 * NEAR), jnp.float32)
    blank = jnp.zeros((8, NEAR), jnp.float32)
    for a in range(CHUNK // 8):
        wider = jnp.concatenate([rows[8 * a : 8 * a + 8, :], blank], axis=1)
        total = total + pltpu.roll(wider, (CHUNK - 8 * a) % (2 * NEAR), 1)
    return total


def bucket_sums(rows, offset, two_sided):
    span = rows.shape[1]
    relative = lax.broadcasted_iota(jnp.int32, (span, 128), 0) - offset
    onehot = bucket_index(relative, two_sided) == lax.broadcasted_iota(jnp.int32, (span, 128), 1)
    return lax.dot_general(
        rows,
        onehot.astype(jnp.float32),
        (((1,), (0,)), ((), ())),
        precision=HIGH,
        preferred_element_type=jnp.float32,
    )


def fold_rows(rows):
    span = rows.shape[1]
    total = rows[0:1, :]
    for b in range(1, 8):
        total = total + pltpu.roll(rows, span - b, 1)[b : b + 1, :]
    return total


class Total:
    def __init__(self, place, held, send, receive):
        self.place, self.held, self.send, self.receive = place, held, send, receive
        partners = (place.sibling(), place.across(), place.beside())
        self.copies = [
            remote(held.at[stage], held.at[4 + stage], send.at[stage], receive.at[stage], partner)
            for stage, partner in enumerate(partners)
        ]
        self.last = [
            remote(held.at[3], held.at[7 + place.far], send.at[2 + step], receive.at[2 + step], place.along(step))
            for step in range(1, place.fars)
        ]

    def start(self):
        self.copies[0].start()

    def step(self, stage):
        held = self.held
        self.copies[stage].wait()
        held[stage + 1] = held[stage] + held[4 + stage]
        for copy in [self.copies[stage + 1]] if stage < 2 else self.last:
            copy.start()

    def finish(self):
        for copy in self.last:
            copy.wait()
        result = None
        for far in range(self.place.fars):
            part = jnp.where(self.place.far == far, self.held[3], self.held[7 + far])
            result = part if result is None else result + part
        return result


def enc_backward_kernel(
    wide,
    x_own,
    cot_own,
    cot_first,
    cot_second,
    gains,
    dec_gains,
    dec_table,
    part_own,
    part_other,
    dw1_in,
    w1_in,
    n0_in,
    qkv_in,
    c_in,
    inv_in,
    e_all,
    e1_all,
    n1_in,
    slope_all,
    a_in,
    ef_all,
    grad_out,
    tile,
    total_sums,
    part_late,
    gain_sums,
    far_sums,
    folded,
    held,
    w1,
    dw1,
    qkv,
    c,
    inv,
    n1,
    active,
    cot,
    e_buf,
    state_buf,
    slope_buf,
    part_buf,
    other_buf,
    g_send,
    g_recv,
    l_recv,
    state_grad,
    gy,
    gu,
    gqkv,
    gk_sum,
    gv_sum,
    strip,
    core_f,
    beside_f,
    along_f,
    beside_a,
    along_a,
    beside_d,
    along_d,
    s_send,
    s_recv,
    t_send,
    t_recv,
    m_sems,
    g_sems,
    l_sems,
    e_sems,
    t_sems,
    i_sems,
):
    place = Place(wide)
    side = place.side
    half = x_own.shape[0]
    rows = 2 * half
    steps = rows // CHUNK
    width = c.shape[1]
    ffn = active.shape[1]
    pairs = width // PAIR
    model = x_own.shape[1]
    bf, f32 = jnp.bfloat16, jnp.float32
    place.greet()

    def swap(i):
        at = pl.ds(i * CHUNK, CHUNK)
        return remote(g_send.at[at], g_recv.at[at], g_sems.at[0, i], g_sems.at[1, i], place.across())

    late = part_late.shape[0] // CHUNK

    def swap_late(i):
        return remote(
            part_own.at[pl.ds((steps - late + i) * CHUNK, CHUNK)],
            part_late.at[pl.ds(i * CHUNK, CHUNK)],
            m_sems.at[0, i],
            m_sems.at[1, i],
            place.across(),
        )

    for i in range(late):
        swap_late(i).start()

    def other_part(i):
        if i < steps - late:
            return part_other.at[pl.ds(i * CHUNK, CHUNK)]
        return part_late.at[pl.ds((i - steps + late) * CHUNK, CHUNK)]

    def fetch(i):
        at = pl.ds(i * CHUNK, CHUNK)
        slot = i % 2
        return [
            pltpu.make_async_copy(ef_all.at[at], state_buf.at[slot], t_sems.at[0, slot]),
            pltpu.make_async_copy(slope_all.at[at], slope_buf.at[slot], t_sems.at[1, slot]),
            pltpu.make_async_copy(part_own.at[at], part_buf.at[slot], t_sems.at[2, slot]),
            pltpu.make_async_copy(other_part(i), other_buf.at[slot], t_sems.at[3, slot]),
        ]

    def fetch_state(i):
        at = pl.ds(i * CHUNK, CHUNK)
        return pltpu.make_async_copy(e1_all.at[at], state_buf.at[i % 2], t_sems.at[0, i % 2])

    def fetch_e(step):
        chunk, pair, slot = step // pairs, lax.rem(step, pairs), lax.rem(step, 2)
        at = pl.ds(pl.multiple_of(chunk * CHUNK, CHUNK), CHUNK)
        return pltpu.make_async_copy(e_all.at[pl.ds(2 * pair, 2), at, :], e_buf.at[slot], e_sems.at[slot])

    mine = pl.ds(pl.multiple_of(side * half, 16), half)
    quarter = half // 2
    theirs_first = pl.ds(pl.multiple_of((1 - side) * half, 16), quarter)
    theirs_second = pl.ds(pl.multiple_of((1 - side) * half + quarter, 16), quarter)
    loads = [
        pltpu.make_async_copy(cot_own, cot.at[mine], i_sems.at[0]),
        pltpu.make_async_copy(cot_first, cot.at[theirs_first], i_sems.at[1]),
        pltpu.make_async_copy(w1_in, w1, i_sems.at[2]),
        pltpu.make_async_copy(a_in, active, i_sems.at[3]),
        pltpu.make_async_copy(n1_in, n1, i_sems.at[4]),
        pltpu.make_async_copy(qkv_in, qkv, i_sems.at[5]),
        pltpu.make_async_copy(c_in, c, i_sems.at[6]),
        pltpu.make_async_copy(inv_in, inv, i_sems.at[7]),
        pltpu.make_async_copy(dw1_in, dw1, i_sems.at[8]),
        pltpu.make_async_copy(cot_second, cot.at[theirs_second], i_sems.at[9]),
    ]
    loads[8].start()
    for index in (0, 1, 9):
        loads[index].start()
    for load in fetch(0):
        load.start()
    for load in loads[2:8]:
        load.start()
    gk_sum[...] = jnp.zeros_like(gk_sum)
    gv_sum[...] = jnp.zeros_like(gv_sum)
    strip[...] = jnp.zeros_like(strip)
    far_sums[...] = jnp.zeros_like(far_sums)
    gain_sums[...] = jnp.zeros_like(gain_sums)
    out_c = 4 * width + 2 * ffn
    core_a = active.at[pl.ds(0, model), pl.ds(0, 2 * width)]
    scatter = Scatter(
        place,
        model // wide,
        [
            dict(grad=dw1, first=0, width=4 * width, out=out_c, core=None, beside=beside_a, along=along_a),
            dict(grad=dw1, first=2 * width, width=4 * width, out=out_c + 4 * width, core=None, beside=beside_d, along=along_d),
            half_group(w1, 4 * width, ffn, 4 * width, 0, core_f, beside_f, along_f),
            half_group(w1, 4 * width + ffn, ffn, 4 * width + ffn, 1, core_f, beside_f, along_f),
            half_group(gu.at[pl.ds(0, model)], 0, 2 * width, 0, 0, core_a, beside_a, along_a),
            half_group(gu.at[pl.ds(0, model)], 2 * width, 2 * width, 2 * width, 1, core_a, beside_a, along_a),
        ],
        tile,
        s_send,
        s_recv,
    )

    def own_weight(i):
        return jnp.where((i * CHUNK) // half == side, 1.0, 0.0).astype(f32)

    loads[8].wait()
    scatter.beside(0)
    scatter.beside(1)
    for index in (0, 1, 9, 2):
        loads[index].wait()

    for i in range(steps):
        at = slice(i * CHUNK, (i + 1) * CHUNK)
        slot = i % 2
        if i + 1 < steps:
            if i + 1 >= steps - late:
                swap_late(i + 1 - steps + late).wait_recv()
            for load in fetch(i + 1):
                load.start()
        for load in fetch(i):
            load.wait()
        grad = part_buf[slot].astype(f32) + other_buf[slot].astype(f32)
        pulled, gain = norm_back(state_buf[slot], gains[5:6, :], grad)
        gain_sums[5:6, :] += gain * own_weight(i)
        total = cot[at, :].astype(f32) + pulled
        state_grad[at, :] = total
        gy[at, :] = total.astype(bf)

        def part(j, carry):
            cols = pl.ds(pl.multiple_of(4 * width + ffn + j * width, PAIR), width)
            here = pl.ds(pl.multiple_of(j * width, PAIR), width)
            grad_active = dot_nn(gy[at, :], w1[:, cols])
            gu[at, here] = (slope_buf[slot, :, here].astype(f32) * grad_active).astype(bf)
            return carry

        lax.fori_loop(0, ffn // width, part, 0)
        g_send[at, :] = dot_nt(gu[at, :], w1[:, 4 * width : 4 * width + ffn]).astype(bf)
        swap(i).start()
    for load in loads[3:8]:
        load.wait()
    fetch_state(0).start()
    fetch_e(0).start()

    def up_grads(t, carry):
        tile_rows = pl.ds(pl.multiple_of(t * CHUNK, CHUNK), CHUNK)
        w1[tile_rows, 4 * width : 4 * width + ffn] = dot_tn(n1[:, tile_rows], gu[...]).astype(bf)
        return carry

    def down_grads(t, carry):
        tile_rows = pl.ds(pl.multiple_of(t * CHUNK, CHUNK), CHUNK)
        w1[tile_rows, 4 * width + ffn :] = dot_tn(gy[:, tile_rows], active[...]).astype(bf)
        return carry

    scatter.along(0)
    lax.fori_loop(0, model // CHUNK, up_grads, 0)
    scatter.start(2)
    lax.fori_loop(0, model // CHUNK, down_grads, 0)
    scatter.start(3)
    scatter.along(1)
    scatter.total(0)
    scatter.beside(2)
    n0 = cot
    late_loads = [
        pltpu.make_async_copy(n0_in, n0, i_sems.at[0]),
        pltpu.make_async_copy(x_own, n1.at[pl.ds(half, half)], i_sems.at[1]),
    ]
    for load in late_loads:
        load.start()

    dw0 = gu
    l_send = n1

    def lanes(base_lane, pair):
        return pl.ds(pl.multiple_of(base_lane + pair * PAIR, PAIR), PAIR)

    def attend_back(i):
        at = slice(i * CHUNK, (i + 1) * CHUNK)
        slot = i % 2
        if i + 1 < steps:
            fetch_state(i + 1).start()
        fetch_state(i).wait()
        swap(i).wait_recv()
        grad = g_send[at, :].astype(f32) + g_recv[at, :].astype(f32)
        pulled, gain = norm_back(state_buf[slot], gains[1:2, :], grad)
        gain_sums[1:2, :] += gain * own_weight(i)
        total = state_grad[at, :] + pulled
        state_grad[at, :] = total
        gy[at, :] = total.astype(bf)
        g_send[at, :width] = dot_nn(gy[at, :], w1[:, 3 * width : 4 * width]).astype(bf)
        low, high, shift = near_window(i, rows)

        def one(pair, carry):
            step = i * pairs + pair

            @pl.when(step + 1 < steps * pairs)
            def _():
                fetch_e(step + 1).start()

            fetch_e(step).wait()
            e_slot = lax.rem(step, 2)

            def near(head, grad):
                strip[2 * pair + head, :, shift : shift + high - low] += grad[:, low:high]
                for edge, (start, end) in enumerate(((0, low), (high, rows))):
                    if end > start:
                        folded = jnp.sum(grad[:, start:end].reshape(CHUNK // 8, 8, end - start), axis=0)
                        wide_sum = folded[:, :128]
                        for lane in range(128, end - start, 128):
                            wide_sum = wide_sum + folded[:, lane : lane + 128]
                        far_sums[edge, 2 * pair + head] += wide_sum

            gq, gk, gv = softmax_back_pair(
                qkv[at, lanes(0, pair)],
                qkv[:, lanes(width, pair)],
                qkv[:, lanes(2 * width, pair)],
                c[at, lanes(0, pair)],
                inv[at, lanes(0, pair)],
                g_send[at, lanes(0, pair)],
                (e_buf[e_slot, 0], e_buf[e_slot, 1]),
                near,
            )
            gqkv[at, lanes(0, pair)] = gq.astype(bf)
            gk_sum[:, lanes(0, pair)] += gk
            gv_sum[:, lanes(0, pair)] += gv
            return carry

        lax.fori_loop(0, pairs, one, 0)

    for i in range(steps):
        swap(i).wait_send()
        attend_back(i)
        if i == 0:
            scatter.beside(3)
        if i == 1:
            scatter.total(1)
            scatter.along(2)
        if i == 2:
            scatter.along(3)
        if i == 3:
            scatter.total(2)
    for load in late_loads:
        load.wait()
    gqkv[:, width : 2 * width] = gk_sum[...].astype(bf)
    gqkv[:, 2 * width :] = gv_sum[...].astype(bf)

    ones = jnp.ones((8, 3 * width), f32)

    def weight_grads_a(t, carry):
        tile_rows = pl.ds(pl.multiple_of(t * CHUNK, CHUNK), CHUNK)
        grads = dot_tn(n0[:, tile_rows], gqkv[...])
        dw0[tile_rows, : 3 * width] = grads.astype(bf)
        products = lax.dot_general(
            ones,
            grads * w1[tile_rows, : 3 * width].astype(f32),
            (((1,), (1,)), ((), ())),
            precision=HIGH,
            preferred_element_type=f32,
        )
        gain_sums[0:1, tile_rows] = products[0:1, :] / gains[0:1, tile_rows]
        return carry

    def weight_grads_o(t, carry):
        tile_rows = pl.ds(pl.multiple_of(t * CHUNK, CHUNK), CHUNK)
        dw0[tile_rows, 3 * width :] = dot_tn(gy[:, tile_rows], c[...]).astype(bf)
        return carry

    lax.fori_loop(0, model // CHUNK, weight_grads_a, 0)
    scatter.start(4)
    last = []
    for part in range(half // CHUNK):
        there = pl.ds(pl.multiple_of((1 - side) * half + part * CHUNK, CHUNK), CHUNK)
        at = pl.ds(part * CHUNK, CHUNK)
        l_send[at, :] = dot_nt(gqkv[there, :], w1[:, : 3 * width]).astype(bf)
        last.append(remote(l_send.at[at], l_recv.at[at], l_sems.at[0, part], l_sems.at[1, part], place.across()))
        last[part].start()
    lax.fori_loop(0, model // CHUNK, weight_grads_o, 0)
    scatter.start(5)
    scatter.beside(4)
    summed = Total(place, held, t_send, t_recv)
    folded[...] = jnp.zeros_like(folded)

    def fold(head, carry):
        folded[pl.ds(head, 1), :] = fold_rows(fold_near(strip[head]))
        return carry

    lax.fori_loop(0, 2 * pairs, fold, 0)
    table = bucket_sums(folded[...], CHUNK + EDGE, True)
    bucket = lax.broadcasted_iota(jnp.int32, (1, 128), 1)
    for head in range(2 * pairs):
        far = [jnp.sum(far_sums[edge, head]) for edge in range(2)]
        folded[head : head + 1, :128] = jnp.where(
            bucket == NB // 2 - 1, far[0], jnp.where(bucket == NB - 1, far[1], 0.0)
        )
    table = table + folded[:, :128]
    held[0] = jnp.zeros_like(held[0])
    held[0, :8, :] = gain_sums[...] + dec_gains[...]
    held[0, 8:, pl.ds(pl.multiple_of(side * 256, 128), 128)] = table
    held[0, 8:, pl.ds(pl.multiple_of(side * 256 + 128, 128), 128)] = dec_table[...]
    summed.start()
    scatter.beside(5)
    summed.step(0)
    scatter.along(4)
    summed.step(1)
    scatter.total(3)
    for part in range(half // CHUNK):
        here = pl.ds(pl.multiple_of(side * half + part * CHUNK, CHUNK), CHUNK)
        at = pl.ds(part * CHUNK, CHUNK)
        own = dot_nt(gqkv[here, :], w1[:, : 3 * width])
        if part == 0:
            scatter.along(5)
            summed.step(2)
        last[part].wait_recv()
        grad = own + l_recv[at, :].astype(f32)
        pulled, unused = norm_back(n1[pl.ds(half + part * CHUNK, CHUNK), :].astype(f32), gains[0:1, :], grad)
        grad_out[at, :] = state_grad[here, :] + pulled
    scatter.total(4)
    scatter.total(5)
    total_sums[...] = summed.finish()
    for group in range(6):
        scatter.finish(group)
    scatter.close()
    for i in range(late):
        swap_late(i).wait_send()
    for copy in last:
        copy.wait_send()


def enc_backward(wide, x_own, cot_own, cot_first, cot_second, gains, dec_gains, dec_table, part_own, part_other, dw1, saved):
    half, model = x_own.shape
    rows = 2 * half
    w1, n0, qkv, c, inv, e_all, e1, n1, slope, active, ef = saved
    width, ffn = c.shape[1], active.shape[1]
    pairs = width // PAIR
    steps = rows // CHUNK
    bf, f32 = jnp.bfloat16, jnp.float32
    shape = jax.ShapeDtypeStruct
    dma = pltpu.SemaphoreType.DMA
    return pl.pallas_call(
        functools.partial(enc_backward_kernel, wide),
        in_specs=[any_spec()] * 4 + [vmem_spec()] * 3 + [any_spec()] * 14,
        out_shape=[
            shape((half, model), f32),
            shape((model // wide, 12 * width + 2 * ffn), bf),
            shape((16, model), f32),
            shape((rows - part_other.shape[0], model), bf),
        ],
        out_specs=[vmem_spec()] * 3 + [any_spec()],
        scratch_shapes=[
            pltpu.VMEM((8, model), f32),
            pltpu.VMEM((2, 2 * pairs, 8, 128), f32),
            pltpu.VMEM((8, 2 * NEAR), f32),
            pltpu.VMEM((7 + wide // 2, 16, model), f32),
            pltpu.VMEM(w1.shape, bf),
            pltpu.VMEM(dw1.shape, bf),
            pltpu.VMEM(qkv.shape, bf),
            pltpu.VMEM(c.shape, bf),
            pltpu.VMEM(inv.shape, f32),
            pltpu.VMEM(n1.shape, bf),
            pltpu.VMEM(active.shape, bf),
            pltpu.VMEM((rows, model), bf),
            pltpu.VMEM((2, 2, CHUNK, rows), bf),
            pltpu.VMEM((2, CHUNK, model), f32),
            pltpu.VMEM((2, CHUNK, ffn), bf),
            pltpu.VMEM((2, CHUNK, model), bf),
            pltpu.VMEM((2, CHUNK, model), bf),
            pltpu.VMEM((rows, model), bf),
            pltpu.VMEM((rows, model), bf),
            pltpu.VMEM((half, model), bf),
            pltpu.VMEM((rows, model), f32),
            pltpu.VMEM((rows, model), bf),
            pltpu.VMEM((rows, ffn), bf),
            pltpu.VMEM((rows, 3 * width), bf),
            pltpu.VMEM((rows, width), f32),
            pltpu.VMEM((rows, width), f32),
            pltpu.VMEM((2 * pairs, CHUNK, NEAR), f32),
        ]
        + scatter_buffers(wide, model, 2 * ffn)
        + scatter_buffers(wide, model, 4 * width)[1:]
        + scatter_buffers(wide, model, 4 * width)[1:]
        + [
            dma((6, scatter_slots(wide))),
            dma((6, scatter_slots(wide))),
            dma((2 + wide // 2,)),
            dma((2 + wide // 2,)),
            dma((2, steps)),
            dma((2, steps)),
            dma((2, half // CHUNK)),
            dma((2,)),
            dma((4, 2)),
            dma((10,)),
        ],
        compiler_params=pltpu.CompilerParams(
            collective_id=1, has_side_effects=True, vmem_limit_bytes=VMEM_BYTES
        ),
        cost_estimate=pl.CostEstimate(flops=2 * 10**10, bytes_accessed=6 * 10**7, transcendentals=0),
    )(x_own, cot_own, cot_first, cot_second, gains, dec_gains, dec_table, part_own, part_other, dw1, w1, n0, qkv, c, inv, e_all, e1, n1, slope, active, ef)


def fold_offsets(grad):
    rows = grad.shape[0]
    total = jnp.zeros((8, 2 * rows), jnp.float32)
    blank = jnp.zeros((8, rows), jnp.float32)
    for a in range(rows // 8):
        wider = jnp.concatenate([grad[8 * a : 8 * a + 8, :], blank], axis=1)
        total = total + pltpu.roll(wider, (rows - 8 * a) % (2 * rows), 1)
    return total


def decoder_kernel(
    wide,
    dec_own,
    dec_other,
    dcot_own,
    dcot_other,
    cot_own,
    down_in,
    gains,
    base,
    qseg,
    kseg,
    mseg,
    mem_in,
    w_in,
    dec_out,
    dec_grad,
    tile,
    gain_sums,
    table,
    part_own,
    part_other,
    cot_other,
    dw1_all,
    pack,
    folded,
    w,
    mem,
    dec,
    dcot,
    state,
    normals,
    qkv,
    c,
    inv,
    e_self,
    e_cross,
    strip,
    kv,
    active,
    ga,
    gu,
    grad_state,
    gy,
    gqkv,
    gkv,
    y_send,
    y_recv,
    dw,
    core_f,
    beside_f,
    along_f,
    core_d,
    core_c,
    s_send,
    s_recv,
    g_send,
    g_recv,
    g_local,
    y_sems,
    x_sems,
    p_sems,
    o_sems,
    i_sems,
):
    place = Place(wide)
    side = place.side
    half = dec_own.shape[0]
    rows = 2 * half
    model = dec_own.shape[1]
    width = c.shape[2]
    ffn = active.shape[1]
    pairs = width // PAIR
    span = mem.shape[0]
    bf, f32 = jnp.bfloat16, jnp.float32
    place.greet()
    mine = pl.ds(pl.multiple_of(side * half, 16), half)
    theirs = pl.ds(pl.multiple_of((1 - side) * half, 16), half)
    at_d, at_f = 4 * width, 8 * width

    gather = Gather(place, pack, [(0, ffn // 2, w, at_f + ffn), (ffn // 2, ffn // 2, w, at_f + ffn + ffn // 2)], g_send, g_recv, g_local)
    def load_w(first, count, sem):
        cols = pl.ds(first, count)
        return pltpu.make_async_copy(w_in.at[:, cols], w.at[:, cols], i_sems.at[sem])

    loads = [
        load_w(0, 4 * width, 0),
        load_w(at_d, 4 * width, 1),
        pltpu.make_async_copy(mem_in, mem, i_sems.at[2]),
        load_w(at_f, ffn, 3),
        pltpu.make_async_copy(dec_own, dec.at[mine], i_sems.at[4]),
        pltpu.make_async_copy(dcot_own, dcot.at[mine], i_sems.at[5]),
        pltpu.make_async_copy(dec_other, dec.at[theirs], i_sems.at[6]),
        pltpu.make_async_copy(dcot_other, dcot.at[theirs], i_sems.at[7]),
        pltpu.make_async_copy(down_in, pack, i_sems.at[8]),
    ]
    for index in (8, 4, 6, 0, 5, 7, 2, 1, 3):
        loads[index].start()
    rest = cot_other.shape[0]
    swap_cot = remote(
        cot_own.at[pl.ds(cot_own.shape[0] - rest, rest)], cot_other, x_sems.at[0], x_sems.at[1], place.across()
    )
    swap_cot.start()
    loads[8].wait()
    gather.start(0)
    gather.start(1)
    build_strip(strip, base, pairs, rows, rows)
    gain_sums[...] = jnp.zeros_like(gain_sums)
    folded[...] = jnp.zeros_like(folded)
    scatter = Scatter(
        place,
        model // wide,
        [
            half_group(w, at_f, ffn, 0, 0, core_f, beside_f, along_f),
            half_group(w, at_f + ffn, ffn, ffn, 1, core_f, beside_f, along_f),
            dict(grad=dw, first=at_d, width=4 * width, core=core_d),
            dict(grad=dw, first=0, width=4 * width, core=core_c),
        ],
        tile,
        s_send,
        s_recv,
    )

    def swap(kind):
        return remote(y_send.at[kind], y_recv.at[kind], y_sems.at[0, kind], y_sems.at[1, kind], place.across())

    def send_branch(kind, value):
        y_send[kind] = value.astype(bf)
        swap(kind).start()

    def branch(kind):
        swap(kind).wait_recv()
        return y_send[kind].astype(f32) + y_recv[kind].astype(f32)

    def lanes(base_lane, pair):
        return pl.ds(pl.multiple_of(base_lane + pair * PAIR, PAIR), PAIR)

    def norm_to(index, gain, value):
        state[index] = value
        normals[index] = normed(value, gains[gain : gain + 1, :]).astype(bf)

    loads[4].wait()
    loads[6].wait()
    norm_to(0, 2, dec[...].astype(f32))
    loads[0].wait()
    qkv[:, : 3 * width] = dot_nn(normals[0], w[:, : 3 * width]).astype(bf)

    def self_pair(pair, carry):
        allowed = qseg[...] == kseg[...]
        allowed = allowed & (
            lax.broadcasted_iota(jnp.int32, (rows, rows), 1) <= lax.broadcasted_iota(jnp.int32, (rows, rows), 0)
        )

        def bias(head):
            return strip[2 * pair + head, :, :rows]

        def store(head, weights):
            e_self[2 * pair + head] = weights

        inverse, context = softmax_pair(
            qkv[:, lanes(0, pair)], qkv[:, lanes(width, pair)], qkv[:, lanes(2 * width, pair)], allowed, bias, store
        )
        inv[0, :, lanes(0, pair)] = inverse
        c[0, :, lanes(0, pair)] = context
        return carry

    lax.fori_loop(0, pairs, self_pair, 0)
    send_branch(0, dot_nt(c[0], w[:, 3 * width : 4 * width]))

    gather.relay_along(0)
    gather.relay_along(1)

    loads[2].wait()
    loads[1].wait()

    def cross_keys(i, carry):
        at = pl.ds(pl.multiple_of(i * CHUNK, CHUNK), CHUNK)
        kv[at, :] = dot_nn(mem[at, :], w[:, at_d + width : at_d + 3 * width]).astype(bf)
        return carry

    lax.fori_loop(0, span // CHUNK, cross_keys, 0)
    gather.relay_beside(0)
    gather.relay_beside(1)
    norm_to(1, 3, state[0] + branch(0))
    qkv[:, 3 * width :] = dot_nn(normals[1], w[:, at_d : at_d + width]).astype(bf)

    def cross_pair(pair, carry):
        allowed = qseg[...] == mseg[...]

        def store(head, weights):
            e_cross[2 * pair + head] = weights

        inverse, context = softmax_pair(
            qkv[:, lanes(3 * width, pair)], kv[:, lanes(0, pair)], kv[:, lanes(width, pair)], allowed, None, store
        )
        inv[1, :, lanes(0, pair)] = inverse
        c[1, :, lanes(0, pair)] = context
        return carry

    lax.fori_loop(0, pairs, cross_pair, 0)
    send_branch(1, dot_nt(c[1], w[:, at_d + 3 * width : at_d + 4 * width]))

    for index in (5, 7, 3):
        loads[index].wait()
    gather.finish(0)
    gather.finish(1)
    ga[...] = dot_nn(dcot[...], w[:, at_f + ffn :]).astype(f32)
    norm_to(2, 4, state[1] + branch(1))

    def hidden(j, carry):
        here = pl.ds(pl.multiple_of(j * width, PAIR), width)
        cols = pl.ds(pl.multiple_of(at_f + j * width, PAIR), width)
        value, turn = gelu_pair(dot_nn(normals[2], w[:, cols]))
        active[:, here] = value.astype(bf)
        gu[:, here] = (turn * ga[:, here]).astype(bf)
        return carry

    lax.fori_loop(0, ffn // width, hidden, 0)
    send_branch(3, dot_nt(gu[...], w[:, at_f : at_f + ffn]))
    y_send[2] = dot_nt(active[...], w[:, at_f + ffn :]).astype(bf)

    def up_grads(t, carry):
        tile_rows = pl.ds(pl.multiple_of(t * CHUNK, CHUNK), CHUNK)
        w[tile_rows, at_f : at_f + ffn] = dot_tn(normals[2, :, tile_rows], gu[...]).astype(bf)
        return carry

    def down_grads(t, carry):
        tile_rows = pl.ds(pl.multiple_of(t * CHUNK, CHUNK), CHUNK)
        w[tile_rows, at_f + ffn :] = dot_tn(dcot[:, tile_rows], active[...]).astype(bf)
        return carry

    gather.close()
    lax.fori_loop(0, model // CHUNK, up_grads, 0)
    scatter.start(0)
    lax.fori_loop(0, model // CHUNK, down_grads, 0)
    scatter.start(1)
    scatter.beside(0)

    row = lax.broadcasted_iota(jnp.int32, (rows, 1), 0)
    counted = jnp.where(row // half == side, 1.0, 0.0).astype(f32)

    def pull(index, gain, grad):
        values = state[index]
        pulled, unused = norm_back(values, gains[gain : gain + 1, :], grad)
        scale = lax.rsqrt(jnp.mean(values * values, axis=1, keepdims=True) + EPS) * counted
        gain_sums[gain : gain + 1, :] += jnp.sum(grad * values * scale, axis=0, keepdims=True)
        return pulled

    grad_state[...] = dcot[...].astype(f32) + pull(2, 4, branch(3))
    swap(2).start()
    gy[1] = grad_state[...].astype(bf)
    gc = dot_nn(gy[1], w[:, at_d + 3 * width : at_d + 4 * width]).astype(bf)
    y_send[5, :, :width] = gc
    scatter.beside(1)

    def cross_back(pair, carry):
        gq, gk, gv = softmax_back_pair(
            qkv[:, lanes(3 * width, pair)],
            kv[:, lanes(0, pair)],
            kv[:, lanes(width, pair)],
            c[1, :, lanes(0, pair)],
            inv[1, :, lanes(0, pair)],
            y_send[5, :, lanes(0, pair)],
            (e_cross[2 * pair], e_cross[2 * pair + 1]),
            None,
        )
        gqkv[:, lanes(3 * width, pair)] = gq.astype(bf)
        gkv[:, lanes(0, pair)] = gk.astype(bf)
        gkv[:, lanes(width, pair)] = gv.astype(bf)
        return carry

    lax.fori_loop(0, pairs, cross_back, 0)
    send_branch(4, dot_nt(gqkv[:, 3 * width :], w[:, at_d : at_d + width]))

    part = kv

    def swap_part(i):
        at = pl.ds(pl.multiple_of(i * CHUNK, CHUNK), CHUNK)
        return remote(part.at[at], part_other.at[at], p_sems.at[0, i], p_sems.at[1, i], place.across())

    def keep_part(i):
        at = pl.ds(pl.multiple_of(i * CHUNK, CHUNK), CHUNK)
        return pltpu.make_async_copy(part.at[at], part_own.at[at], o_sems.at[i])

    for i in range(span // CHUNK):
        at = pl.ds(i * CHUNK, CHUNK)
        part[at, :] = dot_nt(gkv[at, :], w[:, at_d + width : at_d + 3 * width]).astype(bf)
        keep_part(i).start()

    def cross_grads(t, carry):
        tile_rows = pl.ds(pl.multiple_of(t * CHUNK, CHUNK), CHUNK)
        dw[tile_rows, at_d : at_d + width] = dot_tn(normals[1, :, tile_rows], gqkv[:, 3 * width :]).astype(bf)
        dw[tile_rows, at_d + width : at_d + 3 * width] = dot_tn(mem[:, tile_rows], gkv[...]).astype(bf)
        dw[tile_rows, at_d + 3 * width : at_f] = dot_tn(gy[1, :, tile_rows], c[1]).astype(bf)
        return carry

    lax.fori_loop(0, model // CHUNK, cross_grads, 0)
    scatter.start(2)
    scatter.along(0)

    grad_state[...] = grad_state[...] + pull(1, 3, branch(4))
    early = part_other.shape[0] // CHUNK
    swap_part(0).start()
    gy[0] = grad_state[...].astype(bf)
    y_send[5, :, :width] = dot_nn(gy[0], w[:, 3 * width : 4 * width]).astype(bf)

    def self_back(pair, carry):
        def near(head, grad):
            folded[pl.ds(2 * pair + head, 1), :] = fold_rows(fold_offsets(grad))

        gq, gk, gv = softmax_back_pair(
            qkv[:, lanes(0, pair)],
            qkv[:, lanes(width, pair)],
            qkv[:, lanes(2 * width, pair)],
            c[0, :, lanes(0, pair)],
            inv[0, :, lanes(0, pair)],
            y_send[5, :, lanes(0, pair)],
            (e_self[2 * pair], e_self[2 * pair + 1]),
            near,
        )
        gqkv[:, lanes(0, pair)] = gq.astype(bf)
        gqkv[:, lanes(width, pair)] = gk.astype(bf)
        gqkv[:, lanes(2 * width, pair)] = gv.astype(bf)
        return carry

    lax.fori_loop(0, pairs, self_back, 0)

    y_send[5] = dot_nt(gqkv[:, : 3 * width], w[:, : 3 * width]).astype(bf)
    back = remote(y_send.at[5, theirs], y_recv.at[5, theirs], y_sems.at[0, 5], y_sems.at[1, 5], place.across())
    back.start()
    for i in range(1, early):
        swap_part(i).start()
    scatter.along(1)
    scatter.merge(2)
    keep_dw = [
        pltpu.make_async_copy(
            dw.at[:, scatter.columns(2 + i, place.core)],
            dw1_all.at[:, pl.ds((1 - i) * 2 * width, 2 * width)],
            i_sems.at[i],
        )
        for i in range(2)
    ]
    keep_dw[0].start()

    def self_grads(t, carry):
        tile_rows = pl.ds(pl.multiple_of(t * CHUNK, CHUNK), CHUNK)
        dw[tile_rows, : 3 * width] = dot_tn(normals[0, :, tile_rows], gqkv[:, : 3 * width]).astype(bf)
        dw[tile_rows, 3 * width : at_d] = dot_tn(gy[0, :, tile_rows], c[0]).astype(bf)
        return carry

    lax.fori_loop(0, model // CHUNK, self_grads, 0)
    scatter.start(3)
    table[...] = bucket_sums(folded[...], rows, False)
    scatter.total(0)
    scatter.total(1)
    back.wait_recv()
    grad = y_send[5, mine, :].astype(f32) + y_recv[5, mine, :].astype(f32)
    pulled, gain = norm_back(state[0, mine, :], gains[2:3, :], grad)
    gain_sums[2:3, :] += gain
    dec_grad[...] = grad_state[mine, :] + pulled
    swap(2).wait_recv()
    dec_out[...] = (state[2, mine, :] + y_send[2, mine, :].astype(f32) + y_recv[2, mine, :].astype(f32)).astype(bf)
    scatter.merge(3)
    keep_dw[1].start()
    for i in range(early):
        swap_part(i).wait()
    for i in range(span // CHUNK):
        keep_part(i).wait()
    for copy in keep_dw:
        copy.wait()
    swap_cot.wait()
    for group in range(2):
        scatter.finish(group)
    scatter.close()
    for kind in range(5):
        swap(kind).wait_send()
    back.wait_send()


def decoder(wide, dec_rows, dcot_rows, cot_own, down, gains, base, dec_segments, enc_segments, mem, w2):
    half, model = dec_rows[0].shape
    rows = 2 * half
    span = mem.shape[0]
    pairs = base.shape[0]
    width = pairs * PAIR
    ffn = down.shape[1]
    late = span // CHUNK // 2 * CHUNK
    bf, f32 = jnp.bfloat16, jnp.float32
    shape = jax.ShapeDtypeStruct
    dma = pltpu.SemaphoreType.DMA
    return pl.pallas_call(
        functools.partial(decoder_kernel, wide),
        in_specs=[any_spec()] * 6 + [vmem_spec()] * 5 + [any_spec()] * 2,
        out_shape=[
            shape((half, model), bf),
            shape((half, model), f32),
            shape((model // wide, 2 * ffn), bf),
            shape((8, model), f32),
            shape((8, 128), f32),
            shape((span, model), bf),
            shape((late, model), bf),
            shape((cot_own.shape[0] // 2, model), bf),
            shape((model, 4 * width), bf),
        ],
        out_specs=[vmem_spec()] * 5 + [any_spec()] * 4,
        scratch_shapes=[
            pltpu.VMEM(down.shape, bf),
            pltpu.VMEM((8, 2 * rows), f32),
            pltpu.VMEM((model, 8 * width + 2 * ffn), bf),
            pltpu.VMEM((span, model), bf),
            pltpu.VMEM((rows, model), bf),
            pltpu.VMEM((rows, model), bf),
            pltpu.VMEM((3, rows, model), f32),
            pltpu.VMEM((3, rows, model), bf),
            pltpu.VMEM((rows, 4 * width), bf),
            pltpu.VMEM((2, rows, width), bf),
            pltpu.VMEM((2, rows, width), f32),
            pltpu.VMEM((2 * pairs, rows, rows), bf),
            pltpu.VMEM((2 * pairs, rows, span), bf),
            pltpu.VMEM((2 * pairs, rows, 2 * rows), f32),
            pltpu.VMEM((span, 2 * width), bf),
            pltpu.VMEM((rows, ffn), bf),
            pltpu.VMEM((rows, ffn), f32),
            pltpu.VMEM((rows, ffn), bf),
            pltpu.VMEM((rows, model), f32),
            pltpu.VMEM((2, rows, model), bf),
            pltpu.VMEM((rows, 4 * width), bf),
            pltpu.VMEM((span, 2 * width), bf),
            pltpu.VMEM((6, rows, model), bf),
            pltpu.VMEM((6, rows, model), bf),
            pltpu.VMEM((model, 8 * width), bf),
        ]
        + scatter_buffers(wide, model, 2 * ffn)
        + scatter_buffers(wide, model, 4 * width)[:1]
        + scatter_buffers(wide, model, 4 * width)[:1]
        + [
            dma((4, scatter_slots(wide))),
            dma((4, scatter_slots(wide))),
            dma((2, gather_slots(wide))),
            dma((2, gather_slots(wide))),
            dma((2,)),
            dma((2, 6)),
            dma((2,)),
            dma((2, span // CHUNK)),
            dma((span // CHUNK,)),
            dma((9,)),
        ],
        compiler_params=pltpu.CompilerParams(
            collective_id=2, has_side_effects=True, vmem_limit_bytes=VMEM_BYTES
        ),
        cost_estimate=pl.CostEstimate(flops=10**10, bytes_accessed=6 * 10**7, transcendentals=0),
    )(
        *dec_rows,
        *dcot_rows,
        cot_own,
        down,
        gains,
        base,
        dec_segments[:, None],
        dec_segments[None, :],
        enc_segments[None, :],
        mem,
        w2,
    )


def on_device(
    wide,
    enc_input,
    dec_input,
    enc_lengths,
    dec_lengths,
    attn_query,
    attn_kv,
    attn_out,
    ffn_up,
    ffn_down,
    gains,
    rel_bias,
    enc_cotangent,
    dec_cotangent,
):
    gain_rows = gains.astype(jnp.float32)
    heads_local = rel_bias.shape[2]
    enc_segments = segment_ids(enc_lengths[0], ENC)
    dec_segments = segment_ids(dec_lengths[0], DEC)
    side = lax.axis_index("narrow")
    width, ffn = DK * heads_local, ffn_up.shape[2]
    half = enc_input.shape[0]
    down = ffn_down.transpose(0, 2, 1)
    weights = (attn_query, attn_kv, attn_out.transpose(0, 2, 1), ffn_up, down)
    w1, w2, n0, qkv, context, inverse, exps, e1, n1, slope, active, ef, memory, dec_other, dcot_other, cot_first = enc_forward(
        wide, enc_input, dec_input, dec_cotangent, enc_cotangent, weights, gain_rows, near_rows(rel_bias[0]), enc_segments
    )
    dec_output, grad_dec, tile_two, dec_gains, dec_table, part_own, part_other, cot_second, dw1 = decoder(
        wide,
        (dec_input, dec_other),
        (dec_cotangent, dcot_other),
        enc_cotangent,
        down[1],
        gain_rows,
        base_rows(rel_bias[1], DEC, False),
        dec_segments,
        enc_segments,
        memory,
        w2,
    )
    grad_enc, tile_one, sums, unused = enc_backward(
        wide,
        enc_input,
        enc_cotangent,
        cot_first,
        cot_second,
        gain_rows,
        dec_gains,
        dec_table,
        part_own,
        part_other,
        dw1,
        (w1, n0, qkv, context, inverse, exps, e1, n1, slope, active, ef),
    )
    tables = lax.dynamic_slice_in_dim(sums[8 : 8 + heads_local], side * 256, 256, 1)
    bias_grad = jnp.stack([tables[:, :NB].T, tables[:, 128 : 128 + NB].T])
    tile_one, tile_two = tile_one.astype(jnp.float32), tile_two.astype(jnp.float32)
    late = tile_one[:, 4 * width + 2 * ffn :]
    layers = (tile_one[:, : 4 * width], late[:, : 4 * width], late[:, 4 * width :])
    feeds = (tile_one[:, 4 * width : 4 * width + 2 * ffn], tile_two)
    return (
        lax.dynamic_slice_in_dim(ef, side * half, half).astype(jnp.bfloat16),
        dec_output,
        grad_enc,
        grad_dec,
        jnp.stack([layer[:, :width] for layer in layers]),
        jnp.stack([jnp.stack([layer[:, width : 2 * width], layer[:, 2 * width : 3 * width]]) for layer in layers]),
        jnp.stack([layer[:, 3 * width :].T for layer in layers]),
        jnp.stack([feed[:, :ffn] for feed in feeds]),
        jnp.stack([feed[:, ffn:].T for feed in feeds]),
        sums[:6],
        bias_grad,
    )


def ffn_backward(grad_rows, normed_rows, hidden, active, weight_up, weight_down):
    grad_active = jnp.einsum(
        "rd,fd->rf", grad_rows, weight_down, preferred_element_type=jnp.float32
    )
    grad_down = jnp.einsum("rf,rd->fd", active, grad_rows, preferred_element_type=jnp.float32)
    unused, pull = jax.vjp(gelu_tanh, hidden)
    grad_hidden = pull(grad_active)[0].astype(jnp.bfloat16)
    grad_up = jnp.einsum("rd,rf->df", normed_rows, grad_hidden, preferred_element_type=jnp.float32)
    grad_normed = jnp.einsum(
        "rf,df->rd", grad_hidden, weight_up, preferred_element_type=jnp.float32
    )
    return (grad_normed, grad_up, grad_down)


def norm_backward(values, gain, grad_normed):
    unused, pull = jax.vjp(rms_norm, values, gain)
    return pull(grad_normed)


def on_device_general(
    enc_input,
    dec_input,
    enc_lengths,
    dec_lengths,
    attn_query,
    attn_kv,
    attn_out,
    ffn_up,
    ffn_down,
    gains,
    rel_bias,
    enc_cotangent,
    dec_cotangent,
):
    weights = (
        lax.all_gather(attn_query, "wide", axis=1, tiled=True),
        lax.all_gather(attn_kv, "wide", axis=2, tiled=True),
        lax.all_gather(attn_out, "wide", axis=2, tiled=True),
        lax.all_gather(ffn_up, "wide", axis=1, tiled=True),
        lax.all_gather(ffn_down, "wide", axis=2, tiled=True),
    )
    gain_rows = gains.astype(jnp.float32)
    heads_local = rel_bias.shape[2]
    enc_segments = segment_ids(enc_lengths[0], ENC)
    dec_segments = segment_ids(dec_lengths[0], DEC)

    side = lax.axis_index("narrow")
    swap = [(0, 1), (1, 0)]

    def spread_rows(values):
        own = values.astype(jnp.bfloat16)
        other = lax.ppermute(own, "narrow", swap)
        return jnp.where(side == 0, jnp.concatenate([own, other]), jnp.concatenate([other, own]))

    def collect_rows(parts):
        half = parts.shape[0] // 2
        parts = parts.astype(jnp.bfloat16)
        other = lax.ppermute(lax.dynamic_slice_in_dim(parts, (1 - side) * half, half), "narrow", swap)
        own = lax.dynamic_slice_in_dim(parts, side * half, half)
        return own.astype(jnp.float32) + other.astype(jnp.float32)

    def attention_layer(normed_query, normed_keys, layer, base, query_segments, key_segments, causal):
        query = jnp.dot(normed_query, weights[0][layer], preferred_element_type=jnp.float32).astype(jnp.bfloat16)
        keys = jnp.dot(normed_keys, weights[1][layer, 0], preferred_element_type=jnp.float32).astype(jnp.bfloat16)
        values = jnp.dot(normed_keys, weights[1][layer, 1], preferred_element_type=jnp.float32).astype(jnp.bfloat16)
        saved = attend_forward(query, keys, values, base, query_segments, key_segments, causal)
        parts = jnp.dot(saved[1], weights[2][layer], preferred_element_type=jnp.float32)
        return ((query, keys, values, saved), collect_rows(parts))

    enc_start = enc_input.astype(jnp.float32)
    rows_a = spread_rows(rms_norm(enc_start, gain_rows[0]))
    kept_a, branch = attention_layer(
        rows_a, rows_a, 0, base_rows(rel_bias[0], ENC, True), enc_segments, enc_segments, False
    )
    enc_mid = enc_start + branch
    rows_b = spread_rows(rms_norm(enc_mid, gain_rows[1]))
    hidden_b = jnp.dot(rows_b, weights[3][0], preferred_element_type=jnp.float32)
    active_b = gelu_tanh(hidden_b).astype(jnp.bfloat16)
    enc_final = enc_mid + collect_rows(
        jnp.dot(active_b, weights[4][0], preferred_element_type=jnp.float32)
    )
    memory = spread_rows(rms_norm(enc_final, gain_rows[5]))
    dec_start = dec_input.astype(jnp.float32)
    rows_c = spread_rows(rms_norm(dec_start, gain_rows[2]))
    kept_c, branch = attention_layer(
        rows_c, rows_c, 1, base_rows(rel_bias[1], DEC, False), dec_segments, dec_segments, True
    )
    dec_one = dec_start + branch
    rows_d = spread_rows(rms_norm(dec_one, gain_rows[3]))
    kept_d, branch = attention_layer(
        rows_d, memory, 2, None, dec_segments, enc_segments, False
    )
    dec_two = dec_one + branch
    rows_e = spread_rows(rms_norm(dec_two, gain_rows[4]))
    hidden_e = jnp.dot(rows_e, weights[3][1], preferred_element_type=jnp.float32)
    active_e = gelu_tanh(hidden_e).astype(jnp.bfloat16)
    dec_final = dec_two + collect_rows(
        jnp.dot(active_e, weights[4][1], preferred_element_type=jnp.float32)
    )
    def attention_back(grad_state, kept, normed_query, normed_keys, layer, span, two_sided):
        grad_rows = spread_rows(grad_state)
        query, keys, values, saved = kept
        grad_context = dot_nt(grad_rows, weights[2][layer]).astype(jnp.bfloat16)
        grad_out = dot_tn(saved[1], grad_rows)
        result = attend_backward(query, keys, values, saved, grad_context, span > 0)
        grad_q, grad_k, grad_v = result[:3]
        sums = [
            dot_tn(normed_query, grad_q),
            dot_tn(normed_keys, grad_k),
            dot_tn(normed_keys, grad_v),
            grad_out,
            table_grad(result[3], span, two_sided) if span else None,
        ]
        query_part = dot_nt(grad_q, weights[0][layer])
        key_part = dot_nt(grad_k, weights[1][layer, 0]) + dot_nt(grad_v, weights[1][layer, 1])
        return (query_part, key_part, sums)

    grad_dec = dec_cotangent.astype(jnp.float32)
    grad_normed, up_e, down_e = ffn_backward(
        spread_rows(grad_dec), rows_e, hidden_e, active_e, weights[3][1], weights[4][1]
    )
    grad_back, gain_e = norm_backward(dec_two, gain_rows[4], collect_rows(grad_normed))
    grad_dec = grad_dec + grad_back
    query_part, memory_part, sums_d = attention_back(
        grad_dec, kept_d, rows_d, memory, 2, 0, False
    )
    grad_normed, grad_memory = collect_rows(query_part), collect_rows(memory_part)
    grad_back, gain_d = norm_backward(dec_one, gain_rows[3], grad_normed)
    grad_dec = grad_dec + grad_back
    query_part, key_part, sums_c = attention_back(
        grad_dec, kept_c, rows_c, rows_c, 1, DEC, False
    )
    grad_back, gain_c = norm_backward(dec_start, gain_rows[2], collect_rows(query_part + key_part))
    grad_dec = grad_dec + grad_back
    grad_enc = enc_cotangent.astype(jnp.float32)
    grad_back, gain_m = norm_backward(enc_final, gain_rows[5], grad_memory)
    grad_enc = grad_enc + grad_back
    grad_normed, up_b, down_b = ffn_backward(
        spread_rows(grad_enc), rows_b, hidden_b, active_b, weights[3][0], weights[4][0]
    )
    grad_back, gain_b = norm_backward(enc_mid, gain_rows[1], collect_rows(grad_normed))
    grad_enc = grad_enc + grad_back
    query_part, key_part, sums_a = attention_back(
        grad_enc, kept_a, rows_a, rows_a, 0, ENC, True
    )
    grad_back, gain_a = norm_backward(enc_start, gain_rows[0], collect_rows(query_part + key_part))
    grad_enc = grad_enc + grad_back
    grad_query = jnp.stack([sums_a[0], sums_c[0], sums_d[0]])
    grad_kv = jnp.stack(
        [
            jnp.stack([sums_a[1], sums_a[2]]),
            jnp.stack([sums_c[1], sums_c[2]]),
            jnp.stack([sums_d[1], sums_d[2]]),
        ]
    )
    grad_out = jnp.stack([sums_a[3], sums_c[3], sums_d[3]])
    grad_up = jnp.stack([up_b, up_e])
    grad_down = jnp.stack([down_b, down_e])
    tiles = (
        lax.psum_scatter(
            grad_query.astype(jnp.bfloat16), "wide", scatter_dimension=1, tiled=True
        ).astype(jnp.float32),
        lax.psum_scatter(
            grad_kv.astype(jnp.bfloat16), "wide", scatter_dimension=2, tiled=True
        ).astype(jnp.float32),
        lax.psum_scatter(
            grad_out.astype(jnp.bfloat16), "wide", scatter_dimension=2, tiled=True
        ).astype(jnp.float32),
        lax.psum_scatter(
            grad_up.astype(jnp.bfloat16), "wide", scatter_dimension=1, tiled=True
        ).astype(jnp.float32),
        lax.psum_scatter(
            grad_down.astype(jnp.bfloat16), "wide", scatter_dimension=2, tiled=True
        ).astype(jnp.float32),
    )
    tiles = (
        lax.psum(tiles[0].astype(jnp.bfloat16), "dp").astype(jnp.float32),
        lax.psum(tiles[1].astype(jnp.bfloat16), "dp").astype(jnp.float32),
        lax.psum(tiles[2].astype(jnp.bfloat16), "dp").astype(jnp.float32),
        lax.psum(tiles[3].astype(jnp.bfloat16), "dp").astype(jnp.float32),
        lax.psum(tiles[4].astype(jnp.bfloat16), "dp").astype(jnp.float32),
    )
    gain_grads = jnp.stack([gain_a, gain_b, gain_c, gain_d, gain_e, gain_m])
    column = lax.axis_index("narrow") * heads_local
    bias_local = jnp.stack([sums_a[4], sums_c[4]])
    bias_full = lax.dynamic_update_slice(
        jnp.zeros((2, NB, H), jnp.float32), bias_local, (0, 0, column)
    )
    gain_total, bias_total = lax.psum((gain_grads, bias_full), ("dp", "wide", "narrow"))
    bias_grad = lax.dynamic_slice(bias_total, (0, 0, column), (2, NB, heads_local))
    return (
        enc_final.astype(jnp.bfloat16),
        dec_final.astype(jnp.bfloat16),
        grad_enc,
        grad_dec,
        tiles[0],
        tiles[1],
        tiles[2],
        tiles[3],
        tiles[4],
        gain_total,
        bias_grad,
    )


def solution(mesh):
    wide = mesh.shape["wide"]

    def body(*args):
        if args[4].shape[1] % 16 or wide % 2:
            return on_device_general(*args)
        return on_device(wide, *args)

    return jax.shard_map(
        body,
        mesh=mesh,
        in_specs=(
            P(("dp", "wide", "narrow"), None),
            P(("dp", "wide", "narrow"), None),
            P(("dp", "wide"), None),
            P(("dp", "wide"), None),
            P(None, "wide", "narrow"),
            P(None, None, "wide", "narrow"),
            P(None, "narrow", "wide"),
            P(None, "wide", "narrow"),
            P(None, "narrow", "wide"),
            P(),
            P(None, None, "narrow"),
            P(("dp", "wide", "narrow"), None),
            P(("dp", "wide", "narrow"), None),
        ),
        out_specs=(
            P(("dp", "wide", "narrow"), None),
            P(("dp", "wide", "narrow"), None),
            P(("dp", "wide", "narrow"), None),
            P(("dp", "wide", "narrow"), None),
            P(None, "wide", "narrow"),
            P(None, None, "wide", "narrow"),
            P(None, "narrow", "wide"),
            P(None, "wide", "narrow"),
            P(None, "narrow", "wide"),
            P(),
            P(None, None, "narrow"),
        ),
        check_vma=False,
    )
```

```python
import functools
import math

import jax
import jax.numpy as jnp
from jax import lax
from jax.sharding import PartitionSpec as P
import jax.experimental.pallas as pl
import jax.experimental.pallas.tpu as pltpu

H = 12
DK = 64
NB = 32
MAXD = 128
ENC = 1024
DEC = 256


EPS = 1e-06
NEG = -1e30
HIGH = lax.Precision.HIGHEST
VMEM_BYTES = 62 * 2**20
GELU_A = math.sqrt(2.0 / math.pi)
GELU_B = 0.044715


def cutoffs(exact, buckets):
    found = []
    reach = exact
    for target in range(exact + 1, buckets):
        while (
            exact + math.floor(math.log(reach / exact) / math.log(MAXD / exact) * (buckets - exact))
            < target
        ):
            reach = reach + 1
        found.append(reach)
    return found


def bucket_index(relative, two_sided):
    if two_sided:
        width = NB // 2
        offset = jnp.where(relative > 0, width, 0)
        distance = jnp.abs(relative)
    else:
        width = NB
        offset = jnp.zeros_like(relative)
        distance = jnp.maximum(-relative, 0)
    exact = width // 2
    beyond = exact + sum(((distance >= limit).astype(jnp.int32) for limit in cutoffs(exact, width)))
    return offset + jnp.where(distance < exact, distance, beyond)


def segment_ids(lengths, count):
    bounds = jnp.cumsum(lengths)
    places = jnp.arange(count, dtype=jnp.int32)
    return jnp.sum((places[:, None] >= bounds[None, :]).astype(jnp.int32), axis=1)


def rms_norm(values, gain):
    return values * lax.rsqrt(jnp.mean(values * values, axis=-1, keepdims=True) + EPS) * gain


def gelu_tanh(values):
    return jax.nn.gelu(values, approximate=True)


PAIR = 128


def offset_buckets(span, two_sided):
    places = jnp.arange(2 * span, dtype=jnp.int32)[None, :]
    relative = lax.rem(places - jnp.arange(8, dtype=jnp.int32)[:, None] + 2 * span, 2 * span) - span
    buckets = bucket_index(relative.reshape(-1), two_sided)
    return (buckets[None, :] == jnp.arange(NB, dtype=jnp.int32)[:, None]).astype(jnp.bfloat16)


def base_rows(table, span, two_sided):
    heads = table.shape[1]
    rows = lax.dot_general(
        table, offset_buckets(span, two_sided), (((0,), (0,)), ((), ())), preferred_element_type=jnp.float32
    )
    return rows.reshape(heads // 2, 2, 8, 2 * span)


def table_grad(offset_sums, span, two_sided):
    heads = 2 * offset_sums.shape[0]
    return lax.dot_general(
        offset_buckets(span, two_sided).astype(jnp.float32),
        offset_sums.reshape(heads, 16 * span),
        (((1,), (1,)), ((), ())),
        precision=HIGH,
        preferred_element_type=jnp.float32,
    )


def dot_nt(a, b):
    return lax.dot_general(a, b, (((1,), (1,)), ((), ())), preferred_element_type=jnp.float32)


def dot_tn(a, b):
    return lax.dot_general(a, b, (((0,), (0,)), ((), ())), preferred_element_type=jnp.float32)


def dot_nn(a, b):
    return lax.dot_general(a, b, (((1,), (0,)), ((), ())), preferred_element_type=jnp.float32)


def split_heads(block):
    lane = lax.broadcasted_iota(jnp.int32, block.shape, 1)
    zero = jnp.zeros_like(block)
    return jnp.where(lane < DK, block, zero), jnp.where(lane < DK, zero, block)


def attend_kernel(block, keys_count, causal, biased, *refs):
    if biased:
        qseg, kseg, base, q_ref, k_ref, v_ref, e_ref, c_ref, inv_ref, strip = refs
    else:
        qseg, kseg, q_ref, k_ref, v_ref, e_ref, c_ref, inv_ref = refs
    i = pl.program_id(1)
    if biased:
        wide = 2 * keys_count

        @pl.when(i == 0)
        def _():
            for head in range(2):
                rows = base[0, head]
                for a in range(block // 8):
                    strip[head, 8 * a : 8 * a + 8, :] = pltpu.roll(rows, (8 * a + wide - block) % wide, 1)

    allowed = qseg[...] == kseg[...]
    if causal:
        rows = lax.broadcasted_iota(jnp.int32, (block, keys_count), 0) + i * block
        allowed = allowed & (lax.broadcasted_iota(jnp.int32, (block, keys_count), 1) <= rows)
    q_heads = split_heads(q_ref[...])
    v_heads = split_heads(v_ref[...])
    inverses = []
    context = None
    for head in range(2):
        scores = dot_nt(q_heads[head], k_ref[...])
        if biased:
            start = pl.multiple_of((keys_count // block - 1 - i) * block, block)
            scores = scores + strip[head, :, pl.ds(start, keys_count)]
        scores = jnp.where(allowed, scores, NEG)
        highest = jnp.max(scores, axis=1, keepdims=True)
        weights = jnp.exp(scores - highest)
        inverses.append(1.0 / jnp.sum(weights, axis=1, keepdims=True))
        weights = weights.astype(jnp.bfloat16)
        e_ref[head] = weights
        part = dot_nn(weights, v_heads[head])
        context = part if context is None else context + part
    lane = lax.broadcasted_iota(jnp.int32, (block, PAIR), 1)
    inverse = jnp.where(lane < DK, inverses[0], inverses[1])
    inv_ref[...] = inverse
    c_ref[...] = (context * inverse).astype(jnp.bfloat16)


def attend_back_kernel(block, keys_count, steps, biased, *refs):
    if biased:
        q_ref, k_ref, v_ref, e_ref, c_ref, inv_ref, gc_ref, gq_ref, gk_ref, gv_ref, off_ref, gk_sum, gv_sum, strip = refs
    else:
        q_ref, k_ref, v_ref, e_ref, c_ref, inv_ref, gc_ref, gq_ref, gk_ref, gv_ref, gk_sum, gv_sum = refs
    i = pl.program_id(1)

    @pl.when(i == 0)
    def _():
        gk_sum[...] = jnp.zeros_like(gk_sum)
        gv_sum[...] = jnp.zeros_like(gv_sum)
        if biased:
            strip[...] = jnp.zeros_like(strip)

    scaled = (gc_ref[...].astype(jnp.float32) * inv_ref[...]).astype(jnp.bfloat16)
    product = scaled.astype(jnp.float32) * c_ref[...].astype(jnp.float32)
    lane = lax.broadcasted_iota(jnp.int32, (block, PAIR), 1)
    inner = (
        jnp.sum(jnp.where(lane < DK, product, 0.0), axis=1, keepdims=True),
        jnp.sum(jnp.where(lane < DK, 0.0, product), axis=1, keepdims=True),
    )
    g_heads = split_heads(scaled)
    q_heads = split_heads(q_ref[...])
    k_heads = split_heads(k_ref[...])
    gq = None
    for head in range(2):
        weights = e_ref[head]
        grad = dot_nt(g_heads[head], v_ref[...])
        grad = weights.astype(jnp.float32) * (grad - inner[head])
        if biased:
            start = pl.multiple_of((keys_count // block - 1 - i) * block, block)
            strip[head, :, pl.ds(start, keys_count)] += grad
        grad = grad.astype(jnp.bfloat16)
        part = dot_nn(grad, k_heads[head])
        gq = part if gq is None else gq + part
        gk_sum[...] += dot_tn(grad, q_heads[head])
        gv_sum[...] += dot_tn(weights, g_heads[head])
    gq_ref[...] = gq.astype(jnp.bfloat16)

    @pl.when(i == steps - 1)
    def _():
        gk_ref[...] = gk_sum[...].astype(jnp.bfloat16)
        gv_ref[...] = gv_sum[...].astype(jnp.bfloat16)
        if biased:
            wide = 2 * keys_count
            for head in range(2):
                total = jnp.zeros((8, wide), jnp.float32)
                for a in range(block // 8):
                    total = total + pltpu.roll(strip[head, 8 * a : 8 * a + 8, :], (block - 8 * a) % wide, 1)
                off_ref[0, head] = total


def attend_forward(query, keys, values, base, query_segments, key_segments, causal):
    count, cols = query.shape[0], keys.shape[0]
    pairs = query.shape[1] // PAIR
    block = min(256, count)
    steps = count // block
    row_spec = pl.BlockSpec((block, PAIR), lambda h, i: (i, h))
    key_spec = pl.BlockSpec((cols, PAIR), lambda h, i: (0, h))
    in_specs = [
        pl.BlockSpec((block, 1), lambda h, i: (i, 0)),
        pl.BlockSpec((1, cols), lambda h, i: (0, 0)),
    ]
    args = [query_segments[:, None], key_segments[None, :]]
    scratch = []
    if base is not None:
        in_specs.append(pl.BlockSpec((1, 2, 8, 2 * cols), lambda h, i: (h, 0, 0, 0)))
        args.append(base)
        scratch.append(pltpu.VMEM((2, block, 2 * cols), jnp.float32))
    return pl.pallas_call(
        functools.partial(attend_kernel, block, cols, causal, base is not None),
        grid=(pairs, steps),
        in_specs=in_specs + [row_spec, key_spec, key_spec],
        out_specs=[
            pl.BlockSpec((2, block, cols), lambda h, i: (h, i, 0)),
            row_spec,
            row_spec,
        ],
        out_shape=[
            jax.ShapeDtypeStruct((2 * pairs, count, cols), jnp.bfloat16),
            jax.ShapeDtypeStruct((count, pairs * PAIR), jnp.bfloat16),
            jax.ShapeDtypeStruct((count, pairs * PAIR), jnp.float32),
        ],
        scratch_shapes=scratch,
        compiler_params=pltpu.CompilerParams(vmem_limit_bytes=VMEM_BYTES),
        cost_estimate=pl.CostEstimate(
            flops=4 * count * cols * PAIR * 2 * pairs, bytes_accessed=2 * pairs * count * cols * 2, transcendentals=0
        ),
    )(*args, query, keys, values)


def attend_backward(query, keys, values, saved, grad_context, biased):
    weights, context, inverse = saved
    count, cols = query.shape[0], keys.shape[0]
    pairs = query.shape[1] // PAIR
    block = min(256, count)
    steps = count // block
    row_spec = pl.BlockSpec((block, PAIR), lambda h, i: (i, h))
    key_spec = pl.BlockSpec((cols, PAIR), lambda h, i: (0, h))
    out_specs = [row_spec, key_spec, key_spec]
    out_shape = [
        jax.ShapeDtypeStruct((count, pairs * PAIR), jnp.bfloat16),
        jax.ShapeDtypeStruct((cols, pairs * PAIR), jnp.bfloat16),
        jax.ShapeDtypeStruct((cols, pairs * PAIR), jnp.bfloat16),
    ]
    scratch = [pltpu.VMEM((cols, PAIR), jnp.float32), pltpu.VMEM((cols, PAIR), jnp.float32)]
    if biased:
        out_specs.append(pl.BlockSpec((1, 2, 8, 2 * cols), lambda h, i: (h, 0, 0, 0)))
        out_shape.append(jax.ShapeDtypeStruct((pairs, 2, 8, 2 * cols), jnp.float32))
        scratch.append(pltpu.VMEM((2, block, 2 * cols), jnp.float32))
    return pl.pallas_call(
        functools.partial(attend_back_kernel, block, cols, steps, biased),
        grid=(pairs, steps),
        in_specs=[
            row_spec,
            key_spec,
            key_spec,
            pl.BlockSpec((2, block, cols), lambda h, i: (h, i, 0)),
            row_spec,
            row_spec,
            row_spec,
        ],
        out_specs=out_specs,
        out_shape=out_shape,
        scratch_shapes=scratch,
        compiler_params=pltpu.CompilerParams(vmem_limit_bytes=VMEM_BYTES),
        cost_estimate=pl.CostEstimate(
            flops=8 * count * cols * PAIR * 2 * pairs, bytes_accessed=2 * pairs * count * cols * 2, transcendentals=0
        ),
    )(query, keys, values, weights, context, inverse, grad_context)


MESH_IDS = pl.DeviceIdType.MESH
CHUNK = 256
ATT = 4 * 384


def any_spec():
    return pl.BlockSpec(memory_space=pl.ANY)


def vmem_spec():
    return pl.BlockSpec(memory_space=pltpu.VMEM)


def smem_spec():
    return pl.BlockSpec(memory_space=pltpu.SMEM)


def documents(lengths, shape, first):
    places = lax.broadcasted_iota(jnp.int32, shape, 0 if shape[1] == 1 else 1) + first
    bound = jnp.int32(0)
    total = jnp.zeros(shape, jnp.int32)
    for k in range(lengths.shape[1]):
        bound = bound + lengths[0, k]
        total = total + (places >= bound).astype(jnp.int32)
    return total


def normed(values, gain):
    return values * lax.rsqrt(jnp.mean(values * values, axis=1, keepdims=True) + EPS) * gain


def gelu_pair(values):
    square = values * values
    inner = jnp.tanh(GELU_A * values * (1.0 + GELU_B * square))
    half = 0.5 * (1.0 + inner)
    slope = half + 0.5 * values * (1.0 - inner * inner) * (GELU_A * (1.0 + 3.0 * GELU_B * square))
    return values * half, slope


class Place:
    def __init__(self, wide):
        self.core = lax.axis_index("dp")
        self.wide = lax.axis_index("wide")
        self.side = lax.axis_index("narrow")
        self.count = wide
        self.fars = wide // 2
        self.far = self.wide // 2
        self.near = self.wide % 2

    def sibling(self):
        return (1 - self.core, self.wide, self.side)

    def across(self):
        return (self.core, self.wide, 1 - self.side)

    def beside(self):
        return (self.core, 2 * self.far + 1 - self.near, self.side)

    def along(self, step):
        return (self.core, 2 * lax.rem(self.far + step, self.fars) + self.near, self.side)

    def index_from(self, step):
        return 2 * lax.rem(self.far - step + self.fars, self.fars) + self.near

    def index_beside(self, step):
        return 2 * lax.rem(self.far - step + self.fars, self.fars) + 1 - self.near

    def greet(self):
        partners = [self.sibling(), self.across(), self.beside()]
        partners += [self.along(step) for step in range(1, self.fars)]
        barrier = pltpu.get_barrier_semaphore()
        for partner in partners:
            pl.semaphore_signal(barrier, inc=1, device_id=partner, device_id_type=MESH_IDS)
        pl.semaphore_wait(barrier, len(partners))


def remote(source, target, send, receive, partner):
    return pltpu.make_async_remote_copy(
        src_ref=source,
        dst_ref=target,
        send_sem=send,
        recv_sem=receive,
        device_id=partner,
        device_id_type=MESH_IDS,
    )


class Gather:
    def __init__(self, place, pack, groups, send, receive, local):
        self.place, self.pack, self.groups = place, pack, groups
        self.send, self.receive, self.local = send, receive, local
        self.rows = pack.shape[0]
        self.sent = []

    def at(self, group, index, core):
        first, width, target, offset = self.groups[group]
        half = width // 2
        start = pl.multiple_of(offset + core * half, 128)
        return target.at[pl.ds(pl.multiple_of(index * self.rows, 16), self.rows), pl.ds(start, half)]

    def own(self, group):
        first, width, target, offset = self.groups[group]
        half = width // 2
        return self.pack.at[:, pl.ds(pl.multiple_of(first + self.place.core * half, 128), half)]

    def local_copy(self, group):
        first, width, target, offset = self.groups[group]
        rows = pl.ds(pl.multiple_of(self.place.wide * self.rows, 16), self.rows)
        return pltpu.make_async_copy(
            self.pack.at[:, pl.ds(first, width)], target.at[rows, pl.ds(offset, width)], self.local.at[group]
        )

    def push(self, group, slot, source, index, partner):
        copy = remote(
            source,
            self.at(group, index, self.place.core),
            self.send.at[group, slot],
            self.receive.at[group, slot],
            partner,
        )
        copy.start()
        self.sent.append(copy)

    def await_slot(self, group, slot, index, core):
        block = self.at(group, index, core)
        remote(block, block, self.send.at[group, slot], self.receive.at[group, slot], self.place.sibling()).wait_recv()

    def start(self, group):
        place, fars = self.place, self.place.fars
        for step in range(1, fars):
            self.push(group, step - 1, self.own(group), place.wide, place.along(step))
        self.push(group, fars - 1, self.own(group), place.wide, place.beside())
        self.local_copy(group).start()

    def relay_along(self, group):
        place, fars = self.place, self.place.fars
        for step in range(1, fars):
            index = place.index_from(step)
            self.await_slot(group, step - 1, index, place.core)
            block = self.at(group, index, place.core)
            self.push(group, fars - 1 + step, block, index, place.beside())
            self.push(group, 2 * fars - 2 + step, block, index, place.sibling())

    def relay_beside(self, group):
        place, fars = self.place, self.place.fars
        for step in range(fars):
            index = place.index_beside(step)
            self.await_slot(group, fars - 1 + step, index, place.core)
            block = self.at(group, index, place.core)
            self.push(group, 3 * fars - 2 + step, block, index, place.sibling())

    def finish(self, group):
        place, fars = self.place, self.place.fars
        for step in range(1, fars):
            self.await_slot(group, 2 * fars - 2 + step, place.index_from(step), 1 - place.core)
        for step in range(fars):
            self.await_slot(group, 3 * fars - 2 + step, place.index_beside(step), 1 - place.core)
        self.local_copy(group).wait()

    def close(self):
        for copy in self.sent:
            copy.wait_send()


def gather_slots(wide):
    return 4 * (wide // 2) - 2


def softmax_pair(q_pair, k_pair, v_pair, allowed, biases, e_store):
    q_heads = split_heads(q_pair)
    v_heads = split_heads(v_pair)
    inverses = []
    context = None
    for head in range(2):
        scores = dot_nt(q_heads[head], k_pair)
        if biases is not None:
            scores = scores + biases(head)
        scores = jnp.where(allowed, scores, NEG)
        highest = jnp.max(scores, axis=1, keepdims=True)
        weights = jnp.exp(scores - highest)
        inverses.append(1.0 / jnp.sum(weights, axis=1, keepdims=True))
        weights = weights.astype(jnp.bfloat16)
        e_store(head, weights)
        part = dot_nn(weights, v_heads[head])
        context = part if context is None else context + part
    lane = lax.broadcasted_iota(jnp.int32, context.shape, 1)
    inverse = jnp.where(lane < DK, inverses[0], inverses[1])
    return inverse, (context * inverse).astype(jnp.bfloat16)


def build_strip(strip, base, pairs, block, span):
    def one(pair, carry):
        for head in range(2):
            rows = base[pair, head]
            for a in range(block // 8):
                strip[2 * pair + head, 8 * a : 8 * a + 8, :] = pltpu.roll(rows, (8 * a + 2 * span - block) % (2 * span), 1)
        return carry

    lax.fori_loop(0, pairs, one, 0)


NEAR = 2 * CHUNK
EDGE = NEAR // 4


def near_buckets():
    places = jnp.arange(2 * NEAR, dtype=jnp.int32)[None, :]
    relative = places - jnp.arange(8, dtype=jnp.int32)[:, None] - CHUNK - EDGE
    buckets = bucket_index(relative.reshape(-1), True)
    return (buckets[None, :] == jnp.arange(NB, dtype=jnp.int32)[:, None]).astype(jnp.bfloat16)


def near_rows(table):
    rows = lax.dot_general(
        table, near_buckets(), (((0,), (0,)), ((), ())), preferred_element_type=jnp.float32
    )
    return rows.reshape(table.shape[1] // 2, 2, 8, 2 * NEAR)


def build_near(strip, base, pairs):
    def one(pair, carry):
        for head in range(2):
            rows = base[pair, head]
            for a in range(CHUNK // 8):
                turned = pltpu.roll(rows, (2 * NEAR - CHUNK + 8 * a) % (2 * NEAR), 1)
                strip[2 * pair + head, 8 * a : 8 * a + 8, :] = turned[:, :NEAR]
        return carry

    lax.fori_loop(0, pairs, one, 0)


def near_window(i, rows):
    low, high = max(i * CHUNK - EDGE, 0), min(i * CHUNK + CHUNK + EDGE, rows)
    return low, high, low - (i * CHUNK - EDGE)


def near_bias(strip, base, pair, head, i, rows):
    low, high, shift = near_window(i, rows)
    parts = [strip[2 * pair + head, :, shift : shift + high - low]]
    if low > 0:
        parts.insert(0, jnp.broadcast_to(base[pair, head, 0:1, 0:1], (CHUNK, low)))
    if high < rows:
        parts.append(jnp.broadcast_to(base[pair, head, 0:1, 2 * NEAR - 1 : 2 * NEAR], (CHUNK, rows - high)))
    return jnp.concatenate(parts, axis=1)


def enc_forward_kernel(
    wide,
    x_own,
    dec_own,
    dcot_own,
    query_in,
    kv_in,
    out_in,
    up_in,
    down_in,
    gains,
    base,
    lengths,
    w1_all,
    w2,
    n0_all,
    qkv_all,
    c_all,
    inv_all,
    e_all,
    e1_all,
    n1_all,
    slope_all,
    a_all,
    ef_all,
    mem_all,
    dec_other,
    dcot_other,
    pack,
    w1,
    n0,
    qkv,
    c,
    inv,
    e1,
    n1,
    ef,
    mem,
    x_full,
    strip,
    e_buf,
    slope_buf,
    a_buf,
    y_send,
    y_recv,
    g_send,
    g_recv,
    g_local,
    x_sems,
    y_sems,
    z_sems,
    l_sems,
    p_sems,
    o_sems,
):
    place = Place(wide)
    side = place.side
    half = x_own.shape[0]
    rows = 2 * half
    steps = rows // CHUNK
    width = c.shape[1]
    ffn = up_in.shape[2]
    pairs = width // PAIR
    pieces = []
    for layer in range(3):
        first = (0, 4 * width + 2 * ffn, 8 * width + 2 * ffn)[layer]
        pieces += [(query_in.at[layer], first), (kv_in.at[layer, 0], first + width)]
        pieces += [(kv_in.at[layer, 1], first + 2 * width), (out_in.at[layer], first + 3 * width)]
    pieces += [(up_in.at[0], 4 * width), (down_in.at[0], 4 * width + ffn), (up_in.at[1], 12 * width + 2 * ffn)]
    packs = [
        pltpu.make_async_copy(piece, pack.at[:, pl.ds(first, piece.shape[1])], p_sems.at[index])
        for index, (piece, first) in enumerate(pieces)
    ]
    for copy in packs:
        copy.start()
    place.greet()
    gather = Gather(
        place,
        pack,
        [
            (0, 2 * width, w1, 0),
            (2 * width, 2 * width, w1, 2 * width),
            (4 * width, ffn, w1, 4 * width),
            (4 * width + ffn, ffn, w1, 4 * width + ffn),
            (4 * width + 2 * ffn, 4 * width, w2, 0),
            (8 * width + 2 * ffn, 4 * width, w2, 4 * width),
            (12 * width + 2 * ffn, ffn, w2, 8 * width),
        ],
        g_send,
        g_recv,
        g_local,
    )
    mine = pl.ds(pl.multiple_of(side * half, 16), half)
    swap_x = remote(x_own, x_full.at[mine], x_sems.at[0], x_sems.at[1], place.across())
    swap_x.start()
    for copy in packs[:4]:
        copy.wait()
    gather.start(0)
    gather.start(1)
    for copy in packs[4:]:
        copy.wait()
    keep_x = pltpu.make_async_copy(x_own, x_full.at[mine], l_sems.at[6])
    keep_x.start()
    build_near(strip, base, pairs)
    gather.relay_along(0)
    gather.relay_along(1)
    gather.start(2)
    keep_x.wait()
    gather.relay_beside(0)
    gather.relay_beside(1)
    swap_x.wait()
    later = [
        remote(dec_own, dec_other, x_sems.at[2], x_sems.at[3], place.across()),
        remote(dcot_own, dcot_other, x_sems.at[4], x_sems.at[5], place.across()),
    ]
    for copy in later:
        copy.start()
    stores = []

    def store_out(source, target):
        stores.append(pltpu.make_async_copy(source, target, o_sems.at[len(stores)]))
        stores[-1].start()


    def norm_rows(i, carry):
        at = pl.ds(pl.multiple_of(i * CHUNK, CHUNK), CHUNK)
        n0[at, :] = normed(x_full[at, :].astype(jnp.float32), gains[0:1, :]).astype(jnp.bfloat16)
        return carry

    lax.fori_loop(0, steps, norm_rows, 0)
    gather.finish(0)
    gather.finish(1)

    def project(i, carry):
        at = pl.ds(pl.multiple_of(i * CHUNK, CHUNK), CHUNK)
        qkv[at, :] = dot_nn(n0[at, :], w1[:, : 3 * width]).astype(jnp.bfloat16)
        return carry

    lax.fori_loop(0, steps, project, 0)
    store_out(n0, n0_all)
    store_out(qkv, qkv_all)

    def lanes(base_lane, pair):
        return pl.ds(pl.multiple_of(base_lane + pair * PAIR, PAIR), PAIR)

    def save(i, kind):
        slot = i % 2
        at = pl.ds(i * CHUNK, CHUNK)
        if kind == 0:
            return pltpu.make_async_copy(e_buf.at[slot], e_all.at[:, at, :], l_sems.at[slot])
        if kind == 1:
            return pltpu.make_async_copy(slope_buf.at[slot], slope_all.at[at, :], l_sems.at[2 + slot])
        return pltpu.make_async_copy(a_buf.at[slot], a_all.at[at, :], l_sems.at[4 + slot])

    def swap_y(layer, i):
        at = pl.ds(i * CHUNK, CHUNK)
        sems = y_sems if layer == 0 else z_sems
        return remote(y_send.at[layer, at], y_recv.at[layer, at], sems.at[0, i], sems.at[1, i], place.across())

    def attend(i):
        at = pl.ds(i * CHUNK, CHUNK)
        slot = i % 2
        if i >= 2:
            save(i - 2, 0).wait()

        def one(pair, carry):
            allowed = documents(lengths, (CHUNK, 1), i * CHUNK) == documents(lengths, (1, rows), 0)

            def bias(head):
                return near_bias(strip, base, pair, head, i, rows)

            def store(head, weights):
                e_buf[slot, 2 * pair + head] = weights

            inverse, context = softmax_pair(
                qkv[at, lanes(0, pair)],
                qkv[:, lanes(width, pair)],
                qkv[:, lanes(2 * width, pair)],
                allowed,
                bias,
                store,
            )
            inv[at, lanes(0, pair)] = inverse
            c[at, lanes(0, pair)] = context
            return carry

        lax.fori_loop(0, pairs, one, 0)
        save(i, 0).start()
        store_out(c.at[at], c_all.at[at])
        store_out(inv.at[at], inv_all.at[at])
        y_send[0, at, :] = dot_nt(c[at, :], w1[:, 3 * width : 4 * width]).astype(jnp.bfloat16)
        swap_y(0, i).start()

    def feed(i):
        at = pl.ds(i * CHUNK, CHUNK)
        slot = i % 2
        swap_y(0, i).wait_recv()
        both = y_send[0, at, :].astype(jnp.float32) + y_recv[0, at, :].astype(jnp.float32)
        middle = x_full[at, :].astype(jnp.float32) + both
        e1[at, :] = middle
        rounded = normed(middle, gains[1:2, :]).astype(jnp.bfloat16)
        n1[at, :] = rounded
        store_out(e1.at[at], e1_all.at[at])
        store_out(n1.at[at], n1_all.at[at])
        if i >= 2:
            save(i - 2, 1).wait()
            save(i - 2, 2).wait()

        def part(j, carry):
            cols = pl.ds(pl.multiple_of(4 * width + j * width, PAIR), width)
            here = pl.ds(pl.multiple_of(j * width, PAIR), width)
            active, slope = gelu_pair(dot_nn(n1[at, :], w1[:, cols]))
            a_buf[slot, :, here] = active.astype(jnp.bfloat16)
            slope_buf[slot, :, here] = slope.astype(jnp.bfloat16)
            return carry

        lax.fori_loop(0, ffn // width, part, 0)
        save(i, 1).start()
        save(i, 2).start()
        y_send[1, at, :] = dot_nt(a_buf[slot], w1[:, 4 * width + ffn :]).astype(jnp.bfloat16)
        swap_y(1, i).start()

    def last(i):
        at = pl.ds(i * CHUNK, CHUNK)
        swap_y(1, i).wait_recv()
        both = y_send[1, at, :].astype(jnp.float32) + y_recv[1, at, :].astype(jnp.float32)
        final = e1[at, :] + both
        ef[at, :] = final
        mem[at, :] = normed(final, gains[5:6, :]).astype(jnp.bfloat16)
        store_out(ef.at[at], ef_all.at[at])
        store_out(mem.at[at], mem_all.at[at])

    gather.start(3)
    gather.relay_along(2)
    attend(0)
    gather.start(4)
    gather.relay_along(3)
    gather.relay_beside(2)
    attend(1)
    gather.start(5)
    gather.relay_along(4)
    gather.relay_beside(3)
    gather.finish(2)
    attend(2)
    gather.finish(3)
    store_out(w1, w1_all)
    feed(0)
    gather.start(6)
    gather.relay_along(5)
    gather.relay_beside(4)
    attend(3)
    feed(1)
    gather.relay_beside(5)
    gather.relay_along(6)
    feed(2)
    feed(3)
    last(0)
    gather.relay_beside(6)
    last(1)
    last(2)
    last(3)
    for group in range(4, 7):
        gather.finish(group)
    gather.close()
    for copy in later:
        copy.wait()
    for copy in stores:
        copy.wait()
    for i in range(steps):
        swap_y(0, i).wait_send()
        swap_y(1, i).wait_send()
    for i in range(steps - 2, steps):
        for kind in range(3):
            save(i, kind).wait()


def enc_forward(wide, x_own, dec_own, dcot_own, weights, gains, base, lengths):
    half, model = x_own.shape
    rows = 2 * half
    pairs = base.shape[0]
    width = pairs * PAIR
    ffn = weights[3].shape[2]
    bf, f32 = jnp.bfloat16, jnp.float32
    shape = jax.ShapeDtypeStruct
    dma = pltpu.SemaphoreType.DMA
    slots = gather_slots(wide)
    steps = rows // CHUNK
    saved = [
        ((model, 4 * width + 2 * ffn), bf),
        ((rows, model), bf),
        ((rows, 3 * width), bf),
        ((rows, width), bf),
        ((rows, width), f32),
        ((rows, model), f32),
        ((rows, model), bf),
        ((rows, model), f32),
        ((rows, model), bf),
    ]
    kept = [shape(*pair) for pair in saved]
    out_shape = (
        [kept[0], shape((model, 8 * width + ffn), bf)]
        + kept[1:5]
        + [shape((2 * pairs, rows, rows), bf)]
        + kept[5:7]
        + [shape((rows, ffn), bf), shape((rows, ffn), bf)]
        + kept[7:]
        + [shape(dec_own.shape, bf), shape(dcot_own.shape, bf)]
    )
    return pl.pallas_call(
        functools.partial(enc_forward_kernel, wide),
        in_specs=[vmem_spec()] + [any_spec()] * 7 + [vmem_spec()] * 2 + [smem_spec()],
        out_shape=out_shape,
        out_specs=[any_spec()] * len(out_shape),
        scratch_shapes=[pltpu.VMEM((x_own.shape[1] // wide, 12 * width + 3 * ffn), bf)]
        + [pltpu.VMEM(*pair) for pair in saved]
        + [
            pltpu.VMEM((rows, model), bf),
            pltpu.VMEM((2 * pairs, CHUNK, NEAR), f32),
            pltpu.VMEM((2, 2 * pairs, CHUNK, rows), bf),
            pltpu.VMEM((2, CHUNK, ffn), bf),
            pltpu.VMEM((2, CHUNK, ffn), bf),
            pltpu.VMEM((2, rows, model), bf),
            pltpu.VMEM((2, rows, model), bf),
            dma((7, slots)),
            dma((7, slots)),
            dma((7,)),
            dma((8,)),
            dma((2, steps)),
            dma((2, steps)),
            dma((7,)),
            dma((15,)),
            dma((3 + 6 * steps,)),
        ],
        compiler_params=pltpu.CompilerParams(
            collective_id=0, has_side_effects=True, vmem_limit_bytes=VMEM_BYTES
        ),
        cost_estimate=pl.CostEstimate(flops=10**10, bytes_accessed=6 * 10**7, transcendentals=0),
    )(x_own, dec_own, dcot_own, *weights, gains, base, lengths)


def norm_back(values, gain, grad):
    scale = lax.rsqrt(jnp.mean(values * values, axis=1, keepdims=True) + EPS)
    scaled = grad * gain
    pulled = scale * (scaled - values * (scale * scale) * jnp.mean(scaled * values, axis=1, keepdims=True))
    return pulled, jnp.sum(grad * values * scale, axis=0, keepdims=True)


class Scatter:
    def __init__(self, place, rows, groups, tile, send, receive):
        self.place, self.rows, self.groups, self.tile = place, rows, groups, tile
        self.send, self.receive = send, receive
        self.sent = []

    def columns(self, group, core):
        first, width = self.groups[group]["first"], self.groups[group]["width"]
        if self.groups[group]["core"] is None:
            return pl.ds(first, width // 2)
        return pl.ds(pl.multiple_of(first + core * (width // 2), 128), width // 2)

    def block(self, group, index):
        return self.groups[group]["grad"].at[
            pl.ds(pl.multiple_of(index * self.rows, 16), self.rows), self.columns(group, self.place.core)
        ]

    def push(self, group, slot, source, target, partner, arrival=None):
        arrival = slot if arrival is None else arrival
        copy = remote(source, target, self.send.at[group, slot], self.receive.at[group, arrival], partner)
        copy.start()
        self.sent.append(copy)

    def await_slot(self, group, slot, block):
        remote(block, block, self.send.at[group, 0], self.receive.at[group, slot], self.place.sibling()).wait_recv()

    def start(self, group):
        parts = self.groups[group]
        self.push(
            group, 0, parts["grad"].at[:, self.columns(group, 1 - self.place.core)], parts["core"], self.place.sibling()
        )

    def add_block(self, group, index, other):
        block = self.block(group, index)
        block[...] = (block[...].astype(jnp.float32) + other.astype(jnp.float32)).astype(jnp.bfloat16)
        return block

    def merge(self, group):
        parts = self.groups[group]
        self.await_slot(group, 0, parts["core"])
        for index in range(self.place.count):
            self.add_block(group, index, parts["core"][index * self.rows : (index + 1) * self.rows, :])

    def beside(self, group):
        parts, place = self.groups[group], self.place
        if parts["core"] is None:
            for step in range(place.fars):
                index = 2 * lax.rem(place.far + 1 + step, place.fars) + 1 - place.near
                self.push(group, 1 + step, self.block(group, index), parts["beside"].at[step], place.beside())
            return
        self.await_slot(group, 0, parts["core"])

        def received(index):
            return parts["core"][pl.ds(pl.multiple_of(index * self.rows, 16), self.rows), :]

        for step in range(place.fars):
            far = lax.rem(place.far + 1 + step, place.fars)
            index = 2 * far + 1 - place.near
            block = self.add_block(group, index, received(index))
            self.push(group, 1 + step, block, parts["beside"].at[step], place.beside())
        for step in range(place.fars):
            far = lax.rem(place.far + 1 + step, place.fars)
            index = 2 * far + place.near
            self.add_block(group, index, received(index))

    def along(self, group):
        parts, place = self.groups[group], self.place
        for step in range(1, place.fars):
            index = 2 * lax.rem(place.far + step, place.fars) + place.near
            self.await_slot(group, step, parts["beside"].at[step - 1])
            block = self.add_block(group, index, parts["beside"][step - 1])
            self.push(group, place.fars + step, block, parts["along"].at[step - 1], place.along(step))

    def total(self, group):
        parts, place = self.groups[group], self.place
        self.await_slot(group, place.fars, parts["beside"].at[place.fars - 1])
        value = self.block(group, place.wide)[...].astype(jnp.float32) + parts["beside"][place.fars - 1].astype(jnp.float32)
        for step in range(1, place.fars):
            self.await_slot(group, place.fars + step, parts["along"].at[step - 1])
            value = value + parts["along"][step - 1].astype(jnp.float32)
        half = parts["width"] // 2
        block = self.tile.at[:, pl.ds(pl.multiple_of(parts["out"] + place.core * half, 128), half)]
        block[...] = value.astype(jnp.bfloat16)
        self.push(group, 2 * place.fars, block, block, place.sibling())

    def finish(self, group):
        parts, place = self.groups[group], self.place
        half = parts["width"] // 2
        block = self.tile.at[:, pl.ds(pl.multiple_of(parts["out"] + (1 - place.core) * half, 128), half)]
        self.await_slot(group, 2 * place.fars, block)

    def close(self):
        for copy in self.sent:
            copy.wait_send()


def half_group(grad, first, width, out, part, core, beside, along):
    at = pl.ds(part * (width // 2), width // 2)
    return dict(
        grad=grad,
        first=first,
        width=width,
        out=out,
        core=core.at[:, at],
        beside=beside.at[:, :, at],
        along=along.at[:, :, at],
    )


def scatter_slots(wide):
    return 2 * (wide // 2) + 1


def scatter_buffers(wide, model, width):
    half, rows, fars = width // 2, model // wide, wide // 2
    return [
        pltpu.VMEM((model, half), jnp.bfloat16),
        pltpu.VMEM((fars, rows, half), jnp.bfloat16),
        pltpu.VMEM((fars - 1, rows, half), jnp.bfloat16),
    ]


def softmax_back_pair(q_pair, k_pair, v_pair, c_pair, inverse, gc_pair, weights, near):
    scaled = (gc_pair.astype(jnp.float32) * inverse).astype(jnp.bfloat16)
    product = scaled.astype(jnp.float32) * c_pair.astype(jnp.float32)
    lane = lax.broadcasted_iota(jnp.int32, product.shape, 1)
    inner = (
        jnp.sum(jnp.where(lane < DK, product, 0.0), axis=1, keepdims=True),
        jnp.sum(jnp.where(lane < DK, 0.0, product), axis=1, keepdims=True),
    )
    g_heads = split_heads(scaled)
    q_heads = split_heads(q_pair)
    k_heads = split_heads(k_pair)
    gq = None
    grads = []
    for head in range(2):
        grad = weights[head].astype(jnp.float32) * (dot_nt(g_heads[head], v_pair) - inner[head])
        if near is not None:
            near(head, grad)
        grad = grad.astype(jnp.bfloat16)
        grads.append(grad)
        part = dot_nn(grad, k_heads[head])
        gq = part if gq is None else gq + part
    gk = dot_tn(jnp.concatenate(grads, axis=0), jnp.concatenate(q_heads, axis=0))
    gv = dot_tn(jnp.concatenate([weights[0], weights[1]], axis=0), jnp.concatenate(g_heads, axis=0))
    return gq, gk, gv


def fold_near(rows):
    total = jnp.zeros((8, 2 * NEAR), jnp.float32)
    blank = jnp.zeros((8, NEAR), jnp.float32)
    for a in range(CHUNK // 8):
        wider = jnp.concatenate([rows[8 * a : 8 * a + 8, :], blank], axis=1)
        total = total + pltpu.roll(wider, (CHUNK - 8 * a) % (2 * NEAR), 1)
    return total


def bucket_sums(rows, offset, two_sided):
    span = rows.shape[1]
    relative = lax.broadcasted_iota(jnp.int32, (span, 128), 0) - offset
    onehot = bucket_index(relative, two_sided) == lax.broadcasted_iota(jnp.int32, (span, 128), 1)
    return lax.dot_general(
        rows,
        onehot.astype(jnp.float32),
        (((1,), (0,)), ((), ())),
        precision=HIGH,
        preferred_element_type=jnp.float32,
    )


def fold_rows(rows):
    span = rows.shape[1]
    total = rows[0:1, :]
    for b in range(1, 8):
        total = total + pltpu.roll(rows, span - b, 1)[b : b + 1, :]
    return total


class Total:
    def __init__(self, place, held, send, receive):
        self.place, self.held, self.send, self.receive = place, held, send, receive
        partners = (place.sibling(), place.across(), place.beside())
        self.copies = [
            remote(held.at[stage], held.at[4 + stage], send.at[stage], receive.at[stage], partner)
            for stage, partner in enumerate(partners)
        ]
        self.last = [
            remote(held.at[3], held.at[7 + place.far], send.at[2 + step], receive.at[2 + step], place.along(step))
            for step in range(1, place.fars)
        ]

    def start(self):
        self.copies[0].start()

    def step(self, stage):
        held = self.held
        self.copies[stage].wait()
        held[stage + 1] = held[stage] + held[4 + stage]
        for copy in [self.copies[stage + 1]] if stage < 2 else self.last:
            copy.start()

    def finish(self):
        for copy in self.last:
            copy.wait()
        result = None
        for far in range(self.place.fars):
            part = jnp.where(self.place.far == far, self.held[3], self.held[7 + far])
            result = part if result is None else result + part
        return result


def enc_backward_kernel(
    wide,
    x_own,
    cot_own,
    cot_other,
    gains,
    dec_gains,
    dec_table,
    part_own,
    part_other,
    dw1_in,
    w1_in,
    n0_in,
    qkv_in,
    c_in,
    inv_in,
    e_all,
    e1_all,
    n1_in,
    slope_all,
    a_in,
    ef_all,
    grad_out,
    tile,
    total_sums,
    part_late,
    gain_sums,
    far_sums,
    folded,
    held,
    w1,
    dw1,
    qkv,
    c,
    inv,
    n1,
    active,
    cot,
    e_buf,
    state_buf,
    slope_buf,
    part_buf,
    other_buf,
    g_send,
    g_recv,
    l_recv,
    state_grad,
    gy,
    gu,
    gqkv,
    gk_sum,
    gv_sum,
    strip,
    core_f,
    beside_f,
    along_f,
    beside_a,
    along_a,
    beside_d,
    along_d,
    s_send,
    s_recv,
    t_send,
    t_recv,
    m_sems,
    g_sems,
    l_sems,
    e_sems,
    t_sems,
    i_sems,
):
    place = Place(wide)
    side = place.side
    half = x_own.shape[0]
    rows = 2 * half
    steps = rows // CHUNK
    width = c.shape[1]
    ffn = active.shape[1]
    pairs = width // PAIR
    model = x_own.shape[1]
    bf, f32 = jnp.bfloat16, jnp.float32
    place.greet()

    def swap(i):
        at = pl.ds(i * CHUNK, CHUNK)
        return remote(g_send.at[at], g_recv.at[at], g_sems.at[0, i], g_sems.at[1, i], place.across())

    late = part_late.shape[0] // CHUNK

    def swap_late(i):
        return remote(
            part_own.at[pl.ds((steps - late + i) * CHUNK, CHUNK)],
            part_late.at[pl.ds(i * CHUNK, CHUNK)],
            m_sems.at[0, i],
            m_sems.at[1, i],
            place.across(),
        )

    for i in range(late):
        swap_late(i).start()

    def other_part(i):
        if i < steps - late:
            return part_other.at[pl.ds(i * CHUNK, CHUNK)]
        return part_late.at[pl.ds((i - steps + late) * CHUNK, CHUNK)]

    def fetch(i):
        at = pl.ds(i * CHUNK, CHUNK)
        slot = i % 2
        return [
            pltpu.make_async_copy(ef_all.at[at], state_buf.at[slot], t_sems.at[0, slot]),
            pltpu.make_async_copy(slope_all.at[at], slope_buf.at[slot], t_sems.at[1, slot]),
            pltpu.make_async_copy(part_own.at[at], part_buf.at[slot], t_sems.at[2, slot]),
            pltpu.make_async_copy(other_part(i), other_buf.at[slot], t_sems.at[3, slot]),
        ]

    def fetch_state(i):
        at = pl.ds(i * CHUNK, CHUNK)
        return pltpu.make_async_copy(e1_all.at[at], state_buf.at[i % 2], t_sems.at[0, i % 2])

    def fetch_e(step):
        chunk, pair, slot = step // pairs, lax.rem(step, pairs), lax.rem(step, 2)
        at = pl.ds(pl.multiple_of(chunk * CHUNK, CHUNK), CHUNK)
        return pltpu.make_async_copy(e_all.at[pl.ds(2 * pair, 2), at, :], e_buf.at[slot], e_sems.at[slot])

    mine = pl.ds(pl.multiple_of(side * half, 16), half)
    theirs = pl.ds(pl.multiple_of((1 - side) * half, 16), half)
    loads = [
        pltpu.make_async_copy(cot_own, cot.at[mine], i_sems.at[0]),
        pltpu.make_async_copy(cot_other, cot.at[theirs], i_sems.at[1]),
        pltpu.make_async_copy(w1_in, w1, i_sems.at[2]),
        pltpu.make_async_copy(a_in, active, i_sems.at[3]),
        pltpu.make_async_copy(n1_in, n1, i_sems.at[4]),
        pltpu.make_async_copy(qkv_in, qkv, i_sems.at[5]),
        pltpu.make_async_copy(c_in, c, i_sems.at[6]),
        pltpu.make_async_copy(inv_in, inv, i_sems.at[7]),
        pltpu.make_async_copy(dw1_in, dw1, i_sems.at[8]),
    ]
    loads[8].start()
    for index in (0, 1):
        loads[index].start()
    for load in fetch(0):
        load.start()
    for load in loads[2:8]:
        load.start()
    gk_sum[...] = jnp.zeros_like(gk_sum)
    gv_sum[...] = jnp.zeros_like(gv_sum)
    strip[...] = jnp.zeros_like(strip)
    far_sums[...] = jnp.zeros_like(far_sums)
    gain_sums[...] = jnp.zeros_like(gain_sums)
    out_c = 4 * width + 2 * ffn
    core_a = active.at[pl.ds(0, model), pl.ds(0, 2 * width)]
    scatter = Scatter(
        place,
        model // wide,
        [
            dict(grad=dw1, first=0, width=4 * width, out=out_c, core=None, beside=beside_a, along=along_a),
            dict(grad=dw1, first=2 * width, width=4 * width, out=out_c + 4 * width, core=None, beside=beside_d, along=along_d),
            half_group(w1, 4 * width, ffn, 4 * width, 0, core_f, beside_f, along_f),
            half_group(w1, 4 * width + ffn, ffn, 4 * width + ffn, 1, core_f, beside_f, along_f),
            half_group(gu.at[pl.ds(0, model)], 0, 2 * width, 0, 0, core_a, beside_a, along_a),
            half_group(gu.at[pl.ds(0, model)], 2 * width, 2 * width, 2 * width, 1, core_a, beside_a, along_a),
        ],
        tile,
        s_send,
        s_recv,
    )

    def own_weight(i):
        return jnp.where((i * CHUNK) // half == side, 1.0, 0.0).astype(f32)

    loads[8].wait()
    scatter.beside(0)
    scatter.beside(1)
    for index in (0, 1, 2):
        loads[index].wait()

    for i in range(steps):
        at = slice(i * CHUNK, (i + 1) * CHUNK)
        slot = i % 2
        if i + 1 < steps:
            if i + 1 >= steps - late:
                swap_late(i + 1 - steps + late).wait_recv()
            for load in fetch(i + 1):
                load.start()
        for load in fetch(i):
            load.wait()
        grad = part_buf[slot].astype(f32) + other_buf[slot].astype(f32)
        pulled, gain = norm_back(state_buf[slot], gains[5:6, :], grad)
        gain_sums[5:6, :] += gain * own_weight(i)
        total = cot[at, :].astype(f32) + pulled
        state_grad[at, :] = total
        gy[at, :] = total.astype(bf)

        def part(j, carry):
            cols = pl.ds(pl.multiple_of(4 * width + ffn + j * width, PAIR), width)
            here = pl.ds(pl.multiple_of(j * width, PAIR), width)
            grad_active = dot_nn(gy[at, :], w1[:, cols])
            gu[at, here] = (slope_buf[slot, :, here].astype(f32) * grad_active).astype(bf)
            return carry

        lax.fori_loop(0, ffn // width, part, 0)
        g_send[at, :] = dot_nt(gu[at, :], w1[:, 4 * width : 4 * width + ffn]).astype(bf)
        swap(i).start()
    for load in loads[3:8]:
        load.wait()
    fetch_state(0).start()
    fetch_e(0).start()

    def up_grads(t, carry):
        tile_rows = pl.ds(pl.multiple_of(t * CHUNK, CHUNK), CHUNK)
        w1[tile_rows, 4 * width : 4 * width + ffn] = dot_tn(n1[:, tile_rows], gu[...]).astype(bf)
        return carry

    def down_grads(t, carry):
        tile_rows = pl.ds(pl.multiple_of(t * CHUNK, CHUNK), CHUNK)
        w1[tile_rows, 4 * width + ffn :] = dot_tn(gy[:, tile_rows], active[...]).astype(bf)
        return carry

    scatter.along(0)
    lax.fori_loop(0, model // CHUNK, up_grads, 0)
    scatter.start(2)
    lax.fori_loop(0, model // CHUNK, down_grads, 0)
    scatter.start(3)
    scatter.along(1)
    scatter.total(0)
    scatter.beside(2)
    n0 = cot
    late_loads = [
        pltpu.make_async_copy(n0_in, n0, i_sems.at[0]),
        pltpu.make_async_copy(x_own, n1.at[pl.ds(half, half)], i_sems.at[1]),
    ]
    for load in late_loads:
        load.start()

    dw0 = gu
    l_send = n1

    def lanes(base_lane, pair):
        return pl.ds(pl.multiple_of(base_lane + pair * PAIR, PAIR), PAIR)

    def attend_back(i):
        at = slice(i * CHUNK, (i + 1) * CHUNK)
        slot = i % 2
        if i + 1 < steps:
            fetch_state(i + 1).start()
        fetch_state(i).wait()
        swap(i).wait_recv()
        grad = g_send[at, :].astype(f32) + g_recv[at, :].astype(f32)
        pulled, gain = norm_back(state_buf[slot], gains[1:2, :], grad)
        gain_sums[1:2, :] += gain * own_weight(i)
        total = state_grad[at, :] + pulled
        state_grad[at, :] = total
        gy[at, :] = total.astype(bf)
        g_send[at, :width] = dot_nn(gy[at, :], w1[:, 3 * width : 4 * width]).astype(bf)
        low, high, shift = near_window(i, rows)

        def one(pair, carry):
            step = i * pairs + pair

            @pl.when(step + 1 < steps * pairs)
            def _():
                fetch_e(step + 1).start()

            fetch_e(step).wait()
            e_slot = lax.rem(step, 2)

            def near(head, grad):
                strip[2 * pair + head, :, shift : shift + high - low] += grad[:, low:high]
                for edge, (start, end) in enumerate(((0, low), (high, rows))):
                    if end > start:
                        folded = jnp.sum(grad[:, start:end].reshape(CHUNK // 8, 8, end - start), axis=0)
                        wide_sum = folded[:, :128]
                        for lane in range(128, end - start, 128):
                            wide_sum = wide_sum + folded[:, lane : lane + 128]
                        far_sums[edge, 2 * pair + head] += wide_sum

            gq, gk, gv = softmax_back_pair(
                qkv[at, lanes(0, pair)],
                qkv[:, lanes(width, pair)],
                qkv[:, lanes(2 * width, pair)],
                c[at, lanes(0, pair)],
                inv[at, lanes(0, pair)],
                g_send[at, lanes(0, pair)],
                (e_buf[e_slot, 0], e_buf[e_slot, 1]),
                near,
            )
            gqkv[at, lanes(0, pair)] = gq.astype(bf)
            gk_sum[:, lanes(0, pair)] += gk
            gv_sum[:, lanes(0, pair)] += gv
            return carry

        lax.fori_loop(0, pairs, one, 0)

    for i in range(steps):
        swap(i).wait_send()
        attend_back(i)
        if i == 0:
            scatter.beside(3)
        if i == 1:
            scatter.total(1)
            scatter.along(2)
        if i == 2:
            scatter.along(3)
        if i == 3:
            scatter.total(2)
    for load in late_loads:
        load.wait()
    gqkv[:, width : 2 * width] = gk_sum[...].astype(bf)
    gqkv[:, 2 * width :] = gv_sum[...].astype(bf)

    ones = jnp.ones((8, 3 * width), f32)

    def weight_grads_a(t, carry):
        tile_rows = pl.ds(pl.multiple_of(t * CHUNK, CHUNK), CHUNK)
        grads = dot_tn(n0[:, tile_rows], gqkv[...])
        dw0[tile_rows, : 3 * width] = grads.astype(bf)
        products = lax.dot_general(
            ones,
            grads * w1[tile_rows, : 3 * width].astype(f32),
            (((1,), (1,)), ((), ())),
            precision=HIGH,
            preferred_element_type=f32,
        )
        gain_sums[0:1, tile_rows] = products[0:1, :] / gains[0:1, tile_rows]
        return carry

    def weight_grads_o(t, carry):
        tile_rows = pl.ds(pl.multiple_of(t * CHUNK, CHUNK), CHUNK)
        dw0[tile_rows, 3 * width :] = dot_tn(gy[:, tile_rows], c[...]).astype(bf)
        return carry

    lax.fori_loop(0, model // CHUNK, weight_grads_a, 0)
    scatter.start(4)
    last = []
    for part in range(half // CHUNK):
        there = pl.ds(pl.multiple_of((1 - side) * half + part * CHUNK, CHUNK), CHUNK)
        at = pl.ds(part * CHUNK, CHUNK)
        l_send[at, :] = dot_nt(gqkv[there, :], w1[:, : 3 * width]).astype(bf)
        last.append(remote(l_send.at[at], l_recv.at[at], l_sems.at[0, part], l_sems.at[1, part], place.across()))
        last[part].start()
    lax.fori_loop(0, model // CHUNK, weight_grads_o, 0)
    scatter.start(5)
    scatter.beside(4)
    summed = Total(place, held, t_send, t_recv)
    folded[...] = jnp.zeros_like(folded)

    def fold(head, carry):
        folded[pl.ds(head, 1), :] = fold_rows(fold_near(strip[head]))
        return carry

    lax.fori_loop(0, 2 * pairs, fold, 0)
    table = bucket_sums(folded[...], CHUNK + EDGE, True)
    bucket = lax.broadcasted_iota(jnp.int32, (1, 128), 1)
    for head in range(2 * pairs):
        far = [jnp.sum(far_sums[edge, head]) for edge in range(2)]
        folded[head : head + 1, :128] = jnp.where(
            bucket == NB // 2 - 1, far[0], jnp.where(bucket == NB - 1, far[1], 0.0)
        )
    table = table + folded[:, :128]
    held[0] = jnp.zeros_like(held[0])
    held[0, :8, :] = gain_sums[...] + dec_gains[...]
    held[0, 8:, pl.ds(pl.multiple_of(side * 256, 128), 128)] = table
    held[0, 8:, pl.ds(pl.multiple_of(side * 256 + 128, 128), 128)] = dec_table[...]
    summed.start()
    scatter.beside(5)
    summed.step(0)
    scatter.along(4)
    summed.step(1)
    scatter.total(3)
    for part in range(half // CHUNK):
        here = pl.ds(pl.multiple_of(side * half + part * CHUNK, CHUNK), CHUNK)
        at = pl.ds(part * CHUNK, CHUNK)
        own = dot_nt(gqkv[here, :], w1[:, : 3 * width])
        if part == 0:
            scatter.along(5)
            summed.step(2)
        last[part].wait_recv()
        grad = own + l_recv[at, :].astype(f32)
        pulled, unused = norm_back(n1[pl.ds(half + part * CHUNK, CHUNK), :].astype(f32), gains[0:1, :], grad)
        grad_out[at, :] = state_grad[here, :] + pulled
    scatter.total(4)
    scatter.total(5)
    total_sums[...] = summed.finish()
    for group in range(6):
        scatter.finish(group)
    scatter.close()
    for i in range(late):
        swap_late(i).wait_send()
    for copy in last:
        copy.wait_send()


def enc_backward(wide, x_own, cot_own, cot_other, gains, dec_gains, dec_table, part_own, part_other, dw1, saved):
    half, model = x_own.shape
    rows = 2 * half
    w1, n0, qkv, c, inv, e_all, e1, n1, slope, active, ef = saved
    width, ffn = c.shape[1], active.shape[1]
    pairs = width // PAIR
    steps = rows // CHUNK
    bf, f32 = jnp.bfloat16, jnp.float32
    shape = jax.ShapeDtypeStruct
    dma = pltpu.SemaphoreType.DMA
    return pl.pallas_call(
        functools.partial(enc_backward_kernel, wide),
        in_specs=[any_spec()] * 3 + [vmem_spec()] * 3 + [any_spec()] * 14,
        out_shape=[
            shape((half, model), f32),
            shape((model // wide, 12 * width + 2 * ffn), bf),
            shape((16, model), f32),
            shape((rows - part_other.shape[0], model), bf),
        ],
        out_specs=[vmem_spec()] * 3 + [any_spec()],
        scratch_shapes=[
            pltpu.VMEM((8, model), f32),
            pltpu.VMEM((2, 2 * pairs, 8, 128), f32),
            pltpu.VMEM((8, 2 * NEAR), f32),
            pltpu.VMEM((7 + wide // 2, 16, model), f32),
            pltpu.VMEM(w1.shape, bf),
            pltpu.VMEM(dw1.shape, bf),
            pltpu.VMEM(qkv.shape, bf),
            pltpu.VMEM(c.shape, bf),
            pltpu.VMEM(inv.shape, f32),
            pltpu.VMEM(n1.shape, bf),
            pltpu.VMEM(active.shape, bf),
            pltpu.VMEM((rows, model), bf),
            pltpu.VMEM((2, 2, CHUNK, rows), bf),
            pltpu.VMEM((2, CHUNK, model), f32),
            pltpu.VMEM((2, CHUNK, ffn), bf),
            pltpu.VMEM((2, CHUNK, model), bf),
            pltpu.VMEM((2, CHUNK, model), bf),
            pltpu.VMEM((rows, model), bf),
            pltpu.VMEM((rows, model), bf),
            pltpu.VMEM((half, model), bf),
            pltpu.VMEM((rows, model), f32),
            pltpu.VMEM((rows, model), bf),
            pltpu.VMEM((rows, ffn), bf),
            pltpu.VMEM((rows, 3 * width), bf),
            pltpu.VMEM((rows, width), f32),
            pltpu.VMEM((rows, width), f32),
            pltpu.VMEM((2 * pairs, CHUNK, NEAR), f32),
        ]
        + scatter_buffers(wide, model, 2 * ffn)
        + scatter_buffers(wide, model, 4 * width)[1:]
        + scatter_buffers(wide, model, 4 * width)[1:]
        + [
            dma((6, scatter_slots(wide))),
            dma((6, scatter_slots(wide))),
            dma((2 + wide // 2,)),
            dma((2 + wide // 2,)),
            dma((2, steps)),
            dma((2, steps)),
            dma((2, half // CHUNK)),
            dma((2,)),
            dma((4, 2)),
            dma((10,)),
        ],
        compiler_params=pltpu.CompilerParams(
            collective_id=1, has_side_effects=True, vmem_limit_bytes=VMEM_BYTES
        ),
        cost_estimate=pl.CostEstimate(flops=2 * 10**10, bytes_accessed=6 * 10**7, transcendentals=0),
    )(x_own, cot_own, cot_other, gains, dec_gains, dec_table, part_own, part_other, dw1, w1, n0, qkv, c, inv, e_all, e1, n1, slope, active, ef)


def fold_offsets(grad):
    rows = grad.shape[0]
    total = jnp.zeros((8, 2 * rows), jnp.float32)
    blank = jnp.zeros((8, rows), jnp.float32)
    for a in range(rows // 8):
        wider = jnp.concatenate([grad[8 * a : 8 * a + 8, :], blank], axis=1)
        total = total + pltpu.roll(wider, (rows - 8 * a) % (2 * rows), 1)
    return total


def decoder_kernel(
    wide,
    dec_own,
    dec_other,
    dcot_own,
    dcot_other,
    cot_own,
    down_in,
    gains,
    base,
    dec_lengths,
    enc_lengths,
    mem_in,
    w_in,
    dec_out,
    dec_grad,
    tile,
    gain_sums,
    table,
    part_own,
    part_other,
    cot_other,
    dw1_all,
    pack,
    folded,
    w,
    mem,
    dec,
    dcot,
    state,
    normals,
    qkv,
    c,
    inv,
    e_self,
    e_cross,
    strip,
    kv,
    active,
    ga,
    gu,
    grad_state,
    gy,
    gqkv,
    gkv,
    y_send,
    y_recv,
    dw,
    core_f,
    beside_f,
    along_f,
    core_d,
    core_c,
    s_send,
    s_recv,
    g_send,
    g_recv,
    g_local,
    y_sems,
    x_sems,
    p_sems,
    o_sems,
    i_sems,
):
    place = Place(wide)
    side = place.side
    half = dec_own.shape[0]
    rows = 2 * half
    model = dec_own.shape[1]
    width = c.shape[2]
    ffn = active.shape[1]
    pairs = width // PAIR
    span = mem.shape[0]
    bf, f32 = jnp.bfloat16, jnp.float32
    place.greet()
    mine = pl.ds(pl.multiple_of(side * half, 16), half)
    theirs = pl.ds(pl.multiple_of((1 - side) * half, 16), half)
    at_d, at_f = 4 * width, 8 * width

    gather = Gather(place, pack, [(0, ffn // 2, w, at_f + ffn), (ffn // 2, ffn // 2, w, at_f + ffn + ffn // 2)], g_send, g_recv, g_local)
    def load_w(first, count, sem):
        cols = pl.ds(first, count)
        return pltpu.make_async_copy(w_in.at[:, cols], w.at[:, cols], i_sems.at[sem])

    loads = [
        load_w(0, 4 * width, 0),
        load_w(at_d, 4 * width, 1),
        pltpu.make_async_copy(mem_in, mem, i_sems.at[2]),
        load_w(at_f, ffn, 3),
        pltpu.make_async_copy(dec_own, dec.at[mine], i_sems.at[4]),
        pltpu.make_async_copy(dcot_own, dcot.at[mine], i_sems.at[5]),
        pltpu.make_async_copy(dec_other, dec.at[theirs], i_sems.at[6]),
        pltpu.make_async_copy(dcot_other, dcot.at[theirs], i_sems.at[7]),
        pltpu.make_async_copy(down_in.at[1], pack, i_sems.at[8]),
    ]
    for index in (8, 4, 6, 0, 5, 7, 2, 1, 3):
        loads[index].start()
    cot_part = cot_own.shape[0] // 4

    def swap_cot(i):
        at = pl.ds(i * cot_part, cot_part)
        return remote(cot_own.at[at], cot_other.at[at], x_sems.at[0, i], x_sems.at[1, i], place.across())

    swap_cot(0).start()
    swap_cot(1).start()
    loads[8].wait()
    gather.start(0)
    gather.start(1)
    build_strip(strip, base, pairs, rows, rows)
    gain_sums[...] = jnp.zeros_like(gain_sums)
    folded[...] = jnp.zeros_like(folded)
    scatter = Scatter(
        place,
        model // wide,
        [
            half_group(w, at_f, ffn, 0, 0, core_f, beside_f, along_f),
            half_group(w, at_f + ffn, ffn, ffn, 1, core_f, beside_f, along_f),
            dict(grad=dw, first=at_d, width=4 * width, core=core_d),
            dict(grad=dw, first=0, width=4 * width, core=core_c),
        ],
        tile,
        s_send,
        s_recv,
    )

    def swap(kind):
        return remote(y_send.at[kind], y_recv.at[kind], y_sems.at[0, kind], y_sems.at[1, kind], place.across())

    def send_branch(kind, value):
        y_send[kind] = value.astype(bf)
        swap(kind).start()

    def branch(kind):
        swap(kind).wait_recv()
        return y_send[kind].astype(f32) + y_recv[kind].astype(f32)

    def lanes(base_lane, pair):
        return pl.ds(pl.multiple_of(base_lane + pair * PAIR, PAIR), PAIR)

    def norm_to(index, gain, value):
        state[index] = value
        normals[index] = normed(value, gains[gain : gain + 1, :]).astype(bf)

    loads[4].wait()
    loads[6].wait()
    norm_to(0, 2, dec[...].astype(f32))
    loads[0].wait()
    qkv[:, : 3 * width] = dot_nn(normals[0], w[:, : 3 * width]).astype(bf)

    def self_pair(pair, carry):
        allowed = documents(dec_lengths, (rows, 1), 0) == documents(dec_lengths, (1, rows), 0)
        allowed = allowed & (
            lax.broadcasted_iota(jnp.int32, (rows, rows), 1) <= lax.broadcasted_iota(jnp.int32, (rows, rows), 0)
        )

        def bias(head):
            return strip[2 * pair + head, :, :rows]

        def store(head, weights):
            e_self[2 * pair + head] = weights

        inverse, context = softmax_pair(
            qkv[:, lanes(0, pair)], qkv[:, lanes(width, pair)], qkv[:, lanes(2 * width, pair)], allowed, bias, store
        )
        inv[0, :, lanes(0, pair)] = inverse
        c[0, :, lanes(0, pair)] = context
        return carry

    lax.fori_loop(0, pairs, self_pair, 0)
    send_branch(0, dot_nt(c[0], w[:, 3 * width : 4 * width]))

    gather.relay_along(0)
    gather.relay_along(1)

    loads[2].wait()
    loads[1].wait()

    def cross_keys(i, carry):
        at = pl.ds(pl.multiple_of(i * CHUNK, CHUNK), CHUNK)
        kv[at, :] = dot_nn(mem[at, :], w[:, at_d + width : at_d + 3 * width]).astype(bf)
        return carry

    lax.fori_loop(0, span // CHUNK, cross_keys, 0)
    gather.relay_beside(0)
    gather.relay_beside(1)
    norm_to(1, 3, state[0] + branch(0))
    swap_cot(2).start()
    qkv[:, 3 * width :] = dot_nn(normals[1], w[:, at_d : at_d + width]).astype(bf)

    def cross_pair(pair, carry):
        allowed = documents(dec_lengths, (rows, 1), 0) == documents(enc_lengths, (1, span), 0)

        def store(head, weights):
            e_cross[2 * pair + head] = weights

        inverse, context = softmax_pair(
            qkv[:, lanes(3 * width, pair)], kv[:, lanes(0, pair)], kv[:, lanes(width, pair)], allowed, None, store
        )
        inv[1, :, lanes(0, pair)] = inverse
        c[1, :, lanes(0, pair)] = context
        return carry

    lax.fori_loop(0, pairs, cross_pair, 0)
    send_branch(1, dot_nt(c[1], w[:, at_d + 3 * width : at_d + 4 * width]))

    for index in (5, 7, 3):
        loads[index].wait()
    gather.finish(0)
    gather.finish(1)
    ga[...] = dot_nn(dcot[...], w[:, at_f + ffn :]).astype(f32)
    norm_to(2, 4, state[1] + branch(1))
    swap_cot(3).start()

    def hidden(j, carry):
        here = pl.ds(pl.multiple_of(j * width, PAIR), width)
        cols = pl.ds(pl.multiple_of(at_f + j * width, PAIR), width)
        value, turn = gelu_pair(dot_nn(normals[2], w[:, cols]))
        active[:, here] = value.astype(bf)
        gu[:, here] = (turn * ga[:, here]).astype(bf)
        return carry

    lax.fori_loop(0, ffn // width, hidden, 0)
    send_branch(3, dot_nt(gu[...], w[:, at_f : at_f + ffn]))
    y_send[2] = dot_nt(active[...], w[:, at_f + ffn :]).astype(bf)

    def up_grads(t, carry):
        tile_rows = pl.ds(pl.multiple_of(t * CHUNK, CHUNK), CHUNK)
        w[tile_rows, at_f : at_f + ffn] = dot_tn(normals[2, :, tile_rows], gu[...]).astype(bf)
        return carry

    def down_grads(t, carry):
        tile_rows = pl.ds(pl.multiple_of(t * CHUNK, CHUNK), CHUNK)
        w[tile_rows, at_f + ffn :] = dot_tn(dcot[:, tile_rows], active[...]).astype(bf)
        return carry

    gather.close()
    lax.fori_loop(0, model // CHUNK, up_grads, 0)
    scatter.start(0)
    lax.fori_loop(0, model // CHUNK, down_grads, 0)
    scatter.start(1)
    scatter.beside(0)

    row = lax.broadcasted_iota(jnp.int32, (rows, 1), 0)
    counted = jnp.where(row // half == side, 1.0, 0.0).astype(f32)

    def pull(index, gain, grad):
        values = state[index]
        pulled, unused = norm_back(values, gains[gain : gain + 1, :], grad)
        scale = lax.rsqrt(jnp.mean(values * values, axis=1, keepdims=True) + EPS) * counted
        gain_sums[gain : gain + 1, :] += jnp.sum(grad * values * scale, axis=0, keepdims=True)
        return pulled

    grad_state[...] = dcot[...].astype(f32) + pull(2, 4, branch(3))
    swap(2).start()
    gy[1] = grad_state[...].astype(bf)
    gc = dot_nn(gy[1], w[:, at_d + 3 * width : at_d + 4 * width]).astype(bf)
    y_send[5, :, :width] = gc
    scatter.beside(1)

    def cross_back(pair, carry):
        gq, gk, gv = softmax_back_pair(
            qkv[:, lanes(3 * width, pair)],
            kv[:, lanes(0, pair)],
            kv[:, lanes(width, pair)],
            c[1, :, lanes(0, pair)],
            inv[1, :, lanes(0, pair)],
            y_send[5, :, lanes(0, pair)],
            (e_cross[2 * pair], e_cross[2 * pair + 1]),
            None,
        )
        gqkv[:, lanes(3 * width, pair)] = gq.astype(bf)
        gkv[:, lanes(0, pair)] = gk.astype(bf)
        gkv[:, lanes(width, pair)] = gv.astype(bf)
        return carry

    lax.fori_loop(0, pairs, cross_back, 0)
    send_branch(4, dot_nt(gqkv[:, 3 * width :], w[:, at_d : at_d + width]))

    part = kv

    def swap_part(i):
        at = pl.ds(pl.multiple_of(i * CHUNK, CHUNK), CHUNK)
        return remote(part.at[at], part_other.at[at], p_sems.at[0, i], p_sems.at[1, i], place.across())

    def keep_part(i):
        at = pl.ds(pl.multiple_of(i * CHUNK, CHUNK), CHUNK)
        return pltpu.make_async_copy(part.at[at], part_own.at[at], o_sems.at[i])

    for i in range(span // CHUNK):
        at = pl.ds(i * CHUNK, CHUNK)
        part[at, :] = dot_nt(gkv[at, :], w[:, at_d + width : at_d + 3 * width]).astype(bf)
        keep_part(i).start()

    def cross_grads(t, carry):
        tile_rows = pl.ds(pl.multiple_of(t * CHUNK, CHUNK), CHUNK)
        dw[tile_rows, at_d : at_d + width] = dot_tn(normals[1, :, tile_rows], gqkv[:, 3 * width :]).astype(bf)
        dw[tile_rows, at_d + width : at_d + 3 * width] = dot_tn(mem[:, tile_rows], gkv[...]).astype(bf)
        dw[tile_rows, at_d + 3 * width : at_f] = dot_tn(gy[1, :, tile_rows], c[1]).astype(bf)
        return carry

    lax.fori_loop(0, model // CHUNK, cross_grads, 0)
    scatter.start(2)
    scatter.along(0)

    grad_state[...] = grad_state[...] + pull(1, 3, branch(4))
    early = part_other.shape[0] // CHUNK
    swap_part(0).start()
    gy[0] = grad_state[...].astype(bf)
    y_send[5, :, :width] = dot_nn(gy[0], w[:, 3 * width : 4 * width]).astype(bf)

    def self_back(pair, carry):
        def near(head, grad):
            folded[pl.ds(2 * pair + head, 1), :] = fold_rows(fold_offsets(grad))

        gq, gk, gv = softmax_back_pair(
            qkv[:, lanes(0, pair)],
            qkv[:, lanes(width, pair)],
            qkv[:, lanes(2 * width, pair)],
            c[0, :, lanes(0, pair)],
            inv[0, :, lanes(0, pair)],
            y_send[5, :, lanes(0, pair)],
            (e_self[2 * pair], e_self[2 * pair + 1]),
            near,
        )
        gqkv[:, lanes(0, pair)] = gq.astype(bf)
        gqkv[:, lanes(width, pair)] = gk.astype(bf)
        gqkv[:, lanes(2 * width, pair)] = gv.astype(bf)
        return carry

    lax.fori_loop(0, pairs, self_back, 0)

    y_send[5] = dot_nt(gqkv[:, : 3 * width], w[:, : 3 * width]).astype(bf)
    back = remote(y_send.at[5, theirs], y_recv.at[5, theirs], y_sems.at[0, 5], y_sems.at[1, 5], place.across())
    back.start()
    for i in range(1, early):
        swap_part(i).start()
    scatter.along(1)
    scatter.merge(2)
    keep_dw = [
        pltpu.make_async_copy(
            dw.at[:, scatter.columns(2 + i, place.core)],
            dw1_all.at[:, pl.ds((1 - i) * 2 * width, 2 * width)],
            i_sems.at[i],
        )
        for i in range(2)
    ]
    keep_dw[0].start()

    def self_grads(t, carry):
        tile_rows = pl.ds(pl.multiple_of(t * CHUNK, CHUNK), CHUNK)
        dw[tile_rows, : 3 * width] = dot_tn(normals[0, :, tile_rows], gqkv[:, : 3 * width]).astype(bf)
        dw[tile_rows, 3 * width : at_d] = dot_tn(gy[0, :, tile_rows], c[0]).astype(bf)
        return carry

    lax.fori_loop(0, model // CHUNK, self_grads, 0)
    scatter.start(3)
    table[...] = bucket_sums(folded[...], rows, False)
    scatter.total(0)
    scatter.total(1)
    back.wait_recv()
    grad = y_send[5, mine, :].astype(f32) + y_recv[5, mine, :].astype(f32)
    pulled, gain = norm_back(state[0, mine, :], gains[2:3, :], grad)
    gain_sums[2:3, :] += gain
    dec_grad[...] = grad_state[mine, :] + pulled
    swap(2).wait_recv()
    dec_out[...] = (state[2, mine, :] + y_send[2, mine, :].astype(f32) + y_recv[2, mine, :].astype(f32)).astype(bf)
    scatter.merge(3)
    keep_dw[1].start()
    for i in range(early):
        swap_part(i).wait()
    for i in range(span // CHUNK):
        keep_part(i).wait()
    for copy in keep_dw:
        copy.wait()
    for i in range(4):
        swap_cot(i).wait()
    for group in range(2):
        scatter.finish(group)
    scatter.close()
    for kind in range(5):
        swap(kind).wait_send()
    back.wait_send()


def decoder(wide, dec_rows, dcot_rows, cot_own, down, gains, base, dec_lengths, enc_lengths, mem, w2):
    half, model = dec_rows[0].shape
    rows = 2 * half
    span = mem.shape[0]
    pairs = base.shape[0]
    width = pairs * PAIR
    ffn = down.shape[2]
    late = span // CHUNK // 2 * CHUNK
    bf, f32 = jnp.bfloat16, jnp.float32
    shape = jax.ShapeDtypeStruct
    dma = pltpu.SemaphoreType.DMA
    return pl.pallas_call(
        functools.partial(decoder_kernel, wide),
        in_specs=[any_spec()] * 6 + [vmem_spec()] * 2 + [smem_spec()] * 2 + [any_spec()] * 2,
        out_shape=[
            shape((half, model), bf),
            shape((half, model), f32),
            shape((model // wide, 2 * ffn), bf),
            shape((8, model), f32),
            shape((8, 128), f32),
            shape((span, model), bf),
            shape((late, model), bf),
            shape(cot_own.shape, bf),
            shape((model, 4 * width), bf),
        ],
        out_specs=[vmem_spec()] * 5 + [any_spec()] * 4,
        scratch_shapes=[
            pltpu.VMEM(down.shape[1:], bf),
            pltpu.VMEM((8, 2 * rows), f32),
            pltpu.VMEM((model, 8 * width + 2 * ffn), bf),
            pltpu.VMEM((span, model), bf),
            pltpu.VMEM((rows, model), bf),
            pltpu.VMEM((rows, model), bf),
            pltpu.VMEM((3, rows, model), f32),
            pltpu.VMEM((3, rows, model), bf),
            pltpu.VMEM((rows, 4 * width), bf),
            pltpu.VMEM((2, rows, width), bf),
            pltpu.VMEM((2, rows, width), f32),
            pltpu.VMEM((2 * pairs, rows, rows), bf),
            pltpu.VMEM((2 * pairs, rows, span), bf),
            pltpu.VMEM((2 * pairs, rows, 2 * rows), f32),
            pltpu.VMEM((span, 2 * width), bf),
            pltpu.VMEM((rows, ffn), bf),
            pltpu.VMEM((rows, ffn), f32),
            pltpu.VMEM((rows, ffn), bf),
            pltpu.VMEM((rows, model), f32),
            pltpu.VMEM((2, rows, model), bf),
            pltpu.VMEM((rows, 4 * width), bf),
            pltpu.VMEM((span, 2 * width), bf),
            pltpu.VMEM((6, rows, model), bf),
            pltpu.VMEM((6, rows, model), bf),
            pltpu.VMEM((model, 8 * width), bf),
        ]
        + scatter_buffers(wide, model, 2 * ffn)
        + scatter_buffers(wide, model, 4 * width)[:1]
        + scatter_buffers(wide, model, 4 * width)[:1]
        + [
            dma((4, scatter_slots(wide))),
            dma((4, scatter_slots(wide))),
            dma((2, gather_slots(wide))),
            dma((2, gather_slots(wide))),
            dma((2,)),
            dma((2, 6)),
            dma((2, 4)),
            dma((2, span // CHUNK)),
            dma((span // CHUNK,)),
            dma((9,)),
        ],
        compiler_params=pltpu.CompilerParams(
            collective_id=2, has_side_effects=True, vmem_limit_bytes=VMEM_BYTES
        ),
        cost_estimate=pl.CostEstimate(flops=10**10, bytes_accessed=6 * 10**7, transcendentals=0),
    )(
        *dec_rows,
        *dcot_rows,
        cot_own,
        down,
        gains,
        base,
        dec_lengths,
        enc_lengths,
        mem,
        w2,
    )


def on_device(
    wide,
    enc_input,
    dec_input,
    enc_lengths,
    dec_lengths,
    attn_query,
    attn_kv,
    attn_out,
    ffn_up,
    ffn_down,
    gains,
    rel_bias,
    enc_cotangent,
    dec_cotangent,
):
    gain_rows = gains.astype(jnp.float32)
    heads_local = rel_bias.shape[2]
    side = lax.axis_index("narrow")
    width, ffn = DK * heads_local, ffn_up.shape[2]
    half = enc_input.shape[0]
    down = ffn_down.transpose(0, 2, 1)
    weights = (attn_query, attn_kv, attn_out.transpose(0, 2, 1), ffn_up, down)
    w1, w2, n0, qkv, context, inverse, exps, e1, n1, slope, active, ef, memory, dec_other, dcot_other = enc_forward(
        wide, enc_input, dec_input, dec_cotangent, weights, gain_rows, near_rows(rel_bias[0]), enc_lengths
    )
    dec_output, grad_dec, tile_two, dec_gains, dec_table, part_own, part_other, cot_other, dw1 = decoder(
        wide,
        (dec_input, dec_other),
        (dec_cotangent, dcot_other),
        enc_cotangent,
        down,
        gain_rows,
        base_rows(rel_bias[1], DEC, False),
        dec_lengths,
        enc_lengths,
        memory,
        w2,
    )
    grad_enc, tile_one, sums, unused = enc_backward(
        wide,
        enc_input,
        enc_cotangent,
        cot_other,
        gain_rows,
        dec_gains,
        dec_table,
        part_own,
        part_other,
        dw1,
        (w1, n0, qkv, context, inverse, exps, e1, n1, slope, active, ef),
    )
    tables = lax.dynamic_slice_in_dim(sums[8 : 8 + heads_local], side * 256, 256, 1)
    bias_grad = jnp.stack([tables[:, :NB].T, tables[:, 128 : 128 + NB].T])
    late = tile_one[:, 4 * width + 2 * ffn :]
    layers = (tile_one[:, : 4 * width], late[:, : 4 * width], late[:, 4 * width :])
    feeds = (tile_one[:, 4 * width : 4 * width + 2 * ffn], tile_two)
    return (
        lax.dynamic_slice_in_dim(ef, side * half, half).astype(jnp.bfloat16),
        dec_output,
        grad_enc,
        grad_dec,
        jnp.stack([layer[:, :width] for layer in layers]).astype(jnp.float32),
        jnp.stack(
            [jnp.stack([layer[:, width : 2 * width], layer[:, 2 * width : 3 * width]]) for layer in layers]
        ).astype(jnp.float32),
        jnp.stack([layer[:, 3 * width :].T for layer in layers]).astype(jnp.float32),
        jnp.stack([feed[:, :ffn] for feed in feeds]).astype(jnp.float32),
        jnp.stack([feed[:, ffn:].T for feed in feeds]).astype(jnp.float32),
        sums[:6],
        bias_grad,
    )


def ffn_backward(grad_rows, normed_rows, hidden, active, weight_up, weight_down):
    grad_active = jnp.einsum(
        "rd,fd->rf", grad_rows, weight_down, preferred_element_type=jnp.float32
    )
    grad_down = jnp.einsum("rf,rd->fd", active, grad_rows, preferred_element_type=jnp.float32)
    unused, pull = jax.vjp(gelu_tanh, hidden)
    grad_hidden = pull(grad_active)[0].astype(jnp.bfloat16)
    grad_up = jnp.einsum("rd,rf->df", normed_rows, grad_hidden, preferred_element_type=jnp.float32)
    grad_normed = jnp.einsum(
        "rf,df->rd", grad_hidden, weight_up, preferred_element_type=jnp.float32
    )
    return (grad_normed, grad_up, grad_down)


def norm_backward(values, gain, grad_normed):
    unused, pull = jax.vjp(rms_norm, values, gain)
    return pull(grad_normed)


def on_device_general(
    enc_input,
    dec_input,
    enc_lengths,
    dec_lengths,
    attn_query,
    attn_kv,
    attn_out,
    ffn_up,
    ffn_down,
    gains,
    rel_bias,
    enc_cotangent,
    dec_cotangent,
):
    weights = (
        lax.all_gather(attn_query, "wide", axis=1, tiled=True),
        lax.all_gather(attn_kv, "wide", axis=2, tiled=True),
        lax.all_gather(attn_out, "wide", axis=2, tiled=True),
        lax.all_gather(ffn_up, "wide", axis=1, tiled=True),
        lax.all_gather(ffn_down, "wide", axis=2, tiled=True),
    )
    gain_rows = gains.astype(jnp.float32)
    heads_local = rel_bias.shape[2]
    enc_segments = segment_ids(enc_lengths[0], ENC)
    dec_segments = segment_ids(dec_lengths[0], DEC)

    side = lax.axis_index("narrow")
    swap = [(0, 1), (1, 0)]

    def spread_rows(values):
        own = values.astype(jnp.bfloat16)
        other = lax.ppermute(own, "narrow", swap)
        return jnp.where(side == 0, jnp.concatenate([own, other]), jnp.concatenate([other, own]))

    def collect_rows(parts):
        half = parts.shape[0] // 2
        parts = parts.astype(jnp.bfloat16)
        other = lax.ppermute(lax.dynamic_slice_in_dim(parts, (1 - side) * half, half), "narrow", swap)
        own = lax.dynamic_slice_in_dim(parts, side * half, half)
        return own.astype(jnp.float32) + other.astype(jnp.float32)

    def attention_layer(normed_query, normed_keys, layer, base, query_segments, key_segments, causal):
        query = jnp.dot(normed_query, weights[0][layer], preferred_element_type=jnp.float32).astype(jnp.bfloat16)
        keys = jnp.dot(normed_keys, weights[1][layer, 0], preferred_element_type=jnp.float32).astype(jnp.bfloat16)
        values = jnp.dot(normed_keys, weights[1][layer, 1], preferred_element_type=jnp.float32).astype(jnp.bfloat16)
        saved = attend_forward(query, keys, values, base, query_segments, key_segments, causal)
        parts = jnp.dot(saved[1], weights[2][layer], preferred_element_type=jnp.float32)
        return ((query, keys, values, saved), collect_rows(parts))

    enc_start = enc_input.astype(jnp.float32)
    rows_a = spread_rows(rms_norm(enc_start, gain_rows[0]))
    kept_a, branch = attention_layer(
        rows_a, rows_a, 0, base_rows(rel_bias[0], ENC, True), enc_segments, enc_segments, False
    )
    enc_mid = enc_start + branch
    rows_b = spread_rows(rms_norm(enc_mid, gain_rows[1]))
    hidden_b = jnp.dot(rows_b, weights[3][0], preferred_element_type=jnp.float32)
    active_b = gelu_tanh(hidden_b).astype(jnp.bfloat16)
    enc_final = enc_mid + collect_rows(
        jnp.dot(active_b, weights[4][0], preferred_element_type=jnp.float32)
    )
    memory = spread_rows(rms_norm(enc_final, gain_rows[5]))
    dec_start = dec_input.astype(jnp.float32)
    rows_c = spread_rows(rms_norm(dec_start, gain_rows[2]))
    kept_c, branch = attention_layer(
        rows_c, rows_c, 1, base_rows(rel_bias[1], DEC, False), dec_segments, dec_segments, True
    )
    dec_one = dec_start + branch
    rows_d = spread_rows(rms_norm(dec_one, gain_rows[3]))
    kept_d, branch = attention_layer(
        rows_d, memory, 2, None, dec_segments, enc_segments, False
    )
    dec_two = dec_one + branch
    rows_e = spread_rows(rms_norm(dec_two, gain_rows[4]))
    hidden_e = jnp.dot(rows_e, weights[3][1], preferred_element_type=jnp.float32)
    active_e = gelu_tanh(hidden_e).astype(jnp.bfloat16)
    dec_final = dec_two + collect_rows(
        jnp.dot(active_e, weights[4][1], preferred_element_type=jnp.float32)
    )
    def attention_back(grad_state, kept, normed_query, normed_keys, layer, span, two_sided):
        grad_rows = spread_rows(grad_state)
        query, keys, values, saved = kept
        grad_context = dot_nt(grad_rows, weights[2][layer]).astype(jnp.bfloat16)
        grad_out = dot_tn(saved[1], grad_rows)
        result = attend_backward(query, keys, values, saved, grad_context, span > 0)
        grad_q, grad_k, grad_v = result[:3]
        sums = [
            dot_tn(normed_query, grad_q),
            dot_tn(normed_keys, grad_k),
            dot_tn(normed_keys, grad_v),
            grad_out,
            table_grad(result[3], span, two_sided) if span else None,
        ]
        query_part = dot_nt(grad_q, weights[0][layer])
        key_part = dot_nt(grad_k, weights[1][layer, 0]) + dot_nt(grad_v, weights[1][layer, 1])
        return (query_part, key_part, sums)

    grad_dec = dec_cotangent.astype(jnp.float32)
    grad_normed, up_e, down_e = ffn_backward(
        spread_rows(grad_dec), rows_e, hidden_e, active_e, weights[3][1], weights[4][1]
    )
    grad_back, gain_e = norm_backward(dec_two, gain_rows[4], collect_rows(grad_normed))
    grad_dec = grad_dec + grad_back
    query_part, memory_part, sums_d = attention_back(
        grad_dec, kept_d, rows_d, memory, 2, 0, False
    )
    grad_normed, grad_memory = collect_rows(query_part), collect_rows(memory_part)
    grad_back, gain_d = norm_backward(dec_one, gain_rows[3], grad_normed)
    grad_dec = grad_dec + grad_back
    query_part, key_part, sums_c = attention_back(
        grad_dec, kept_c, rows_c, rows_c, 1, DEC, False
    )
    grad_back, gain_c = norm_backward(dec_start, gain_rows[2], collect_rows(query_part + key_part))
    grad_dec = grad_dec + grad_back
    grad_enc = enc_cotangent.astype(jnp.float32)
    grad_back, gain_m = norm_backward(enc_final, gain_rows[5], grad_memory)
    grad_enc = grad_enc + grad_back
    grad_normed, up_b, down_b = ffn_backward(
        spread_rows(grad_enc), rows_b, hidden_b, active_b, weights[3][0], weights[4][0]
    )
    grad_back, gain_b = norm_backward(enc_mid, gain_rows[1], collect_rows(grad_normed))
    grad_enc = grad_enc + grad_back
    query_part, key_part, sums_a = attention_back(
        grad_enc, kept_a, rows_a, rows_a, 0, ENC, True
    )
    grad_back, gain_a = norm_backward(enc_start, gain_rows[0], collect_rows(query_part + key_part))
    grad_enc = grad_enc + grad_back
    grad_query = jnp.stack([sums_a[0], sums_c[0], sums_d[0]])
    grad_kv = jnp.stack(
        [
            jnp.stack([sums_a[1], sums_a[2]]),
            jnp.stack([sums_c[1], sums_c[2]]),
            jnp.stack([sums_d[1], sums_d[2]]),
        ]
    )
    grad_out = jnp.stack([sums_a[3], sums_c[3], sums_d[3]])
    grad_up = jnp.stack([up_b, up_e])
    grad_down = jnp.stack([down_b, down_e])
    tiles = (
        lax.psum_scatter(
            grad_query.astype(jnp.bfloat16), "wide", scatter_dimension=1, tiled=True
        ).astype(jnp.float32),
        lax.psum_scatter(
            grad_kv.astype(jnp.bfloat16), "wide", scatter_dimension=2, tiled=True
        ).astype(jnp.float32),
        lax.psum_scatter(
            grad_out.astype(jnp.bfloat16), "wide", scatter_dimension=2, tiled=True
        ).astype(jnp.float32),
        lax.psum_scatter(
            grad_up.astype(jnp.bfloat16), "wide", scatter_dimension=1, tiled=True
        ).astype(jnp.float32),
        lax.psum_scatter(
            grad_down.astype(jnp.bfloat16), "wide", scatter_dimension=2, tiled=True
        ).astype(jnp.float32),
    )
    tiles = (
        lax.psum(tiles[0].astype(jnp.bfloat16), "dp").astype(jnp.float32),
        lax.psum(tiles[1].astype(jnp.bfloat16), "dp").astype(jnp.float32),
        lax.psum(tiles[2].astype(jnp.bfloat16), "dp").astype(jnp.float32),
        lax.psum(tiles[3].astype(jnp.bfloat16), "dp").astype(jnp.float32),
        lax.psum(tiles[4].astype(jnp.bfloat16), "dp").astype(jnp.float32),
    )
    gain_grads = jnp.stack([gain_a, gain_b, gain_c, gain_d, gain_e, gain_m])
    column = lax.axis_index("narrow") * heads_local
    bias_local = jnp.stack([sums_a[4], sums_c[4]])
    bias_full = lax.dynamic_update_slice(
        jnp.zeros((2, NB, H), jnp.float32), bias_local, (0, 0, column)
    )
    gain_total, bias_total = lax.psum((gain_grads, bias_full), ("dp", "wide", "narrow"))
    bias_grad = lax.dynamic_slice(bias_total, (0, 0, column), (2, NB, heads_local))
    return (
        enc_final.astype(jnp.bfloat16),
        dec_final.astype(jnp.bfloat16),
        grad_enc,
        grad_dec,
        tiles[0],
        tiles[1],
        tiles[2],
        tiles[3],
        tiles[4],
        gain_total,
        bias_grad,
    )


def solution(mesh):
    wide = mesh.shape["wide"]

    def body(*args):
        if args[4].shape[1] % 16 or wide % 2:
            return on_device_general(*args)
        return on_device(wide, *args)

    return jax.shard_map(
        body,
        mesh=mesh,
        in_specs=(
            P(("dp", "wide", "narrow"), None),
            P(("dp", "wide", "narrow"), None),
            P(("dp", "wide"), None),
            P(("dp", "wide"), None),
            P(None, "wide", "narrow"),
            P(None, None, "wide", "narrow"),
            P(None, "narrow", "wide"),
            P(None, "wide", "narrow"),
            P(None, "narrow", "wide"),
            P(),
            P(None, None, "narrow"),
            P(("dp", "wide", "narrow"), None),
            P(("dp", "wide", "narrow"), None),
        ),
        out_specs=(
            P(("dp", "wide", "narrow"), None),
            P(("dp", "wide", "narrow"), None),
            P(("dp", "wide", "narrow"), None),
            P(("dp", "wide", "narrow"), None),
            P(None, "wide", "narrow"),
            P(None, None, "wide", "narrow"),
            P(None, "narrow", "wide"),
            P(None, "wide", "narrow"),
            P(None, "narrow", "wide"),
            P(),
            P(None, None, "narrow"),
        ),
        check_vma=False,
    )
```

```python
import functools
import math

import jax
import jax.numpy as jnp
from jax import lax
from jax.sharding import PartitionSpec as P
import jax.experimental.pallas as pl
import jax.experimental.pallas.tpu as pltpu

H = 12
DK = 64
NB = 32
MAXD = 128
ENC = 1024
DEC = 256


EPS = 1e-06
NEG = -1e30
HIGH = lax.Precision.HIGHEST
VMEM_BYTES = 62 * 2**20
GELU_A = math.sqrt(2.0 / math.pi)
GELU_B = 0.044715


def cutoffs(exact, buckets):
    found = []
    reach = exact
    for target in range(exact + 1, buckets):
        while (
            exact + math.floor(math.log(reach / exact) / math.log(MAXD / exact) * (buckets - exact))
            < target
        ):
            reach = reach + 1
        found.append(reach)
    return found


def bucket_index(relative, two_sided):
    if two_sided:
        width = NB // 2
        offset = jnp.where(relative > 0, width, 0)
        distance = jnp.abs(relative)
    else:
        width = NB
        offset = jnp.zeros_like(relative)
        distance = jnp.maximum(-relative, 0)
    exact = width // 2
    beyond = exact + sum(((distance >= limit).astype(jnp.int32) for limit in cutoffs(exact, width)))
    return offset + jnp.where(distance < exact, distance, beyond)


def segment_ids(lengths, count):
    bounds = jnp.cumsum(lengths)
    places = jnp.arange(count, dtype=jnp.int32)
    return jnp.sum((places[:, None] >= bounds[None, :]).astype(jnp.int32), axis=1)


def rms_norm(values, gain):
    return values * lax.rsqrt(jnp.mean(values * values, axis=-1, keepdims=True) + EPS) * gain


def gelu_tanh(values):
    return jax.nn.gelu(values, approximate=True)


PAIR = 128


def offset_buckets(span, two_sided):
    places = jnp.arange(2 * span, dtype=jnp.int32)[None, :]
    relative = lax.rem(places - jnp.arange(8, dtype=jnp.int32)[:, None] + 2 * span, 2 * span) - span
    buckets = bucket_index(relative.reshape(-1), two_sided)
    return (buckets[None, :] == jnp.arange(NB, dtype=jnp.int32)[:, None]).astype(jnp.bfloat16)


def base_rows(table, span, two_sided):
    heads = table.shape[1]
    rows = lax.dot_general(
        table, offset_buckets(span, two_sided), (((0,), (0,)), ((), ())), preferred_element_type=jnp.float32
    )
    return rows.reshape(heads // 2, 2, 8, 2 * span)


def table_grad(offset_sums, span, two_sided):
    heads = 2 * offset_sums.shape[0]
    return lax.dot_general(
        offset_buckets(span, two_sided).astype(jnp.float32),
        offset_sums.reshape(heads, 16 * span),
        (((1,), (1,)), ((), ())),
        precision=HIGH,
        preferred_element_type=jnp.float32,
    )


def dot_nt(a, b):
    return lax.dot_general(a, b, (((1,), (1,)), ((), ())), preferred_element_type=jnp.float32)


def dot_tn(a, b):
    return lax.dot_general(a, b, (((0,), (0,)), ((), ())), preferred_element_type=jnp.float32)


def dot_nn(a, b):
    return lax.dot_general(a, b, (((1,), (0,)), ((), ())), preferred_element_type=jnp.float32)


def split_heads(block):
    lane = lax.broadcasted_iota(jnp.int32, block.shape, 1)
    zero = jnp.zeros_like(block)
    return jnp.where(lane < DK, block, zero), jnp.where(lane < DK, zero, block)


def attend_kernel(block, keys_count, causal, biased, *refs):
    if biased:
        qseg, kseg, base, q_ref, k_ref, v_ref, e_ref, c_ref, inv_ref, strip = refs
    else:
        qseg, kseg, q_ref, k_ref, v_ref, e_ref, c_ref, inv_ref = refs
    i = pl.program_id(1)
    if biased:
        wide = 2 * keys_count

        @pl.when(i == 0)
        def _():
            for head in range(2):
                rows = base[0, head]
                for a in range(block // 8):
                    strip[head, 8 * a : 8 * a + 8, :] = pltpu.roll(rows, (8 * a + wide - block) % wide, 1)

    allowed = qseg[...] == kseg[...]
    if causal:
        rows = lax.broadcasted_iota(jnp.int32, (block, keys_count), 0) + i * block
        allowed = allowed & (lax.broadcasted_iota(jnp.int32, (block, keys_count), 1) <= rows)
    q_heads = split_heads(q_ref[...])
    v_heads = split_heads(v_ref[...])
    inverses = []
    context = None
    for head in range(2):
        scores = dot_nt(q_heads[head], k_ref[...])
        if biased:
            start = pl.multiple_of((keys_count // block - 1 - i) * block, block)
            scores = scores + strip[head, :, pl.ds(start, keys_count)]
        scores = jnp.where(allowed, scores, NEG)
        highest = jnp.max(scores, axis=1, keepdims=True)
        weights = jnp.exp(scores - highest)
        inverses.append(1.0 / jnp.sum(weights, axis=1, keepdims=True))
        weights = weights.astype(jnp.bfloat16)
        e_ref[head] = weights
        part = dot_nn(weights, v_heads[head])
        context = part if context is None else context + part
    lane = lax.broadcasted_iota(jnp.int32, (block, PAIR), 1)
    inverse = jnp.where(lane < DK, inverses[0], inverses[1])
    inv_ref[...] = inverse
    c_ref[...] = (context * inverse).astype(jnp.bfloat16)


def attend_back_kernel(block, keys_count, steps, biased, *refs):
    if biased:
        q_ref, k_ref, v_ref, e_ref, c_ref, inv_ref, gc_ref, gq_ref, gk_ref, gv_ref, off_ref, gk_sum, gv_sum, strip = refs
    else:
        q_ref, k_ref, v_ref, e_ref, c_ref, inv_ref, gc_ref, gq_ref, gk_ref, gv_ref, gk_sum, gv_sum = refs
    i = pl.program_id(1)

    @pl.when(i == 0)
    def _():
        gk_sum[...] = jnp.zeros_like(gk_sum)
        gv_sum[...] = jnp.zeros_like(gv_sum)
        if biased:
            strip[...] = jnp.zeros_like(strip)

    scaled = (gc_ref[...].astype(jnp.float32) * inv_ref[...]).astype(jnp.bfloat16)
    product = scaled.astype(jnp.float32) * c_ref[...].astype(jnp.float32)
    lane = lax.broadcasted_iota(jnp.int32, (block, PAIR), 1)
    inner = (
        jnp.sum(jnp.where(lane < DK, product, 0.0), axis=1, keepdims=True),
        jnp.sum(jnp.where(lane < DK, 0.0, product), axis=1, keepdims=True),
    )
    g_heads = split_heads(scaled)
    q_heads = split_heads(q_ref[...])
    k_heads = split_heads(k_ref[...])
    gq = None
    for head in range(2):
        weights = e_ref[head]
        grad = dot_nt(g_heads[head], v_ref[...])
        grad = weights.astype(jnp.float32) * (grad - inner[head])
        if biased:
            start = pl.multiple_of((keys_count // block - 1 - i) * block, block)
            strip[head, :, pl.ds(start, keys_count)] += grad
        grad = grad.astype(jnp.bfloat16)
        part = dot_nn(grad, k_heads[head])
        gq = part if gq is None else gq + part
        gk_sum[...] += dot_tn(grad, q_heads[head])
        gv_sum[...] += dot_tn(weights, g_heads[head])
    gq_ref[...] = gq.astype(jnp.bfloat16)

    @pl.when(i == steps - 1)
    def _():
        gk_ref[...] = gk_sum[...].astype(jnp.bfloat16)
        gv_ref[...] = gv_sum[...].astype(jnp.bfloat16)
        if biased:
            wide = 2 * keys_count
            for head in range(2):
                total = jnp.zeros((8, wide), jnp.float32)
                for a in range(block // 8):
                    total = total + pltpu.roll(strip[head, 8 * a : 8 * a + 8, :], (block - 8 * a) % wide, 1)
                off_ref[0, head] = total


def attend_forward(query, keys, values, base, query_segments, key_segments, causal):
    count, cols = query.shape[0], keys.shape[0]
    pairs = query.shape[1] // PAIR
    block = min(256, count)
    steps = count // block
    row_spec = pl.BlockSpec((block, PAIR), lambda h, i: (i, h))
    key_spec = pl.BlockSpec((cols, PAIR), lambda h, i: (0, h))
    in_specs = [
        pl.BlockSpec((block, 1), lambda h, i: (i, 0)),
        pl.BlockSpec((1, cols), lambda h, i: (0, 0)),
    ]
    args = [query_segments[:, None], key_segments[None, :]]
    scratch = []
    if base is not None:
        in_specs.append(pl.BlockSpec((1, 2, 8, 2 * cols), lambda h, i: (h, 0, 0, 0)))
        args.append(base)
        scratch.append(pltpu.VMEM((2, block, 2 * cols), jnp.float32))
    return pl.pallas_call(
        functools.partial(attend_kernel, block, cols, causal, base is not None),
        grid=(pairs, steps),
        in_specs=in_specs + [row_spec, key_spec, key_spec],
        out_specs=[
            pl.BlockSpec((2, block, cols), lambda h, i: (h, i, 0)),
            row_spec,
            row_spec,
        ],
        out_shape=[
            jax.ShapeDtypeStruct((2 * pairs, count, cols), jnp.bfloat16),
            jax.ShapeDtypeStruct((count, pairs * PAIR), jnp.bfloat16),
            jax.ShapeDtypeStruct((count, pairs * PAIR), jnp.float32),
        ],
        scratch_shapes=scratch,
        compiler_params=pltpu.CompilerParams(vmem_limit_bytes=VMEM_BYTES),
        cost_estimate=pl.CostEstimate(
            flops=4 * count * cols * PAIR * 2 * pairs, bytes_accessed=2 * pairs * count * cols * 2, transcendentals=0
        ),
    )(*args, query, keys, values)


def attend_backward(query, keys, values, saved, grad_context, biased):
    weights, context, inverse = saved
    count, cols = query.shape[0], keys.shape[0]
    pairs = query.shape[1] // PAIR
    block = min(256, count)
    steps = count // block
    row_spec = pl.BlockSpec((block, PAIR), lambda h, i: (i, h))
    key_spec = pl.BlockSpec((cols, PAIR), lambda h, i: (0, h))
    out_specs = [row_spec, key_spec, key_spec]
    out_shape = [
        jax.ShapeDtypeStruct((count, pairs * PAIR), jnp.bfloat16),
        jax.ShapeDtypeStruct((cols, pairs * PAIR), jnp.bfloat16),
        jax.ShapeDtypeStruct((cols, pairs * PAIR), jnp.bfloat16),
    ]
    scratch = [pltpu.VMEM((cols, PAIR), jnp.float32), pltpu.VMEM((cols, PAIR), jnp.float32)]
    if biased:
        out_specs.append(pl.BlockSpec((1, 2, 8, 2 * cols), lambda h, i: (h, 0, 0, 0)))
        out_shape.append(jax.ShapeDtypeStruct((pairs, 2, 8, 2 * cols), jnp.float32))
        scratch.append(pltpu.VMEM((2, block, 2 * cols), jnp.float32))
    return pl.pallas_call(
        functools.partial(attend_back_kernel, block, cols, steps, biased),
        grid=(pairs, steps),
        in_specs=[
            row_spec,
            key_spec,
            key_spec,
            pl.BlockSpec((2, block, cols), lambda h, i: (h, i, 0)),
            row_spec,
            row_spec,
            row_spec,
        ],
        out_specs=out_specs,
        out_shape=out_shape,
        scratch_shapes=scratch,
        compiler_params=pltpu.CompilerParams(vmem_limit_bytes=VMEM_BYTES),
        cost_estimate=pl.CostEstimate(
            flops=8 * count * cols * PAIR * 2 * pairs, bytes_accessed=2 * pairs * count * cols * 2, transcendentals=0
        ),
    )(query, keys, values, weights, context, inverse, grad_context)


MESH_IDS = pl.DeviceIdType.MESH
CHUNK = 256
ATT = 4 * 384


def any_spec():
    return pl.BlockSpec(memory_space=pl.ANY)


def vmem_spec():
    return pl.BlockSpec(memory_space=pltpu.VMEM)


def smem_spec():
    return pl.BlockSpec(memory_space=pltpu.SMEM)


def documents(lengths, shape, first):
    places = lax.broadcasted_iota(jnp.int32, shape, 0 if shape[1] == 1 else 1) + first
    bound = jnp.int32(0)
    total = jnp.zeros(shape, jnp.int32)
    for k in range(lengths.shape[1]):
        bound = bound + lengths[0, k]
        total = total + (places >= bound).astype(jnp.int32)
    return total


def normed(values, gain):
    return values * lax.rsqrt(jnp.mean(values * values, axis=1, keepdims=True) + EPS) * gain


def gelu_pair(values):
    square = values * values
    inner = jnp.tanh(GELU_A * values * (1.0 + GELU_B * square))
    half = 0.5 * (1.0 + inner)
    slope = half + 0.5 * values * (1.0 - inner * inner) * (GELU_A * (1.0 + 3.0 * GELU_B * square))
    return values * half, slope


class Place:
    def __init__(self, wide):
        self.core = lax.axis_index("dp")
        self.wide = lax.axis_index("wide")
        self.side = lax.axis_index("narrow")
        self.count = wide
        self.fars = wide // 2
        self.far = self.wide // 2
        self.near = self.wide % 2

    def sibling(self):
        return (1 - self.core, self.wide, self.side)

    def across(self):
        return (self.core, self.wide, 1 - self.side)

    def beside(self):
        return (self.core, 2 * self.far + 1 - self.near, self.side)

    def along(self, step):
        return (self.core, 2 * lax.rem(self.far + step, self.fars) + self.near, self.side)

    def index_from(self, step):
        return 2 * lax.rem(self.far - step + self.fars, self.fars) + self.near

    def index_beside(self, step):
        return 2 * lax.rem(self.far - step + self.fars, self.fars) + 1 - self.near

    def greet(self):
        partners = [self.sibling(), self.across(), self.beside()]
        partners += [self.along(step) for step in range(1, self.fars)]
        barrier = pltpu.get_barrier_semaphore()
        for partner in partners:
            pl.semaphore_signal(barrier, inc=1, device_id=partner, device_id_type=MESH_IDS)
        pl.semaphore_wait(barrier, len(partners))


def remote(source, target, send, receive, partner):
    return pltpu.make_async_remote_copy(
        src_ref=source,
        dst_ref=target,
        send_sem=send,
        recv_sem=receive,
        device_id=partner,
        device_id_type=MESH_IDS,
    )


class Gather:
    def __init__(self, place, pack, groups, send, receive, local):
        self.place, self.pack, self.groups = place, pack, groups
        self.send, self.receive, self.local = send, receive, local
        self.rows = pack.shape[0]
        self.sent = []

    def at(self, group, index, core):
        first, width, target, offset = self.groups[group]
        half = width // 2
        start = pl.multiple_of(offset + core * half, 128)
        return target.at[pl.ds(pl.multiple_of(index * self.rows, 16), self.rows), pl.ds(start, half)]

    def own(self, group):
        first, width, target, offset = self.groups[group]
        half = width // 2
        return self.pack.at[:, pl.ds(pl.multiple_of(first + self.place.core * half, 128), half)]

    def local_copy(self, group):
        first, width, target, offset = self.groups[group]
        rows = pl.ds(pl.multiple_of(self.place.wide * self.rows, 16), self.rows)
        return pltpu.make_async_copy(
            self.pack.at[:, pl.ds(first, width)], target.at[rows, pl.ds(offset, width)], self.local.at[group]
        )

    def push(self, group, slot, source, index, partner):
        copy = remote(
            source,
            self.at(group, index, self.place.core),
            self.send.at[group, slot],
            self.receive.at[group, slot],
            partner,
        )
        copy.start()
        self.sent.append(copy)

    def await_slot(self, group, slot, index, core):
        block = self.at(group, index, core)
        remote(block, block, self.send.at[group, slot], self.receive.at[group, slot], self.place.sibling()).wait_recv()

    def start(self, group):
        place, fars = self.place, self.place.fars
        for step in range(1, fars):
            self.push(group, step - 1, self.own(group), place.wide, place.along(step))
        self.push(group, fars - 1, self.own(group), place.wide, place.beside())
        self.local_copy(group).start()

    def relay_along(self, group):
        place, fars = self.place, self.place.fars
        for step in range(1, fars):
            index = place.index_from(step)
            self.await_slot(group, step - 1, index, place.core)
            block = self.at(group, index, place.core)
            self.push(group, fars - 1 + step, block, index, place.beside())
            self.push(group, 2 * fars - 2 + step, block, index, place.sibling())

    def relay_beside(self, group):
        place, fars = self.place, self.place.fars
        for step in range(fars):
            index = place.index_beside(step)
            self.await_slot(group, fars - 1 + step, index, place.core)
            block = self.at(group, index, place.core)
            self.push(group, 3 * fars - 2 + step, block, index, place.sibling())

    def finish(self, group):
        place, fars = self.place, self.place.fars
        for step in range(1, fars):
            self.await_slot(group, 2 * fars - 2 + step, place.index_from(step), 1 - place.core)
        for step in range(fars):
            self.await_slot(group, 3 * fars - 2 + step, place.index_beside(step), 1 - place.core)
        self.local_copy(group).wait()

    def close(self):
        for copy in self.sent:
            copy.wait_send()


def gather_slots(wide):
    return 4 * (wide // 2) - 2


def softmax_pair(q_pair, k_pair, v_pair, allowed, biases, e_store):
    q_heads = split_heads(q_pair)
    v_heads = split_heads(v_pair)
    inverses = []
    context = None
    for head in range(2):
        scores = dot_nt(q_heads[head], k_pair)
        if biases is not None:
            scores = scores + biases(head)
        scores = jnp.where(allowed, scores, NEG)
        highest = jnp.max(scores, axis=1, keepdims=True)
        weights = jnp.exp(scores - highest)
        inverses.append(1.0 / jnp.sum(weights, axis=1, keepdims=True))
        weights = weights.astype(jnp.bfloat16)
        e_store(head, weights)
        part = dot_nn(weights, v_heads[head])
        context = part if context is None else context + part
    lane = lax.broadcasted_iota(jnp.int32, context.shape, 1)
    inverse = jnp.where(lane < DK, inverses[0], inverses[1])
    return inverse, (context * inverse).astype(jnp.bfloat16)


def build_strip(strip, base, pairs, block, span):
    def one(pair, carry):
        for head in range(2):
            rows = base[pair, head]
            for a in range(block // 8):
                strip[2 * pair + head, 8 * a : 8 * a + 8, :] = pltpu.roll(rows, (8 * a + 2 * span - block) % (2 * span), 1)
        return carry

    lax.fori_loop(0, pairs, one, 0)


NEAR = 2 * CHUNK
EDGE = NEAR // 4


def near_buckets():
    places = jnp.arange(2 * NEAR, dtype=jnp.int32)[None, :]
    relative = places - jnp.arange(8, dtype=jnp.int32)[:, None] - CHUNK - EDGE
    buckets = bucket_index(relative.reshape(-1), True)
    return (buckets[None, :] == jnp.arange(NB, dtype=jnp.int32)[:, None]).astype(jnp.bfloat16)


def near_rows(table):
    rows = lax.dot_general(
        table, near_buckets(), (((0,), (0,)), ((), ())), preferred_element_type=jnp.float32
    )
    return rows.reshape(table.shape[1] // 2, 2, 8, 2 * NEAR)


def build_near(strip, base, pairs):
    def one(pair, carry):
        for head in range(2):
            rows = base[pair, head]
            for a in range(CHUNK // 8):
                turned = pltpu.roll(rows, (2 * NEAR - CHUNK + 8 * a) % (2 * NEAR), 1)
                strip[2 * pair + head, 8 * a : 8 * a + 8, :] = turned[:, :NEAR]
        return carry

    lax.fori_loop(0, pairs, one, 0)


def near_window(i, rows):
    low, high = max(i * CHUNK - EDGE, 0), min(i * CHUNK + CHUNK + EDGE, rows)
    return low, high, low - (i * CHUNK - EDGE)


def near_bias(strip, base, pair, head, i, rows):
    low, high, shift = near_window(i, rows)
    parts = [strip[2 * pair + head, :, shift : shift + high - low]]
    if low > 0:
        parts.insert(0, jnp.broadcast_to(base[pair, head, 0:1, 0:1], (CHUNK, low)))
    if high < rows:
        parts.append(jnp.broadcast_to(base[pair, head, 0:1, 2 * NEAR - 1 : 2 * NEAR], (CHUNK, rows - high)))
    return jnp.concatenate(parts, axis=1)


def enc_forward_kernel(
    wide,
    x_own,
    dec_own,
    dcot_own,
    query_in,
    kv_in,
    out_in,
    up_in,
    down_in,
    gains_in,
    base,
    lengths,
    w1_all,
    w2,
    n0_all,
    qkv_all,
    c_all,
    inv_all,
    e_all,
    e1_all,
    n1_all,
    slope_all,
    a_all,
    ef_all,
    mem_all,
    dec_other,
    dcot_other,
    out_all,
    gains,
    pack,
    w1,
    n0,
    qkv,
    c,
    inv,
    e1,
    n1,
    ef,
    mem,
    x_full,
    strip,
    e_buf,
    slope_buf,
    a_buf,
    y_send,
    y_recv,
    g_send,
    g_recv,
    g_local,
    x_sems,
    y_sems,
    z_sems,
    l_sems,
    p_sems,
    o_sems,
):
    place = Place(wide)
    side = place.side
    half = x_own.shape[0]
    rows = 2 * half
    steps = rows // CHUNK
    width = c.shape[1]
    ffn = up_in.shape[2]
    pairs = width // PAIR
    pieces = []
    for layer in range(3):
        first = (0, 4 * width + 2 * ffn, 8 * width + 2 * ffn)[layer]
        pieces += [(query_in.at[layer], first), (kv_in.at[layer, 0], first + width)]
        pieces += [(kv_in.at[layer, 1], first + 2 * width), (out_in.at[layer], first + 3 * width)]
    pieces += [(up_in.at[0], 4 * width), (down_in.at[0], 4 * width + ffn), (up_in.at[1], 12 * width + 2 * ffn)]
    packs = [
        pltpu.make_async_copy(piece, pack.at[:, pl.ds(first, piece.shape[1])], p_sems.at[index])
        for index, (piece, first) in enumerate(pieces)
    ]
    for copy in packs:
        copy.start()
    gains[...] = gains_in[...].astype(jnp.float32)
    place.greet()
    gather = Gather(
        place,
        pack,
        [
            (0, 2 * width, w1, 0),
            (2 * width, 2 * width, w1, 2 * width),
            (4 * width, ffn, w1, 4 * width),
            (4 * width + ffn, ffn, w1, 4 * width + ffn),
            (4 * width + 2 * ffn, 4 * width, w2, 0),
            (8 * width + 2 * ffn, 4 * width, w2, 4 * width),
            (12 * width + 2 * ffn, ffn, w2, 8 * width),
        ],
        g_send,
        g_recv,
        g_local,
    )
    mine = pl.ds(pl.multiple_of(side * half, 16), half)
    swap_x = remote(x_own, x_full.at[mine], x_sems.at[0], x_sems.at[1], place.across())
    swap_x.start()
    for copy in packs[:4]:
        copy.wait()
    gather.start(0)
    gather.start(1)
    for copy in packs[4:]:
        copy.wait()
    keep_x = pltpu.make_async_copy(x_own, x_full.at[mine], l_sems.at[6])
    keep_x.start()
    build_near(strip, base, pairs)
    gather.relay_along(0)
    gather.relay_along(1)
    gather.start(2)
    keep_x.wait()
    gather.relay_beside(0)
    gather.relay_beside(1)
    swap_x.wait()
    later = [
        remote(dec_own, dec_other, x_sems.at[2], x_sems.at[3], place.across()),
        remote(dcot_own, dcot_other, x_sems.at[4], x_sems.at[5], place.across()),
    ]
    for copy in later:
        copy.start()
    stores = []

    def store_out(source, target):
        stores.append(pltpu.make_async_copy(source, target, o_sems.at[len(stores)]))
        stores[-1].start()


    def norm_rows(i, carry):
        at = pl.ds(pl.multiple_of(i * CHUNK, CHUNK), CHUNK)
        n0[at, :] = normed(x_full[at, :].astype(jnp.float32), gains[0:1, :]).astype(jnp.bfloat16)
        return carry

    lax.fori_loop(0, steps, norm_rows, 0)
    gather.finish(0)
    gather.finish(1)

    def project(i, carry):
        at = pl.ds(pl.multiple_of(i * CHUNK, CHUNK), CHUNK)
        qkv[at, :] = dot_nn(n0[at, :], w1[:, : 3 * width]).astype(jnp.bfloat16)
        return carry

    lax.fori_loop(0, steps, project, 0)
    store_out(n0, n0_all)
    store_out(qkv, qkv_all)

    def lanes(base_lane, pair):
        return pl.ds(pl.multiple_of(base_lane + pair * PAIR, PAIR), PAIR)

    def save(i, kind):
        slot = i % 2
        at = pl.ds(i * CHUNK, CHUNK)
        if kind == 0:
            return pltpu.make_async_copy(e_buf.at[slot], e_all.at[:, at, :], l_sems.at[slot])
        if kind == 1:
            return pltpu.make_async_copy(slope_buf.at[slot], slope_all.at[at, :], l_sems.at[2 + slot])
        return pltpu.make_async_copy(a_buf.at[slot], a_all.at[at, :], l_sems.at[4 + slot])

    def swap_y(layer, i):
        at = pl.ds(i * CHUNK, CHUNK)
        sems = y_sems if layer == 0 else z_sems
        return remote(y_send.at[layer, at], y_recv.at[layer, at], sems.at[0, i], sems.at[1, i], place.across())

    def attend(i):
        at = pl.ds(i * CHUNK, CHUNK)
        slot = i % 2
        if i >= 2:
            save(i - 2, 0).wait()

        def one(pair, carry):
            allowed = documents(lengths, (CHUNK, 1), i * CHUNK) == documents(lengths, (1, rows), 0)

            def bias(head):
                return near_bias(strip, base, pair, head, i, rows)

            def store(head, weights):
                e_buf[slot, 2 * pair + head] = weights

            inverse, context = softmax_pair(
                qkv[at, lanes(0, pair)],
                qkv[:, lanes(width, pair)],
                qkv[:, lanes(2 * width, pair)],
                allowed,
                bias,
                store,
            )
            inv[at, lanes(0, pair)] = inverse
            c[at, lanes(0, pair)] = context
            return carry

        lax.fori_loop(0, pairs, one, 0)
        save(i, 0).start()
        store_out(c.at[at], c_all.at[at])
        store_out(inv.at[at], inv_all.at[at])
        y_send[0, at, :] = dot_nt(c[at, :], w1[:, 3 * width : 4 * width]).astype(jnp.bfloat16)
        swap_y(0, i).start()

    def feed(i):
        at = pl.ds(i * CHUNK, CHUNK)
        slot = i % 2
        swap_y(0, i).wait_recv()
        both = y_send[0, at, :].astype(jnp.float32) + y_recv[0, at, :].astype(jnp.float32)
        middle = x_full[at, :].astype(jnp.float32) + both
        e1[at, :] = middle
        rounded = normed(middle, gains[1:2, :]).astype(jnp.bfloat16)
        n1[at, :] = rounded
        store_out(e1.at[at], e1_all.at[at])
        store_out(n1.at[at], n1_all.at[at])
        if i >= 2:
            save(i - 2, 1).wait()
            save(i - 2, 2).wait()

        def part(j, carry):
            cols = pl.ds(pl.multiple_of(4 * width + j * width, PAIR), width)
            here = pl.ds(pl.multiple_of(j * width, PAIR), width)
            active, slope = gelu_pair(dot_nn(n1[at, :], w1[:, cols]))
            a_buf[slot, :, here] = active.astype(jnp.bfloat16)
            slope_buf[slot, :, here] = slope.astype(jnp.bfloat16)
            return carry

        lax.fori_loop(0, ffn // width, part, 0)
        save(i, 1).start()
        save(i, 2).start()
        y_send[1, at, :] = dot_nt(a_buf[slot], w1[:, 4 * width + ffn :]).astype(jnp.bfloat16)
        swap_y(1, i).start()

    def last(i):
        at = pl.ds(i * CHUNK, CHUNK)
        swap_y(1, i).wait_recv()
        both = y_send[1, at, :].astype(jnp.float32) + y_recv[1, at, :].astype(jnp.float32)
        final = e1[at, :] + both
        ef[at, :] = final
        mem[at, :] = normed(final, gains[5:6, :]).astype(jnp.bfloat16)
        store_out(ef.at[at], ef_all.at[at])
        store_out(mem.at[at], mem_all.at[at])

    gather.start(3)
    gather.relay_along(2)
    attend(0)
    gather.start(4)
    gather.relay_along(3)
    gather.relay_beside(2)
    attend(1)
    gather.start(5)
    gather.relay_along(4)
    gather.relay_beside(3)
    gather.finish(2)
    attend(2)
    gather.finish(3)
    store_out(w1, w1_all)
    feed(0)
    gather.start(6)
    gather.relay_along(5)
    gather.relay_beside(4)
    attend(3)
    feed(1)
    gather.relay_beside(5)
    gather.relay_along(6)
    feed(2)
    feed(3)
    last(0)
    gather.relay_beside(6)
    last(1)
    last(2)
    last(3)
    x_full[:half, :] = ef[mine, :].astype(jnp.bfloat16)
    store_out(x_full.at[pl.ds(0, half)], out_all)
    for group in range(4, 7):
        gather.finish(group)
    gather.close()
    for copy in later:
        copy.wait()
    for copy in stores:
        copy.wait()
    for i in range(steps):
        swap_y(0, i).wait_send()
        swap_y(1, i).wait_send()
    for i in range(steps - 2, steps):
        for kind in range(3):
            save(i, kind).wait()


def enc_forward(wide, x_own, dec_own, dcot_own, weights, gains, base, lengths):
    half, model = x_own.shape
    rows = 2 * half
    pairs = base.shape[0]
    width = pairs * PAIR
    ffn = weights[3].shape[2]
    bf, f32 = jnp.bfloat16, jnp.float32
    shape = jax.ShapeDtypeStruct
    dma = pltpu.SemaphoreType.DMA
    slots = gather_slots(wide)
    steps = rows // CHUNK
    saved = [
        ((model, 4 * width + 2 * ffn), bf),
        ((rows, model), bf),
        ((rows, 3 * width), bf),
        ((rows, width), bf),
        ((rows, width), f32),
        ((rows, model), f32),
        ((rows, model), bf),
        ((rows, model), f32),
        ((rows, model), bf),
    ]
    kept = [shape(*pair) for pair in saved]
    out_shape = (
        [kept[0], shape((model, 8 * width + ffn), bf)]
        + kept[1:5]
        + [shape((2 * pairs, rows, rows), bf)]
        + kept[5:7]
        + [shape((rows, ffn), bf), shape((rows, ffn), bf)]
        + kept[7:]
        + [shape(dec_own.shape, bf), shape(dcot_own.shape, bf), shape(x_own.shape, bf)]
    )
    return pl.pallas_call(
        functools.partial(enc_forward_kernel, wide),
        in_specs=[vmem_spec()] + [any_spec()] * 7 + [vmem_spec()] * 2 + [smem_spec()],
        out_shape=out_shape,
        out_specs=[any_spec()] * len(out_shape),
        scratch_shapes=[pltpu.VMEM(gains.shape, f32), pltpu.VMEM((x_own.shape[1] // wide, 12 * width + 3 * ffn), bf)]
        + [pltpu.VMEM(*pair) for pair in saved]
        + [
            pltpu.VMEM((rows, model), bf),
            pltpu.VMEM((2 * pairs, CHUNK, NEAR), f32),
            pltpu.VMEM((2, 2 * pairs, CHUNK, rows), bf),
            pltpu.VMEM((2, CHUNK, ffn), bf),
            pltpu.VMEM((2, CHUNK, ffn), bf),
            pltpu.VMEM((2, rows, model), bf),
            pltpu.VMEM((2, rows, model), bf),
            dma((7, slots)),
            dma((7, slots)),
            dma((7,)),
            dma((8,)),
            dma((2, steps)),
            dma((2, steps)),
            dma((7,)),
            dma((15,)),
            dma((4 + 6 * steps,)),
        ],
        compiler_params=pltpu.CompilerParams(
            collective_id=0, has_side_effects=True, vmem_limit_bytes=VMEM_BYTES
        ),
        cost_estimate=pl.CostEstimate(flops=10**10, bytes_accessed=6 * 10**7, transcendentals=0),
    )(x_own, dec_own, dcot_own, *weights, gains, base, lengths)


def norm_back(values, gain, grad):
    scale = lax.rsqrt(jnp.mean(values * values, axis=1, keepdims=True) + EPS)
    scaled = grad * gain
    pulled = scale * (scaled - values * (scale * scale) * jnp.mean(scaled * values, axis=1, keepdims=True))
    return pulled, jnp.sum(grad * values * scale, axis=0, keepdims=True)


class Scatter:
    def __init__(self, place, rows, groups, tile, send, receive):
        self.place, self.rows, self.groups, self.tile = place, rows, groups, tile
        self.send, self.receive = send, receive
        self.sent = []

    def columns(self, group, core):
        first, width = self.groups[group]["first"], self.groups[group]["width"]
        if self.groups[group]["core"] is None:
            return pl.ds(first, width // 2)
        return pl.ds(pl.multiple_of(first + core * (width // 2), 128), width // 2)

    def block(self, group, index):
        return self.groups[group]["grad"].at[
            pl.ds(pl.multiple_of(index * self.rows, 16), self.rows), self.columns(group, self.place.core)
        ]

    def push(self, group, slot, source, target, partner, arrival=None):
        arrival = slot if arrival is None else arrival
        copy = remote(source, target, self.send.at[group, slot], self.receive.at[group, arrival], partner)
        copy.start()
        self.sent.append(copy)

    def await_slot(self, group, slot, block):
        remote(block, block, self.send.at[group, 0], self.receive.at[group, slot], self.place.sibling()).wait_recv()

    def start(self, group):
        parts = self.groups[group]
        self.push(
            group, 0, parts["grad"].at[:, self.columns(group, 1 - self.place.core)], parts["core"], self.place.sibling()
        )

    def add_block(self, group, index, other):
        block = self.block(group, index)
        block[...] = (block[...].astype(jnp.float32) + other.astype(jnp.float32)).astype(jnp.bfloat16)
        return block

    def merge(self, group):
        parts = self.groups[group]
        self.await_slot(group, 0, parts["core"])
        for index in range(self.place.count):
            self.add_block(group, index, parts["core"][index * self.rows : (index + 1) * self.rows, :])

    def beside(self, group):
        parts, place = self.groups[group], self.place
        if parts["core"] is None:
            for step in range(place.fars):
                index = 2 * lax.rem(place.far + 1 + step, place.fars) + 1 - place.near
                self.push(group, 1 + step, self.block(group, index), parts["beside"].at[step], place.beside())
            return
        self.await_slot(group, 0, parts["core"])

        def received(index):
            return parts["core"][pl.ds(pl.multiple_of(index * self.rows, 16), self.rows), :]

        for step in range(place.fars):
            far = lax.rem(place.far + 1 + step, place.fars)
            index = 2 * far + 1 - place.near
            block = self.add_block(group, index, received(index))
            self.push(group, 1 + step, block, parts["beside"].at[step], place.beside())
        for step in range(place.fars):
            far = lax.rem(place.far + 1 + step, place.fars)
            index = 2 * far + place.near
            self.add_block(group, index, received(index))

    def along(self, group):
        parts, place = self.groups[group], self.place
        for step in range(1, place.fars):
            index = 2 * lax.rem(place.far + step, place.fars) + place.near
            self.await_slot(group, step, parts["beside"].at[step - 1])
            block = self.add_block(group, index, parts["beside"][step - 1])
            self.push(group, place.fars + step, block, parts["along"].at[step - 1], place.along(step))

    def total(self, group):
        parts, place = self.groups[group], self.place
        self.await_slot(group, place.fars, parts["beside"].at[place.fars - 1])
        value = self.block(group, place.wide)[...].astype(jnp.float32) + parts["beside"][place.fars - 1].astype(jnp.float32)
        for step in range(1, place.fars):
            self.await_slot(group, place.fars + step, parts["along"].at[step - 1])
            value = value + parts["along"][step - 1].astype(jnp.float32)
        half = parts["width"] // 2
        block = self.tile.at[:, pl.ds(pl.multiple_of(parts["out"] + place.core * half, 128), half)]
        block[...] = value.astype(jnp.bfloat16)
        self.push(group, 2 * place.fars, block, block, place.sibling())

    def finish(self, group):
        parts, place = self.groups[group], self.place
        half = parts["width"] // 2
        block = self.tile.at[:, pl.ds(pl.multiple_of(parts["out"] + (1 - place.core) * half, 128), half)]
        self.await_slot(group, 2 * place.fars, block)

    def close(self):
        for copy in self.sent:
            copy.wait_send()


def half_group(grad, first, width, out, part, core, beside, along):
    at = pl.ds(part * (width // 2), width // 2)
    return dict(
        grad=grad,
        first=first,
        width=width,
        out=out,
        core=core.at[:, at],
        beside=beside.at[:, :, at],
        along=along.at[:, :, at],
    )


def scatter_slots(wide):
    return 2 * (wide // 2) + 1


def scatter_buffers(wide, model, width):
    half, rows, fars = width // 2, model // wide, wide // 2
    return [
        pltpu.VMEM((model, half), jnp.bfloat16),
        pltpu.VMEM((fars, rows, half), jnp.bfloat16),
        pltpu.VMEM((fars - 1, rows, half), jnp.bfloat16),
    ]


def softmax_back_pair(q_pair, k_pair, v_pair, c_pair, inverse, gc_pair, weights, near):
    scaled = (gc_pair.astype(jnp.float32) * inverse).astype(jnp.bfloat16)
    product = scaled.astype(jnp.float32) * c_pair.astype(jnp.float32)
    lane = lax.broadcasted_iota(jnp.int32, product.shape, 1)
    inner = (
        jnp.sum(jnp.where(lane < DK, product, 0.0), axis=1, keepdims=True),
        jnp.sum(jnp.where(lane < DK, 0.0, product), axis=1, keepdims=True),
    )
    g_heads = split_heads(scaled)
    q_heads = split_heads(q_pair)
    k_heads = split_heads(k_pair)
    gq = None
    grads = []
    for head in range(2):
        grad = weights[head].astype(jnp.float32) * (dot_nt(g_heads[head], v_pair) - inner[head])
        if near is not None:
            near(head, grad)
        grad = grad.astype(jnp.bfloat16)
        grads.append(grad)
        part = dot_nn(grad, k_heads[head])
        gq = part if gq is None else gq + part
    gk = dot_tn(jnp.concatenate(grads, axis=0), jnp.concatenate(q_heads, axis=0))
    gv = dot_tn(jnp.concatenate([weights[0], weights[1]], axis=0), jnp.concatenate(g_heads, axis=0))
    return gq, gk, gv


def fold_near(rows):
    total = jnp.zeros((8, 2 * NEAR), jnp.float32)
    blank = jnp.zeros((8, NEAR), jnp.float32)
    for a in range(CHUNK // 8):
        wider = jnp.concatenate([rows[8 * a : 8 * a + 8, :], blank], axis=1)
        total = total + pltpu.roll(wider, (CHUNK - 8 * a) % (2 * NEAR), 1)
    return total


def bucket_sums(rows, offset, two_sided):
    span = rows.shape[1]
    relative = lax.broadcasted_iota(jnp.int32, (span, 128), 0) - offset
    onehot = bucket_index(relative, two_sided) == lax.broadcasted_iota(jnp.int32, (span, 128), 1)
    return lax.dot_general(
        rows,
        onehot.astype(jnp.float32),
        (((1,), (0,)), ((), ())),
        precision=HIGH,
        preferred_element_type=jnp.float32,
    )


def fold_rows(rows):
    span = rows.shape[1]
    total = rows[0:1, :]
    for b in range(1, 8):
        total = total + pltpu.roll(rows, span - b, 1)[b : b + 1, :]
    return total


class Total:
    def __init__(self, place, held, send, receive):
        self.place, self.held, self.send, self.receive = place, held, send, receive
        partners = (place.sibling(), place.across(), place.beside())
        self.copies = [
            remote(held.at[stage], held.at[4 + stage], send.at[stage], receive.at[stage], partner)
            for stage, partner in enumerate(partners)
        ]
        self.last = [
            remote(held.at[3], held.at[7 + place.far], send.at[2 + step], receive.at[2 + step], place.along(step))
            for step in range(1, place.fars)
        ]

    def start(self):
        self.copies[0].start()

    def step(self, stage):
        held = self.held
        self.copies[stage].wait()
        held[stage + 1] = held[stage] + held[4 + stage]
        for copy in [self.copies[stage + 1]] if stage < 2 else self.last:
            copy.start()

    def finish(self):
        for copy in self.last:
            copy.wait()
        result = None
        for far in range(self.place.fars):
            part = jnp.where(self.place.far == far, self.held[3], self.held[7 + far])
            result = part if result is None else result + part
        return result


def enc_backward_kernel(
    wide,
    x_own,
    cot_own,
    cot_other,
    gains_in,
    dec_gains,
    dec_table,
    part_own,
    part_other,
    dw1_in,
    w1_in,
    n0_in,
    qkv_in,
    c_in,
    inv_in,
    e_all,
    e1_all,
    n1_in,
    slope_all,
    a_in,
    ef_all,
    grad_out,
    tile,
    total_sums,
    part_late,
    gains,
    gain_sums,
    far_sums,
    folded,
    held,
    w1,
    dw1,
    qkv,
    c,
    inv,
    n1,
    active,
    cot,
    e_buf,
    state_buf,
    slope_buf,
    part_buf,
    other_buf,
    g_send,
    g_recv,
    l_recv,
    state_grad,
    gy,
    gu,
    gqkv,
    gk_sum,
    gv_sum,
    strip,
    core_f,
    beside_f,
    along_f,
    beside_a,
    along_a,
    beside_d,
    along_d,
    s_send,
    s_recv,
    t_send,
    t_recv,
    m_sems,
    g_sems,
    l_sems,
    e_sems,
    t_sems,
    i_sems,
):
    place = Place(wide)
    side = place.side
    half = x_own.shape[0]
    rows = 2 * half
    steps = rows // CHUNK
    width = c.shape[1]
    ffn = active.shape[1]
    pairs = width // PAIR
    model = x_own.shape[1]
    bf, f32 = jnp.bfloat16, jnp.float32
    place.greet()

    def swap(i):
        at = pl.ds(i * CHUNK, CHUNK)
        return remote(g_send.at[at], g_recv.at[at], g_sems.at[0, i], g_sems.at[1, i], place.across())

    late = part_late.shape[0] // CHUNK

    def swap_late(i):
        return remote(
            part_own.at[pl.ds((steps - late + i) * CHUNK, CHUNK)],
            part_late.at[pl.ds(i * CHUNK, CHUNK)],
            m_sems.at[0, i],
            m_sems.at[1, i],
            place.across(),
        )

    for i in range(late):
        swap_late(i).start()

    def other_part(i):
        if i < steps - late:
            return part_other.at[pl.ds(i * CHUNK, CHUNK)]
        return part_late.at[pl.ds((i - steps + late) * CHUNK, CHUNK)]

    def fetch(i):
        at = pl.ds(i * CHUNK, CHUNK)
        slot = i % 2
        return [
            pltpu.make_async_copy(ef_all.at[at], state_buf.at[slot], t_sems.at[0, slot]),
            pltpu.make_async_copy(slope_all.at[at], slope_buf.at[slot], t_sems.at[1, slot]),
            pltpu.make_async_copy(part_own.at[at], part_buf.at[slot], t_sems.at[2, slot]),
            pltpu.make_async_copy(other_part(i), other_buf.at[slot], t_sems.at[3, slot]),
        ]

    def fetch_state(i):
        at = pl.ds(i * CHUNK, CHUNK)
        return pltpu.make_async_copy(e1_all.at[at], state_buf.at[i % 2], t_sems.at[0, i % 2])

    def fetch_e(step):
        chunk, pair, slot = step // pairs, lax.rem(step, pairs), lax.rem(step, 2)
        at = pl.ds(pl.multiple_of(chunk * CHUNK, CHUNK), CHUNK)
        return pltpu.make_async_copy(e_all.at[pl.ds(2 * pair, 2), at, :], e_buf.at[slot], e_sems.at[slot])

    mine = pl.ds(pl.multiple_of(side * half, 16), half)
    theirs = pl.ds(pl.multiple_of((1 - side) * half, 16), half)
    loads = [
        pltpu.make_async_copy(cot_own, cot.at[mine], i_sems.at[0]),
        pltpu.make_async_copy(cot_other, cot.at[theirs], i_sems.at[1]),
        pltpu.make_async_copy(w1_in, w1, i_sems.at[2]),
        pltpu.make_async_copy(a_in, active, i_sems.at[3]),
        pltpu.make_async_copy(n1_in, n1, i_sems.at[4]),
        pltpu.make_async_copy(qkv_in, qkv, i_sems.at[5]),
        pltpu.make_async_copy(c_in, c, i_sems.at[6]),
        pltpu.make_async_copy(inv_in, inv, i_sems.at[7]),
        pltpu.make_async_copy(dw1_in, dw1, i_sems.at[8]),
    ]
    loads[8].start()
    for index in (0, 1):
        loads[index].start()
    for load in fetch(0):
        load.start()
    for load in loads[2:8]:
        load.start()
    gk_sum[...] = jnp.zeros_like(gk_sum)
    gv_sum[...] = jnp.zeros_like(gv_sum)
    strip[...] = jnp.zeros_like(strip)
    far_sums[...] = jnp.zeros_like(far_sums)
    gains[...] = gains_in[...].astype(f32)
    gain_sums[...] = jnp.zeros_like(gain_sums)
    out_c = 4 * width + 2 * ffn
    core_a = active.at[pl.ds(0, model), pl.ds(0, 2 * width)]
    scatter = Scatter(
        place,
        model // wide,
        [
            dict(grad=dw1, first=0, width=4 * width, out=out_c, core=None, beside=beside_a, along=along_a),
            dict(grad=dw1, first=2 * width, width=4 * width, out=out_c + 4 * width, core=None, beside=beside_d, along=along_d),
            half_group(w1, 4 * width, ffn, 4 * width, 0, core_f, beside_f, along_f),
            half_group(w1, 4 * width + ffn, ffn, 4 * width + ffn, 1, core_f, beside_f, along_f),
            half_group(gu.at[pl.ds(0, model)], 0, 2 * width, 0, 0, core_a, beside_a, along_a),
            half_group(gu.at[pl.ds(0, model)], 2 * width, 2 * width, 2 * width, 1, core_a, beside_a, along_a),
        ],
        tile,
        s_send,
        s_recv,
    )

    def own_weight(i):
        return jnp.where((i * CHUNK) // half == side, 1.0, 0.0).astype(f32)

    loads[8].wait()
    scatter.beside(0)
    scatter.beside(1)
    for index in (0, 1, 2):
        loads[index].wait()

    for i in range(steps):
        at = slice(i * CHUNK, (i + 1) * CHUNK)
        slot = i % 2
        if i + 1 < steps:
            if i + 1 >= steps - late:
                swap_late(i + 1 - steps + late).wait_recv()
            for load in fetch(i + 1):
                load.start()
        for load in fetch(i):
            load.wait()
        grad = part_buf[slot].astype(f32) + other_buf[slot].astype(f32)
        pulled, gain = norm_back(state_buf[slot], gains[5:6, :], grad)
        gain_sums[5:6, :] += gain * own_weight(i)
        total = cot[at, :].astype(f32) + pulled
        state_grad[at, :] = total
        gy[at, :] = total.astype(bf)

        def part(j, carry):
            cols = pl.ds(pl.multiple_of(4 * width + ffn + j * width, PAIR), width)
            here = pl.ds(pl.multiple_of(j * width, PAIR), width)
            grad_active = dot_nn(gy[at, :], w1[:, cols])
            gu[at, here] = (slope_buf[slot, :, here].astype(f32) * grad_active).astype(bf)
            return carry

        lax.fori_loop(0, ffn // width, part, 0)
        g_send[at, :] = dot_nt(gu[at, :], w1[:, 4 * width : 4 * width + ffn]).astype(bf)
        swap(i).start()
    for load in loads[3:8]:
        load.wait()
    fetch_state(0).start()
    fetch_e(0).start()

    def up_grads(t, carry):
        tile_rows = pl.ds(pl.multiple_of(t * CHUNK, CHUNK), CHUNK)
        w1[tile_rows, 4 * width : 4 * width + ffn] = dot_tn(n1[:, tile_rows], gu[...]).astype(bf)
        return carry

    def down_grads(t, carry):
        tile_rows = pl.ds(pl.multiple_of(t * CHUNK, CHUNK), CHUNK)
        w1[tile_rows, 4 * width + ffn :] = dot_tn(gy[:, tile_rows], active[...]).astype(bf)
        return carry

    scatter.along(0)
    lax.fori_loop(0, model // CHUNK, up_grads, 0)
    scatter.start(2)
    lax.fori_loop(0, model // CHUNK, down_grads, 0)
    scatter.start(3)
    scatter.along(1)
    scatter.beside(2)
    n0 = cot
    late_loads = [
        pltpu.make_async_copy(n0_in, n0, i_sems.at[0]),
        pltpu.make_async_copy(x_own, n1.at[pl.ds(half, half)], i_sems.at[1]),
    ]
    for load in late_loads:
        load.start()

    dw0 = gu
    l_send = n1

    def lanes(base_lane, pair):
        return pl.ds(pl.multiple_of(base_lane + pair * PAIR, PAIR), PAIR)

    def attend_back(i):
        at = slice(i * CHUNK, (i + 1) * CHUNK)
        slot = i % 2
        if i + 1 < steps:
            fetch_state(i + 1).start()
        fetch_state(i).wait()
        swap(i).wait_recv()
        grad = g_send[at, :].astype(f32) + g_recv[at, :].astype(f32)
        pulled, gain = norm_back(state_buf[slot], gains[1:2, :], grad)
        gain_sums[1:2, :] += gain * own_weight(i)
        total = state_grad[at, :] + pulled
        state_grad[at, :] = total
        gy[at, :] = total.astype(bf)
        g_send[at, :width] = dot_nn(gy[at, :], w1[:, 3 * width : 4 * width]).astype(bf)
        low, high, shift = near_window(i, rows)

        def one(pair, carry):
            step = i * pairs + pair

            @pl.when(step + 1 < steps * pairs)
            def _():
                fetch_e(step + 1).start()

            fetch_e(step).wait()
            e_slot = lax.rem(step, 2)

            def near(head, grad):
                strip[2 * pair + head, :, shift : shift + high - low] += grad[:, low:high]
                for edge, (start, end) in enumerate(((0, low), (high, rows))):
                    if end > start:
                        folded = jnp.sum(grad[:, start:end].reshape(CHUNK // 8, 8, end - start), axis=0)
                        wide_sum = folded[:, :128]
                        for lane in range(128, end - start, 128):
                            wide_sum = wide_sum + folded[:, lane : lane + 128]
                        far_sums[edge, 2 * pair + head] += wide_sum

            gq, gk, gv = softmax_back_pair(
                qkv[at, lanes(0, pair)],
                qkv[:, lanes(width, pair)],
                qkv[:, lanes(2 * width, pair)],
                c[at, lanes(0, pair)],
                inv[at, lanes(0, pair)],
                g_send[at, lanes(0, pair)],
                (e_buf[e_slot, 0], e_buf[e_slot, 1]),
                near,
            )
            gqkv[at, lanes(0, pair)] = gq.astype(bf)
            gk_sum[:, lanes(0, pair)] += gk
            gv_sum[:, lanes(0, pair)] += gv
            return carry

        lax.fori_loop(0, pairs, one, 0)

    for i in range(steps):
        swap(i).wait_send()
        attend_back(i)
        if i == 0:
            scatter.total(0)
            scatter.beside(3)
            scatter.along(2)
        if i == 1:
            scatter.total(1)
        if i == 2:
            scatter.along(3)
        if i == 3:
            scatter.total(2)
    for load in late_loads:
        load.wait()
    gqkv[:, width : 2 * width] = gk_sum[...].astype(bf)
    gqkv[:, 2 * width :] = gv_sum[...].astype(bf)

    ones = jnp.ones((8, 3 * width), f32)

    def weight_grads_a(t, carry):
        tile_rows = pl.ds(pl.multiple_of(t * CHUNK, CHUNK), CHUNK)
        grads = dot_tn(n0[:, tile_rows], gqkv[...])
        dw0[tile_rows, : 3 * width] = grads.astype(bf)
        products = lax.dot_general(
            ones,
            grads * w1[tile_rows, : 3 * width].astype(f32),
            (((1,), (1,)), ((), ())),
            precision=HIGH,
            preferred_element_type=f32,
        )
        gain_sums[0:1, tile_rows] = products[0:1, :] / gains[0:1, tile_rows]
        return carry

    def weight_grads_o(t, carry):
        tile_rows = pl.ds(pl.multiple_of(t * CHUNK, CHUNK), CHUNK)
        dw0[tile_rows, 3 * width :] = dot_tn(gy[:, tile_rows], c[...]).astype(bf)
        return carry

    lax.fori_loop(0, model // CHUNK, weight_grads_a, 0)
    scatter.start(4)
    last = []
    for part in range(half // CHUNK):
        there = pl.ds(pl.multiple_of((1 - side) * half + part * CHUNK, CHUNK), CHUNK)
        at = pl.ds(part * CHUNK, CHUNK)
        l_send[at, :] = dot_nt(gqkv[there, :], w1[:, : 3 * width]).astype(bf)
        last.append(remote(l_send.at[at], l_recv.at[at], l_sems.at[0, part], l_sems.at[1, part], place.across()))
        last[part].start()
    lax.fori_loop(0, model // CHUNK, weight_grads_o, 0)
    scatter.start(5)
    scatter.beside(4)
    summed = Total(place, held, t_send, t_recv)
    folded[...] = jnp.zeros_like(folded)

    def fold(head, carry):
        folded[pl.ds(head, 1), :] = fold_rows(fold_near(strip[head]))
        return carry

    lax.fori_loop(0, 2 * pairs, fold, 0)
    table = bucket_sums(folded[...], CHUNK + EDGE, True)
    bucket = lax.broadcasted_iota(jnp.int32, (1, 128), 1)
    for head in range(2 * pairs):
        far = [jnp.sum(far_sums[edge, head]) for edge in range(2)]
        folded[head : head + 1, :128] = jnp.where(
            bucket == NB // 2 - 1, far[0], jnp.where(bucket == NB - 1, far[1], 0.0)
        )
    table = table + folded[:, :128]
    held[0] = jnp.zeros_like(held[0])
    held[0, :8, :] = gain_sums[...] + dec_gains[...]
    held[0, 8:, pl.ds(pl.multiple_of(side * 256, 128), 128)] = table
    held[0, 8:, pl.ds(pl.multiple_of(side * 256 + 128, 128), 128)] = dec_table[...]
    summed.start()
    scatter.beside(5)
    summed.step(0)
    scatter.along(4)
    summed.step(1)
    scatter.total(3)
    for part in range(half // CHUNK):
        here = pl.ds(pl.multiple_of(side * half + part * CHUNK, CHUNK), CHUNK)
        at = pl.ds(part * CHUNK, CHUNK)
        own = dot_nt(gqkv[here, :], w1[:, : 3 * width])
        if part == 0:
            scatter.along(5)
            summed.step(2)
        last[part].wait_recv()
        grad = own + l_recv[at, :].astype(f32)
        pulled, unused = norm_back(n1[pl.ds(half + part * CHUNK, CHUNK), :].astype(f32), gains[0:1, :], grad)
        grad_out[at, :] = state_grad[here, :] + pulled
    scatter.total(4)
    scatter.total(5)
    total_sums[...] = summed.finish()
    for group in range(6):
        scatter.finish(group)
    scatter.close()
    for i in range(late):
        swap_late(i).wait_send()
    for copy in last:
        copy.wait_send()


def enc_backward(wide, x_own, cot_own, cot_other, gains, dec_gains, dec_table, part_own, part_other, dw1, saved):
    half, model = x_own.shape
    rows = 2 * half
    w1, n0, qkv, c, inv, e_all, e1, n1, slope, active, ef = saved
    width, ffn = c.shape[1], active.shape[1]
    pairs = width // PAIR
    steps = rows // CHUNK
    bf, f32 = jnp.bfloat16, jnp.float32
    shape = jax.ShapeDtypeStruct
    dma = pltpu.SemaphoreType.DMA
    return pl.pallas_call(
        functools.partial(enc_backward_kernel, wide),
        in_specs=[any_spec()] * 3 + [vmem_spec()] * 3 + [any_spec()] * 14,
        out_shape=[
            shape((half, model), f32),
            shape((model // wide, 12 * width + 2 * ffn), bf),
            shape((16, model), f32),
            shape((rows - part_other.shape[0], model), bf),
        ],
        out_specs=[vmem_spec()] * 3 + [any_spec()],
        scratch_shapes=[
            pltpu.VMEM(gains.shape, f32),
            pltpu.VMEM((8, model), f32),
            pltpu.VMEM((2, 2 * pairs, 8, 128), f32),
            pltpu.VMEM((8, 2 * NEAR), f32),
            pltpu.VMEM((7 + wide // 2, 16, model), f32),
            pltpu.VMEM(w1.shape, bf),
            pltpu.VMEM(dw1.shape, bf),
            pltpu.VMEM(qkv.shape, bf),
            pltpu.VMEM(c.shape, bf),
            pltpu.VMEM(inv.shape, f32),
            pltpu.VMEM(n1.shape, bf),
            pltpu.VMEM(active.shape, bf),
            pltpu.VMEM((rows, model), bf),
            pltpu.VMEM((2, 2, CHUNK, rows), bf),
            pltpu.VMEM((2, CHUNK, model), f32),
            pltpu.VMEM((2, CHUNK, ffn), bf),
            pltpu.VMEM((2, CHUNK, model), bf),
            pltpu.VMEM((2, CHUNK, model), bf),
            pltpu.VMEM((rows, model), bf),
            pltpu.VMEM((rows, model), bf),
            pltpu.VMEM((half, model), bf),
            pltpu.VMEM((rows, model), f32),
            pltpu.VMEM((rows, model), bf),
            pltpu.VMEM((rows, ffn), bf),
            pltpu.VMEM((rows, 3 * width), bf),
            pltpu.VMEM((rows, width), f32),
            pltpu.VMEM((rows, width), f32),
            pltpu.VMEM((2 * pairs, CHUNK, NEAR), f32),
        ]
        + scatter_buffers(wide, model, 2 * ffn)
        + scatter_buffers(wide, model, 4 * width)[1:]
        + scatter_buffers(wide, model, 4 * width)[1:]
        + [
            dma((6, scatter_slots(wide))),
            dma((6, scatter_slots(wide))),
            dma((2 + wide // 2,)),
            dma((2 + wide // 2,)),
            dma((2, steps)),
            dma((2, steps)),
            dma((2, half // CHUNK)),
            dma((2,)),
            dma((4, 2)),
            dma((10,)),
        ],
        compiler_params=pltpu.CompilerParams(
            collective_id=1, has_side_effects=True, vmem_limit_bytes=VMEM_BYTES
        ),
        cost_estimate=pl.CostEstimate(flops=2 * 10**10, bytes_accessed=6 * 10**7, transcendentals=0),
    )(x_own, cot_own, cot_other, gains, dec_gains, dec_table, part_own, part_other, dw1, w1, n0, qkv, c, inv, e_all, e1, n1, slope, active, ef)


def fold_offsets(grad):
    rows = grad.shape[0]
    total = jnp.zeros((8, 2 * rows), jnp.float32)
    blank = jnp.zeros((8, rows), jnp.float32)
    for a in range(rows // 8):
        wider = jnp.concatenate([grad[8 * a : 8 * a + 8, :], blank], axis=1)
        total = total + pltpu.roll(wider, (rows - 8 * a) % (2 * rows), 1)
    return total


def decoder_kernel(
    wide,
    dec_own,
    dec_other,
    dcot_own,
    dcot_other,
    cot_own,
    down_in,
    gains_in,
    base,
    dec_lengths,
    enc_lengths,
    mem_in,
    w_in,
    dec_out,
    dec_grad,
    tile,
    gain_sums,
    table,
    part_own,
    part_other,
    cot_other,
    dw1_all,
    gains,
    pack,
    folded,
    w,
    mem,
    dec,
    dcot,
    state,
    normals,
    qkv,
    c,
    inv,
    e_self,
    e_cross,
    strip,
    kv,
    active,
    ga,
    gu,
    grad_state,
    gy,
    gqkv,
    gkv,
    y_send,
    y_recv,
    dw,
    core_f,
    beside_f,
    along_f,
    core_d,
    core_c,
    s_send,
    s_recv,
    g_send,
    g_recv,
    g_local,
    y_sems,
    x_sems,
    p_sems,
    o_sems,
    i_sems,
):
    place = Place(wide)
    side = place.side
    half = dec_own.shape[0]
    rows = 2 * half
    model = dec_own.shape[1]
    width = c.shape[2]
    ffn = active.shape[1]
    pairs = width // PAIR
    span = mem.shape[0]
    bf, f32 = jnp.bfloat16, jnp.float32
    place.greet()
    mine = pl.ds(pl.multiple_of(side * half, 16), half)
    theirs = pl.ds(pl.multiple_of((1 - side) * half, 16), half)
    at_d, at_f = 4 * width, 8 * width

    gather = Gather(place, pack, [(0, ffn // 2, w, at_f + ffn), (ffn // 2, ffn // 2, w, at_f + ffn + ffn // 2)], g_send, g_recv, g_local)
    def load_w(first, count, sem):
        cols = pl.ds(first, count)
        return pltpu.make_async_copy(w_in.at[:, cols], w.at[:, cols], i_sems.at[sem])

    loads = [
        load_w(0, 4 * width, 0),
        load_w(at_d, 4 * width, 1),
        pltpu.make_async_copy(mem_in, mem, i_sems.at[2]),
        load_w(at_f, ffn, 3),
        pltpu.make_async_copy(dec_own, dec.at[mine], i_sems.at[4]),
        pltpu.make_async_copy(dcot_own, dcot.at[mine], i_sems.at[5]),
        pltpu.make_async_copy(dec_other, dec.at[theirs], i_sems.at[6]),
        pltpu.make_async_copy(dcot_other, dcot.at[theirs], i_sems.at[7]),
        pltpu.make_async_copy(down_in.at[1], pack, i_sems.at[8]),
    ]
    for index in (8, 4, 6, 0, 5, 7, 2, 1, 3):
        loads[index].start()
    cot_part = cot_own.shape[0] // 4

    def swap_cot(i):
        at = pl.ds(i * cot_part, cot_part)
        return remote(cot_own.at[at], cot_other.at[at], x_sems.at[0, i], x_sems.at[1, i], place.across())

    swap_cot(0).start()
    swap_cot(1).start()
    loads[8].wait()
    gather.start(0)
    gather.start(1)
    build_strip(strip, base, pairs, rows, rows)
    gains[...] = gains_in[...].astype(f32)
    gain_sums[...] = jnp.zeros_like(gain_sums)
    folded[...] = jnp.zeros_like(folded)
    scatter = Scatter(
        place,
        model // wide,
        [
            half_group(w, at_f, ffn, 0, 0, core_f, beside_f, along_f),
            half_group(w, at_f + ffn, ffn, ffn, 1, core_f, beside_f, along_f),
            dict(grad=dw, first=at_d, width=4 * width, core=core_d),
            dict(grad=dw, first=0, width=4 * width, core=core_c),
        ],
        tile,
        s_send,
        s_recv,
    )

    def swap(kind):
        return remote(y_send.at[kind], y_recv.at[kind], y_sems.at[0, kind], y_sems.at[1, kind], place.across())

    def send_branch(kind, value):
        y_send[kind] = value.astype(bf)
        swap(kind).start()

    def branch(kind):
        swap(kind).wait_recv()
        return y_send[kind].astype(f32) + y_recv[kind].astype(f32)

    def lanes(base_lane, pair):
        return pl.ds(pl.multiple_of(base_lane + pair * PAIR, PAIR), PAIR)

    def norm_to(index, gain, value):
        state[index] = value
        normals[index] = normed(value, gains[gain : gain + 1, :]).astype(bf)

    loads[4].wait()
    loads[6].wait()
    norm_to(0, 2, dec[...].astype(f32))
    loads[0].wait()
    qkv[:, : 3 * width] = dot_nn(normals[0], w[:, : 3 * width]).astype(bf)

    def self_pair(pair, carry):
        allowed = documents(dec_lengths, (rows, 1), 0) == documents(dec_lengths, (1, rows), 0)
        allowed = allowed & (
            lax.broadcasted_iota(jnp.int32, (rows, rows), 1) <= lax.broadcasted_iota(jnp.int32, (rows, rows), 0)
        )

        def bias(head):
            return strip[2 * pair + head, :, :rows]

        def store(head, weights):
            e_self[2 * pair + head] = weights

        inverse, context = softmax_pair(
            qkv[:, lanes(0, pair)], qkv[:, lanes(width, pair)], qkv[:, lanes(2 * width, pair)], allowed, bias, store
        )
        inv[0, :, lanes(0, pair)] = inverse
        c[0, :, lanes(0, pair)] = context
        return carry

    lax.fori_loop(0, pairs, self_pair, 0)
    send_branch(0, dot_nt(c[0], w[:, 3 * width : 4 * width]))

    gather.relay_along(0)
    gather.relay_along(1)

    loads[2].wait()
    loads[1].wait()

    def cross_keys(i, carry):
        at = pl.ds(pl.multiple_of(i * CHUNK, CHUNK), CHUNK)
        kv[at, :] = dot_nn(mem[at, :], w[:, at_d + width : at_d + 3 * width]).astype(bf)
        return carry

    lax.fori_loop(0, span // CHUNK, cross_keys, 0)
    gather.relay_beside(0)
    gather.relay_beside(1)
    norm_to(1, 3, state[0] + branch(0))
    swap_cot(2).start()
    qkv[:, 3 * width :] = dot_nn(normals[1], w[:, at_d : at_d + width]).astype(bf)

    def cross_pair(pair, carry):
        allowed = documents(dec_lengths, (rows, 1), 0) == documents(enc_lengths, (1, span), 0)

        def store(head, weights):
            e_cross[2 * pair + head] = weights

        inverse, context = softmax_pair(
            qkv[:, lanes(3 * width, pair)], kv[:, lanes(0, pair)], kv[:, lanes(width, pair)], allowed, None, store
        )
        inv[1, :, lanes(0, pair)] = inverse
        c[1, :, lanes(0, pair)] = context
        return carry

    lax.fori_loop(0, pairs, cross_pair, 0)
    send_branch(1, dot_nt(c[1], w[:, at_d + 3 * width : at_d + 4 * width]))

    for index in (5, 7, 3):
        loads[index].wait()
    gather.finish(0)
    gather.finish(1)
    ga[...] = dot_nn(dcot[...], w[:, at_f + ffn :]).astype(f32)
    norm_to(2, 4, state[1] + branch(1))
    swap_cot(3).start()

    def hidden(j, carry):
        here = pl.ds(pl.multiple_of(j * width, PAIR), width)
        cols = pl.ds(pl.multiple_of(at_f + j * width, PAIR), width)
        value, turn = gelu_pair(dot_nn(normals[2], w[:, cols]))
        active[:, here] = value.astype(bf)
        gu[:, here] = (turn * ga[:, here]).astype(bf)
        return carry

    lax.fori_loop(0, ffn // width, hidden, 0)
    send_branch(3, dot_nt(gu[...], w[:, at_f : at_f + ffn]))
    y_send[2] = dot_nt(active[...], w[:, at_f + ffn :]).astype(bf)

    def up_grads(t, carry):
        tile_rows = pl.ds(pl.multiple_of(t * CHUNK, CHUNK), CHUNK)
        w[tile_rows, at_f : at_f + ffn] = dot_tn(normals[2, :, tile_rows], gu[...]).astype(bf)
        return carry

    def down_grads(t, carry):
        tile_rows = pl.ds(pl.multiple_of(t * CHUNK, CHUNK), CHUNK)
        w[tile_rows, at_f + ffn :] = dot_tn(dcot[:, tile_rows], active[...]).astype(bf)
        return carry

    gather.close()
    lax.fori_loop(0, model // CHUNK, up_grads, 0)
    scatter.start(0)
    lax.fori_loop(0, model // CHUNK, down_grads, 0)
    scatter.start(1)
    scatter.beside(0)

    row = lax.broadcasted_iota(jnp.int32, (rows, 1), 0)
    counted = jnp.where(row // half == side, 1.0, 0.0).astype(f32)

    def pull(index, gain, grad):
        values = state[index]
        pulled, unused = norm_back(values, gains[gain : gain + 1, :], grad)
        scale = lax.rsqrt(jnp.mean(values * values, axis=1, keepdims=True) + EPS) * counted
        gain_sums[gain : gain + 1, :] += jnp.sum(grad * values * scale, axis=0, keepdims=True)
        return pulled

    grad_state[...] = dcot[...].astype(f32) + pull(2, 4, branch(3))
    swap(2).start()
    gy[1] = grad_state[...].astype(bf)
    gc = dot_nn(gy[1], w[:, at_d + 3 * width : at_d + 4 * width]).astype(bf)
    y_send[5, :, :width] = gc
    scatter.beside(1)

    def cross_back(pair, carry):
        gq, gk, gv = softmax_back_pair(
            qkv[:, lanes(3 * width, pair)],
            kv[:, lanes(0, pair)],
            kv[:, lanes(width, pair)],
            c[1, :, lanes(0, pair)],
            inv[1, :, lanes(0, pair)],
            y_send[5, :, lanes(0, pair)],
            (e_cross[2 * pair], e_cross[2 * pair + 1]),
            None,
        )
        gqkv[:, lanes(3 * width, pair)] = gq.astype(bf)
        gkv[:, lanes(0, pair)] = gk.astype(bf)
        gkv[:, lanes(width, pair)] = gv.astype(bf)
        return carry

    lax.fori_loop(0, pairs, cross_back, 0)
    send_branch(4, dot_nt(gqkv[:, 3 * width :], w[:, at_d : at_d + width]))

    part = kv

    def swap_part(i):
        at = pl.ds(pl.multiple_of(i * CHUNK, CHUNK), CHUNK)
        return remote(part.at[at], part_other.at[at], p_sems.at[0, i], p_sems.at[1, i], place.across())

    def keep_part(i):
        at = pl.ds(pl.multiple_of(i * CHUNK, CHUNK), CHUNK)
        return pltpu.make_async_copy(part.at[at], part_own.at[at], o_sems.at[i])

    for i in range(span // CHUNK):
        at = pl.ds(i * CHUNK, CHUNK)
        part[at, :] = dot_nt(gkv[at, :], w[:, at_d + width : at_d + 3 * width]).astype(bf)
        keep_part(i).start()

    def cross_grads(t, carry):
        tile_rows = pl.ds(pl.multiple_of(t * CHUNK, CHUNK), CHUNK)
        dw[tile_rows, at_d : at_d + width] = dot_tn(normals[1, :, tile_rows], gqkv[:, 3 * width :]).astype(bf)
        dw[tile_rows, at_d + width : at_d + 3 * width] = dot_tn(mem[:, tile_rows], gkv[...]).astype(bf)
        dw[tile_rows, at_d + 3 * width : at_f] = dot_tn(gy[1, :, tile_rows], c[1]).astype(bf)
        return carry

    lax.fori_loop(0, model // CHUNK, cross_grads, 0)
    scatter.start(2)
    scatter.along(0)

    grad_state[...] = grad_state[...] + pull(1, 3, branch(4))
    early = part_other.shape[0] // CHUNK
    swap_part(0).start()
    gy[0] = grad_state[...].astype(bf)
    y_send[5, :, :width] = dot_nn(gy[0], w[:, 3 * width : 4 * width]).astype(bf)

    def self_back(pair, carry):
        def near(head, grad):
            folded[pl.ds(2 * pair + head, 1), :] = fold_rows(fold_offsets(grad))

        gq, gk, gv = softmax_back_pair(
            qkv[:, lanes(0, pair)],
            qkv[:, lanes(width, pair)],
            qkv[:, lanes(2 * width, pair)],
            c[0, :, lanes(0, pair)],
            inv[0, :, lanes(0, pair)],
            y_send[5, :, lanes(0, pair)],
            (e_self[2 * pair], e_self[2 * pair + 1]),
            near,
        )
        gqkv[:, lanes(0, pair)] = gq.astype(bf)
        gqkv[:, lanes(width, pair)] = gk.astype(bf)
        gqkv[:, lanes(2 * width, pair)] = gv.astype(bf)
        return carry

    lax.fori_loop(0, pairs, self_back, 0)

    y_send[5] = dot_nt(gqkv[:, : 3 * width], w[:, : 3 * width]).astype(bf)
    back = remote(y_send.at[5, theirs], y_recv.at[5, theirs], y_sems.at[0, 5], y_sems.at[1, 5], place.across())
    back.start()
    for i in range(1, early):
        swap_part(i).start()
    scatter.along(1)
    scatter.merge(2)
    keep_dw = [
        pltpu.make_async_copy(
            dw.at[:, scatter.columns(2 + i, place.core)],
            dw1_all.at[:, pl.ds((1 - i) * 2 * width, 2 * width)],
            i_sems.at[i],
        )
        for i in range(2)
    ]
    keep_dw[0].start()

    def self_grads(t, carry):
        tile_rows = pl.ds(pl.multiple_of(t * CHUNK, CHUNK), CHUNK)
        dw[tile_rows, : 3 * width] = dot_tn(normals[0, :, tile_rows], gqkv[:, : 3 * width]).astype(bf)
        dw[tile_rows, 3 * width : at_d] = dot_tn(gy[0, :, tile_rows], c[0]).astype(bf)
        return carry

    lax.fori_loop(0, model // CHUNK, self_grads, 0)
    scatter.start(3)
    table[...] = bucket_sums(folded[...], rows, False)
    scatter.total(0)
    scatter.total(1)
    back.wait_recv()
    grad = y_send[5, mine, :].astype(f32) + y_recv[5, mine, :].astype(f32)
    pulled, gain = norm_back(state[0, mine, :], gains[2:3, :], grad)
    gain_sums[2:3, :] += gain
    dec_grad[...] = grad_state[mine, :] + pulled
    swap(2).wait_recv()
    dec_out[...] = (state[2, mine, :] + y_send[2, mine, :].astype(f32) + y_recv[2, mine, :].astype(f32)).astype(bf)
    scatter.merge(3)
    keep_dw[1].start()
    for i in range(early):
        swap_part(i).wait()
    for i in range(span // CHUNK):
        keep_part(i).wait()
    for copy in keep_dw:
        copy.wait()
    for i in range(4):
        swap_cot(i).wait()
    for group in range(2):
        scatter.finish(group)
    scatter.close()
    for kind in range(5):
        swap(kind).wait_send()
    back.wait_send()


def decoder(wide, dec_rows, dcot_rows, cot_own, down, gains, base, dec_lengths, enc_lengths, mem, w2):
    half, model = dec_rows[0].shape
    rows = 2 * half
    span = mem.shape[0]
    pairs = base.shape[0]
    width = pairs * PAIR
    ffn = down.shape[2]
    late = span // CHUNK // 2 * CHUNK
    bf, f32 = jnp.bfloat16, jnp.float32
    shape = jax.ShapeDtypeStruct
    dma = pltpu.SemaphoreType.DMA
    return pl.pallas_call(
        functools.partial(decoder_kernel, wide),
        in_specs=[any_spec()] * 6 + [vmem_spec()] * 2 + [smem_spec()] * 2 + [any_spec()] * 2,
        out_shape=[
            shape((half, model), bf),
            shape((half, model), f32),
            shape((model // wide, 2 * ffn), bf),
            shape((8, model), f32),
            shape((8, 128), f32),
            shape((span, model), bf),
            shape((late, model), bf),
            shape(cot_own.shape, bf),
            shape((model, 4 * width), bf),
        ],
        out_specs=[vmem_spec()] * 5 + [any_spec()] * 4,
        scratch_shapes=[
            pltpu.VMEM(gains.shape, f32),
            pltpu.VMEM(down.shape[1:], bf),
            pltpu.VMEM((8, 2 * rows), f32),
            pltpu.VMEM((model, 8 * width + 2 * ffn), bf),
            pltpu.VMEM((span, model), bf),
            pltpu.VMEM((rows, model), bf),
            pltpu.VMEM((rows, model), bf),
            pltpu.VMEM((3, rows, model), f32),
            pltpu.VMEM((3, rows, model), bf),
            pltpu.VMEM((rows, 4 * width), bf),
            pltpu.VMEM((2, rows, width), bf),
            pltpu.VMEM((2, rows, width), f32),
            pltpu.VMEM((2 * pairs, rows, rows), bf),
            pltpu.VMEM((2 * pairs, rows, span), bf),
            pltpu.VMEM((2 * pairs, rows, 2 * rows), f32),
            pltpu.VMEM((span, 2 * width), bf),
            pltpu.VMEM((rows, ffn), bf),
            pltpu.VMEM((rows, ffn), f32),
            pltpu.VMEM((rows, ffn), bf),
            pltpu.VMEM((rows, model), f32),
            pltpu.VMEM((2, rows, model), bf),
            pltpu.VMEM((rows, 4 * width), bf),
            pltpu.VMEM((span, 2 * width), bf),
            pltpu.VMEM((6, rows, model), bf),
            pltpu.VMEM((6, rows, model), bf),
            pltpu.VMEM((model, 8 * width), bf),
        ]
        + scatter_buffers(wide, model, 2 * ffn)
        + scatter_buffers(wide, model, 4 * width)[:1]
        + scatter_buffers(wide, model, 4 * width)[:1]
        + [
            dma((4, scatter_slots(wide))),
            dma((4, scatter_slots(wide))),
            dma((2, gather_slots(wide))),
            dma((2, gather_slots(wide))),
            dma((2,)),
            dma((2, 6)),
            dma((2, 4)),
            dma((2, span // CHUNK)),
            dma((span // CHUNK,)),
            dma((9,)),
        ],
        compiler_params=pltpu.CompilerParams(
            collective_id=2, has_side_effects=True, vmem_limit_bytes=VMEM_BYTES
        ),
        cost_estimate=pl.CostEstimate(flops=10**10, bytes_accessed=6 * 10**7, transcendentals=0),
    )(
        *dec_rows,
        *dcot_rows,
        cot_own,
        down,
        gains,
        base,
        dec_lengths,
        enc_lengths,
        mem,
        w2,
    )


def on_device(
    wide,
    enc_input,
    dec_input,
    enc_lengths,
    dec_lengths,
    attn_query,
    attn_kv,
    attn_out,
    ffn_up,
    ffn_down,
    gains,
    rel_bias,
    enc_cotangent,
    dec_cotangent,
):
    heads_local = rel_bias.shape[2]
    side = lax.axis_index("narrow")
    width, ffn = DK * heads_local, ffn_up.shape[2]
    down = ffn_down.transpose(0, 2, 1)
    weights = (attn_query, attn_kv, attn_out.transpose(0, 2, 1), ffn_up, down)
    w1, w2, n0, qkv, context, inverse, exps, e1, n1, slope, active, ef, memory, dec_other, dcot_other, enc_output = enc_forward(
        wide, enc_input, dec_input, dec_cotangent, weights, gains, near_rows(rel_bias[0]), enc_lengths
    )
    dec_output, grad_dec, tile_two, dec_gains, dec_table, part_own, part_other, cot_other, dw1 = decoder(
        wide,
        (dec_input, dec_other),
        (dec_cotangent, dcot_other),
        enc_cotangent,
        down,
        gains,
        base_rows(rel_bias[1], DEC, False),
        dec_lengths,
        enc_lengths,
        memory,
        w2,
    )
    grad_enc, tile_one, sums, unused = enc_backward(
        wide,
        enc_input,
        enc_cotangent,
        cot_other,
        gains,
        dec_gains,
        dec_table,
        part_own,
        part_other,
        dw1,
        (w1, n0, qkv, context, inverse, exps, e1, n1, slope, active, ef),
    )
    tables = lax.dynamic_slice_in_dim(sums[8 : 8 + heads_local], side * 256, 256, 1)
    bias_grad = jnp.stack([tables[:, :NB].T, tables[:, 128 : 128 + NB].T])
    late = tile_one[:, 4 * width + 2 * ffn :]
    layers = (tile_one[:, : 4 * width], late[:, : 4 * width], late[:, 4 * width :])
    feeds = (tile_one[:, 4 * width : 4 * width + 2 * ffn], tile_two)
    return (
        enc_output,
        dec_output,
        grad_enc,
        grad_dec,
        jnp.stack([layer[:, :width] for layer in layers]).astype(jnp.float32),
        jnp.stack(
            [jnp.stack([layer[:, width : 2 * width], layer[:, 2 * width : 3 * width]]) for layer in layers]
        ).astype(jnp.float32),
        jnp.stack([layer[:, 3 * width :].T for layer in layers]).astype(jnp.float32),
        jnp.stack([feed[:, :ffn] for feed in feeds]).astype(jnp.float32),
        jnp.stack([feed[:, ffn:].T for feed in feeds]).astype(jnp.float32),
        sums[:6],
        bias_grad,
    )


def ffn_backward(grad_rows, normed_rows, hidden, active, weight_up, weight_down):
    grad_active = jnp.einsum(
        "rd,fd->rf", grad_rows, weight_down, preferred_element_type=jnp.float32
    )
    grad_down = jnp.einsum("rf,rd->fd", active, grad_rows, preferred_element_type=jnp.float32)
    unused, pull = jax.vjp(gelu_tanh, hidden)
    grad_hidden = pull(grad_active)[0].astype(jnp.bfloat16)
    grad_up = jnp.einsum("rd,rf->df", normed_rows, grad_hidden, preferred_element_type=jnp.float32)
    grad_normed = jnp.einsum(
        "rf,df->rd", grad_hidden, weight_up, preferred_element_type=jnp.float32
    )
    return (grad_normed, grad_up, grad_down)


def norm_backward(values, gain, grad_normed):
    unused, pull = jax.vjp(rms_norm, values, gain)
    return pull(grad_normed)


def on_device_general(
    enc_input,
    dec_input,
    enc_lengths,
    dec_lengths,
    attn_query,
    attn_kv,
    attn_out,
    ffn_up,
    ffn_down,
    gains,
    rel_bias,
    enc_cotangent,
    dec_cotangent,
):
    weights = (
        lax.all_gather(attn_query, "wide", axis=1, tiled=True),
        lax.all_gather(attn_kv, "wide", axis=2, tiled=True),
        lax.all_gather(attn_out, "wide", axis=2, tiled=True),
        lax.all_gather(ffn_up, "wide", axis=1, tiled=True),
        lax.all_gather(ffn_down, "wide", axis=2, tiled=True),
    )
    gain_rows = gains.astype(jnp.float32)
    heads_local = rel_bias.shape[2]
    enc_segments = segment_ids(enc_lengths[0], ENC)
    dec_segments = segment_ids(dec_lengths[0], DEC)

    side = lax.axis_index("narrow")
    swap = [(0, 1), (1, 0)]

    def spread_rows(values):
        own = values.astype(jnp.bfloat16)
        other = lax.ppermute(own, "narrow", swap)
        return jnp.where(side == 0, jnp.concatenate([own, other]), jnp.concatenate([other, own]))

    def collect_rows(parts):
        half = parts.shape[0] // 2
        parts = parts.astype(jnp.bfloat16)
        other = lax.ppermute(lax.dynamic_slice_in_dim(parts, (1 - side) * half, half), "narrow", swap)
        own = lax.dynamic_slice_in_dim(parts, side * half, half)
        return own.astype(jnp.float32) + other.astype(jnp.float32)

    def attention_layer(normed_query, normed_keys, layer, base, query_segments, key_segments, causal):
        query = jnp.dot(normed_query, weights[0][layer], preferred_element_type=jnp.float32).astype(jnp.bfloat16)
        keys = jnp.dot(normed_keys, weights[1][layer, 0], preferred_element_type=jnp.float32).astype(jnp.bfloat16)
        values = jnp.dot(normed_keys, weights[1][layer, 1], preferred_element_type=jnp.float32).astype(jnp.bfloat16)
        saved = attend_forward(query, keys, values, base, query_segments, key_segments, causal)
        parts = jnp.dot(saved[1], weights[2][layer], preferred_element_type=jnp.float32)
        return ((query, keys, values, saved), collect_rows(parts))

    enc_start = enc_input.astype(jnp.float32)
    rows_a = spread_rows(rms_norm(enc_start, gain_rows[0]))
    kept_a, branch = attention_layer(
        rows_a, rows_a, 0, base_rows(rel_bias[0], ENC, True), enc_segments, enc_segments, False
    )
    enc_mid = enc_start + branch
    rows_b = spread_rows(rms_norm(enc_mid, gain_rows[1]))
    hidden_b = jnp.dot(rows_b, weights[3][0], preferred_element_type=jnp.float32)
    active_b = gelu_tanh(hidden_b).astype(jnp.bfloat16)
    enc_final = enc_mid + collect_rows(
        jnp.dot(active_b, weights[4][0], preferred_element_type=jnp.float32)
    )
    memory = spread_rows(rms_norm(enc_final, gain_rows[5]))
    dec_start = dec_input.astype(jnp.float32)
    rows_c = spread_rows(rms_norm(dec_start, gain_rows[2]))
    kept_c, branch = attention_layer(
        rows_c, rows_c, 1, base_rows(rel_bias[1], DEC, False), dec_segments, dec_segments, True
    )
    dec_one = dec_start + branch
    rows_d = spread_rows(rms_norm(dec_one, gain_rows[3]))
    kept_d, branch = attention_layer(
        rows_d, memory, 2, None, dec_segments, enc_segments, False
    )
    dec_two = dec_one + branch
    rows_e = spread_rows(rms_norm(dec_two, gain_rows[4]))
    hidden_e = jnp.dot(rows_e, weights[3][1], preferred_element_type=jnp.float32)
    active_e = gelu_tanh(hidden_e).astype(jnp.bfloat16)
    dec_final = dec_two + collect_rows(
        jnp.dot(active_e, weights[4][1], preferred_element_type=jnp.float32)
    )
    def attention_back(grad_state, kept, normed_query, normed_keys, layer, span, two_sided):
        grad_rows = spread_rows(grad_state)
        query, keys, values, saved = kept
        grad_context = dot_nt(grad_rows, weights[2][layer]).astype(jnp.bfloat16)
        grad_out = dot_tn(saved[1], grad_rows)
        result = attend_backward(query, keys, values, saved, grad_context, span > 0)
        grad_q, grad_k, grad_v = result[:3]
        sums = [
            dot_tn(normed_query, grad_q),
            dot_tn(normed_keys, grad_k),
            dot_tn(normed_keys, grad_v),
            grad_out,
            table_grad(result[3], span, two_sided) if span else None,
        ]
        query_part = dot_nt(grad_q, weights[0][layer])
        key_part = dot_nt(grad_k, weights[1][layer, 0]) + dot_nt(grad_v, weights[1][layer, 1])
        return (query_part, key_part, sums)

    grad_dec = dec_cotangent.astype(jnp.float32)
    grad_normed, up_e, down_e = ffn_backward(
        spread_rows(grad_dec), rows_e, hidden_e, active_e, weights[3][1], weights[4][1]
    )
    grad_back, gain_e = norm_backward(dec_two, gain_rows[4], collect_rows(grad_normed))
    grad_dec = grad_dec + grad_back
    query_part, memory_part, sums_d = attention_back(
        grad_dec, kept_d, rows_d, memory, 2, 0, False
    )
    grad_normed, grad_memory = collect_rows(query_part), collect_rows(memory_part)
    grad_back, gain_d = norm_backward(dec_one, gain_rows[3], grad_normed)
    grad_dec = grad_dec + grad_back
    query_part, key_part, sums_c = attention_back(
        grad_dec, kept_c, rows_c, rows_c, 1, DEC, False
    )
    grad_back, gain_c = norm_backward(dec_start, gain_rows[2], collect_rows(query_part + key_part))
    grad_dec = grad_dec + grad_back
    grad_enc = enc_cotangent.astype(jnp.float32)
    grad_back, gain_m = norm_backward(enc_final, gain_rows[5], grad_memory)
    grad_enc = grad_enc + grad_back
    grad_normed, up_b, down_b = ffn_backward(
        spread_rows(grad_enc), rows_b, hidden_b, active_b, weights[3][0], weights[4][0]
    )
    grad_back, gain_b = norm_backward(enc_mid, gain_rows[1], collect_rows(grad_normed))
    grad_enc = grad_enc + grad_back
    query_part, key_part, sums_a = attention_back(
        grad_enc, kept_a, rows_a, rows_a, 0, ENC, True
    )
    grad_back, gain_a = norm_backward(enc_start, gain_rows[0], collect_rows(query_part + key_part))
    grad_enc = grad_enc + grad_back
    grad_query = jnp.stack([sums_a[0], sums_c[0], sums_d[0]])
    grad_kv = jnp.stack(
        [
            jnp.stack([sums_a[1], sums_a[2]]),
            jnp.stack([sums_c[1], sums_c[2]]),
            jnp.stack([sums_d[1], sums_d[2]]),
        ]
    )
    grad_out = jnp.stack([sums_a[3], sums_c[3], sums_d[3]])
    grad_up = jnp.stack([up_b, up_e])
    grad_down = jnp.stack([down_b, down_e])
    tiles = (
        lax.psum_scatter(
            grad_query.astype(jnp.bfloat16), "wide", scatter_dimension=1, tiled=True
        ).astype(jnp.float32),
        lax.psum_scatter(
            grad_kv.astype(jnp.bfloat16), "wide", scatter_dimension=2, tiled=True
        ).astype(jnp.float32),
        lax.psum_scatter(
            grad_out.astype(jnp.bfloat16), "wide", scatter_dimension=2, tiled=True
        ).astype(jnp.float32),
        lax.psum_scatter(
            grad_up.astype(jnp.bfloat16), "wide", scatter_dimension=1, tiled=True
        ).astype(jnp.float32),
        lax.psum_scatter(
            grad_down.astype(jnp.bfloat16), "wide", scatter_dimension=2, tiled=True
        ).astype(jnp.float32),
    )
    tiles = (
        lax.psum(tiles[0].astype(jnp.bfloat16), "dp").astype(jnp.float32),
        lax.psum(tiles[1].astype(jnp.bfloat16), "dp").astype(jnp.float32),
        lax.psum(tiles[2].astype(jnp.bfloat16), "dp").astype(jnp.float32),
        lax.psum(tiles[3].astype(jnp.bfloat16), "dp").astype(jnp.float32),
        lax.psum(tiles[4].astype(jnp.bfloat16), "dp").astype(jnp.float32),
    )
    gain_grads = jnp.stack([gain_a, gain_b, gain_c, gain_d, gain_e, gain_m])
    column = lax.axis_index("narrow") * heads_local
    bias_local = jnp.stack([sums_a[4], sums_c[4]])
    bias_full = lax.dynamic_update_slice(
        jnp.zeros((2, NB, H), jnp.float32), bias_local, (0, 0, column)
    )
    gain_total, bias_total = lax.psum((gain_grads, bias_full), ("dp", "wide", "narrow"))
    bias_grad = lax.dynamic_slice(bias_total, (0, 0, column), (2, NB, heads_local))
    return (
        enc_final.astype(jnp.bfloat16),
        dec_final.astype(jnp.bfloat16),
        grad_enc,
        grad_dec,
        tiles[0],
        tiles[1],
        tiles[2],
        tiles[3],
        tiles[4],
        gain_total,
        bias_grad,
    )


def solution(mesh):
    wide = mesh.shape["wide"]

    def body(*args):
        if args[4].shape[1] % 16 or wide % 2:
            return on_device_general(*args)
        return on_device(wide, *args)

    return jax.shard_map(
        body,
        mesh=mesh,
        in_specs=(
            P(("dp", "wide", "narrow"), None),
            P(("dp", "wide", "narrow"), None),
            P(("dp", "wide"), None),
            P(("dp", "wide"), None),
            P(None, "wide", "narrow"),
            P(None, None, "wide", "narrow"),
            P(None, "narrow", "wide"),
            P(None, "wide", "narrow"),
            P(None, "narrow", "wide"),
            P(),
            P(None, None, "narrow"),
            P(("dp", "wide", "narrow"), None),
            P(("dp", "wide", "narrow"), None),
        ),
        out_specs=(
            P(("dp", "wide", "narrow"), None),
            P(("dp", "wide", "narrow"), None),
            P(("dp", "wide", "narrow"), None),
            P(("dp", "wide", "narrow"), None),
            P(None, "wide", "narrow"),
            P(None, None, "wide", "narrow"),
            P(None, "narrow", "wide"),
            P(None, "wide", "narrow"),
            P(None, "narrow", "wide"),
            P(),
            P(None, None, "narrow"),
        ),
        check_vma=False,
    )
```

```python
import functools
import math

import jax
import jax.numpy as jnp
from jax import lax
from jax.sharding import PartitionSpec as P
import jax.experimental.pallas as pl
import jax.experimental.pallas.tpu as pltpu

H = 12
DK = 64
NB = 32
MAXD = 128
ENC = 1024
DEC = 256


EPS = 1e-06
NEG = -1e30
HIGH = lax.Precision.HIGHEST
VMEM_BYTES = 62 * 2**20
GELU_A = math.sqrt(2.0 / math.pi)
GELU_B = 0.044715


def cutoffs(exact, buckets):
    found = []
    reach = exact
    for target in range(exact + 1, buckets):
        while (
            exact + math.floor(math.log(reach / exact) / math.log(MAXD / exact) * (buckets - exact))
            < target
        ):
            reach = reach + 1
        found.append(reach)
    return found


def bucket_index(relative, two_sided):
    if two_sided:
        width = NB // 2
        offset = jnp.where(relative > 0, width, 0)
        distance = jnp.abs(relative)
    else:
        width = NB
        offset = jnp.zeros_like(relative)
        distance = jnp.maximum(-relative, 0)
    exact = width // 2
    beyond = exact + sum(((distance >= limit).astype(jnp.int32) for limit in cutoffs(exact, width)))
    return offset + jnp.where(distance < exact, distance, beyond)


def segment_ids(lengths, count):
    bounds = jnp.cumsum(lengths)
    places = jnp.arange(count, dtype=jnp.int32)
    return jnp.sum((places[:, None] >= bounds[None, :]).astype(jnp.int32), axis=1)


def rms_norm(values, gain):
    return values * lax.rsqrt(jnp.mean(values * values, axis=-1, keepdims=True) + EPS) * gain


def gelu_tanh(values):
    return jax.nn.gelu(values, approximate=True)


PAIR = 128


def offset_buckets(span, two_sided):
    places = jnp.arange(2 * span, dtype=jnp.int32)[None, :]
    relative = lax.rem(places - jnp.arange(8, dtype=jnp.int32)[:, None] + 2 * span, 2 * span) - span
    buckets = bucket_index(relative.reshape(-1), two_sided)
    return (buckets[None, :] == jnp.arange(NB, dtype=jnp.int32)[:, None]).astype(jnp.bfloat16)


def base_rows(table, span, two_sided):
    heads = table.shape[1]
    rows = lax.dot_general(
        table, offset_buckets(span, two_sided), (((0,), (0,)), ((), ())), preferred_element_type=jnp.float32
    )
    return rows.reshape(heads // 2, 2, 8, 2 * span)


def table_grad(offset_sums, span, two_sided):
    heads = 2 * offset_sums.shape[0]
    return lax.dot_general(
        offset_buckets(span, two_sided).astype(jnp.float32),
        offset_sums.reshape(heads, 16 * span),
        (((1,), (1,)), ((), ())),
        precision=HIGH,
        preferred_element_type=jnp.float32,
    )


def dot_nt(a, b):
    return lax.dot_general(a, b, (((1,), (1,)), ((), ())), preferred_element_type=jnp.float32)


def dot_tn(a, b):
    return lax.dot_general(a, b, (((0,), (0,)), ((), ())), preferred_element_type=jnp.float32)


def dot_nn(a, b):
    return lax.dot_general(a, b, (((1,), (0,)), ((), ())), preferred_element_type=jnp.float32)


def split_heads(block):
    lane = lax.broadcasted_iota(jnp.int32, block.shape, 1)
    zero = jnp.zeros_like(block)
    return jnp.where(lane < DK, block, zero), jnp.where(lane < DK, zero, block)


def attend_kernel(block, keys_count, causal, biased, *refs):
    if biased:
        qseg, kseg, base, q_ref, k_ref, v_ref, e_ref, c_ref, inv_ref, strip = refs
    else:
        qseg, kseg, q_ref, k_ref, v_ref, e_ref, c_ref, inv_ref = refs
    i = pl.program_id(1)
    if biased:
        wide = 2 * keys_count

        @pl.when(i == 0)
        def _():
            for head in range(2):
                rows = base[0, head]
                for a in range(block // 8):
                    strip[head, 8 * a : 8 * a + 8, :] = pltpu.roll(rows, (8 * a + wide - block) % wide, 1)

    allowed = qseg[...] == kseg[...]
    if causal:
        rows = lax.broadcasted_iota(jnp.int32, (block, keys_count), 0) + i * block
        allowed = allowed & (lax.broadcasted_iota(jnp.int32, (block, keys_count), 1) <= rows)
    q_heads = split_heads(q_ref[...])
    v_heads = split_heads(v_ref[...])
    inverses = []
    context = None
    for head in range(2):
        scores = dot_nt(q_heads[head], k_ref[...])
        if biased:
            start = pl.multiple_of((keys_count // block - 1 - i) * block, block)
            scores = scores + strip[head, :, pl.ds(start, keys_count)]
        scores = jnp.where(allowed, scores, NEG)
        highest = jnp.max(scores, axis=1, keepdims=True)
        weights = jnp.exp(scores - highest)
        inverses.append(1.0 / jnp.sum(weights, axis=1, keepdims=True))
        weights = weights.astype(jnp.bfloat16)
        e_ref[head] = weights
        part = dot_nn(weights, v_heads[head])
        context = part if context is None else context + part
    lane = lax.broadcasted_iota(jnp.int32, (block, PAIR), 1)
    inverse = jnp.where(lane < DK, inverses[0], inverses[1])
    inv_ref[...] = inverse
    c_ref[...] = (context * inverse).astype(jnp.bfloat16)


def attend_back_kernel(block, keys_count, steps, biased, *refs):
    if biased:
        q_ref, k_ref, v_ref, e_ref, c_ref, inv_ref, gc_ref, gq_ref, gk_ref, gv_ref, off_ref, gk_sum, gv_sum, strip = refs
    else:
        q_ref, k_ref, v_ref, e_ref, c_ref, inv_ref, gc_ref, gq_ref, gk_ref, gv_ref, gk_sum, gv_sum = refs
    i = pl.program_id(1)

    @pl.when(i == 0)
    def _():
        gk_sum[...] = jnp.zeros_like(gk_sum)
        gv_sum[...] = jnp.zeros_like(gv_sum)
        if biased:
            strip[...] = jnp.zeros_like(strip)

    scaled = (gc_ref[...].astype(jnp.float32) * inv_ref[...]).astype(jnp.bfloat16)
    product = scaled.astype(jnp.float32) * c_ref[...].astype(jnp.float32)
    lane = lax.broadcasted_iota(jnp.int32, (block, PAIR), 1)
    inner = (
        jnp.sum(jnp.where(lane < DK, product, 0.0), axis=1, keepdims=True),
        jnp.sum(jnp.where(lane < DK, 0.0, product), axis=1, keepdims=True),
    )
    g_heads = split_heads(scaled)
    q_heads = split_heads(q_ref[...])
    k_heads = split_heads(k_ref[...])
    gq = None
    for head in range(2):
        weights = e_ref[head]
        grad = dot_nt(g_heads[head], v_ref[...])
        grad = weights.astype(jnp.float32) * (grad - inner[head])
        if biased:
            start = pl.multiple_of((keys_count // block - 1 - i) * block, block)
            strip[head, :, pl.ds(start, keys_count)] += grad
        grad = grad.astype(jnp.bfloat16)
        part = dot_nn(grad, k_heads[head])
        gq = part if gq is None else gq + part
        gk_sum[...] += dot_tn(grad, q_heads[head])
        gv_sum[...] += dot_tn(weights, g_heads[head])
    gq_ref[...] = gq.astype(jnp.bfloat16)

    @pl.when(i == steps - 1)
    def _():
        gk_ref[...] = gk_sum[...].astype(jnp.bfloat16)
        gv_ref[...] = gv_sum[...].astype(jnp.bfloat16)
        if biased:
            wide = 2 * keys_count
            for head in range(2):
                total = jnp.zeros((8, wide), jnp.float32)
                for a in range(block // 8):
                    total = total + pltpu.roll(strip[head, 8 * a : 8 * a + 8, :], (block - 8 * a) % wide, 1)
                off_ref[0, head] = total


def attend_forward(query, keys, values, base, query_segments, key_segments, causal):
    count, cols = query.shape[0], keys.shape[0]
    pairs = query.shape[1] // PAIR
    block = min(256, count)
    steps = count // block
    row_spec = pl.BlockSpec((block, PAIR), lambda h, i: (i, h))
    key_spec = pl.BlockSpec((cols, PAIR), lambda h, i: (0, h))
    in_specs = [
        pl.BlockSpec((block, 1), lambda h, i: (i, 0)),
        pl.BlockSpec((1, cols), lambda h, i: (0, 0)),
    ]
    args = [query_segments[:, None], key_segments[None, :]]
    scratch = []
    if base is not None:
        in_specs.append(pl.BlockSpec((1, 2, 8, 2 * cols), lambda h, i: (h, 0, 0, 0)))
        args.append(base)
        scratch.append(pltpu.VMEM((2, block, 2 * cols), jnp.float32))
    return pl.pallas_call(
        functools.partial(attend_kernel, block, cols, causal, base is not None),
        grid=(pairs, steps),
        in_specs=in_specs + [row_spec, key_spec, key_spec],
        out_specs=[
            pl.BlockSpec((2, block, cols), lambda h, i: (h, i, 0)),
            row_spec,
            row_spec,
        ],
        out_shape=[
            jax.ShapeDtypeStruct((2 * pairs, count, cols), jnp.bfloat16),
            jax.ShapeDtypeStruct((count, pairs * PAIR), jnp.bfloat16),
            jax.ShapeDtypeStruct((count, pairs * PAIR), jnp.float32),
        ],
        scratch_shapes=scratch,
        compiler_params=pltpu.CompilerParams(vmem_limit_bytes=VMEM_BYTES),
        cost_estimate=pl.CostEstimate(
            flops=4 * count * cols * PAIR * 2 * pairs, bytes_accessed=2 * pairs * count * cols * 2, transcendentals=0
        ),
    )(*args, query, keys, values)


def attend_backward(query, keys, values, saved, grad_context, biased):
    weights, context, inverse = saved
    count, cols = query.shape[0], keys.shape[0]
    pairs = query.shape[1] // PAIR
    block = min(256, count)
    steps = count // block
    row_spec = pl.BlockSpec((block, PAIR), lambda h, i: (i, h))
    key_spec = pl.BlockSpec((cols, PAIR), lambda h, i: (0, h))
    out_specs = [row_spec, key_spec, key_spec]
    out_shape = [
        jax.ShapeDtypeStruct((count, pairs * PAIR), jnp.bfloat16),
        jax.ShapeDtypeStruct((cols, pairs * PAIR), jnp.bfloat16),
        jax.ShapeDtypeStruct((cols, pairs * PAIR), jnp.bfloat16),
    ]
    scratch = [pltpu.VMEM((cols, PAIR), jnp.float32), pltpu.VMEM((cols, PAIR), jnp.float32)]
    if biased:
        out_specs.append(pl.BlockSpec((1, 2, 8, 2 * cols), lambda h, i: (h, 0, 0, 0)))
        out_shape.append(jax.ShapeDtypeStruct((pairs, 2, 8, 2 * cols), jnp.float32))
        scratch.append(pltpu.VMEM((2, block, 2 * cols), jnp.float32))
    return pl.pallas_call(
        functools.partial(attend_back_kernel, block, cols, steps, biased),
        grid=(pairs, steps),
        in_specs=[
            row_spec,
            key_spec,
            key_spec,
            pl.BlockSpec((2, block, cols), lambda h, i: (h, i, 0)),
            row_spec,
            row_spec,
            row_spec,
        ],
        out_specs=out_specs,
        out_shape=out_shape,
        scratch_shapes=scratch,
        compiler_params=pltpu.CompilerParams(vmem_limit_bytes=VMEM_BYTES),
        cost_estimate=pl.CostEstimate(
            flops=8 * count * cols * PAIR * 2 * pairs, bytes_accessed=2 * pairs * count * cols * 2, transcendentals=0
        ),
    )(query, keys, values, weights, context, inverse, grad_context)


MESH_IDS = pl.DeviceIdType.MESH
CHUNK = 256
ATT = 4 * 384


def any_spec():
    return pl.BlockSpec(memory_space=pl.ANY)


def vmem_spec():
    return pl.BlockSpec(memory_space=pltpu.VMEM)


def smem_spec():
    return pl.BlockSpec(memory_space=pltpu.SMEM)


def documents(lengths, shape, first):
    places = lax.broadcasted_iota(jnp.int32, shape, 0 if shape[1] == 1 else 1) + first
    bound = jnp.int32(0)
    total = jnp.zeros(shape, jnp.int32)
    for k in range(lengths.shape[1]):
        bound = bound + lengths[0, k]
        total = total + (places >= bound).astype(jnp.int32)
    return total


def normed(values, gain):
    return values * lax.rsqrt(jnp.mean(values * values, axis=1, keepdims=True) + EPS) * gain


def gelu_pair(values):
    square = values * values
    inner = jnp.tanh(GELU_A * values * (1.0 + GELU_B * square))
    half = 0.5 * (1.0 + inner)
    slope = half + 0.5 * values * (1.0 - inner * inner) * (GELU_A * (1.0 + 3.0 * GELU_B * square))
    return values * half, slope


class Place:
    def __init__(self, wide):
        self.core = lax.axis_index("dp")
        self.wide = lax.axis_index("wide")
        self.side = lax.axis_index("narrow")
        self.count = wide
        self.fars = wide // 2
        self.far = self.wide // 2
        self.near = self.wide % 2

    def sibling(self):
        return (1 - self.core, self.wide, self.side)

    def across(self):
        return (self.core, self.wide, 1 - self.side)

    def beside(self):
        return (self.core, 2 * self.far + 1 - self.near, self.side)

    def along(self, step):
        return (self.core, 2 * lax.rem(self.far + step, self.fars) + self.near, self.side)

    def index_from(self, step):
        return 2 * lax.rem(self.far - step + self.fars, self.fars) + self.near

    def index_beside(self, step):
        return 2 * lax.rem(self.far - step + self.fars, self.fars) + 1 - self.near

    def greet(self):
        partners = [self.sibling(), self.across(), self.beside()]
        partners += [self.along(step) for step in range(1, self.fars)]
        barrier = pltpu.get_barrier_semaphore()
        for partner in partners:
            pl.semaphore_signal(barrier, inc=1, device_id=partner, device_id_type=MESH_IDS)
        pl.semaphore_wait(barrier, len(partners))


def remote(source, target, send, receive, partner):
    return pltpu.make_async_remote_copy(
        src_ref=source,
        dst_ref=target,
        send_sem=send,
        recv_sem=receive,
        device_id=partner,
        device_id_type=MESH_IDS,
    )


class Gather:
    def __init__(self, place, pack, groups, send, receive, local):
        self.place, self.pack, self.groups = place, pack, groups
        self.send, self.receive, self.local = send, receive, local
        self.rows = pack.shape[0]
        self.sent = []

    def at(self, group, index, core):
        first, width, target, offset = self.groups[group]
        half = width // 2
        start = pl.multiple_of(offset + core * half, 128)
        return target.at[pl.ds(pl.multiple_of(index * self.rows, 16), self.rows), pl.ds(start, half)]

    def own(self, group):
        first, width, target, offset = self.groups[group]
        half = width // 2
        return self.pack.at[:, pl.ds(pl.multiple_of(first + self.place.core * half, 128), half)]

    def local_copy(self, group):
        first, width, target, offset = self.groups[group]
        rows = pl.ds(pl.multiple_of(self.place.wide * self.rows, 16), self.rows)
        return pltpu.make_async_copy(
            self.pack.at[:, pl.ds(first, width)], target.at[rows, pl.ds(offset, width)], self.local.at[group]
        )

    def push(self, group, slot, source, index, partner):
        copy = remote(
            source,
            self.at(group, index, self.place.core),
            self.send.at[group, slot],
            self.receive.at[group, slot],
            partner,
        )
        copy.start()
        self.sent.append(copy)

    def await_slot(self, group, slot, index, core):
        block = self.at(group, index, core)
        remote(block, block, self.send.at[group, slot], self.receive.at[group, slot], self.place.sibling()).wait_recv()

    def start(self, group):
        place, fars = self.place, self.place.fars
        for step in range(1, fars):
            self.push(group, step - 1, self.own(group), place.wide, place.along(step))
        self.push(group, fars - 1, self.own(group), place.wide, place.beside())
        self.local_copy(group).start()

    def relay_along(self, group):
        place, fars = self.place, self.place.fars
        for step in range(1, fars):
            index = place.index_from(step)
            self.await_slot(group, step - 1, index, place.core)
            block = self.at(group, index, place.core)
            self.push(group, fars - 1 + step, block, index, place.beside())
            self.push(group, 2 * fars - 2 + step, block, index, place.sibling())

    def relay_beside(self, group):
        place, fars = self.place, self.place.fars
        for step in range(fars):
            index = place.index_beside(step)
            self.await_slot(group, fars - 1 + step, index, place.core)
            block = self.at(group, index, place.core)
            self.push(group, 3 * fars - 2 + step, block, index, place.sibling())

    def finish(self, group):
        place, fars = self.place, self.place.fars
        for step in range(1, fars):
            self.await_slot(group, 2 * fars - 2 + step, place.index_from(step), 1 - place.core)
        for step in range(fars):
            self.await_slot(group, 3 * fars - 2 + step, place.index_beside(step), 1 - place.core)
        self.local_copy(group).wait()

    def close(self):
        for copy in self.sent:
            copy.wait_send()


def gather_slots(wide):
    return 4 * (wide // 2) - 2


def softmax_pair(q_pair, k_pair, v_pair, allowed, biases, e_store):
    q_heads = split_heads(q_pair)
    v_heads = split_heads(v_pair)
    inverses = []
    context = None
    for head in range(2):
        scores = dot_nt(q_heads[head], k_pair)
        if biases is not None:
            scores = scores + biases(head)
        scores = jnp.where(allowed, scores, NEG)
        highest = jnp.max(scores, axis=1, keepdims=True)
        weights = jnp.exp(scores - highest)
        inverses.append(1.0 / jnp.sum(weights, axis=1, keepdims=True))
        weights = weights.astype(jnp.bfloat16)
        e_store(head, weights)
        part = dot_nn(weights, v_heads[head])
        context = part if context is None else context + part
    lane = lax.broadcasted_iota(jnp.int32, context.shape, 1)
    inverse = jnp.where(lane < DK, inverses[0], inverses[1])
    return inverse, (context * inverse).astype(jnp.bfloat16)


def build_strip(strip, base, pairs, block, span):
    def one(pair, carry):
        for head in range(2):
            rows = base[pair, head]
            for a in range(block // 8):
                strip[2 * pair + head, 8 * a : 8 * a + 8, :] = pltpu.roll(rows, (8 * a + 2 * span - block) % (2 * span), 1)
        return carry

    lax.fori_loop(0, pairs, one, 0)


NEAR = 2 * CHUNK
EDGE = NEAR // 4


def near_buckets():
    places = jnp.arange(2 * NEAR, dtype=jnp.int32)[None, :]
    relative = places - jnp.arange(8, dtype=jnp.int32)[:, None] - CHUNK - EDGE
    buckets = bucket_index(relative.reshape(-1), True)
    return (buckets[None, :] == jnp.arange(NB, dtype=jnp.int32)[:, None]).astype(jnp.bfloat16)


def near_rows(table):
    rows = lax.dot_general(
        table, near_buckets(), (((0,), (0,)), ((), ())), preferred_element_type=jnp.float32
    )
    return rows.reshape(table.shape[1] // 2, 2, 8, 2 * NEAR)


def build_near(strip, base, pairs):
    def one(pair, carry):
        for head in range(2):
            rows = base[pair, head]
            for a in range(CHUNK // 8):
                turned = pltpu.roll(rows, (2 * NEAR - CHUNK + 8 * a) % (2 * NEAR), 1)
                strip[2 * pair + head, 8 * a : 8 * a + 8, :] = turned[:, :NEAR]
        return carry

    lax.fori_loop(0, pairs, one, 0)


def near_window(i, rows):
    low, high = max(i * CHUNK - EDGE, 0), min(i * CHUNK + CHUNK + EDGE, rows)
    return low, high, low - (i * CHUNK - EDGE)


def near_bias(strip, base, pair, head, i, rows):
    low, high, shift = near_window(i, rows)
    parts = [strip[2 * pair + head, :, shift : shift + high - low]]
    if low > 0:
        parts.insert(0, jnp.broadcast_to(base[pair, head, 0:1, 0:1], (CHUNK, low)))
    if high < rows:
        parts.append(jnp.broadcast_to(base[pair, head, 0:1, 2 * NEAR - 1 : 2 * NEAR], (CHUNK, rows - high)))
    return jnp.concatenate(parts, axis=1)


def enc_forward_kernel(
    wide,
    x_own,
    dec_own,
    dcot_own,
    query_in,
    kv_in,
    out_in,
    up_in,
    down_in,
    gains_in,
    base,
    lengths,
    w1_all,
    w2,
    n0_all,
    qkv_all,
    c_all,
    inv_all,
    e_all,
    e1_all,
    n1_all,
    slope_all,
    a_all,
    ef_all,
    mem_all,
    dec_other,
    dcot_other,
    out_all,
    gains,
    pack,
    w1,
    n0,
    qkv,
    c,
    inv,
    e1,
    n1,
    ef,
    mem,
    x_full,
    strip,
    e_buf,
    slope_buf,
    a_buf,
    y_send,
    y_recv,
    g_send,
    g_recv,
    g_local,
    x_sems,
    y_sems,
    z_sems,
    l_sems,
    p_sems,
    o_sems,
):
    place = Place(wide)
    side = place.side
    half = x_own.shape[0]
    rows = 2 * half
    steps = rows // CHUNK
    width = c.shape[1]
    ffn = up_in.shape[2]
    pairs = width // PAIR
    pieces = []
    for layer in range(3):
        first = (0, 4 * width + 2 * ffn, 8 * width + 2 * ffn)[layer]
        pieces += [(query_in.at[layer], first), (kv_in.at[layer, 0], first + width)]
        pieces += [(kv_in.at[layer, 1], first + 2 * width), (out_in.at[layer], first + 3 * width)]
    pieces += [(up_in.at[0], 4 * width), (down_in.at[0], 4 * width + ffn), (up_in.at[1], 12 * width + 2 * ffn)]
    packs = [
        pltpu.make_async_copy(piece, pack.at[:, pl.ds(first, piece.shape[1])], p_sems.at[index])
        for index, (piece, first) in enumerate(pieces)
    ]
    for copy in packs:
        copy.start()
    gains[...] = gains_in[...].astype(jnp.float32)
    place.greet()
    gather = Gather(
        place,
        pack,
        [
            (0, 2 * width, w1, 0),
            (2 * width, 2 * width, w1, 2 * width),
            (4 * width, ffn, w1, 4 * width),
            (4 * width + ffn, ffn, w1, 4 * width + ffn),
            (4 * width + 2 * ffn, 4 * width, w2, 0),
            (8 * width + 2 * ffn, 4 * width, w2, 4 * width),
            (12 * width + 2 * ffn, ffn, w2, 8 * width),
        ],
        g_send,
        g_recv,
        g_local,
    )
    mine = pl.ds(pl.multiple_of(side * half, 16), half)
    swap_x = remote(x_own, x_full.at[mine], x_sems.at[0], x_sems.at[1], place.across())
    swap_x.start()
    for copy in packs[:4]:
        copy.wait()
    gather.start(0)
    gather.start(1)
    for copy in packs[4:]:
        copy.wait()
    keep_x = pltpu.make_async_copy(x_own, x_full.at[mine], l_sems.at[6])
    keep_x.start()
    build_near(strip, base, pairs)
    gather.relay_along(0)
    gather.relay_along(1)
    gather.start(2)
    keep_x.wait()
    gather.relay_beside(0)
    gather.relay_beside(1)
    swap_x.wait()
    later = [
        remote(dec_own, dec_other, x_sems.at[2], x_sems.at[3], place.across()),
        remote(dcot_own, dcot_other, x_sems.at[4], x_sems.at[5], place.across()),
    ]
    for copy in later:
        copy.start()
    stores = []

    def store_out(source, target):
        stores.append(pltpu.make_async_copy(source, target, o_sems.at[len(stores)]))
        stores[-1].start()


    def norm_rows(i, carry):
        at = pl.ds(pl.multiple_of(i * CHUNK, CHUNK), CHUNK)
        n0[at, :] = normed(x_full[at, :].astype(jnp.float32), gains[0:1, :]).astype(jnp.bfloat16)
        return carry

    lax.fori_loop(0, steps, norm_rows, 0)
    gather.finish(0)
    gather.finish(1)

    def project(i, carry):
        at = pl.ds(pl.multiple_of(i * CHUNK, CHUNK), CHUNK)
        qkv[at, width:] = dot_nn(n0[at, :], w1[:, width : 3 * width]).astype(jnp.bfloat16)
        return carry

    def project_queries(i, carry):
        at = pl.ds(pl.multiple_of(i * CHUNK, CHUNK), CHUNK)
        qkv[at, :width] = dot_nn(n0[at, :], w1[:, :width]).astype(jnp.bfloat16)
        return carry

    lax.fori_loop(0, steps, project, 0)
    project_queries(0, 0)
    store_out(n0, n0_all)

    def lanes(base_lane, pair):
        return pl.ds(pl.multiple_of(base_lane + pair * PAIR, PAIR), PAIR)

    def save(i, kind):
        slot = i % 2
        at = pl.ds(i * CHUNK, CHUNK)
        if kind == 0:
            return pltpu.make_async_copy(e_buf.at[slot], e_all.at[:, at, :], l_sems.at[slot])
        if kind == 1:
            return pltpu.make_async_copy(slope_buf.at[slot], slope_all.at[at, :], l_sems.at[2 + slot])
        return pltpu.make_async_copy(a_buf.at[slot], a_all.at[at, :], l_sems.at[4 + slot])

    def swap_y(layer, i):
        at = pl.ds(i * CHUNK, CHUNK)
        sems = y_sems if layer == 0 else z_sems
        return remote(y_send.at[layer, at], y_recv.at[layer, at], sems.at[0, i], sems.at[1, i], place.across())

    def attend(i):
        at = pl.ds(i * CHUNK, CHUNK)
        slot = i % 2
        if i >= 2:
            save(i - 2, 0).wait()

        def one(pair, carry):
            allowed = documents(lengths, (CHUNK, 1), i * CHUNK) == documents(lengths, (1, rows), 0)

            def bias(head):
                return near_bias(strip, base, pair, head, i, rows)

            def store(head, weights):
                e_buf[slot, 2 * pair + head] = weights

            inverse, context = softmax_pair(
                qkv[at, lanes(0, pair)],
                qkv[:, lanes(width, pair)],
                qkv[:, lanes(2 * width, pair)],
                allowed,
                bias,
                store,
            )
            inv[at, lanes(0, pair)] = inverse
            c[at, lanes(0, pair)] = context
            return carry

        lax.fori_loop(0, pairs, one, 0)
        save(i, 0).start()
        store_out(c.at[at], c_all.at[at])
        store_out(inv.at[at], inv_all.at[at])
        y_send[0, at, :] = dot_nt(c[at, :], w1[:, 3 * width : 4 * width]).astype(jnp.bfloat16)
        swap_y(0, i).start()

    def feed(i):
        at = pl.ds(i * CHUNK, CHUNK)
        slot = i % 2
        swap_y(0, i).wait_recv()
        both = y_send[0, at, :].astype(jnp.float32) + y_recv[0, at, :].astype(jnp.float32)
        middle = x_full[at, :].astype(jnp.float32) + both
        e1[at, :] = middle
        rounded = normed(middle, gains[1:2, :]).astype(jnp.bfloat16)
        n1[at, :] = rounded
        store_out(e1.at[at], e1_all.at[at])
        store_out(n1.at[at], n1_all.at[at])
        if i >= 2:
            save(i - 2, 1).wait()
            save(i - 2, 2).wait()

        def part(j, carry):
            cols = pl.ds(pl.multiple_of(4 * width + j * width, PAIR), width)
            here = pl.ds(pl.multiple_of(j * width, PAIR), width)
            active, slope = gelu_pair(dot_nn(n1[at, :], w1[:, cols]))
            a_buf[slot, :, here] = active.astype(jnp.bfloat16)
            slope_buf[slot, :, here] = slope.astype(jnp.bfloat16)
            return carry

        lax.fori_loop(0, ffn // width, part, 0)
        save(i, 1).start()
        save(i, 2).start()
        y_send[1, at, :] = dot_nt(a_buf[slot], w1[:, 4 * width + ffn :]).astype(jnp.bfloat16)
        swap_y(1, i).start()

    def last(i):
        at = pl.ds(i * CHUNK, CHUNK)
        swap_y(1, i).wait_recv()
        both = y_send[1, at, :].astype(jnp.float32) + y_recv[1, at, :].astype(jnp.float32)
        final = e1[at, :] + both
        ef[at, :] = final
        mem[at, :] = normed(final, gains[5:6, :]).astype(jnp.bfloat16)
        store_out(ef.at[at], ef_all.at[at])
        store_out(mem.at[at], mem_all.at[at])

    attend(0)
    gather.start(3)
    gather.relay_along(2)
    lax.fori_loop(1, steps, project_queries, 0)
    store_out(qkv, qkv_all)
    gather.start(4)
    gather.relay_along(3)
    gather.relay_beside(2)
    attend(1)
    gather.start(5)
    gather.relay_along(4)
    gather.relay_beside(3)
    gather.finish(2)
    attend(2)
    gather.finish(3)
    store_out(w1, w1_all)
    feed(0)
    gather.start(6)
    gather.relay_along(5)
    gather.relay_beside(4)
    attend(3)
    feed(1)
    gather.relay_beside(5)
    gather.relay_along(6)
    feed(2)
    feed(3)
    last(0)
    gather.relay_beside(6)
    last(1)
    last(2)
    last(3)
    x_full[:half, :] = ef[mine, :].astype(jnp.bfloat16)
    store_out(x_full.at[pl.ds(0, half)], out_all)
    for group in range(4, 7):
        gather.finish(group)
    gather.close()
    for copy in later:
        copy.wait()
    for copy in stores:
        copy.wait()
    for i in range(steps):
        swap_y(0, i).wait_send()
        swap_y(1, i).wait_send()
    for i in range(steps - 2, steps):
        for kind in range(3):
            save(i, kind).wait()


def enc_forward(wide, x_own, dec_own, dcot_own, weights, gains, base, lengths):
    half, model = x_own.shape
    rows = 2 * half
    pairs = base.shape[0]
    width = pairs * PAIR
    ffn = weights[3].shape[2]
    bf, f32 = jnp.bfloat16, jnp.float32
    shape = jax.ShapeDtypeStruct
    dma = pltpu.SemaphoreType.DMA
    slots = gather_slots(wide)
    steps = rows // CHUNK
    saved = [
        ((model, 4 * width + 2 * ffn), bf),
        ((rows, model), bf),
        ((rows, 3 * width), bf),
        ((rows, width), bf),
        ((rows, width), f32),
        ((rows, model), f32),
        ((rows, model), bf),
        ((rows, model), f32),
        ((rows, model), bf),
    ]
    kept = [shape(*pair) for pair in saved]
    out_shape = (
        [kept[0], shape((model, 8 * width + ffn), bf)]
        + kept[1:5]
        + [shape((2 * pairs, rows, rows), bf)]
        + kept[5:7]
        + [shape((rows, ffn), bf), shape((rows, ffn), bf)]
        + kept[7:]
        + [shape(dec_own.shape, bf), shape(dcot_own.shape, bf), shape(x_own.shape, bf)]
    )
    return pl.pallas_call(
        functools.partial(enc_forward_kernel, wide),
        in_specs=[vmem_spec()] + [any_spec()] * 7 + [vmem_spec()] * 2 + [smem_spec()],
        out_shape=out_shape,
        out_specs=[any_spec()] * len(out_shape),
        scratch_shapes=[pltpu.VMEM(gains.shape, f32), pltpu.VMEM((x_own.shape[1] // wide, 12 * width + 3 * ffn), bf)]
        + [pltpu.VMEM(*pair) for pair in saved]
        + [
            pltpu.VMEM((rows, model), bf),
            pltpu.VMEM((2 * pairs, CHUNK, NEAR), f32),
            pltpu.VMEM((2, 2 * pairs, CHUNK, rows), bf),
            pltpu.VMEM((2, CHUNK, ffn), bf),
            pltpu.VMEM((2, CHUNK, ffn), bf),
            pltpu.VMEM((2, rows, model), bf),
            pltpu.VMEM((2, rows, model), bf),
            dma((7, slots)),
            dma((7, slots)),
            dma((7,)),
            dma((8,)),
            dma((2, steps)),
            dma((2, steps)),
            dma((7,)),
            dma((15,)),
            dma((4 + 6 * steps,)),
        ],
        compiler_params=pltpu.CompilerParams(
            collective_id=0, has_side_effects=True, vmem_limit_bytes=VMEM_BYTES
        ),
        cost_estimate=pl.CostEstimate(flops=10**10, bytes_accessed=6 * 10**7, transcendentals=0),
    )(x_own, dec_own, dcot_own, *weights, gains, base, lengths)


def norm_back(values, gain, grad):
    scale = lax.rsqrt(jnp.mean(values * values, axis=1, keepdims=True) + EPS)
    scaled = grad * gain
    pulled = scale * (scaled - values * (scale * scale) * jnp.mean(scaled * values, axis=1, keepdims=True))
    return pulled, jnp.sum(grad * values * scale, axis=0, keepdims=True)


class Scatter:
    def __init__(self, place, rows, groups, tile, send, receive):
        self.place, self.rows, self.groups, self.tile = place, rows, groups, tile
        self.send, self.receive = send, receive
        self.sent = []

    def columns(self, group, core):
        first, width = self.groups[group]["first"], self.groups[group]["width"]
        if self.groups[group]["core"] is None:
            return pl.ds(first, width // 2)
        return pl.ds(pl.multiple_of(first + core * (width // 2), 128), width // 2)

    def block(self, group, index):
        return self.groups[group]["grad"].at[
            pl.ds(pl.multiple_of(index * self.rows, 16), self.rows), self.columns(group, self.place.core)
        ]

    def push(self, group, slot, source, target, partner, arrival=None):
        arrival = slot if arrival is None else arrival
        copy = remote(source, target, self.send.at[group, slot], self.receive.at[group, arrival], partner)
        copy.start()
        self.sent.append(copy)

    def await_slot(self, group, slot, block):
        remote(block, block, self.send.at[group, 0], self.receive.at[group, slot], self.place.sibling()).wait_recv()

    def start(self, group):
        parts = self.groups[group]
        self.push(
            group, 0, parts["grad"].at[:, self.columns(group, 1 - self.place.core)], parts["core"], self.place.sibling()
        )

    def add_block(self, group, index, other):
        block = self.block(group, index)
        block[...] = (block[...].astype(jnp.float32) + other.astype(jnp.float32)).astype(jnp.bfloat16)
        return block

    def merge(self, group):
        parts = self.groups[group]
        self.await_slot(group, 0, parts["core"])
        for index in range(self.place.count):
            self.add_block(group, index, parts["core"][index * self.rows : (index + 1) * self.rows, :])

    def beside(self, group):
        parts, place = self.groups[group], self.place
        if parts["core"] is None:
            for step in range(place.fars):
                index = 2 * lax.rem(place.far + 1 + step, place.fars) + 1 - place.near
                self.push(group, 1 + step, self.block(group, index), parts["beside"].at[step], place.beside())
            return
        self.await_slot(group, 0, parts["core"])

        def received(index):
            return parts["core"][pl.ds(pl.multiple_of(index * self.rows, 16), self.rows), :]

        for step in range(place.fars):
            far = lax.rem(place.far + 1 + step, place.fars)
            index = 2 * far + 1 - place.near
            block = self.add_block(group, index, received(index))
            self.push(group, 1 + step, block, parts["beside"].at[step], place.beside())
        for step in range(place.fars):
            far = lax.rem(place.far + 1 + step, place.fars)
            index = 2 * far + place.near
            self.add_block(group, index, received(index))

    def along(self, group):
        parts, place = self.groups[group], self.place
        for step in range(1, place.fars):
            index = 2 * lax.rem(place.far + step, place.fars) + place.near
            self.await_slot(group, step, parts["beside"].at[step - 1])
            block = self.add_block(group, index, parts["beside"][step - 1])
            self.push(group, place.fars + step, block, parts["along"].at[step - 1], place.along(step))

    def total(self, group):
        parts, place = self.groups[group], self.place
        self.await_slot(group, place.fars, parts["beside"].at[place.fars - 1])
        value = self.block(group, place.wide)[...].astype(jnp.float32) + parts["beside"][place.fars - 1].astype(jnp.float32)
        for step in range(1, place.fars):
            self.await_slot(group, place.fars + step, parts["along"].at[step - 1])
            value = value + parts["along"][step - 1].astype(jnp.float32)
        half = parts["width"] // 2
        block = self.tile.at[:, pl.ds(pl.multiple_of(parts["out"] + place.core * half, 128), half)]
        block[...] = value.astype(jnp.bfloat16)
        self.push(group, 2 * place.fars, block, block, place.sibling())

    def finish(self, group):
        parts, place = self.groups[group], self.place
        half = parts["width"] // 2
        block = self.tile.at[:, pl.ds(pl.multiple_of(parts["out"] + (1 - place.core) * half, 128), half)]
        self.await_slot(group, 2 * place.fars, block)

    def close(self):
        for copy in self.sent:
            copy.wait_send()


def half_group(grad, first, width, out, part, core, beside, along):
    at = pl.ds(part * (width // 2), width // 2)
    return dict(
        grad=grad,
        first=first,
        width=width,
        out=out,
        core=core.at[:, at],
        beside=beside.at[:, :, at],
        along=along.at[:, :, at],
    )


def scatter_slots(wide):
    return 2 * (wide // 2) + 1


def scatter_buffers(wide, model, width):
    half, rows, fars = width // 2, model // wide, wide // 2
    return [
        pltpu.VMEM((model, half), jnp.bfloat16),
        pltpu.VMEM((fars, rows, half), jnp.bfloat16),
        pltpu.VMEM((fars - 1, rows, half), jnp.bfloat16),
    ]


def softmax_back_pair(q_pair, k_pair, v_pair, c_pair, inverse, gc_pair, weights, near):
    scaled = (gc_pair.astype(jnp.float32) * inverse).astype(jnp.bfloat16)
    product = scaled.astype(jnp.float32) * c_pair.astype(jnp.float32)
    lane = lax.broadcasted_iota(jnp.int32, product.shape, 1)
    inner = (
        jnp.sum(jnp.where(lane < DK, product, 0.0), axis=1, keepdims=True),
        jnp.sum(jnp.where(lane < DK, 0.0, product), axis=1, keepdims=True),
    )
    g_heads = split_heads(scaled)
    q_heads = split_heads(q_pair)
    k_heads = split_heads(k_pair)
    gq = None
    grads = []
    for head in range(2):
        grad = weights[head].astype(jnp.float32) * (dot_nt(g_heads[head], v_pair) - inner[head])
        if near is not None:
            near(head, grad)
        grad = grad.astype(jnp.bfloat16)
        grads.append(grad)
        part = dot_nn(grad, k_heads[head])
        gq = part if gq is None else gq + part
    gk = dot_tn(jnp.concatenate(grads, axis=0), jnp.concatenate(q_heads, axis=0))
    gv = dot_tn(jnp.concatenate([weights[0], weights[1]], axis=0), jnp.concatenate(g_heads, axis=0))
    return gq, gk, gv


def fold_near(rows):
    total = jnp.zeros((8, 2 * NEAR), jnp.float32)
    blank = jnp.zeros((8, NEAR), jnp.float32)
    for a in range(CHUNK // 8):
        wider = jnp.concatenate([rows[8 * a : 8 * a + 8, :], blank], axis=1)
        total = total + pltpu.roll(wider, (CHUNK - 8 * a) % (2 * NEAR), 1)
    return total


def bucket_sums(rows, offset, two_sided):
    span = rows.shape[1]
    relative = lax.broadcasted_iota(jnp.int32, (span, 128), 0) - offset
    onehot = bucket_index(relative, two_sided) == lax.broadcasted_iota(jnp.int32, (span, 128), 1)
    return lax.dot_general(
        rows,
        onehot.astype(jnp.float32),
        (((1,), (0,)), ((), ())),
        precision=HIGH,
        preferred_element_type=jnp.float32,
    )


def fold_rows(rows):
    span = rows.shape[1]
    total = rows[0:1, :]
    for b in range(1, 8):
        total = total + pltpu.roll(rows, span - b, 1)[b : b + 1, :]
    return total


class Total:
    def __init__(self, place, held, send, receive):
        self.place, self.held, self.send, self.receive = place, held, send, receive
        partners = (place.sibling(), place.across(), place.beside())
        self.copies = [
            remote(held.at[stage], held.at[4 + stage], send.at[stage], receive.at[stage], partner)
            for stage, partner in enumerate(partners)
        ]
        self.last = [
            remote(held.at[3], held.at[7 + place.far], send.at[2 + step], receive.at[2 + step], place.along(step))
            for step in range(1, place.fars)
        ]

    def start(self):
        self.copies[0].start()

    def step(self, stage):
        held = self.held
        self.copies[stage].wait()
        held[stage + 1] = held[stage] + held[4 + stage]
        for copy in [self.copies[stage + 1]] if stage < 2 else self.last:
            copy.start()

    def finish(self):
        for copy in self.last:
            copy.wait()
        result = None
        for far in range(self.place.fars):
            part = jnp.where(self.place.far == far, self.held[3], self.held[7 + far])
            result = part if result is None else result + part
        return result


def enc_backward_kernel(
    wide,
    x_own,
    cot_own,
    cot_other,
    gains_in,
    dec_gains,
    dec_table,
    part_own,
    part_other,
    dw1_in,
    w1_in,
    n0_in,
    qkv_in,
    c_in,
    inv_in,
    e_all,
    e1_all,
    n1_in,
    slope_all,
    a_in,
    ef_all,
    grad_out,
    tile,
    total_sums,
    part_late,
    gains,
    gain_sums,
    far_sums,
    folded,
    held,
    w1,
    dw1,
    qkv,
    c,
    inv,
    n1,
    active,
    cot,
    e_buf,
    state_buf,
    slope_buf,
    part_buf,
    other_buf,
    g_send,
    g_recv,
    l_recv,
    state_grad,
    gy,
    gu,
    gqkv,
    gk_sum,
    gv_sum,
    strip,
    core_f,
    beside_f,
    along_f,
    beside_a,
    along_a,
    beside_d,
    along_d,
    s_send,
    s_recv,
    t_send,
    t_recv,
    m_sems,
    g_sems,
    l_sems,
    e_sems,
    t_sems,
    i_sems,
):
    place = Place(wide)
    side = place.side
    half = x_own.shape[0]
    rows = 2 * half
    steps = rows // CHUNK
    width = c.shape[1]
    ffn = active.shape[1]
    pairs = width // PAIR
    model = x_own.shape[1]
    bf, f32 = jnp.bfloat16, jnp.float32
    place.greet()

    def swap(i):
        at = pl.ds(i * CHUNK, CHUNK)
        return remote(g_send.at[at], g_recv.at[at], g_sems.at[0, i], g_sems.at[1, i], place.across())

    late = part_late.shape[0] // CHUNK

    def swap_late(i):
        return remote(
            part_own.at[pl.ds((steps - late + i) * CHUNK, CHUNK)],
            part_late.at[pl.ds(i * CHUNK, CHUNK)],
            m_sems.at[0, i],
            m_sems.at[1, i],
            place.across(),
        )

    for i in range(late):
        swap_late(i).start()

    def other_part(i):
        if i < steps - late:
            return part_other.at[pl.ds(i * CHUNK, CHUNK)]
        return part_late.at[pl.ds((i - steps + late) * CHUNK, CHUNK)]

    def fetch(i):
        at = pl.ds(i * CHUNK, CHUNK)
        slot = i % 2
        return [
            pltpu.make_async_copy(ef_all.at[at], state_buf.at[slot], t_sems.at[0, slot]),
            pltpu.make_async_copy(slope_all.at[at], slope_buf.at[slot], t_sems.at[1, slot]),
            pltpu.make_async_copy(part_own.at[at], part_buf.at[slot], t_sems.at[2, slot]),
            pltpu.make_async_copy(other_part(i), other_buf.at[slot], t_sems.at[3, slot]),
        ]

    def fetch_state(i):
        at = pl.ds(i * CHUNK, CHUNK)
        return pltpu.make_async_copy(e1_all.at[at], state_buf.at[i % 2], t_sems.at[0, i % 2])

    def fetch_e(step):
        chunk, pair, slot = step // pairs, lax.rem(step, pairs), lax.rem(step, 2)
        at = pl.ds(pl.multiple_of(chunk * CHUNK, CHUNK), CHUNK)
        return pltpu.make_async_copy(e_all.at[pl.ds(2 * pair, 2), at, :], e_buf.at[slot], e_sems.at[slot])

    mine = pl.ds(pl.multiple_of(side * half, 16), half)
    theirs = pl.ds(pl.multiple_of((1 - side) * half, 16), half)
    loads = [
        pltpu.make_async_copy(cot_own, cot.at[mine], i_sems.at[0]),
        pltpu.make_async_copy(cot_other, cot.at[theirs], i_sems.at[1]),
        pltpu.make_async_copy(w1_in, w1, i_sems.at[2]),
        pltpu.make_async_copy(a_in, active, i_sems.at[3]),
        pltpu.make_async_copy(n1_in, n1, i_sems.at[4]),
        pltpu.make_async_copy(qkv_in, qkv, i_sems.at[5]),
        pltpu.make_async_copy(c_in, c, i_sems.at[6]),
        pltpu.make_async_copy(inv_in, inv, i_sems.at[7]),
        pltpu.make_async_copy(dw1_in, dw1, i_sems.at[8]),
    ]
    loads[8].start()
    for index in (0, 1):
        loads[index].start()
    for load in fetch(0):
        load.start()
    for load in loads[2:8]:
        load.start()
    gk_sum[...] = jnp.zeros_like(gk_sum)
    gv_sum[...] = jnp.zeros_like(gv_sum)
    strip[...] = jnp.zeros_like(strip)
    far_sums[...] = jnp.zeros_like(far_sums)
    gains[...] = gains_in[...].astype(f32)
    gain_sums[...] = jnp.zeros_like(gain_sums)
    out_c = 4 * width + 2 * ffn
    core_a = active.at[pl.ds(0, model), pl.ds(0, 2 * width)]
    scatter = Scatter(
        place,
        model // wide,
        [
            dict(grad=dw1, first=0, width=4 * width, out=out_c, core=None, beside=beside_a, along=along_a),
            dict(grad=dw1, first=2 * width, width=4 * width, out=out_c + 4 * width, core=None, beside=beside_d, along=along_d),
            half_group(w1, 4 * width, ffn, 4 * width, 0, core_f, beside_f, along_f),
            half_group(w1, 4 * width + ffn, ffn, 4 * width + ffn, 1, core_f, beside_f, along_f),
            half_group(gu.at[pl.ds(0, model)], 0, 2 * width, 0, 0, core_a, beside_a, along_a),
            half_group(gu.at[pl.ds(0, model)], 2 * width, 2 * width, 2 * width, 1, core_a, beside_a, along_a),
        ],
        tile,
        s_send,
        s_recv,
    )

    def own_weight(i):
        return jnp.where((i * CHUNK) // half == side, 1.0, 0.0).astype(f32)

    loads[8].wait()
    scatter.beside(0)
    scatter.beside(1)
    for index in (0, 1, 2):
        loads[index].wait()

    for i in range(steps):
        at = slice(i * CHUNK, (i + 1) * CHUNK)
        slot = i % 2
        if i + 1 < steps:
            if i + 1 >= steps - late:
                swap_late(i + 1 - steps + late).wait_recv()
            for load in fetch(i + 1):
                load.start()
        for load in fetch(i):
            load.wait()
        grad = part_buf[slot].astype(f32) + other_buf[slot].astype(f32)
        pulled, gain = norm_back(state_buf[slot], gains[5:6, :], grad)
        gain_sums[5:6, :] += gain * own_weight(i)
        total = cot[at, :].astype(f32) + pulled
        state_grad[at, :] = total
        gy[at, :] = total.astype(bf)

        def part(j, carry):
            cols = pl.ds(pl.multiple_of(4 * width + ffn + j * width, PAIR), width)
            here = pl.ds(pl.multiple_of(j * width, PAIR), width)
            grad_active = dot_nn(gy[at, :], w1[:, cols])
            gu[at, here] = (slope_buf[slot, :, here].astype(f32) * grad_active).astype(bf)
            return carry

        lax.fori_loop(0, ffn // width, part, 0)
        g_send[at, :] = dot_nt(gu[at, :], w1[:, 4 * width : 4 * width + ffn]).astype(bf)
        swap(i).start()
    for load in loads[3:8]:
        load.wait()
    fetch_state(0).start()
    fetch_e(0).start()

    def up_grads(t, carry):
        tile_rows = pl.ds(pl.multiple_of(t * CHUNK, CHUNK), CHUNK)
        w1[tile_rows, 4 * width : 4 * width + ffn] = dot_tn(n1[:, tile_rows], gu[...]).astype(bf)
        return carry

    def down_grads(t, carry):
        tile_rows = pl.ds(pl.multiple_of(t * CHUNK, CHUNK), CHUNK)
        w1[tile_rows, 4 * width + ffn :] = dot_tn(gy[:, tile_rows], active[...]).astype(bf)
        return carry

    scatter.along(0)
    lax.fori_loop(0, model // CHUNK, up_grads, 0)
    scatter.start(2)
    lax.fori_loop(0, model // CHUNK, down_grads, 0)
    scatter.start(3)
    scatter.along(1)
    scatter.beside(2)
    n0 = cot
    late_loads = [
        pltpu.make_async_copy(n0_in, n0, i_sems.at[0]),
        pltpu.make_async_copy(x_own, n1.at[pl.ds(half, half)], i_sems.at[1]),
    ]
    for load in late_loads:
        load.start()

    dw0 = gu
    l_send = n1

    def lanes(base_lane, pair):
        return pl.ds(pl.multiple_of(base_lane + pair * PAIR, PAIR), PAIR)

    def attend_back(i):
        at = slice(i * CHUNK, (i + 1) * CHUNK)
        slot = i % 2
        if i + 1 < steps:
            fetch_state(i + 1).start()
        fetch_state(i).wait()
        swap(i).wait_recv()
        grad = g_send[at, :].astype(f32) + g_recv[at, :].astype(f32)
        pulled, gain = norm_back(state_buf[slot], gains[1:2, :], grad)
        gain_sums[1:2, :] += gain * own_weight(i)
        total = state_grad[at, :] + pulled
        state_grad[at, :] = total
        gy[at, :] = total.astype(bf)
        g_send[at, :width] = dot_nn(gy[at, :], w1[:, 3 * width : 4 * width]).astype(bf)
        low, high, shift = near_window(i, rows)

        def one(pair, carry):
            step = i * pairs + pair

            @pl.when(step + 1 < steps * pairs)
            def _():
                fetch_e(step + 1).start()

            fetch_e(step).wait()
            e_slot = lax.rem(step, 2)

            def near(head, grad):
                strip[2 * pair + head, :, shift : shift + high - low] += grad[:, low:high]
                for edge, (start, end) in enumerate(((0, low), (high, rows))):
                    if end > start:
                        folded = jnp.sum(grad[:, start:end].reshape(CHUNK // 8, 8, end - start), axis=0)
                        wide_sum = folded[:, :128]
                        for lane in range(128, end - start, 128):
                            wide_sum = wide_sum + folded[:, lane : lane + 128]
                        far_sums[edge, 2 * pair + head] += wide_sum

            gq, gk, gv = softmax_back_pair(
                qkv[at, lanes(0, pair)],
                qkv[:, lanes(width, pair)],
                qkv[:, lanes(2 * width, pair)],
                c[at, lanes(0, pair)],
                inv[at, lanes(0, pair)],
                g_send[at, lanes(0, pair)],
                (e_buf[e_slot, 0], e_buf[e_slot, 1]),
                near,
            )
            gqkv[at, lanes(0, pair)] = gq.astype(bf)
            gk_sum[:, lanes(0, pair)] += gk
            gv_sum[:, lanes(0, pair)] += gv
            return carry

        lax.fori_loop(0, pairs, one, 0)

    for i in range(steps):
        swap(i).wait_send()
        attend_back(i)
        if i == 0:
            scatter.total(0)
            scatter.beside(3)
            scatter.along(2)
        if i == 1:
            scatter.total(1)
        if i == 2:
            scatter.along(3)
        if i == 3:
            scatter.total(2)
    for load in late_loads:
        load.wait()
    gqkv[:, width : 2 * width] = gk_sum[...].astype(bf)
    gqkv[:, 2 * width :] = gv_sum[...].astype(bf)

    ones = jnp.ones((8, 3 * width), f32)

    def weight_grads_a(t, carry, at_grads=slice(0, 2 * width)):
        tile_rows = pl.ds(pl.multiple_of(t * CHUNK, CHUNK), CHUNK)
        grads = dot_tn(n0[:, tile_rows], gqkv[:, at_grads])
        dw0[tile_rows, at_grads] = grads.astype(bf)
        products = lax.dot_general(
            ones[:, at_grads],
            grads * w1[tile_rows, at_grads].astype(f32),
            (((1,), (1,)), ((), ())),
            precision=HIGH,
            preferred_element_type=f32,
        )
        gain_sums[0:1, tile_rows] += products[0:1, :] / gains[0:1, tile_rows]
        return carry

    def weight_grads_o(t, carry):
        tile_rows = pl.ds(pl.multiple_of(t * CHUNK, CHUNK), CHUNK)
        weight_grads_a(t, carry, slice(2 * width, 3 * width))
        dw0[tile_rows, 3 * width :] = dot_tn(gy[:, tile_rows], c[...]).astype(bf)
        return carry

    lax.fori_loop(0, model // CHUNK, weight_grads_a, 0)
    scatter.start(4)
    lax.fori_loop(0, model // CHUNK, weight_grads_o, 0)
    scatter.start(5)
    last = []
    for part in range(half // CHUNK):
        there = pl.ds(pl.multiple_of((1 - side) * half + part * CHUNK, CHUNK), CHUNK)
        at = pl.ds(part * CHUNK, CHUNK)
        l_send[at, :] = dot_nt(gqkv[there, :], w1[:, : 3 * width]).astype(bf)
        last.append(remote(l_send.at[at], l_recv.at[at], l_sems.at[0, part], l_sems.at[1, part], place.across()))
        last[part].start()
    scatter.beside(4)
    summed = Total(place, held, t_send, t_recv)
    folded[...] = jnp.zeros_like(folded)

    def fold(head, carry):
        folded[pl.ds(head, 1), :] = fold_rows(fold_near(strip[head]))
        return carry

    lax.fori_loop(0, 2 * pairs, fold, 0)
    table = bucket_sums(folded[...], CHUNK + EDGE, True)
    bucket = lax.broadcasted_iota(jnp.int32, (1, 128), 1)
    for head in range(2 * pairs):
        far = [jnp.sum(far_sums[edge, head]) for edge in range(2)]
        folded[head : head + 1, :128] = jnp.where(
            bucket == NB // 2 - 1, far[0], jnp.where(bucket == NB - 1, far[1], 0.0)
        )
    table = table + folded[:, :128]
    held[0] = jnp.zeros_like(held[0])
    held[0, :8, :] = gain_sums[...] + dec_gains[...]
    held[0, 8:, pl.ds(pl.multiple_of(side * 256, 128), 128)] = table
    held[0, 8:, pl.ds(pl.multiple_of(side * 256 + 128, 128), 128)] = dec_table[...]
    summed.start()
    scatter.beside(5)
    summed.step(0)
    scatter.along(4)
    summed.step(1)
    scatter.total(3)
    for part in range(half // CHUNK):
        here = pl.ds(pl.multiple_of(side * half + part * CHUNK, CHUNK), CHUNK)
        at = pl.ds(part * CHUNK, CHUNK)
        own = dot_nt(gqkv[here, :], w1[:, : 3 * width])
        if part == 0:
            scatter.along(5)
            summed.step(2)
        last[part].wait_recv()
        grad = own + l_recv[at, :].astype(f32)
        pulled, unused = norm_back(n1[pl.ds(half + part * CHUNK, CHUNK), :].astype(f32), gains[0:1, :], grad)
        grad_out[at, :] = state_grad[here, :] + pulled
    scatter.total(4)
    scatter.total(5)
    total_sums[...] = summed.finish()
    for group in range(6):
        scatter.finish(group)
    scatter.close()
    for i in range(late):
        swap_late(i).wait_send()
    for copy in last:
        copy.wait_send()


def enc_backward(wide, x_own, cot_own, cot_other, gains, dec_gains, dec_table, part_own, part_other, dw1, saved):
    half, model = x_own.shape
    rows = 2 * half
    w1, n0, qkv, c, inv, e_all, e1, n1, slope, active, ef = saved
    width, ffn = c.shape[1], active.shape[1]
    pairs = width // PAIR
    steps = rows // CHUNK
    bf, f32 = jnp.bfloat16, jnp.float32
    shape = jax.ShapeDtypeStruct
    dma = pltpu.SemaphoreType.DMA
    return pl.pallas_call(
        functools.partial(enc_backward_kernel, wide),
        in_specs=[any_spec()] * 3 + [vmem_spec()] * 3 + [any_spec()] * 14,
        out_shape=[
            shape((half, model), f32),
            shape((model // wide, 12 * width + 2 * ffn), bf),
            shape((16, model), f32),
            shape((rows - part_other.shape[0], model), bf),
        ],
        out_specs=[vmem_spec()] * 3 + [any_spec()],
        scratch_shapes=[
            pltpu.VMEM(gains.shape, f32),
            pltpu.VMEM((8, model), f32),
            pltpu.VMEM((2, 2 * pairs, 8, 128), f32),
            pltpu.VMEM((8, 2 * NEAR), f32),
            pltpu.VMEM((7 + wide // 2, 16, model), f32),
            pltpu.VMEM(w1.shape, bf),
            pltpu.VMEM(dw1.shape, bf),
            pltpu.VMEM(qkv.shape, bf),
            pltpu.VMEM(c.shape, bf),
            pltpu.VMEM(inv.shape, f32),
            pltpu.VMEM(n1.shape, bf),
            pltpu.VMEM(active.shape, bf),
            pltpu.VMEM((rows, model), bf),
            pltpu.VMEM((2, 2, CHUNK, rows), bf),
            pltpu.VMEM((2, CHUNK, model), f32),
            pltpu.VMEM((2, CHUNK, ffn), bf),
            pltpu.VMEM((2, CHUNK, model), bf),
            pltpu.VMEM((2, CHUNK, model), bf),
            pltpu.VMEM((rows, model), bf),
            pltpu.VMEM((rows, model), bf),
            pltpu.VMEM((half, model), bf),
            pltpu.VMEM((rows, model), f32),
            pltpu.VMEM((rows, model), bf),
            pltpu.VMEM((rows, ffn), bf),
            pltpu.VMEM((rows, 3 * width), bf),
            pltpu.VMEM((rows, width), f32),
            pltpu.VMEM((rows, width), f32),
            pltpu.VMEM((2 * pairs, CHUNK, NEAR), f32),
        ]
        + scatter_buffers(wide, model, 2 * ffn)
        + scatter_buffers(wide, model, 4 * width)[1:]
        + scatter_buffers(wide, model, 4 * width)[1:]
        + [
            dma((6, scatter_slots(wide))),
            dma((6, scatter_slots(wide))),
            dma((2 + wide // 2,)),
            dma((2 + wide // 2,)),
            dma((2, steps)),
            dma((2, steps)),
            dma((2, half // CHUNK)),
            dma((2,)),
            dma((4, 2)),
            dma((10,)),
        ],
        compiler_params=pltpu.CompilerParams(
            collective_id=1, has_side_effects=True, vmem_limit_bytes=VMEM_BYTES
        ),
        cost_estimate=pl.CostEstimate(flops=2 * 10**10, bytes_accessed=6 * 10**7, transcendentals=0),
    )(x_own, cot_own, cot_other, gains, dec_gains, dec_table, part_own, part_other, dw1, w1, n0, qkv, c, inv, e_all, e1, n1, slope, active, ef)


def fold_offsets(grad):
    rows = grad.shape[0]
    total = jnp.zeros((8, 2 * rows), jnp.float32)
    blank = jnp.zeros((8, rows), jnp.float32)
    for a in range(rows // 8):
        wider = jnp.concatenate([grad[8 * a : 8 * a + 8, :], blank], axis=1)
        total = total + pltpu.roll(wider, (rows - 8 * a) % (2 * rows), 1)
    return total


def decoder_kernel(
    wide,
    dec_own,
    dec_other,
    dcot_own,
    dcot_other,
    cot_own,
    down_in,
    gains_in,
    base,
    dec_lengths,
    enc_lengths,
    mem_in,
    w_in,
    dec_out,
    dec_grad,
    tile,
    gain_sums,
    table,
    part_own,
    part_other,
    cot_other,
    dw1_all,
    gains,
    pack,
    folded,
    w,
    mem,
    dec,
    dcot,
    state,
    normals,
    qkv,
    c,
    inv,
    e_self,
    e_cross,
    strip,
    kv,
    active,
    ga,
    gu,
    grad_state,
    gy,
    gqkv,
    gkv,
    y_send,
    y_recv,
    dw,
    core_f,
    beside_f,
    along_f,
    core_d,
    core_c,
    s_send,
    s_recv,
    g_send,
    g_recv,
    g_local,
    y_sems,
    x_sems,
    p_sems,
    o_sems,
    i_sems,
):
    place = Place(wide)
    side = place.side
    half = dec_own.shape[0]
    rows = 2 * half
    model = dec_own.shape[1]
    width = c.shape[2]
    ffn = active.shape[1]
    pairs = width // PAIR
    span = mem.shape[0]
    bf, f32 = jnp.bfloat16, jnp.float32
    place.greet()
    mine = pl.ds(pl.multiple_of(side * half, 16), half)
    theirs = pl.ds(pl.multiple_of((1 - side) * half, 16), half)
    at_d, at_f = 4 * width, 8 * width

    gather = Gather(place, pack, [(0, ffn // 2, w, at_f + ffn), (ffn // 2, ffn // 2, w, at_f + ffn + ffn // 2)], g_send, g_recv, g_local)
    def load_w(first, count, sem):
        cols = pl.ds(first, count)
        return pltpu.make_async_copy(w_in.at[:, cols], w.at[:, cols], i_sems.at[sem])

    loads = [
        load_w(0, 4 * width, 0),
        load_w(at_d, 4 * width, 1),
        pltpu.make_async_copy(mem_in, mem, i_sems.at[2]),
        load_w(at_f, ffn, 3),
        pltpu.make_async_copy(dec_own, dec.at[mine], i_sems.at[4]),
        pltpu.make_async_copy(dcot_own, dcot.at[mine], i_sems.at[5]),
        pltpu.make_async_copy(dec_other, dec.at[theirs], i_sems.at[6]),
        pltpu.make_async_copy(dcot_other, dcot.at[theirs], i_sems.at[7]),
        pltpu.make_async_copy(down_in.at[1], pack, i_sems.at[8]),
    ]
    for index in (8, 4, 6, 0, 5, 7, 2, 1, 3):
        loads[index].start()
    cot_part = cot_own.shape[0] // 4

    def swap_cot(i):
        at = pl.ds(i * cot_part, cot_part)
        return remote(cot_own.at[at], cot_other.at[at], x_sems.at[0, i], x_sems.at[1, i], place.across())

    swap_cot(0).start()
    swap_cot(1).start()
    loads[8].wait()
    gather.start(0)
    gather.start(1)
    build_strip(strip, base, pairs, rows, rows)
    gains[...] = gains_in[...].astype(f32)
    gain_sums[...] = jnp.zeros_like(gain_sums)
    folded[...] = jnp.zeros_like(folded)
    scatter = Scatter(
        place,
        model // wide,
        [
            half_group(w, at_f, ffn, 0, 0, core_f, beside_f, along_f),
            half_group(w, at_f + ffn, ffn, ffn, 1, core_f, beside_f, along_f),
            dict(grad=dw, first=at_d, width=4 * width, core=core_d),
            dict(grad=dw, first=0, width=4 * width, core=core_c),
        ],
        tile,
        s_send,
        s_recv,
    )

    def swap(kind):
        return remote(y_send.at[kind], y_recv.at[kind], y_sems.at[0, kind], y_sems.at[1, kind], place.across())

    def send_branch(kind, value):
        y_send[kind] = value.astype(bf)
        swap(kind).start()

    def branch(kind):
        swap(kind).wait_recv()
        return y_send[kind].astype(f32) + y_recv[kind].astype(f32)

    def lanes(base_lane, pair):
        return pl.ds(pl.multiple_of(base_lane + pair * PAIR, PAIR), PAIR)

    def norm_to(index, gain, value):
        state[index] = value
        normals[index] = normed(value, gains[gain : gain + 1, :]).astype(bf)

    loads[4].wait()
    loads[6].wait()
    norm_to(0, 2, dec[...].astype(f32))
    loads[0].wait()
    qkv[:, : 3 * width] = dot_nn(normals[0], w[:, : 3 * width]).astype(bf)

    def self_pair(pair, carry):
        allowed = documents(dec_lengths, (rows, 1), 0) == documents(dec_lengths, (1, rows), 0)
        allowed = allowed & (
            lax.broadcasted_iota(jnp.int32, (rows, rows), 1) <= lax.broadcasted_iota(jnp.int32, (rows, rows), 0)
        )

        def bias(head):
            return strip[2 * pair + head, :, :rows]

        def store(head, weights):
            e_self[2 * pair + head] = weights

        inverse, context = softmax_pair(
            qkv[:, lanes(0, pair)], qkv[:, lanes(width, pair)], qkv[:, lanes(2 * width, pair)], allowed, bias, store
        )
        inv[0, :, lanes(0, pair)] = inverse
        c[0, :, lanes(0, pair)] = context
        return carry

    lax.fori_loop(0, pairs, self_pair, 0)
    send_branch(0, dot_nt(c[0], w[:, 3 * width : 4 * width]))

    gather.relay_along(0)
    gather.relay_along(1)

    loads[2].wait()
    loads[1].wait()

    def cross_keys(i, carry):
        at = pl.ds(pl.multiple_of(i * CHUNK, CHUNK), CHUNK)
        kv[at, :] = dot_nn(mem[at, :], w[:, at_d + width : at_d + 3 * width]).astype(bf)
        return carry

    lax.fori_loop(0, span // CHUNK, cross_keys, 0)
    gather.relay_beside(0)
    gather.relay_beside(1)
    norm_to(1, 3, state[0] + branch(0))
    swap_cot(2).start()
    qkv[:, 3 * width :] = dot_nn(normals[1], w[:, at_d : at_d + width]).astype(bf)

    def cross_pair(pair, carry):
        allowed = documents(dec_lengths, (rows, 1), 0) == documents(enc_lengths, (1, span), 0)

        def store(head, weights):
            e_cross[2 * pair + head] = weights

        inverse, context = softmax_pair(
            qkv[:, lanes(3 * width, pair)], kv[:, lanes(0, pair)], kv[:, lanes(width, pair)], allowed, None, store
        )
        inv[1, :, lanes(0, pair)] = inverse
        c[1, :, lanes(0, pair)] = context
        return carry

    lax.fori_loop(0, pairs, cross_pair, 0)
    send_branch(1, dot_nt(c[1], w[:, at_d + 3 * width : at_d + 4 * width]))

    for index in (5, 7, 3):
        loads[index].wait()
    gather.finish(0)
    gather.finish(1)
    ga[...] = dot_nn(dcot[...], w[:, at_f + ffn :]).astype(f32)
    norm_to(2, 4, state[1] + branch(1))
    swap_cot(3).start()

    def hidden(j, carry):
        here = pl.ds(pl.multiple_of(j * width, PAIR), width)
        cols = pl.ds(pl.multiple_of(at_f + j * width, PAIR), width)
        value, turn = gelu_pair(dot_nn(normals[2], w[:, cols]))
        active[:, here] = value.astype(bf)
        gu[:, here] = (turn * ga[:, here]).astype(bf)
        return carry

    lax.fori_loop(0, ffn // width, hidden, 0)
    send_branch(3, dot_nt(gu[...], w[:, at_f : at_f + ffn]))
    y_send[2] = dot_nt(active[...], w[:, at_f + ffn :]).astype(bf)

    def up_grads(t, carry):
        tile_rows = pl.ds(pl.multiple_of(t * CHUNK, CHUNK), CHUNK)
        w[tile_rows, at_f : at_f + ffn] = dot_tn(normals[2, :, tile_rows], gu[...]).astype(bf)
        return carry

    def down_grads(t, carry):
        tile_rows = pl.ds(pl.multiple_of(t * CHUNK, CHUNK), CHUNK)
        w[tile_rows, at_f + ffn :] = dot_tn(dcot[:, tile_rows], active[...]).astype(bf)
        return carry

    gather.close()
    lax.fori_loop(0, model // CHUNK, up_grads, 0)
    scatter.start(0)
    lax.fori_loop(0, model // CHUNK, down_grads, 0)
    scatter.start(1)
    scatter.beside(0)

    row = lax.broadcasted_iota(jnp.int32, (rows, 1), 0)
    counted = jnp.where(row // half == side, 1.0, 0.0).astype(f32)

    def pull(index, gain, grad):
        values = state[index]
        pulled, unused = norm_back(values, gains[gain : gain + 1, :], grad)
        scale = lax.rsqrt(jnp.mean(values * values, axis=1, keepdims=True) + EPS) * counted
        gain_sums[gain : gain + 1, :] += jnp.sum(grad * values * scale, axis=0, keepdims=True)
        return pulled

    grad_state[...] = dcot[...].astype(f32) + pull(2, 4, branch(3))
    swap(2).start()
    gy[1] = grad_state[...].astype(bf)
    gc = dot_nn(gy[1], w[:, at_d + 3 * width : at_d + 4 * width]).astype(bf)
    y_send[5, :, :width] = gc
    scatter.beside(1)

    def cross_back(pair, carry):
        gq, gk, gv = softmax_back_pair(
            qkv[:, lanes(3 * width, pair)],
            kv[:, lanes(0, pair)],
            kv[:, lanes(width, pair)],
            c[1, :, lanes(0, pair)],
            inv[1, :, lanes(0, pair)],
            y_send[5, :, lanes(0, pair)],
            (e_cross[2 * pair], e_cross[2 * pair + 1]),
            None,
        )
        gqkv[:, lanes(3 * width, pair)] = gq.astype(bf)
        gkv[:, lanes(0, pair)] = gk.astype(bf)
        gkv[:, lanes(width, pair)] = gv.astype(bf)
        return carry

    lax.fori_loop(0, pairs, cross_back, 0)
    send_branch(4, dot_nt(gqkv[:, 3 * width :], w[:, at_d : at_d + width]))

    part = kv

    def swap_part(i):
        at = pl.ds(pl.multiple_of(i * CHUNK, CHUNK), CHUNK)
        return remote(part.at[at], part_other.at[at], p_sems.at[0, i], p_sems.at[1, i], place.across())

    def keep_part(i):
        at = pl.ds(pl.multiple_of(i * CHUNK, CHUNK), CHUNK)
        return pltpu.make_async_copy(part.at[at], part_own.at[at], o_sems.at[i])

    for i in range(span // CHUNK):
        at = pl.ds(i * CHUNK, CHUNK)
        part[at, :] = dot_nt(gkv[at, :], w[:, at_d + width : at_d + 3 * width]).astype(bf)
        keep_part(i).start()

    def cross_grads(t, carry):
        tile_rows = pl.ds(pl.multiple_of(t * CHUNK, CHUNK), CHUNK)
        dw[tile_rows, at_d : at_d + width] = dot_tn(normals[1, :, tile_rows], gqkv[:, 3 * width :]).astype(bf)
        dw[tile_rows, at_d + width : at_d + 3 * width] = dot_tn(mem[:, tile_rows], gkv[...]).astype(bf)
        dw[tile_rows, at_d + 3 * width : at_f] = dot_tn(gy[1, :, tile_rows], c[1]).astype(bf)
        return carry

    lax.fori_loop(0, model // CHUNK, cross_grads, 0)
    scatter.start(2)
    scatter.along(0)

    grad_state[...] = grad_state[...] + pull(1, 3, branch(4))
    early = part_other.shape[0] // CHUNK
    swap_part(0).start()
    gy[0] = grad_state[...].astype(bf)
    y_send[5, :, :width] = dot_nn(gy[0], w[:, 3 * width : 4 * width]).astype(bf)

    def self_back(pair, carry):
        def near(head, grad):
            folded[pl.ds(2 * pair + head, 1), :] = fold_rows(fold_offsets(grad))

        gq, gk, gv = softmax_back_pair(
            qkv[:, lanes(0, pair)],
            qkv[:, lanes(width, pair)],
            qkv[:, lanes(2 * width, pair)],
            c[0, :, lanes(0, pair)],
            inv[0, :, lanes(0, pair)],
            y_send[5, :, lanes(0, pair)],
            (e_self[2 * pair], e_self[2 * pair + 1]),
            near,
        )
        gqkv[:, lanes(0, pair)] = gq.astype(bf)
        gqkv[:, lanes(width, pair)] = gk.astype(bf)
        gqkv[:, lanes(2 * width, pair)] = gv.astype(bf)
        return carry

    lax.fori_loop(0, pairs, self_back, 0)

    y_send[5] = dot_nt(gqkv[:, : 3 * width], w[:, : 3 * width]).astype(bf)
    back = remote(y_send.at[5, theirs], y_recv.at[5, theirs], y_sems.at[0, 5], y_sems.at[1, 5], place.across())
    back.start()
    for i in range(1, early):
        swap_part(i).start()
    scatter.along(1)
    scatter.merge(2)
    keep_dw = [
        pltpu.make_async_copy(
            dw.at[:, scatter.columns(2 + i, place.core)],
            dw1_all.at[:, pl.ds((1 - i) * 2 * width, 2 * width)],
            i_sems.at[i],
        )
        for i in range(2)
    ]
    keep_dw[0].start()

    def self_grads(t, carry):
        tile_rows = pl.ds(pl.multiple_of(t * CHUNK, CHUNK), CHUNK)
        dw[tile_rows, : 3 * width] = dot_tn(normals[0, :, tile_rows], gqkv[:, : 3 * width]).astype(bf)
        dw[tile_rows, 3 * width : at_d] = dot_tn(gy[0, :, tile_rows], c[0]).astype(bf)
        return carry

    lax.fori_loop(0, model // CHUNK, self_grads, 0)
    scatter.start(3)
    table[...] = bucket_sums(folded[...], rows, False)
    scatter.total(0)
    scatter.total(1)
    back.wait_recv()
    grad = y_send[5, mine, :].astype(f32) + y_recv[5, mine, :].astype(f32)
    pulled, gain = norm_back(state[0, mine, :], gains[2:3, :], grad)
    gain_sums[2:3, :] += gain
    dec_grad[...] = grad_state[mine, :] + pulled
    swap(2).wait_recv()
    dec_out[...] = (state[2, mine, :] + y_send[2, mine, :].astype(f32) + y_recv[2, mine, :].astype(f32)).astype(bf)
    scatter.merge(3)
    keep_dw[1].start()
    for i in range(early):
        swap_part(i).wait()
    for i in range(span // CHUNK):
        keep_part(i).wait()
    for copy in keep_dw:
        copy.wait()
    for i in range(4):
        swap_cot(i).wait()
    for group in range(2):
        scatter.finish(group)
    scatter.close()
    for kind in range(5):
        swap(kind).wait_send()
    back.wait_send()


def decoder(wide, dec_rows, dcot_rows, cot_own, down, gains, base, dec_lengths, enc_lengths, mem, w2):
    half, model = dec_rows[0].shape
    rows = 2 * half
    span = mem.shape[0]
    pairs = base.shape[0]
    width = pairs * PAIR
    ffn = down.shape[2]
    late = span // CHUNK // 2 * CHUNK
    bf, f32 = jnp.bfloat16, jnp.float32
    shape = jax.ShapeDtypeStruct
    dma = pltpu.SemaphoreType.DMA
    return pl.pallas_call(
        functools.partial(decoder_kernel, wide),
        in_specs=[any_spec()] * 6 + [vmem_spec()] * 2 + [smem_spec()] * 2 + [any_spec()] * 2,
        out_shape=[
            shape((half, model), bf),
            shape((half, model), f32),
            shape((model // wide, 2 * ffn), bf),
            shape((8, model), f32),
            shape((8, 128), f32),
            shape((span, model), bf),
            shape((late, model), bf),
            shape(cot_own.shape, bf),
            shape((model, 4 * width), bf),
        ],
        out_specs=[vmem_spec()] * 5 + [any_spec()] * 4,
        scratch_shapes=[
            pltpu.VMEM(gains.shape, f32),
            pltpu.VMEM(down.shape[1:], bf),
            pltpu.VMEM((8, 2 * rows), f32),
            pltpu.VMEM((model, 8 * width + 2 * ffn), bf),
            pltpu.VMEM((span, model), bf),
            pltpu.VMEM((rows, model), bf),
            pltpu.VMEM((rows, model), bf),
            pltpu.VMEM((3, rows, model), f32),
            pltpu.VMEM((3, rows, model), bf),
            pltpu.VMEM((rows, 4 * width), bf),
            pltpu.VMEM((2, rows, width), bf),
            pltpu.VMEM((2, rows, width), f32),
            pltpu.VMEM((2 * pairs, rows, rows), bf),
            pltpu.VMEM((2 * pairs, rows, span), bf),
            pltpu.VMEM((2 * pairs, rows, 2 * rows), f32),
            pltpu.VMEM((span, 2 * width), bf),
            pltpu.VMEM((rows, ffn), bf),
            pltpu.VMEM((rows, ffn), f32),
            pltpu.VMEM((rows, ffn), bf),
            pltpu.VMEM((rows, model), f32),
            pltpu.VMEM((2, rows, model), bf),
            pltpu.VMEM((rows, 4 * width), bf),
            pltpu.VMEM((span, 2 * width), bf),
            pltpu.VMEM((6, rows, model), bf),
            pltpu.VMEM((6, rows, model), bf),
            pltpu.VMEM((model, 8 * width), bf),
        ]
        + scatter_buffers(wide, model, 2 * ffn)
        + scatter_buffers(wide, model, 4 * width)[:1]
        + scatter_buffers(wide, model, 4 * width)[:1]
        + [
            dma((4, scatter_slots(wide))),
            dma((4, scatter_slots(wide))),
            dma((2, gather_slots(wide))),
            dma((2, gather_slots(wide))),
            dma((2,)),
            dma((2, 6)),
            dma((2, 4)),
            dma((2, span // CHUNK)),
            dma((span // CHUNK,)),
            dma((9,)),
        ],
        compiler_params=pltpu.CompilerParams(
            collective_id=2, has_side_effects=True, vmem_limit_bytes=VMEM_BYTES
        ),
        cost_estimate=pl.CostEstimate(flops=10**10, bytes_accessed=6 * 10**7, transcendentals=0),
    )(
        *dec_rows,
        *dcot_rows,
        cot_own,
        down,
        gains,
        base,
        dec_lengths,
        enc_lengths,
        mem,
        w2,
    )


def on_device(
    wide,
    enc_input,
    dec_input,
    enc_lengths,
    dec_lengths,
    attn_query,
    attn_kv,
    attn_out,
    ffn_up,
    ffn_down,
    gains,
    rel_bias,
    enc_cotangent,
    dec_cotangent,
):
    heads_local = rel_bias.shape[2]
    side = lax.axis_index("narrow")
    width, ffn = DK * heads_local, ffn_up.shape[2]
    down = ffn_down.transpose(0, 2, 1)
    weights = (attn_query, attn_kv, attn_out.transpose(0, 2, 1), ffn_up, down)
    w1, w2, n0, qkv, context, inverse, exps, e1, n1, slope, active, ef, memory, dec_other, dcot_other, enc_output = enc_forward(
        wide, enc_input, dec_input, dec_cotangent, weights, gains, near_rows(rel_bias[0]), enc_lengths
    )
    dec_output, grad_dec, tile_two, dec_gains, dec_table, part_own, part_other, cot_other, dw1 = decoder(
        wide,
        (dec_input, dec_other),
        (dec_cotangent, dcot_other),
        enc_cotangent,
        down,
        gains,
        base_rows(rel_bias[1], DEC, False),
        dec_lengths,
        enc_lengths,
        memory,
        w2,
    )
    grad_enc, tile_one, sums, unused = enc_backward(
        wide,
        enc_input,
        enc_cotangent,
        cot_other,
        gains,
        dec_gains,
        dec_table,
        part_own,
        part_other,
        dw1,
        (w1, n0, qkv, context, inverse, exps, e1, n1, slope, active, ef),
    )
    tables = lax.dynamic_slice_in_dim(sums[8 : 8 + heads_local], side * 256, 256, 1)
    bias_grad = jnp.stack([tables[:, :NB].T, tables[:, 128 : 128 + NB].T])
    late = tile_one[:, 4 * width + 2 * ffn :]
    layers = (tile_one[:, : 4 * width], late[:, : 4 * width], late[:, 4 * width :])
    feeds = (tile_one[:, 4 * width : 4 * width + 2 * ffn], tile_two)
    return (
        enc_output,
        dec_output,
        grad_enc,
        grad_dec,
        jnp.stack([layer[:, :width] for layer in layers]).astype(jnp.float32),
        jnp.stack(
            [jnp.stack([layer[:, width : 2 * width], layer[:, 2 * width : 3 * width]]) for layer in layers]
        ).astype(jnp.float32),
        jnp.stack([layer[:, 3 * width :].T for layer in layers]).astype(jnp.float32),
        jnp.stack([feed[:, :ffn] for feed in feeds]).astype(jnp.float32),
        jnp.stack([feed[:, ffn:].T for feed in feeds]).astype(jnp.float32),
        sums[:6],
        bias_grad,
    )


def ffn_backward(grad_rows, normed_rows, hidden, active, weight_up, weight_down):
    grad_active = jnp.einsum(
        "rd,fd->rf", grad_rows, weight_down, preferred_element_type=jnp.float32
    )
    grad_down = jnp.einsum("rf,rd->fd", active, grad_rows, preferred_element_type=jnp.float32)
    unused, pull = jax.vjp(gelu_tanh, hidden)
    grad_hidden = pull(grad_active)[0].astype(jnp.bfloat16)
    grad_up = jnp.einsum("rd,rf->df", normed_rows, grad_hidden, preferred_element_type=jnp.float32)
    grad_normed = jnp.einsum(
        "rf,df->rd", grad_hidden, weight_up, preferred_element_type=jnp.float32
    )
    return (grad_normed, grad_up, grad_down)


def norm_backward(values, gain, grad_normed):
    unused, pull = jax.vjp(rms_norm, values, gain)
    return pull(grad_normed)


def on_device_general(
    enc_input,
    dec_input,
    enc_lengths,
    dec_lengths,
    attn_query,
    attn_kv,
    attn_out,
    ffn_up,
    ffn_down,
    gains,
    rel_bias,
    enc_cotangent,
    dec_cotangent,
):
    weights = (
        lax.all_gather(attn_query, "wide", axis=1, tiled=True),
        lax.all_gather(attn_kv, "wide", axis=2, tiled=True),
        lax.all_gather(attn_out, "wide", axis=2, tiled=True),
        lax.all_gather(ffn_up, "wide", axis=1, tiled=True),
        lax.all_gather(ffn_down, "wide", axis=2, tiled=True),
    )
    gain_rows = gains.astype(jnp.float32)
    heads_local = rel_bias.shape[2]
    enc_segments = segment_ids(enc_lengths[0], ENC)
    dec_segments = segment_ids(dec_lengths[0], DEC)

    side = lax.axis_index("narrow")
    swap = [(0, 1), (1, 0)]

    def spread_rows(values):
        own = values.astype(jnp.bfloat16)
        other = lax.ppermute(own, "narrow", swap)
        return jnp.where(side == 0, jnp.concatenate([own, other]), jnp.concatenate([other, own]))

    def collect_rows(parts):
        half = parts.shape[0] // 2
        parts = parts.astype(jnp.bfloat16)
        other = lax.ppermute(lax.dynamic_slice_in_dim(parts, (1 - side) * half, half), "narrow", swap)
        own = lax.dynamic_slice_in_dim(parts, side * half, half)
        return own.astype(jnp.float32) + other.astype(jnp.float32)

    def attention_layer(normed_query, normed_keys, layer, base, query_segments, key_segments, causal):
        query = jnp.dot(normed_query, weights[0][layer], preferred_element_type=jnp.float32).astype(jnp.bfloat16)
        keys = jnp.dot(normed_keys, weights[1][layer, 0], preferred_element_type=jnp.float32).astype(jnp.bfloat16)
        values = jnp.dot(normed_keys, weights[1][layer, 1], preferred_element_type=jnp.float32).astype(jnp.bfloat16)
        saved = attend_forward(query, keys, values, base, query_segments, key_segments, causal)
        parts = jnp.dot(saved[1], weights[2][layer], preferred_element_type=jnp.float32)
        return ((query, keys, values, saved), collect_rows(parts))

    enc_start = enc_input.astype(jnp.float32)
    rows_a = spread_rows(rms_norm(enc_start, gain_rows[0]))
    kept_a, branch = attention_layer(
        rows_a, rows_a, 0, base_rows(rel_bias[0], ENC, True), enc_segments, enc_segments, False
    )
    enc_mid = enc_start + branch
    rows_b = spread_rows(rms_norm(enc_mid, gain_rows[1]))
    hidden_b = jnp.dot(rows_b, weights[3][0], preferred_element_type=jnp.float32)
    active_b = gelu_tanh(hidden_b).astype(jnp.bfloat16)
    enc_final = enc_mid + collect_rows(
        jnp.dot(active_b, weights[4][0], preferred_element_type=jnp.float32)
    )
    memory = spread_rows(rms_norm(enc_final, gain_rows[5]))
    dec_start = dec_input.astype(jnp.float32)
    rows_c = spread_rows(rms_norm(dec_start, gain_rows[2]))
    kept_c, branch = attention_layer(
        rows_c, rows_c, 1, base_rows(rel_bias[1], DEC, False), dec_segments, dec_segments, True
    )
    dec_one = dec_start + branch
    rows_d = spread_rows(rms_norm(dec_one, gain_rows[3]))
    kept_d, branch = attention_layer(
        rows_d, memory, 2, None, dec_segments, enc_segments, False
    )
    dec_two = dec_one + branch
    rows_e = spread_rows(rms_norm(dec_two, gain_rows[4]))
    hidden_e = jnp.dot(rows_e, weights[3][1], preferred_element_type=jnp.float32)
    active_e = gelu_tanh(hidden_e).astype(jnp.bfloat16)
    dec_final = dec_two + collect_rows(
        jnp.dot(active_e, weights[4][1], preferred_element_type=jnp.float32)
    )
    def attention_back(grad_state, kept, normed_query, normed_keys, layer, span, two_sided):
        grad_rows = spread_rows(grad_state)
        query, keys, values, saved = kept
        grad_context = dot_nt(grad_rows, weights[2][layer]).astype(jnp.bfloat16)
        grad_out = dot_tn(saved[1], grad_rows)
        result = attend_backward(query, keys, values, saved, grad_context, span > 0)
        grad_q, grad_k, grad_v = result[:3]
        sums = [
            dot_tn(normed_query, grad_q),
            dot_tn(normed_keys, grad_k),
            dot_tn(normed_keys, grad_v),
            grad_out,
            table_grad(result[3], span, two_sided) if span else None,
        ]
        query_part = dot_nt(grad_q, weights[0][layer])
        key_part = dot_nt(grad_k, weights[1][layer, 0]) + dot_nt(grad_v, weights[1][layer, 1])
        return (query_part, key_part, sums)

    grad_dec = dec_cotangent.astype(jnp.float32)
    grad_normed, up_e, down_e = ffn_backward(
        spread_rows(grad_dec), rows_e, hidden_e, active_e, weights[3][1], weights[4][1]
    )
    grad_back, gain_e = norm_backward(dec_two, gain_rows[4], collect_rows(grad_normed))
    grad_dec = grad_dec + grad_back
    query_part, memory_part, sums_d = attention_back(
        grad_dec, kept_d, rows_d, memory, 2, 0, False
    )
    grad_normed, grad_memory = collect_rows(query_part), collect_rows(memory_part)
    grad_back, gain_d = norm_backward(dec_one, gain_rows[3], grad_normed)
    grad_dec = grad_dec + grad_back
    query_part, key_part, sums_c = attention_back(
        grad_dec, kept_c, rows_c, rows_c, 1, DEC, False
    )
    grad_back, gain_c = norm_backward(dec_start, gain_rows[2], collect_rows(query_part + key_part))
    grad_dec = grad_dec + grad_back
    grad_enc = enc_cotangent.astype(jnp.float32)
    grad_back, gain_m = norm_backward(enc_final, gain_rows[5], grad_memory)
    grad_enc = grad_enc + grad_back
    grad_normed, up_b, down_b = ffn_backward(
        spread_rows(grad_enc), rows_b, hidden_b, active_b, weights[3][0], weights[4][0]
    )
    grad_back, gain_b = norm_backward(enc_mid, gain_rows[1], collect_rows(grad_normed))
    grad_enc = grad_enc + grad_back
    query_part, key_part, sums_a = attention_back(
        grad_enc, kept_a, rows_a, rows_a, 0, ENC, True
    )
    grad_back, gain_a = norm_backward(enc_start, gain_rows[0], collect_rows(query_part + key_part))
    grad_enc = grad_enc + grad_back
    grad_query = jnp.stack([sums_a[0], sums_c[0], sums_d[0]])
    grad_kv = jnp.stack(
        [
            jnp.stack([sums_a[1], sums_a[2]]),
            jnp.stack([sums_c[1], sums_c[2]]),
            jnp.stack([sums_d[1], sums_d[2]]),
        ]
    )
    grad_out = jnp.stack([sums_a[3], sums_c[3], sums_d[3]])
    grad_up = jnp.stack([up_b, up_e])
    grad_down = jnp.stack([down_b, down_e])
    tiles = (
        lax.psum_scatter(
            grad_query.astype(jnp.bfloat16), "wide", scatter_dimension=1, tiled=True
        ).astype(jnp.float32),
        lax.psum_scatter(
            grad_kv.astype(jnp.bfloat16), "wide", scatter_dimension=2, tiled=True
        ).astype(jnp.float32),
        lax.psum_scatter(
            grad_out.astype(jnp.bfloat16), "wide", scatter_dimension=2, tiled=True
        ).astype(jnp.float32),
        lax.psum_scatter(
            grad_up.astype(jnp.bfloat16), "wide", scatter_dimension=1, tiled=True
        ).astype(jnp.float32),
        lax.psum_scatter(
            grad_down.astype(jnp.bfloat16), "wide", scatter_dimension=2, tiled=True
        ).astype(jnp.float32),
    )
    tiles = (
        lax.psum(tiles[0].astype(jnp.bfloat16), "dp").astype(jnp.float32),
        lax.psum(tiles[1].astype(jnp.bfloat16), "dp").astype(jnp.float32),
        lax.psum(tiles[2].astype(jnp.bfloat16), "dp").astype(jnp.float32),
        lax.psum(tiles[3].astype(jnp.bfloat16), "dp").astype(jnp.float32),
        lax.psum(tiles[4].astype(jnp.bfloat16), "dp").astype(jnp.float32),
    )
    gain_grads = jnp.stack([gain_a, gain_b, gain_c, gain_d, gain_e, gain_m])
    column = lax.axis_index("narrow") * heads_local
    bias_local = jnp.stack([sums_a[4], sums_c[4]])
    bias_full = lax.dynamic_update_slice(
        jnp.zeros((2, NB, H), jnp.float32), bias_local, (0, 0, column)
    )
    gain_total, bias_total = lax.psum((gain_grads, bias_full), ("dp", "wide", "narrow"))
    bias_grad = lax.dynamic_slice(bias_total, (0, 0, column), (2, NB, heads_local))
    return (
        enc_final.astype(jnp.bfloat16),
        dec_final.astype(jnp.bfloat16),
        grad_enc,
        grad_dec,
        tiles[0],
        tiles[1],
        tiles[2],
        tiles[3],
        tiles[4],
        gain_total,
        bias_grad,
    )


def solution(mesh):
    wide = mesh.shape["wide"]

    def body(*args):
        if args[4].shape[1] % 16 or wide % 2:
            return on_device_general(*args)
        return on_device(wide, *args)

    return jax.shard_map(
        body,
        mesh=mesh,
        in_specs=(
            P(("dp", "wide", "narrow"), None),
            P(("dp", "wide", "narrow"), None),
            P(("dp", "wide"), None),
            P(("dp", "wide"), None),
            P(None, "wide", "narrow"),
            P(None, None, "wide", "narrow"),
            P(None, "narrow", "wide"),
            P(None, "wide", "narrow"),
            P(None, "narrow", "wide"),
            P(),
            P(None, None, "narrow"),
            P(("dp", "wide", "narrow"), None),
            P(("dp", "wide", "narrow"), None),
        ),
        out_specs=(
            P(("dp", "wide", "narrow"), None),
            P(("dp", "wide", "narrow"), None),
            P(("dp", "wide", "narrow"), None),
            P(("dp", "wide", "narrow"), None),
            P(None, "wide", "narrow"),
            P(None, None, "wide", "narrow"),
            P(None, "narrow", "wide"),
            P(None, "wide", "narrow"),
            P(None, "narrow", "wide"),
            P(),
            P(None, None, "narrow"),
        ),
        check_vma=False,
    )
```
